32 devices in a mesh: seq: 2 (over core), batch: 16 (over z, y, x).
Axes of the slice: x: 2, y: 2, z: 4, core: 2. Of those that a mesh axis runs over, the one named last changes fastest.
Arguments:
- block_input: bfloat16 [16, 1024, 512], P('batch', 'seq')
- lengths: int32 [16], P('batch'), may hold values from 513 to 1024, as said below
- spans: int32 [16, 4], P('batch'), may hold values from 0 to 984, as said below
- cotangent: bfloat16 [16, 1024, 512], P('batch', 'seq'), may hold values from -6 to 6
- ffn_in: bfloat16 [2, 2048, 512], P(None, ('seq', 'batch')), may hold values from -0.25 to 0.25
- ffn_out: bfloat16 [2, 2048, 512], P(None, ('seq', 'batch')), may hold values from -0.125 to 0.125
- qkv_weight: bfloat16 [3, 512, 512], P(None, None, 'seq'), may hold values from -0.25 to 0.25
- out_weight: bfloat16 [512, 512], replicated, may hold values from -1 to 1
- conv_in: bfloat16 [512, 1024], replicated, may hold values from -0.25 to 0.25
- kernel: float32 [32, 512], replicated, may hold values from -1 to 1
- conv_out: bfloat16 [512, 512], replicated, may hold values from -0.25 to 0.25
- vectors: float32 [12, 512], replicated
Outputs:
- block_output: bfloat16 [16, 1024, 512], P('batch', 'seq')
- input_grad: float32 [16, 1024, 512], P('batch', 'seq')
- ffn_in_grad: float32 [2, 2048, 512], P(None, ('seq', 'batch'))
- ffn_out_grad: float32 [2, 2048, 512], P(None, ('seq', 'batch'))
- qkv_grad: float32 [3, 512, 512], P(None, None, 'seq')
- out_weight_grad: float32 [512, 512], replicated
- conv_in_grad: float32 [512, 1024], replicated
- kernel_grad: float32 [32, 512], replicated
- conv_out_grad: float32 [512, 512], replicated
- vectors_grad: float32 [12, 512], replicated
The draws below stay inside these ranges and needn't reach their ends.
Inputs may be any that keep to these rules, and one draw needn't show every extreme that they name: `lengths`: utterance 0 has exactly 1024 frames and utterance 1 exactly 1024 - 1024 // 2 + 1; the others lie between. `spans`: columns: time mask start, time mask width up to 40, channel mask start, channel mask width up to 64; each mask lies inside 0..1023 and 0..511; utterance 0 has both masks of the widest width at the last positions, utterance 1 a time mask from frame 0.
All inputs are finite; a program needn't handle non-finite values.
Results may differ from the reference program's by a relative error of at most 0.02.
Values may be sent and summed in bfloat16 or wider, within the bound.
A program may use at most 192 MiB of HBM per device.

```python
import math
import jax
import jax.numpy as jnp
from jax import lax

D = 512
HEADS = 8
FF = 2048
KERNEL = 32
UTT = 1
LEN = 1024
TMASK = 40
FMASK = 64
UTTERANCES = 16
N_SEQ = 2


def draw_block_input(key, part):
    own_key = jax.random.fold_in(key, 5)
    noise_key, shared_key = jax.random.split(own_key)
    noise_part = jax.random.normal(noise_key, (UTTERANCES, LEN, D), jnp.float32)
    shared = jax.random.normal(shared_key, (D,), jnp.float32)
    rising = 0.5 + 2.5 * jnp.arange(UTTERANCES, dtype=jnp.float32) / max(UTTERANCES - 1, 1)
    return (noise_part + rising[:, None, None] * shared[None, None, :]).astype(jnp.bfloat16)


def draw_lengths(key, part):
    own_key = jax.random.fold_in(key, 7)
    shortest = LEN - LEN // N_SEQ + 1
    drawn = jax.random.randint(own_key, (UTTERANCES,), shortest, LEN + 1)
    drawn = drawn.at[0].set(LEN).at[1].set(shortest)
    return drawn.astype(jnp.int32)


def draw_spans(key, part):
    own_key = jax.random.fold_in(key, 9)
    span_keys = jax.random.split(own_key, 4)
    time_start = jax.random.randint(span_keys[0], (UTTERANCES,), 0, LEN - TMASK + 1)
    time_width = jax.random.randint(span_keys[1], (UTTERANCES,), 0, TMASK + 1)
    chan_start = jax.random.randint(span_keys[2], (UTTERANCES,), 0, D - FMASK + 1)
    chan_width = jax.random.randint(span_keys[3], (UTTERANCES,), 0, FMASK + 1)
    time_start = time_start.at[0].set(LEN - TMASK).at[1].set(0)
    time_width = time_width.at[0].set(TMASK)
    chan_start = chan_start.at[0].set(D - FMASK)
    chan_width = chan_width.at[0].set(FMASK)
    return jnp.stack([time_start, time_width, chan_start, chan_width], axis=1).astype(jnp.int32)


def draw_vectors(key, part):
    own_key = jax.random.fold_in(key, 11)
    noise_part = jax.random.normal(own_key, (12, D), jnp.float32)
    gain_rows = jnp.arange(12)[:, None] % 2 == 0
    return jnp.where(gain_rows, 1.0 + 0.25 * noise_part, 0.3 * noise_part).astype(jnp.float32)


def steps_of(rng, dims, cuts, least, high):
    def one(dim, parts):
        draws = jax.random.uniform(jax.random.fold_in(jax.random.fold_in(rng, 6), dim), (parts,), jnp.float32, least / len(cuts), high / len(cuts))
        return jnp.repeat(jnp.exp(draws), dims[dim] // parts).reshape((-1,) + (1,) * (len(dims) - dim - 1))

    gain = one(*cuts[0])
    for cut in cuts[1:]:
        gain = gain * one(*cut)
    return gain


def scatter_about(key, dims, scale, reach, cuts=(), kind=jnp.bfloat16):
    values = scale * jax.random.normal(key, dims, jnp.float32)
    if cuts:
        values = values * steps_of(key, dims, cuts, -0.22, 0.18)
    return jnp.clip(values, -reach, reach).astype(kind)


def setup_inputs(seed: int = 0) -> dict:
    keys = jax.random.split(jax.random.key(seed), 13)
    return {
        "block_input": draw_block_input(jax.random.fold_in(keys[12], 71), 0),
        "lengths": draw_lengths(jax.random.fold_in(keys[12], 71), 0),
        "spans": draw_spans(jax.random.fold_in(keys[12], 71), 0),
        "cotangent": scatter_about(keys[3], (UTTERANCES, LEN, D), 1.0, 6.0, ((0, 16), (1, 2))),
        "ffn_in": scatter_about(keys[4], (2, FF, D), D ** -0.5, 0.25, ((1, 32),)),
        "ffn_out": scatter_about(keys[5], (2, FF, D), FF ** -0.5, 0.125, ((1, 32),)),
        "qkv_weight": scatter_about(keys[6], (3, D, D), D ** -0.5, 0.25, ((2, 2),)),
        "out_weight": scatter_about(keys[7], (D, D), (D // 16) ** -0.5, 1.0),
        "conv_in": scatter_about(keys[8], (D, 2 * D), D ** -0.5, 0.25),
        "kernel": scatter_about(keys[9], (KERNEL, D), KERNEL ** -0.5, 1.0, (), jnp.float32),
        "conv_out": scatter_about(keys[10], (D, D), D ** -0.5, 0.25),
        "vectors": draw_vectors(jax.random.fold_in(keys[12], 71), 0),
    }


@jax.custom_vjp
def low(v):
    return lax.optimization_barrier(v.astype(jnp.bfloat16)).astype(jnp.float32)

@jax.custom_vjp
def low_back(v):
    return v

def low_keep(v):
    return (low(v), None)

def low_pass(kept, grad):
    return (grad,)

def back_keep(v):
    return (v, None)

def back_low(kept, grad):
    return (low(grad),)
low.defvjp(low_keep, low_pass)
low_back.defvjp(back_keep, back_low)

def layer_norm(values, gain_row, bias_row):
    average = lax.optimization_barrier(jnp.mean(values, -1, keepdims=True))
    centred = values - average
    spread = lax.optimization_barrier(jnp.mean(centred * centred, -1, keepdims=True))
    return centred * lax.rsqrt(spread + 1e-05) * gain_row + bias_row

def feed_forward(values, w_inner, w_outer, gain_row, bias_row):
    normed = low(layer_norm(values, gain_row, bias_row))
    inner = low_back(jnp.einsum('utd,fd->utf', normed, w_inner, precision=lax.Precision.HIGHEST))
    active = low(jax.nn.silu(inner))
    return low_back(jnp.einsum('utf,fd->utd', active, w_outer, precision=lax.Precision.HIGHEST))

def score_block(query_block, key_all, value_all, key_ok):
    score_scale = 1.0 / math.sqrt(key_all.shape[-1])
    scores = low_back(jnp.einsum('uqhd,ukhd->uhqk', query_block, key_all, precision=lax.Precision.HIGHEST) * score_scale)
    scores = jnp.where(key_ok, scores, -1e+30)
    probs = low(jax.nn.softmax(scores, axis=-1))
    return jnp.einsum('uhqk,ukhd->uqhd', probs, value_all, precision=lax.Precision.HIGHEST)

def attention(values, lengths_group, qkv_w, out_w, gain_row, bias_row):
    normed = low(layer_norm(values, gain_row, bias_row))
    projected = low_back(low(jnp.einsum('utd,sde->sute', normed, qkv_w, precision=lax.Precision.HIGHEST)))
    head_size = D // HEADS
    split_heads = projected.reshape(3, UTT, LEN, HEADS, head_size)
    key_ok = (jnp.arange(LEN)[None, :] < lengths_group[:, None])[:, None, None, :]
    block_rows = min(512, LEN)
    block_count = LEN // block_rows
    query_blocks = split_heads[0].reshape(UTT, block_count, block_rows, HEADS, head_size).transpose(1, 0, 2, 3, 4)
    score_ck = jax.checkpoint(score_block)
    outputs = lax.map(lambda query_block: score_ck(query_block, split_heads[1], split_heads[2], key_ok), query_blocks)
    merged = outputs.transpose(1, 0, 2, 3, 4).reshape(UTT, LEN, D)
    merged = low_back(low(merged))
    return low_back(jnp.einsum('utd,de->ute', merged, out_w, precision=lax.Precision.HIGHEST))

def conv_front(values, valid_group, conv_in_w, kernel_w, gain_row, bias_row):
    normed = low(layer_norm(values, gain_row, bias_row))
    pointwise = low_back(jnp.einsum('utd,de->ute', normed, conv_in_w, precision=lax.Precision.HIGHEST))
    gated_rows = pointwise[..., :D] * jax.nn.sigmoid(pointwise[..., D:]) * valid_group
    left_pad = (KERNEL - 1) // 2
    padded = jnp.pad(gated_rows, ((0, 0), (left_pad, KERNEL - 1 - left_pad), (0, 0)))
    depth = jnp.zeros_like(gated_rows)
    for tap_index in range(KERNEL):
        depth = depth + kernel_w[tap_index] * padded[:, tap_index:tap_index + LEN]
    return depth

def section_one(inputs, valid_group, keep_group, lengths_group, front):
    ffn_inner, ffn_outer, qkv_w, out_w, conv_in_w, kernel_w, vector_w = front
    start_rows = inputs * keep_group
    after_first = start_rows + 0.5 * feed_forward(start_rows, ffn_inner[0], ffn_outer[0], vector_w[0], vector_w[1])
    after_att = after_first + attention(after_first, lengths_group, qkv_w, out_w, vector_w[2], vector_w[3])
    depth = conv_front(after_att, valid_group, conv_in_w, kernel_w, vector_w[4], vector_w[5])
    return (after_att, depth)

def section_two(after_att, depth, bn_mean, bn_scale, behind):
    conv_out_w, ffn_inner, ffn_outer, vector_w = behind
    normed = (depth - bn_mean) * bn_scale * vector_w[6] + vector_w[7]
    active = low(jax.nn.silu(normed))
    after_conv = after_att + low_back(jnp.einsum('utd,de->ute', active, conv_out_w, precision=lax.Precision.HIGHEST))
    after_second = after_conv + 0.5 * feed_forward(after_conv, ffn_inner[1], ffn_outer[1], vector_w[8], vector_w[9])
    return layer_norm(after_second, vector_w[10], vector_w[11])

def reference(block_input, lengths, spans, cotangent, ffn_in, ffn_out, qkv_weight, out_weight, conv_in, kernel, conv_out, vectors):
    groups = UTTERANCES // UTT
    frames = jnp.arange(LEN)
    channels = jnp.arange(D)
    valid_mask = (frames[None, :] < lengths[:, None]).astype(jnp.float32)[:, :, None]
    time_cut = ((frames[None, :] >= spans[:, 0:1]) & (frames[None, :] < spans[:, 0:1] + spans[:, 1:2])).astype(jnp.float32)
    chan_cut = ((channels[None, :] >= spans[:, 2:3]) & (channels[None, :] < spans[:, 2:3] + spans[:, 3:4])).astype(jnp.float32)
    keep_mask = valid_mask * (1.0 - time_cut)[:, :, None] * (1.0 - chan_cut)[:, None, :]

    def shape_groups(values):
        return values.reshape((groups, UTT) + values.shape[1:])
    group_valid = shape_groups(valid_mask)
    group_keep = shape_groups(keep_mask)
    group_lengths = shape_groups(lengths)
    first_ck = jax.checkpoint(section_one)
    second_ck = jax.checkpoint(section_two)

    def forward(inputs, ffn_inner, ffn_outer, qkv_w, out_w, conv_in_w, kernel_w, conv_out_w, vector_w):
        front = (ffn_inner, ffn_outer, qkv_w, out_w, conv_in_w, kernel_w, vector_w)
        middle, depth = lax.map(lambda group_data: first_ck(group_data[0], group_data[1], group_data[2], group_data[3], front), (shape_groups(inputs), group_valid, group_keep, group_lengths))
        frame_count = jnp.sum(group_valid)
        bn_mean = lax.optimization_barrier(jnp.sum(depth * group_valid, (0, 1, 2))) / frame_count
        bn_var = lax.optimization_barrier(jnp.sum(depth * depth * group_valid, (0, 1, 2))) / frame_count - bn_mean * bn_mean
        bn_scale = lax.rsqrt(bn_var + 1e-05)
        behind = (conv_out_w, ffn_inner, ffn_outer, vector_w)
        outputs = lax.map(lambda group_data: second_ck(group_data[0], group_data[1], bn_mean, bn_scale, behind), (middle, depth))
        return outputs.reshape(UTTERANCES, LEN, D)
    primal, back_fn = jax.vjp(forward, block_input.astype(jnp.float32), ffn_in.astype(jnp.float32), ffn_out.astype(jnp.float32), qkv_weight.astype(jnp.float32), out_weight.astype(jnp.float32), conv_in.astype(jnp.float32), kernel.astype(jnp.float32), conv_out.astype(jnp.float32), vectors.astype(jnp.float32))
    grads = back_fn(cotangent.astype(jnp.float32))
    return (primal.astype(jnp.bfloat16), grads[0], grads[1], grads[2], grads[3], grads[4], grads[5], grads[6], grads[7], grads[8])
```

```python
import functools
import math

import jax
import jax.numpy as jnp
from jax import lax
from jax.experimental import pallas as pl
from jax.experimental.pallas import tpu as pltpu
from jax.sharding import PartitionSpec as P

HEADS = 8
MESH = pl.DeviceIdType.MESH
VMEM_BYTES = 60 * 1024 * 1024


class Routes:
    def __init__(self, count):
        if count == 16:
            first, last, middle = (1, 2), (2, 2), (4, 4)
        elif count == 128:
            first, last, middle = (1, 4), (32, 4), (4, 8)
        else:
            first, last, middle = (1, 1), (1, 1), (1, count)
        self.count = count
        self.side = first[1]
        self.deep = middle[1]
        self.first, self.last, self.middle = first, last, middle

    def here(self):
        self.core = lax.axis_index("seq")
        self.me = lax.axis_index("batch")
        turn = self.core * (self.last[0] - self.first[0])
        self.one = self.first[0] + turn
        self.two = self.last[0] - turn
        self.mid = self.middle[0]
        self.p = lax.rem(lax.div(self.me, self.one), self.side)
        self.q = lax.rem(lax.div(self.me, self.two), self.side)
        self.z = lax.rem(lax.div(self.me, self.mid), self.deep)
        return self

    def index(self, z, p, q):
        return z * self.mid + p * self.one + q * self.two

    def peers(self):
        found = []
        for k in range(1, self.deep):
            found.append(self.index(lax.rem(self.z + k, self.deep), self.p, self.q))
        for k in range(1, self.side):
            found.append(self.index(self.z, lax.rem(self.p + k, self.side), self.q))
            found.append(self.index(self.z, self.p, lax.rem(self.q + k, self.side)))
        return found

    def greet(self):
        barrier = pltpu.get_barrier_semaphore()
        places = self.peers()
        for place in places:
            pl.semaphore_signal(
                barrier, inc=1, device_id={"batch": place}, device_id_type=MESH
            )
        pl.semaphore_signal(
            barrier, inc=1, device_id={"seq": 1 - self.core}, device_id_type=MESH
        )
        pl.semaphore_wait(barrier, len(places) + 1)


def to_batch(src, dst, send, recv, place):
    return pltpu.make_async_remote_copy(
        src_ref=src, dst_ref=dst, send_sem=send, recv_sem=recv,
        device_id={"batch": place}, device_id_type=MESH,
    )


def to_core(src, dst, send, recv, core):
    return pltpu.make_async_remote_copy(
        src_ref=src, dst_ref=dst, send_sem=send, recv_sem=recv,
        device_id={"seq": core}, device_id_type=MESH,
    )


def gather_steps(route, chunk, held, sends, recv, with_core=True):
    started = []
    core, count = route.core, route.count

    def block(place):
        return core * count + place

    def arrive(place):
        here = held.at[chunk, block(place)]
        to_batch(here, here, recv.at[chunk, block(place)], recv.at[chunk, block(place)], route.me).wait_recv()

    def send(place, target):
        slot = len(started)
        here = held.at[chunk, block(place)]
        copy = to_batch(here, here, sends.at[chunk, slot], recv.at[chunk, block(place)], target)
        copy.start()
        started.append(copy)

    def cross(place):
        if not with_core:
            return
        slot = len(started)
        here = held.at[chunk, block(place)]
        copy = to_core(here, here, sends.at[chunk, slot], recv.at[chunk, block(place)], 1 - core)
        copy.start()
        started.append(copy)

    def step_mid():
        for k in range(1, route.deep):
            send(route.me, route.index(lax.rem(route.z + k, route.deep), route.p, route.q))
        cross(route.me)

    def step_one():
        for d in range(route.deep):
            z = lax.rem(route.z + d, route.deep)
            place = route.index(z, route.p, route.q)
            if d:
                arrive(place)
            for k in range(1, route.side):
                send(place, route.index(route.z, lax.rem(route.p + k, route.side), route.q))
            if d:
                cross(place)

    def step_two():
        for d in range(route.deep):
            z = lax.rem(route.z + d, route.deep)
            for e in range(route.side):
                p = lax.rem(route.p + e, route.side)
                place = route.index(z, p, route.q)
                if e:
                    arrive(place)
                for k in range(1, route.side):
                    send(place, route.index(route.z, route.p, lax.rem(route.q + k, route.side)))
                if e:
                    cross(place)

    def step_last():
        for d in range(route.deep):
            z = lax.rem(route.z + d, route.deep)
            for e in range(route.side):
                p = lax.rem(route.p + e, route.side)
                for f in range(1, route.side):
                    place = route.index(z, p, lax.rem(route.q + f, route.side))
                    arrive(place)
                    cross(place)

    def step_end():
        if with_core:
            for place in range(count):
                other = held.at[chunk, (1 - core) * count + place]
                at = recv.at[chunk, (1 - core) * count + place]
                to_core(other, other, at, at, 1 - core).wait_recv()
        for copy in started:
            copy.wait_send()

    return [step_mid, step_one, step_two, step_last, step_end]


def sends_of(route):
    return (route.deep - 1) + route.deep * (route.side - 1) * (1 + route.side) + route.count


def run_steps(all_steps):
    depth = len(all_steps[0])
    for turn in range(depth + len(all_steps) - 1):
        for chunk, steps in enumerate(all_steps):
            if 0 <= turn - chunk < depth:
                steps[turn - chunk]()


def gather_kernel(count, mine, held, local, sends, recv):
    route = Routes(count).here()
    chunks = mine.shape[0]
    copies = []
    for chunk in range(chunks):
        own = held.at[chunk, route.core * count + route.me]
        copy = pltpu.make_async_copy(mine.at[chunk], own, local.at[chunk])
        copy.start()
        copies.append(copy)
    route.greet()
    for copy in copies:
        copy.wait()
    run_steps([gather_steps(route, chunk, held, sends, recv) for chunk in range(chunks)])


def gather_all(mine, count, collective_id):
    chunks, rows, width = mine.shape
    route = Routes(count)
    return pl.pallas_call(
        functools.partial(gather_kernel, count),
        out_shape=jax.ShapeDtypeStruct((chunks, 2 * count, rows, width), mine.dtype),
        in_specs=[pl.BlockSpec(memory_space=pltpu.VMEM)],
        out_specs=pl.BlockSpec(memory_space=pltpu.VMEM),
        scratch_shapes=[
            pltpu.SemaphoreType.DMA((chunks,)),
            pltpu.SemaphoreType.DMA((chunks, sends_of(route))),
            pltpu.SemaphoreType.DMA((chunks, 2 * count)),
        ],
        compiler_params=pltpu.CompilerParams(
            collective_id=collective_id, has_side_effects=True, vmem_limit_bytes=VMEM_BYTES
        ),
    )(mine)


def reduce_kernel(count, solo, n, *refs):
    pieces, (fin, held, grads, packing, *rest) = refs[:n], refs[n:]
    copies = []
    at = 0
    for i, piece in enumerate(pieces):
        lines = piece.shape[1]
        copy = pltpu.make_async_copy(piece, grads.at[:, pl.ds(at, lines)], packing.at[i])
        copy.start()
        copies.append(copy)
        at += lines
    for copy in copies:
        copy.wait()
    reduce_packed(count, solo, grads, fin, held, *rest)


def reduce_packed(count, solo, grads, fin, held, zero, one, two, three, s0, r0, s1, r1, s2, r2, s3, r3, sends, recv):
    route = Routes(count).here()
    core, me, side, deep = route.core, route.me, route.side, route.deep
    rows, width = grads.shape[1:]
    piece = 16

    def add(target, source):
        @pl.loop(0, rows // piece)
        def _(i):
            at = pl.ds(pl.multiple_of(i * piece, piece), piece)
            target[at] = (target[at].astype(jnp.float32) + source[at].astype(jnp.float32)).astype(target.dtype)

    route.greet()
    waits = []
    order = []
    for f in range(side - 1, -1, -1):
        for d in range(deep):
            for e in range(side - 1, -1, -1):
                order.append((d, e, f))
    for d, e, f in order:
        place = route.index(lax.rem(route.z + d, deep), lax.rem(route.p + e, side), lax.rem(route.q + f, side))
        copy = to_core(grads.at[(1 - core) * count + place], zero.at[place], s0.at[place], r0.at[place], 1 - core)
        copy.start()
        waits.append(copy)
    for e in range(side - 1, -1, -1):
        for d in range(deep):
            for f in range(side - 1, -1, -1):
                z, p, q = lax.rem(route.z + d, deep), lax.rem(route.p + e, side), lax.rem(route.q + f, side)
                place = route.index(z, p, q)
                to_core(zero.at[place], zero.at[place], s0.at[place], r0.at[place], 1 - core).wait_recv()
                add(zero.at[place], grads.at[core * count + place])
                if e:
                    slot = (e - 1) * deep * side + z * side + q
                    copy = to_batch(
                        zero.at[place], one.at[slot], s1.at[slot], r1.at[slot], route.index(route.z, p, route.q)
                    )
                    copy.start()
                    waits.append(copy)
    for f in range(side - 1, -1, -1):
        for d in range(deep):
            z, q = lax.rem(route.z + d, deep), lax.rem(route.q + f, side)
            place = route.index(z, route.p, q)
            for e in range(1, side):
                slot = (e - 1) * deep * side + z * side + q
                to_batch(one.at[slot], one.at[slot], s1.at[slot], r1.at[slot], me).wait_recv()
                add(zero.at[place], one.at[slot])
            if f:
                slot = (f - 1) * deep + z
                copy = to_batch(
                    zero.at[place], two.at[slot], s2.at[slot], r2.at[slot], route.index(route.z, route.p, q)
                )
                copy.start()
                waits.append(copy)
    for d in range(deep - 1, -1, -1):
        z = lax.rem(route.z + d, deep)
        place = route.index(z, route.p, route.q)
        for f in range(1, side):
            slot = (f - 1) * deep + z
            to_batch(two.at[slot], two.at[slot], s2.at[slot], r2.at[slot], me).wait_recv()
            add(zero.at[place], two.at[slot])
        if d:
            copy = to_batch(zero.at[place], three.at[d - 1], s3.at[d - 1], r3.at[d - 1], place)
            copy.start()
            waits.append(copy)
    for d in range(1, deep):
        to_batch(three.at[d - 1], three.at[d - 1], s3.at[d - 1], r3.at[d - 1], me).wait_recv()

    def final(at):
        total = zero[me, at].astype(jnp.float32)
        for d in range(1, deep):
            total = total + three[d - 1, at].astype(jnp.float32)
        return total

    mine = core * count + me

    @pl.loop(0, (rows - solo) // piece)
    def _(i):
        at = pl.ds(pl.multiple_of(i * piece, piece), piece)
        held[0, mine, at] = final(pl.ds(pl.multiple_of(solo + i * piece, piece), piece)).astype(held.dtype)

    steps = gather_steps(route, 0, held, sends, recv)
    steps[0]()

    @pl.loop(0, solo // piece)
    def _(i):
        at = pl.ds(pl.multiple_of(i * piece, piece), piece)
        fin[at] = final(at)

    for step in steps[1:]:
        step()
    for copy in waits:
        copy.wait_send()


def reduce_all(pieces, solo, count, collective_id):
    blocks, _, width = pieces[0].shape
    kind = pieces[0].dtype
    if any(piece.shape[1] % 16 for piece in pieces):
        used = sum(piece.shape[1] for piece in pieces)
        spare = jnp.zeros((blocks, -used % 16, width), kind)
        pieces = [jnp.concatenate([*pieces, spare], axis=1)]
    rows = sum(piece.shape[1] for piece in pieces)
    route = Routes(count)
    side, deep = route.side, route.deep
    n1 = max(1, (side - 1) * side * deep)
    n2 = max(1, (side - 1) * deep)
    n3 = max(1, deep - 1)
    dma = pltpu.SemaphoreType.DMA
    return pl.pallas_call(
        functools.partial(reduce_kernel, count, solo, len(pieces)),
        out_shape=(
            jax.ShapeDtypeStruct((solo, width), jnp.float32),
            jax.ShapeDtypeStruct((1, blocks, rows - solo, width), kind),
        ),
        in_specs=[pl.BlockSpec(memory_space=pl.ANY)] * len(pieces),
        out_specs=(pl.BlockSpec(memory_space=pltpu.VMEM), pl.BlockSpec(memory_space=pltpu.VMEM)),
        scratch_shapes=[
            pltpu.VMEM((blocks, rows, width), kind),
            dma((len(pieces),)),
            pltpu.VMEM((count, rows, width), kind),
            pltpu.VMEM((n1, rows, width), kind),
            pltpu.VMEM((n2, rows, width), kind),
            pltpu.VMEM((n3, rows, width), kind),
            dma((count,)), dma((count,)),
            dma((n1,)), dma((n1,)),
            dma((n2,)), dma((n2,)),
            dma((n3,)), dma((n3,)),
            dma((1, sends_of(route))), dma((1, blocks)),
        ],
        compiler_params=pltpu.CompilerParams(
            collective_id=collective_id, has_side_effects=True, vmem_limit_bytes=VMEM_BYTES
        ),
    )(*pieces)


F32, LOW = jnp.float32, jnp.bfloat16
EPS = 1e-05
HALO = 16


def nn(a, b):
    return lax.dot_general(a, b, (((1,), (0,)), ((), ())), preferred_element_type=F32)


def nt(a, b):
    return lax.dot_general(a, b, (((1,), (1,)), ((), ())), preferred_element_type=F32)


def tn(a, b):
    return lax.dot_general(a, b, (((0,), (0,)), ((), ())), preferred_element_type=F32)


def sigmoid(v):
    return 0.5 * jnp.tanh(0.5 * v) + 0.5


def rows_of(i, size):
    return pl.ds(pl.multiple_of(i * size, size), size)


def normed(v):
    centred = v - jnp.mean(v, -1, keepdims=True)
    scale = lax.rsqrt(jnp.mean(centred * centred, -1, keepdims=True) + EPS)
    return centred * scale, scale


def normed_back(grad, hat, scale):
    return scale * (
        grad - jnp.mean(grad, -1, keepdims=True) - hat * jnp.mean(grad * hat, -1, keepdims=True)
    )


def fold(values):
    return jnp.sum(values.reshape(values.shape[0] // 8, 8, values.shape[1]), 0)


def norm_rows(x_ref, h_ref, vec, row, block=64):
    @pl.loop(0, x_ref.shape[0] // block)
    def _(i):
        at = rows_of(i, block)
        hat, _ = normed(x_ref[at])
        h_ref[at] = (hat * vec[row : row + 1] + vec[row + 1 : row + 2]).astype(h_ref.dtype)


def norm_rows_back(grad_fn, x_ref, g_ref, out_fn, vec, sums, row, block=64):
    width = x_ref.shape[1]

    def step(i, carry):
        gain, bias = carry
        at = rows_of(i, block)
        hat, scale = normed(x_ref[at])
        grad = grad_fn(at)
        out_fn(at, g_ref[at] + normed_back(grad * vec[row : row + 1], hat, scale))
        return gain + fold(grad * hat), bias + fold(grad)

    zero = jnp.zeros((8, width), F32)
    gain, bias = lax.fori_loop(0, x_ref.shape[0] // block, step, (zero, zero))
    sums[row : row + 1] = jnp.sum(gain, 0, keepdims=True)
    sums[row + 1 : row + 2] = jnp.sum(bias, 0, keepdims=True)


def inner_chunk(weight, h_ref, act_ref, slope_ref, at):
    a = nt(weight, h_ref[...])
    s = sigmoid(a)
    u = a * s
    act_ref[at] = u.astype(LOW)
    slope_ref[at] = (s + u * (1.0 - s)).astype(LOW)


def valid_rows(scal, at_row, rows):
    frame = scal[0] + at_row + lax.broadcasted_iota(jnp.int32, (rows, 1), 0)
    return frame, jnp.where(frame < scal[1], 1.0, 0.0)


def keep_rows(scal, at_row, rows, width):
    frame, ok = valid_rows(scal, at_row, rows)
    cut = (frame >= scal[2]) & (frame < scal[2] + scal[3])
    channel = lax.broadcasted_iota(jnp.int32, (1, width), 1)
    lost = (channel >= scal[4]) & (channel < scal[4] + scal[5])
    return (ok * jnp.where(cut, 0.0, 1.0)) * jnp.where(lost, 0.0, 1.0)


def masked_input(scal, x_in, x_ref, block=64):
    @pl.loop(0, x_in.shape[0] // block)
    def _(i):
        at = rows_of(i, block)
        keep = keep_rows(scal, i * block, block, x_in.shape[1])
        x_ref[at] = x_in[at].astype(F32) * keep


def split3(v):
    high = v.astype(LOW).astype(F32)
    rest = v - high
    mid = rest.astype(LOW).astype(F32)
    return high, mid, rest - mid


def key_extra(length, rows):
    key = lax.broadcasted_iota(jnp.int32, (rows, 128), 0)
    lane = lax.broadcasted_iota(jnp.int32, (rows, 128), 1)
    lost = jnp.where(key < length, 0.0, -1e30)
    return jnp.where(lane == 0, lost, jnp.where(lane < 4, 1.0, 0.0)).astype(LOW)


def fill_side(side, first, extra_rows):
    size = first[0].shape[0]
    wide = side.shape[2]
    blank = jnp.zeros((size, wide), LOW)
    rest = jnp.zeros((128 - 8, wide), LOW)
    for half in range(2):
        side[half, half * size : (half + 1) * size] = first[half]
        side[half, (1 - half) * size : (2 - half) * size] = blank
        side[half, 2 * size :] = extra_rows[half]


def extra_of(lead, parts, wide):
    row = lax.broadcasted_iota(jnp.int32, (16, wide), 0)
    out = jnp.where(row == 0, lead, 0.0)
    if parts is not None:
        for n, part in enumerate(parts):
            out = jnp.where(row == n + 1, -part, out)
    return jnp.concatenate([out.astype(LOW), jnp.zeros((112, wide), LOW)], axis=0)


def attention_forward(qT, key, vT, extra, oT, top, side, scale):
    heads, size, queries = qT.shape
    keys = key.shape[1]
    ones = jnp.ones((16, keys), LOW)

    @pl.loop(0, heads // 2)
    def _(pair):
        lead = extra_of(1.0, None, queries)
        fill_side(side, [qT[2 * pair], qT[2 * pair + 1]], [lead, lead])
        left = jnp.concatenate([key[pair], extra[...]], axis=1)
        for half in range(2):
            head = 2 * pair + half
            s = nn(left, side[half])
            m = jnp.max(s, 0, keepdims=True)
            p = jnp.exp2((s - m) * scale).astype(LOW)
            o = nn(jnp.concatenate([vT[head], ones], axis=0), p)
            total = o[size : size + 1]
            oT[rows_of(head, size)] = (o[:size] * (1.0 / total)).astype(LOW)
            top[pl.ds(head, 1)] = m + jnp.log2(total) * (1.0 / scale)


def attention_backward(qT, key, kT, value, extra, doT, delta, top, dqT, dk, dv, qside, oside, scale, shrink):
    heads, size, queries = qT.shape

    @pl.loop(0, heads // 2)
    def _(pair):
        tops = [split3(top[pl.ds(2 * pair + half, 1)]) for half in range(2)]
        deltas = [split3(delta[pl.ds(2 * pair + half, 1)]) for half in range(2)]
        fill_side(qside, [qT[2 * pair], qT[2 * pair + 1]], [extra_of(1.0, t, queries) for t in tops])
        fill_side(oside, [doT[2 * pair], doT[2 * pair + 1]], [extra_of(0.0, t, queries) for t in deltas])
        left_k = jnp.concatenate([key[pair], extra[...]], axis=1)
        left_v = jnp.concatenate([value[pair], extra[...]], axis=1)
        lows, grads = [], []
        for half in range(2):
            head = 2 * pair + half
            p = jnp.exp2(nn(left_k, qside[half]) * scale)
            ds = (p * nn(left_v, oside[half])).astype(LOW)
            lows.append(p.astype(LOW))
            grads.append(ds)
            dqT[rows_of(head, size)] = (nn(kT[head], ds) * shrink).astype(LOW)
        wide = jnp.concatenate(lows, axis=1)
        dv[pair] = nt(wide, jnp.concatenate([oside[0, :128], oside[1, :128]], axis=1)).astype(LOW)
        wide = jnp.concatenate(grads, axis=1)
        dk[pair] = (nt(wide, jnp.concatenate([qside[0, :128], qside[1, :128]], axis=1)) * shrink).astype(LOW)


def shifted_copies(pad_ref, copies):
    rows = copies.shape[1]
    for s in range(1, 8):
        copies[s - 1] = pad_ref[s : s + rows]


def tap_rows(pad_ref, copies, shift, at_row, block, lanes):
    a, s = divmod(shift, 8)
    at = pl.ds(pl.multiple_of(at_row + 8 * a, 8), block)
    if s == 0:
        return pad_ref[at, lanes]
    return copies[s - 1, at, lanes]


def convolve(pad_ref, copies, kern, out_fn, shift_of, rows, width, block=64):
    for lane in range(width // 128):
        lanes = pl.ds(lane * 128, 128)

        @pl.loop(0, rows // block)
        def _(i):
            total = jnp.zeros((block, 128), F32)
            for tap in range(kern.shape[0]):
                total = total + kern[tap : tap + 1, lanes] * tap_rows(
                    pad_ref, copies, shift_of(tap), i * block, block, lanes
                )
            out_fn(rows_of(i, block), lanes, total)


def convolve_weight(pad_ref, copies, grad_ref, out_ref, shift_of, block=64):
    rows, width = grad_ref.shape
    taps = out_ref.shape[0]
    for lane in range(width // 128):
        lanes = pl.ds(lane * 128, 128)

        def step(i, carry):
            grad = grad_ref[rows_of(i, block), lanes]
            return tuple(
                carry[tap] + fold(grad * tap_rows(pad_ref, copies, shift_of(tap), i * block, block, lanes))
                for tap in range(taps)
            )

        sums = lax.fori_loop(0, rows // block, step, tuple(jnp.zeros((8, 128), F32) for _ in range(taps)))
        for tap in range(taps):
            out_ref[tap : tap + 1, lanes] = jnp.sum(sums[tap], 0, keepdims=True)


def place_halo(pad_ref, halo, core):
    rows = pad_ref.shape[0] - 2 * HALO
    got = halo[...]
    zero = jnp.zeros_like(got)
    pad_ref[0:HALO] = jnp.where(core == 1, got, zero)
    pad_ref[rows + HALO :] = jnp.where(core == 0, got, zero)


class Halves:
    def __init__(self, refs, shard):
        self.refs, self.shard = refs, shard
        self.joint = len(refs) == 1

    def part(self, which, i, chunk):
        if not self.joint:
            return self.refs[which][rows_of(i, chunk)]
        count = chunk // self.shard
        got = self.refs[0][pl.ds(i * count, count), which * self.shard : (which + 1) * self.shard]
        return got.reshape(chunk, got.shape[2])

    def whole(self, which):
        if not self.joint:
            return self.refs[which][...]
        got = self.refs[0][:, which * self.shard : (which + 1) * self.shard]
        return got.reshape(got.shape[0] * got.shape[1], got.shape[2])


def ffn_forward(weights, hidden, x_ref, h_ref, act, slope, out_ref, chunk=256, block=256):
    @pl.loop(0, hidden // chunk)
    def _(i):
        inner_chunk(weights.part(0, i, chunk), h_ref, act, slope, rows_of(i, chunk))

    @pl.loop(0, x_ref.shape[0] // block)
    def _(i):
        at = rows_of(i, block)
        out_ref[at] = x_ref[at] + 0.5 * tn(act[:, at], weights.whole(1))


def ffn_backward(weights, hidden, dy, h_ref, act, slope, da, d_in, d_out, dh, chunk=256, block=256):
    @pl.loop(0, hidden // chunk)
    def _(i):
        at = rows_of(i, chunk)
        du = nt(weights.part(1, i, chunk), dy[...])
        low = (du * slope[at].astype(F32)).astype(LOW)
        da[at] = low
        d_out[at] = nn(act[at], dy[...]).astype(d_out.dtype)
        d_in[at] = nn(low, h_ref[...]).astype(d_in.dtype)

    @pl.loop(0, dh.shape[0] // block)
    def _(i):
        at = rows_of(i, block)
        dh[at] = tn(da[:, at], weights.whole(0))


def first_kernel(shard, hidden, n, scal, x_in, vec, *refs):
    weights = Halves(refs[:n], shard)
    x1, h0, h2, act, slope, x0 = refs[n:]
    masked_input(scal, x_in, x0)
    norm_rows(x0, h0, vec, 0)
    ffn_forward(weights, hidden, x0, h0, act, slope, x1)
    norm_rows(x1, h2, vec, 2)


class Everyone:
    def __init__(self, count, pair, slots, pair_sems, sends, recvs):
        self.count, self.pair, self.slots = count, pair, slots
        self.pair_sems, self.sends, self.recvs = pair_sems, sends, recvs

    def greet(self):
        core, me, count = lax.axis_index("seq"), lax.axis_index("batch"), self.count
        barrier = pltpu.get_barrier_semaphore()
        for k in range(1, count):
            pl.semaphore_signal(
                barrier, inc=1, device_id={"batch": lax.rem(me + k, count)}, device_id_type=MESH
            )
        pl.semaphore_signal(barrier, inc=1, device_id={"seq": 1 - core}, device_id_type=MESH)

    def meet(self):
        pl.semaphore_wait(pltpu.get_barrier_semaphore(), self.count)

    def total(self, x, out):
        core, me, count = lax.axis_index("seq"), lax.axis_index("batch"), self.count
        slots, sends, recvs = self.slots, self.sends, self.recvs
        copy = to_core(x, self.pair, self.pair_sems.at[0], self.pair_sems.at[1], 1 - core)
        copy.start()
        copy.wait()
        slots[me] = x[...] + self.pair[...]
        copies = []
        for k in range(1, count):
            copy = to_batch(
                slots.at[me], slots.at[me], sends.at[k - 1], recvs.at[k - 1], lax.rem(me + k, count)
            )
            copy.start()
            copies.append(copy)
        for k in range(1, count):
            source = lax.rem(me + count - k, count)
            to_batch(slots.at[source], slots.at[source], sends.at[k - 1], recvs.at[k - 1], me).wait_recv()
        total = slots[0]
        for place in range(1, count):
            total = total + slots[place]
        out[...] = total
        for copy in copies:
            copy.wait_send()

    @staticmethod
    def scratch(count, rows, width):
        return [
            pltpu.VMEM((rows, width), F32),
            pltpu.VMEM((count, rows, width), F32),
            pltpu.SemaphoreType.DMA((2,)),
            pltpu.SemaphoreType.DMA((count - 1,)),
            pltpu.SemaphoreType.DMA((count - 1,)),
        ]


def attend_kernel(
    count, scal, x1, h2, qkvT, w_out, conv_in, kern, vec,
    x2, oT, top, h_all, qT, key, h3, pad, depth, totals,
    vT, extra, side, copies, halo, part, swap_sems, *ring,
):
    every = Everyone(count, *ring)
    core = lax.axis_index("seq")
    rows, width = x1.shape
    heads, size = qT.shape[:2]
    pairs = heads // 2
    scale = math.log2(math.e) / math.sqrt(size)
    mine, other = core * rows, (1 - core) * rows
    every.greet()

    def project(at):
        here = h_all[at]
        for pair in range(pairs):
            key[pair, at] = nt(here, qkvT[1, pair * 128 : (pair + 1) * 128]).astype(LOW)
        got = nt(qkvT[2], here).astype(LOW)
        vT[:, :, at] = got.reshape(heads, size, rows)

    own = pl.ds(pl.multiple_of(mine, rows), rows)
    theirs = pl.ds(pl.multiple_of(other, rows), rows)
    h_all[own] = h2[...]
    every.meet()
    swap = to_core(h_all.at[own], h_all.at[own], swap_sems.at[0], swap_sems.at[1], 1 - core)
    swap.start()
    qT[...] = nt(qkvT[0], h2[...]).astype(LOW).reshape(heads, size, rows)
    extra[...] = key_extra(scal[1], extra.shape[0])
    project(own)
    swap.wait()
    project(theirs)
    attention_forward(qT, key, vT, extra, oT, top, side, scale)
    block = 256

    @pl.loop(0, rows // block)
    def _(i):
        at = rows_of(i, block)
        x2[at] = x1[at] + tn(oT[:, at], w_out[...])

    norm_rows(x2, h3, vec, 4)

    @pl.loop(0, rows // block)
    def _(i):
        at = rows_of(i, block)
        _, ok = valid_rows(scal, i * block, block)
        here = h3[at]
        gate = sigmoid(nn(here, conv_in[:, width:]))
        pad[pl.ds(pl.multiple_of(i * block + HALO, HALO), block)] = nn(here, conv_in[:, :width]) * gate * ok

    edge = pl.ds(pl.multiple_of(HALO + (1 - core) * (rows - HALO), HALO), HALO)
    swap = to_core(pad.at[edge], halo, swap_sems.at[2], swap_sems.at[3], 1 - core)
    swap.start()
    swap.wait()
    place_halo(pad, halo, core)
    shifted_copies(pad, copies)

    def put(at, lanes, total):
        depth[at, lanes] = total

    convolve(pad, copies, kern, put, lambda tap: tap + 1, rows, width)
    step = 64

    def sums(i, carry):
        first, second = carry
        _, ok = valid_rows(scal, i * step, step)
        here = depth[rows_of(i, step)]
        held = here * ok
        return first + fold(held), second + fold(here * held)

    zero = jnp.zeros((8, width), F32)
    first, second = lax.fori_loop(0, rows // step, sums, (zero, zero))
    number = jnp.clip(scal[1] - scal[0], 0, rows).astype(F32)
    part[...] = jnp.concatenate(
        [
            jnp.sum(first, 0, keepdims=True),
            jnp.sum(second, 0, keepdims=True),
            jnp.full((1, width), 1.0, F32) * number,
            jnp.zeros((5, width), F32),
        ],
        axis=0,
    )
    every.total(part, totals)


def batch_numbers(totals):
    number = totals[2:3]
    mean = totals[0:1] / number
    var = totals[1:2] / number - mean * mean
    return number, mean, lax.rsqrt(var + EPS)


def middle_kernel(
    count, shard, hidden, n, scal, depth, x2, totals, conv_out, cot, vec, *refs,
):
    weights = Halves(refs[:n], shard)
    (out, grad, dz, totals2, d_in, d_out, d_conv, sums,
     act_low, slope_z, x3, h4, act, slope, x4, dy, da, dh, part, *ring) = refs[n:]
    every = Everyone(count, *ring)
    every.greet()
    rows, width = x2.shape
    sums[...] = jnp.zeros_like(sums)
    number, mean, scale = batch_numbers(totals)
    block = 64

    @pl.loop(0, rows // block)
    def _(i):
        at = rows_of(i, block)
        z = (depth[at] - mean) * scale * vec[6:7] + vec[7:8]
        s = sigmoid(z)
        u = z * s
        act_low[at] = u.astype(LOW)
        slope_z[at] = s + u * (1.0 - s)

    @pl.loop(0, rows // 256)
    def _(i):
        at = rows_of(i, 256)
        x3[at] = x2[at] + nn(act_low[at], conv_out[...])

    norm_rows(x3, h4, vec, 8)
    ffn_forward(weights, hidden, x3, h4, act, slope, x4)

    def last(i, carry):
        gain, bias = carry
        at = rows_of(i, block)
        hat, spread = normed(x4[at])
        out[at] = (hat * vec[10:11] + vec[11:12]).astype(LOW)
        g = cot[at].astype(F32)
        back = normed_back(g * vec[10:11], hat, spread)
        grad[at] = back
        dy[at] = (0.5 * back).astype(LOW)
        return gain + fold(g * hat), bias + fold(g)

    zero = jnp.zeros((8, width), F32)
    gain, bias = lax.fori_loop(0, rows // block, last, (zero, zero))
    sums[10:11] = jnp.sum(gain, 0, keepdims=True)
    sums[11:12] = jnp.sum(bias, 0, keepdims=True)
    ffn_backward(weights, hidden, dy, h4, act, slope, da, d_in, d_out, dh)

    def put(at, value):
        grad[at] = value
        dy[at] = value.astype(LOW)

    norm_rows_back(lambda at: dh[at], x3, grad, put, vec, sums, 8)
    d_conv[...] = tn(act_low[...], dy[...]).astype(LOW)

    @pl.loop(0, rows // 256)
    def _(i):
        at = rows_of(i, 256)
        dz[at] = nt(dy[at], conv_out[...])

    def close(i, carry):
        first, second = carry
        at = rows_of(i, block)
        here = dz[at] * slope_z[at]
        dz[at] = here
        return first + fold(here), second + fold(here * (depth[at] - mean))

    first, second = lax.fori_loop(0, rows // block, close, (zero, zero))
    part[...] = jnp.concatenate(
        [jnp.sum(first, 0, keepdims=True), jnp.sum(second, 0, keepdims=True), jnp.zeros((6, width), F32)], axis=0
    )
    every.meet()
    every.total(part, totals2)


def return_kernel(
    scal, grad, dz, depth, totals, totals2, pad, h3, conv_in, x2, oT, w_out, h_all, qT, key, top, qkvT, x1, kern, vec,
    g1, d_kern, d_conv, d_att, d_qkv, sums,
    back, halo, copies, p, dp, dh, datt, doT, delta, value, kT, extra, qside, oside, dqT, dk, dv, rk, rv, own_k, own_v,
    swap_sems,
):
    core = lax.axis_index("seq")
    rows, width = x1.shape
    heads, size = qT.shape[:2]
    pairs = heads // 2
    scale = math.log2(math.e) / math.sqrt(size)
    barrier = pltpu.get_barrier_semaphore()
    pl.semaphore_signal(barrier, inc=1, device_id={"seq": 1 - core}, device_id_type=MESH)
    sums[...] = jnp.zeros_like(sums)
    number, mean, spread = batch_numbers(totals)
    grad_sum, grad_moment = totals2[0:1], totals2[1:2]
    gain = vec[6:7]
    var_grad = -0.5 * (gain * grad_moment) * spread * spread * spread
    flat = (-(gain * spread * grad_sum) - 2.0 * mean * var_grad) / number
    tilt = 2.0 * var_grad / number
    block = 64

    @pl.loop(0, rows // block)
    def _(i):
        at = rows_of(i, block)
        _, ok = valid_rows(scal, i * block, block)
        back[pl.ds(pl.multiple_of(i * block + HALO, HALO), block)] = gain * spread * dz[at] + ok * (
            flat + depth[at] * tilt
        )

    pl.semaphore_wait(barrier, 1)
    edge = pl.ds(pl.multiple_of(HALO + (1 - core) * (rows - HALO), HALO), HALO)
    swap = to_core(back.at[edge], halo, swap_sems.at[0], swap_sems.at[1], 1 - core)
    swap.start()
    shifted_copies(pad, copies)
    convolve_weight(pad, copies, back.at[pl.ds(HALO, rows)], d_kern, lambda tap: tap + 1)

    @pl.loop(0, rows // 256)
    def _(i):
        at = rows_of(i, 256)
        p[at] = nn(h3[at], conv_in[...])

    swap.wait()
    place_halo(back, halo, core)
    shifted_copies(back, copies)

    def put(at, lanes, total):
        _, ok = valid_rows(scal, at.start, at.size)
        gate = sigmoid(p[at, pl.ds(lanes.start + width, 128)])
        total = total * gate * ok
        dp[at, lanes] = total.astype(LOW)
        dp[at, pl.ds(lanes.start + width, 128)] = (total * p[at, lanes] * (1.0 - gate)).astype(LOW)

    taps = kern.shape[0]
    convolve(back, copies, kern, put, lambda tap: taps - 1 - tap, rows, width)
    d_conv[...] = tn(h3[...], dp[...]).astype(LOW)

    @pl.loop(0, rows // 256)
    def _(i):
        at = rows_of(i, 256)
        dh[at] = nt(dp[at], conv_in[...])

    def put_first(at, got):
        g1[at] = got
        datt[at] = got.astype(LOW)

    norm_rows_back(lambda at: dh[at], x2, grad, put_first, vec, sums, 4)
    d_att[...] = nn(oT[...], datt[...]).astype(LOW)
    doT[...] = nt(w_out[...], datt[...]).astype(LOW).reshape(heads, size, rows)
    for head in range(heads):
        o = oT[head * size : (head + 1) * size].astype(F32)
        delta[head : head + 1] = jnp.sum(o * doT[head].astype(F32), 0, keepdims=True)
    extra[...] = key_extra(scal[1], extra.shape[0])
    for half in range(2):
        at = pl.ds(half * rows, rows)
        here = h_all[at]
        for pair in range(pairs):
            value[pair, at] = nt(here, qkvT[2, pair * 128 : (pair + 1) * 128]).astype(LOW)
        kT[:, :, at] = nt(qkvT[1], here).astype(LOW).reshape(heads, size, rows)
    attention_backward(
        qT, key, kT, value, extra, doT, delta, top, dqT, dk, dv, qside, oside, scale, 1.0 / math.sqrt(size)
    )
    own = pl.ds(pl.multiple_of(core * rows, rows), rows)
    theirs = pl.ds(pl.multiple_of((1 - core) * rows, rows), rows)
    swaps = [
        to_core(dk.at[:, theirs], rk, swap_sems.at[2], swap_sems.at[3], 1 - core),
        to_core(dv.at[:, theirs], rv, swap_sems.at[4], swap_sems.at[5], 1 - core),
    ]
    for swap in swaps:
        swap.start()
    h2 = h_all[own]
    dq = dqT[...].astype(F32).T.astype(LOW)
    d_qkv[0] = tn(h2, dq).astype(LOW)
    dh[...] = nn(dq, qkvT[0])
    for swap in swaps:
        swap.wait()
    for pair in range(pairs):
        lanes = pl.ds(pair * 128, 128)
        own_k[:, lanes] = (dk[pair, own].astype(F32) + rk[pair].astype(F32)).astype(LOW)
        own_v[:, lanes] = (dv[pair, own].astype(F32) + rv[pair].astype(F32)).astype(LOW)
    d_qkv[1] = tn(h2, own_k[...]).astype(LOW)
    d_qkv[2] = tn(h2, own_v[...]).astype(LOW)
    dh[...] += nn(own_k[...], qkvT[1])
    dh[...] += nn(own_v[...], qkvT[2])

    def put_second(at, got):
        g1[at] = got

    norm_rows_back(lambda at: dh[at], x1, g1, put_second, vec, sums, 2)


def last_kernel(shard, hidden, n, scal, x_in, grad, h0, act, slope, vec, *refs):
    weights = Halves(refs[:n], shard)
    input_grad, d_in, d_out, sums, x0, dy, da, dh = refs[n:]
    sums[...] = jnp.zeros_like(sums)
    masked_input(scal, x_in, x0)
    block = 64

    @pl.loop(0, x0.shape[0] // block)
    def _(i):
        at = rows_of(i, block)
        dy[at] = (0.5 * grad[at]).astype(LOW)

    ffn_backward(weights, hidden, dy, h0, act, slope, da, d_in, d_out, dh)

    def put(at, got):
        keep = keep_rows(scal, at.start, at.size, x0.shape[1])
        input_grad[at] = got * keep

    norm_rows_back(lambda at: dh[at], x0, grad, put, vec, sums, 0)


def call(body, outs, scratch, args, collective_id=None, scalars=1):
    vm = pl.BlockSpec(memory_space=pltpu.VMEM)
    return pl.pallas_call(
        body,
        out_shape=tuple(jax.ShapeDtypeStruct(shape, kind) for shape, kind in outs),
        in_specs=[pl.BlockSpec(memory_space=pltpu.SMEM)] * scalars + [vm] * (len(args) - scalars),
        out_specs=tuple(vm for _ in outs),
        scratch_shapes=scratch,
        compiler_params=pltpu.CompilerParams(
            collective_id=collective_id, has_side_effects=collective_id is not None, vmem_limit_bytes=VMEM_BYTES
        ),
    )(*args)


def per_device(
    block_input, lengths, spans, cotangent, ffn_in, ffn_out, qkv_weight, out_weight, conv_in, kernel, conv_out, vectors,
):
    _, rows, width = block_input.shape
    count = lax.axis_size("batch")
    core = lax.axis_index("seq")
    shard = ffn_in.shape[1]
    blocks = 2 * count
    hidden = shard * blocks
    heads, size = HEADS, width // HEADS
    keys = 2 * rows
    taps = kernel.shape[0]
    joint = shard % 16 == 0
    vm, dma = pltpu.VMEM, pltpu.SemaphoreType.DMA
    scal = jnp.concatenate(
        [jnp.reshape(core * rows, (1,)), lengths[:1], spans[0], jnp.zeros((2,), jnp.int32)]
    ).astype(jnp.int32)
    x_in, cot = block_input[0], cotangent[0]
    gathered = gather_all(jnp.concatenate([ffn_in, ffn_out], axis=1), count, 0)
    qkvT = lax.all_gather(qkv_weight.transpose(0, 2, 1), "seq", axis=1, tiled=True)

    def weights_of(j):
        if joint:
            return [gathered[j]]
        return [gathered[j, :, :shard].reshape(hidden, width), gathered[j, :, shard:].reshape(hidden, width)]

    first, second = weights_of(0), weights_of(1)
    n = len(first)
    square = (rows, width)
    tall = (hidden, rows)
    x1, h0, h2, act0, slope0 = call(
        functools.partial(first_kernel, shard, hidden, n),
        [(square, F32), (square, LOW), (square, LOW), (tall, LOW), (tall, LOW)],
        [vm(square, F32)],
        [scal, x_in, vectors, *first],
    )
    padded = (rows + 2 * HALO, width)
    copies = vm((7, rows + 24, width), F32)
    ring = Everyone.scratch(count, 8, width)
    x2, oT, top, h_all, qT, key, h3, pad, depth, totals = call(
        functools.partial(attend_kernel, count),
        [
            (square, F32), ((width, rows), LOW), ((heads, rows), F32), ((keys, width), LOW), ((heads, size, rows), LOW),
            ((heads // 2, keys, 128), LOW), (square, LOW), (padded, F32), (square, F32), ((8, width), F32),
        ],
        [
            vm((heads, size, keys), LOW), vm((keys, 128), LOW), vm((2, 256, rows), LOW), copies,
            vm((HALO, width), F32), vm((8, width), F32), dma((4,)), *ring,
        ],
        [scal, x1, h2, qkvT, out_weight, conv_in, kernel, vectors],
        1,
    )
    out, grad, dz, totals2, d_in1, d_out1, d_conv_out, sums1 = call(
        functools.partial(middle_kernel, count, shard, hidden, n),
        [
            (square, LOW), (square, F32), (square, F32), ((8, width), F32), ((hidden, width), LOW), ((hidden, width), LOW),
            ((width, width), LOW), ((16, width), F32),
        ],
        [
            vm(square, LOW), vm(square, F32), vm(square, F32), vm(square, LOW), vm(tall, LOW), vm(tall, LOW),
            vm(square, F32), vm(square, LOW), vm(tall, LOW), vm(square, F32), vm((8, width), F32), *ring,
        ],
        [scal, depth, x2, totals, conv_out, cot, vectors, *second],
        2,
    )
    g1, d_kern, d_conv_in, d_att, d_qkv, sums2 = call(
        return_kernel,
        [
            (square, F32), ((taps, width), F32), ((width, 2 * width), LOW), ((width, width), LOW),
            ((3, width, width), LOW), ((16, width), F32),
        ],
        [
            vm(padded, F32), vm((HALO, width), F32), copies, vm((rows, 2 * width), F32), vm((rows, 2 * width), LOW),
            vm(square, F32), vm(square, LOW), vm((heads, size, rows), LOW), vm((heads, rows), F32),
            vm((heads // 2, keys, 128), LOW), vm((heads, size, keys), LOW), vm((keys, 128), LOW),
            vm((2, 256, rows), LOW), vm((2, 256, rows), LOW), vm((width, rows), LOW),
            vm((heads // 2, keys, 128), LOW), vm((heads // 2, keys, 128), LOW),
            vm((heads // 2, rows, 128), LOW), vm((heads // 2, rows, 128), LOW), vm(square, LOW), vm(square, LOW),
            dma((6,)),
        ],
        [
            scal, grad, dz, depth, totals, totals2, pad, h3, conv_in, x2, oT, out_weight, h_all, qT, key, top, qkvT, x1,
            kernel, vectors,
        ],
        4,
    )
    input_grad, d_in0, d_out0, sums3 = call(
        functools.partial(last_kernel, shard, hidden, n),
        [(square, F32), ((hidden, width), LOW), ((hidden, width), LOW), ((16, width), F32)],
        [vm(square, F32), vm(square, LOW), vm(tall, LOW), vm(square, F32)],
        [scal, x_in, g1, h0, act0, slope0, vectors, *first],
    )
    sums = sums1 + sums2 + sums3

    def spread(values):
        flat = values.astype(LOW).reshape(-1, width)
        lines = -(-flat.shape[0] // blocks)
        if joint:
            lines = -(-lines // 16) * 16
        flat = jnp.pad(flat, ((0, lines * blocks - flat.shape[0]), (0, 0)))
        return flat.reshape(blocks, lines, width)

    small = jnp.concatenate([d_kern, sums])
    lines = 3 * width // (2 * count)
    per_core = d_qkv.reshape(count, 2, lines, 2, width // 2).transpose(3, 0, 2, 1, 4).reshape(blocks, lines, width)
    pieces = [spread(v) for v in (d_in0, d_out0, d_in1, d_out1, d_att, d_conv_in, d_conv_out, small)] + [per_core]
    solo = 4 * shard
    fin, shared = reduce_all(pieces, solo, count, 3)
    ffn_in_grad = jnp.stack([fin[:shard], fin[2 * shard : 3 * shard]])
    ffn_out_grad = jnp.stack([fin[shard : 2 * shard], fin[3 * shard :]])
    at = 0
    whole = []
    for piece, like in zip(pieces[4:8], (d_att, d_conv_in, d_conv_out, small)):
        span = piece.shape[1]
        part = shared[0, :, at : at + span].reshape(-1, width)
        whole.append(part[: like.size // width].reshape(like.shape).astype(F32))
        at += span
    out_weight_grad, conv_in_grad, conv_out_grad, small_total = whole
    mine = lax.dynamic_slice_in_dim(shared[0], core * count, count, axis=0)[:, at : at + lines]
    qkv_grad = mine.reshape(count, lines, 2, width // 2).transpose(0, 2, 1, 3).reshape(3, width, width // 2)
    vectors_grad = small_total[taps : taps + 12]
    gamma = lax.rsqrt(totals[1] / totals[2] - (totals[0] / totals[2]) ** 2 + EPS) * totals2[1]
    row = lax.broadcasted_iota(jnp.int32, (12, 1), 0)
    vectors_grad = jnp.where(row == 6, gamma[None], jnp.where(row == 7, totals2[0][None], vectors_grad))
    return (
        out[None],
        input_grad[None],
        ffn_in_grad,
        ffn_out_grad,
        qkv_grad.astype(F32),
        out_weight_grad,
        conv_in_grad,
        small_total[:taps],
        conv_out_grad,
        vectors_grad,
    )


def solution(mesh):
    placed = (
        P("batch", "seq", None),
        P("batch"),
        P("batch", None),
        P("batch", "seq", None),
        P(None, ("seq", "batch"), None),
        P(None, ("seq", "batch"), None),
        P(None, None, "seq"),
        P(),
        P(),
        P(),
        P(),
        P(),
    )
    return jax.shard_map(
        per_device,
        mesh=mesh,
        in_specs=placed,
        out_specs=(
            P("batch", "seq", None),
            P("batch", "seq", None),
            P(None, ("seq", "batch"), None),
            P(None, ("seq", "batch"), None),
            P(None, None, "seq"),
            P(),
            P(),
            P(),
            P(),
            P(),
        ),
        check_vma=False,
    )
```

```python
import functools
import math
from types import SimpleNamespace

import jax
import jax.numpy as jnp
from jax import lax
from jax.experimental import pallas as pl
from jax.experimental.pallas import tpu as pltpu
from jax.sharding import PartitionSpec as P

HEADS = 8
MESH = pl.DeviceIdType.MESH
VMEM_BYTES = 63 * 1024 * 1024
F32, LOW = jnp.float32, jnp.bfloat16
EPS = 1e-05
HALO = 16


class Routes:
    def __init__(self, count):
        if count == 16:
            first, last, middle = (1, 2), (2, 2), (4, 4)
        elif count == 128:
            first, last, middle = (1, 4), (32, 4), (4, 8)
        else:
            first, last, middle = (1, 1), (1, 1), (1, count)
        self.count = count
        self.side = first[1]
        self.deep = middle[1]
        self.first, self.last, self.middle = first, last, middle

    def here(self):
        self.core = lax.axis_index("seq")
        self.me = lax.axis_index("batch")
        turn = self.core * (self.last[0] - self.first[0])
        self.one = self.first[0] + turn
        self.two = self.last[0] - turn
        self.mid = self.middle[0]
        self.p = lax.rem(lax.div(self.me, self.one), self.side)
        self.q = lax.rem(lax.div(self.me, self.two), self.side)
        self.z = lax.rem(lax.div(self.me, self.mid), self.deep)
        return self

    def index(self, z, p, q):
        return z * self.mid + p * self.one + q * self.two

    def near(self, d, e, f):
        z = lax.rem(self.z + d, self.deep) if d else self.z
        p = lax.rem(self.p + e, self.side) if e else self.p
        q = lax.rem(self.q + f, self.side) if f else self.q
        return self.index(z, p, q)

    def peers(self):
        found = []
        for k in range(1, self.deep):
            found.append(self.index(lax.rem(self.z + k, self.deep), self.p, self.q))
        for k in range(1, self.side):
            found.append(self.index(self.z, lax.rem(self.p + k, self.side), self.q))
            found.append(self.index(self.z, self.p, lax.rem(self.q + k, self.side)))
        return found

    def greet(self):
        barrier = pltpu.get_barrier_semaphore()
        places = self.peers()
        for place in places:
            pl.semaphore_signal(
                barrier, inc=1, device_id={"batch": place}, device_id_type=MESH
            )
        pl.semaphore_signal(
            barrier, inc=1, device_id={"seq": 1 - self.core}, device_id_type=MESH
        )
        pl.semaphore_wait(barrier, len(places) + 1)


def to_batch(src, dst, send, recv, place):
    return pltpu.make_async_remote_copy(
        src_ref=src, dst_ref=dst, send_sem=send, recv_sem=recv,
        device_id={"batch": place}, device_id_type=MESH,
    )


def to_core(src, dst, send, recv, core):
    return pltpu.make_async_remote_copy(
        src_ref=src, dst_ref=dst, send_sem=send, recv_sem=recv,
        device_id={"seq": core}, device_id_type=MESH,
    )


class Gather:
    def __init__(self, route, at, sends, recv):
        self.route, self.at, self.sends, self.recv = route, at, sends, recv
        self.used = 0

    def block(self, place, core=None):
        return (self.route.core if core is None else core) * self.route.count + place

    def arrive(self, place, core=None):
        block = self.block(place, core)
        here = self.at(block)
        to_core(here, here, self.recv.at[block], self.recv.at[block], 1 - self.route.core).wait_recv()

    def send(self, place, target):
        block = self.block(place)
        here = self.at(block)
        to_batch(here, here, self.sends.at[self.used], self.recv.at[block], target).start()
        self.used += 1

    def cross(self, place):
        block = self.block(place)
        here = self.at(block)
        to_core(here, here, self.sends.at[self.used], self.recv.at[block], 1 - self.route.core).start()
        self.used += 1

    def step_mid(self):
        route = self.route
        for k in range(1, route.deep):
            self.send(route.me, route.near(k, 0, 0))
        self.cross(route.me)

    def step_one(self):
        route = self.route
        for d in range(route.deep):
            place = route.near(d, 0, 0)
            if d:
                self.arrive(place)
            for k in range(1, route.side):
                self.send(place, route.near(0, k, 0))
            if d:
                self.cross(place)

    def step_two(self):
        route = self.route
        for e in range(route.side):
            for d in range(route.deep):
                place = route.near(d, e, 0)
                if e:
                    self.arrive(place)
                for k in range(1, route.side):
                    self.send(place, route.near(0, 0, k))
                if e:
                    self.cross(place)

    def step_last(self):
        route = self.route
        for f in range(1, route.side):
            for e in range(route.side):
                for d in range(route.deep):
                    place = route.near(d, e, f)
                    self.arrive(place)
                    self.cross(place)

    def step_other(self):
        for place in range(self.route.count):
            self.arrive(place, 1 - self.route.core)

    def finish(self):
        here = self.at(0)
        for slot in range(self.used):
            to_core(here, here, self.sends.at[slot], self.sends.at[slot], 1 - self.route.core).wait_send()


class Reduce:
    def __init__(self, route, source, stage, sems):
        self.route, self.source = route, source
        self.zero, self.one, self.two, self.three = stage
        (self.s0, self.r0), (self.s1, self.r1), (self.s2, self.r2), (self.s3, self.r3) = sems

    def add(self, place, value):
        self.zero[place] = (self.zero[place].astype(F32) + value.astype(F32)).astype(LOW)

    def send_core(self, d, e, f):
        route = self.route
        place = route.near(d, e, f)
        to_core(
            self.source((1 - route.core) * route.count + place),
            self.zero.at[place], self.s0.at[place], self.r0.at[place], 1 - route.core,
        ).start()

    def start(self):
        route = self.route
        for f in range(route.side - 1, -1, -1):
            for d in range(route.deep):
                for e in range(route.side - 1, -1, -1):
                    self.send_core(d, e, f)

    def merge(self, d, e, f):
        route = self.route
        place = route.near(d, e, f)
        here = self.zero.at[place]
        to_core(here, here, self.s0.at[place], self.r0.at[place], 1 - route.core).wait_recv()
        self.add(place, self.source(route.core * route.count + place)[...])
        return place

    def step_one(self):
        route = self.route
        for e in range(1, route.side):
            for f in range(route.side - 1, -1, -1):
                for d in range(route.deep):
                    place = self.merge(d, e, f)
                    slot = (e - 1) * route.deep * route.side + d * route.side + f
                    to_batch(
                        self.zero.at[place], self.one.at[slot], self.s1.at[slot], self.r1.at[slot], route.near(0, e, 0)
                    ).start()

    def step_own(self):
        route = self.route
        for f in range(route.side - 1, -1, -1):
            for d in range(route.deep):
                self.merge(d, 0, f)

    def step_two(self):
        route = self.route
        for f in range(route.side - 1, -1, -1):
            for d in range(route.deep - 1, -1, -1):
                place = route.near(d, 0, f)
                for e in range(1, route.side):
                    slot = (e - 1) * route.deep * route.side + d * route.side + f
                    here = self.one.at[slot]
                    to_core(here, here, self.s1.at[slot], self.r1.at[slot], 1 - route.core).wait_recv()
                    self.add(place, self.one[slot])
                if f:
                    slot = (f - 1) * route.deep + d
                    to_batch(
                        self.zero.at[place], self.two.at[slot], self.s2.at[slot], self.r2.at[slot], route.near(0, 0, f)
                    ).start()

    def step_three(self):
        route = self.route
        for d in range(route.deep - 1, -1, -1):
            place = route.near(d, 0, 0)
            for f in range(1, route.side):
                slot = (f - 1) * route.deep + d
                here = self.two.at[slot]
                to_core(here, here, self.s2.at[slot], self.r2.at[slot], 1 - route.core).wait_recv()
                self.add(place, self.two[slot])
            if d:
                to_batch(
                    self.zero.at[place], self.three.at[d - 1], self.s3.at[d - 1], self.r3.at[d - 1], place
                ).start()

    def total(self):
        route = self.route
        out = self.zero[route.me].astype(F32)
        for d in range(1, route.deep):
            here = self.three.at[d - 1]
            to_core(here, here, self.s3.at[d - 1], self.r3.at[d - 1], 1 - route.core).wait_recv()
            out = out + self.three[d - 1].astype(F32)
        return out

    def sent_core(self):
        here = self.zero.at[0]
        for slot in range(self.s0.shape[0]):
            to_core(here, here, self.s0.at[slot], self.s0.at[slot], 1 - self.route.core).wait_send()

    def finish(self):
        here = self.zero.at[0]
        for sems in (self.s1, self.s2, self.s3):
            for slot in range(sems.shape[0]):
                to_core(here, here, sems.at[slot], sems.at[slot], 1 - self.route.core).wait_send()


def stage_counts(route):
    side, deep = route.side, route.deep
    return route.count, (side - 1) * side * deep, (side - 1) * deep, deep - 1


class Everyone:
    def __init__(self, count, pair, slots, pair_sems, sends, recvs):
        self.count, self.pair, self.slots = count, pair, slots
        self.pair_sems, self.sends, self.recvs = pair_sems, sends, recvs

    def start(self, x):
        core, me, count = lax.axis_index("seq"), lax.axis_index("batch"), self.count
        copy = to_core(x, self.pair, self.pair_sems.at[0], self.pair_sems.at[1], 1 - core)
        copy.start()
        copy.wait()
        self.slots[me] = x[...] + self.pair[...]
        for k in range(1, count):
            here = self.slots.at[me]
            to_batch(here, here, self.sends.at[k - 1], self.recvs.at[k - 1], lax.rem(me + k, count)).start()

    def total(self):
        me, count = lax.axis_index("batch"), self.count
        for k in range(1, count):
            here = self.slots.at[lax.rem(me + count - k, count)]
            to_batch(here, here, self.sends.at[k - 1], self.recvs.at[k - 1], me).wait_recv()
        out = self.slots[0]
        for place in range(1, count):
            out = out + self.slots[place]
        for k in range(1, count):
            here = self.slots.at[0]
            to_batch(here, here, self.sends.at[k - 1], self.recvs.at[k - 1], me).wait_send()
        return out

    @staticmethod
    def scratch(count, rows):
        return [
            pltpu.VMEM((rows, 128), F32),
            pltpu.VMEM((count, rows, 128), F32),
            pltpu.SemaphoreType.DMA((2,)),
            pltpu.SemaphoreType.DMA((count - 1,)),
            pltpu.SemaphoreType.DMA((count - 1,)),
        ]


def to_tile(rows):
    width = rows.shape[1]
    parts = [rows[i : i + 1, j : j + 128] for i in range(rows.shape[0]) for j in range(0, width, 128)]
    return jnp.concatenate(parts, axis=0)


def from_tile(tile, first, width):
    each = width // 128
    return jnp.concatenate([tile[first * each + j : first * each + j + 1] for j in range(each)], axis=1)


def nn(a, b):
    return lax.dot_general(a, b, (((1,), (0,)), ((), ())), preferred_element_type=F32)


def nt(a, b):
    return lax.dot_general(a, b, (((1,), (1,)), ((), ())), preferred_element_type=F32)


def tn(a, b):
    return lax.dot_general(a, b, (((0,), (0,)), ((), ())), preferred_element_type=F32)


def sigmoid(v):
    return 0.5 * jnp.tanh(0.5 * v) + 0.5


def rows_of(i, size):
    return pl.ds(pl.multiple_of(i * size, size), size)


def normed(v):
    centred = v - jnp.mean(v, -1, keepdims=True)
    scale = lax.rsqrt(jnp.mean(centred * centred, -1, keepdims=True) + EPS)
    return centred * scale, scale


def normed_back(grad, hat, scale):
    return scale * (
        grad - jnp.mean(grad, -1, keepdims=True) - hat * jnp.mean(grad * hat, -1, keepdims=True)
    )


def fold(values):
    return jnp.sum(values.reshape(values.shape[0] // 8, 8, values.shape[1]), 0)


def norm_rows(x_ref, put, vec, row, block=64):
    @pl.loop(0, x_ref.shape[0] // block)
    def _(i):
        at = rows_of(i, block)
        hat, _ = normed(x_ref[at])
        put(at, (hat * vec[row : row + 1] + vec[row + 1 : row + 2]).astype(LOW))


def norm_rows_back(grad_ref, x_ref, g_ref, put, vec, sums, row, block=64):
    width = x_ref.shape[1]

    def step(i, carry):
        gain, bias = carry
        at = rows_of(i, block)
        hat, scale = normed(x_ref[at])
        grad = grad_ref[at]
        put(at, g_ref[at] + normed_back(grad * vec[row : row + 1], hat, scale))
        return gain + fold(grad * hat), bias + fold(grad)

    zero = jnp.zeros((8, width), F32)
    gain, bias = lax.fori_loop(0, x_ref.shape[0] // block, step, (zero, zero))
    sums[row : row + 1] = jnp.sum(gain, 0, keepdims=True)
    sums[row + 1 : row + 2] = jnp.sum(bias, 0, keepdims=True)


def activate(a):
    s = sigmoid(a)
    u = a * s
    return u, s + u * (1.0 - s)


def valid_rows(scal, at_row, rows):
    frame = scal[0] + at_row + lax.broadcasted_iota(jnp.int32, (rows, 1), 0)
    return frame, jnp.where(frame < scal[1], 1.0, 0.0)


def keep_rows(scal, at_row, rows, width):
    frame, ok = valid_rows(scal, at_row, rows)
    cut = (frame >= scal[2]) & (frame < scal[2] + scal[3])
    channel = lax.broadcasted_iota(jnp.int32, (1, width), 1)
    lost = (channel >= scal[4]) & (channel < scal[4] + scal[5])
    return (ok * jnp.where(cut, 0.0, 1.0)) * jnp.where(lost, 0.0, 1.0)


def masked_input(scal, x_in, x_ref, block=64):
    @pl.loop(0, x_in.shape[0] // block)
    def _(i):
        at = rows_of(i, block)
        keep = keep_rows(scal, i * block, block, x_in.shape[1])
        x_ref[at] = x_in[at].astype(F32) * keep


def split3(v):
    high = v.astype(LOW).astype(F32)
    rest = v - high
    mid = rest.astype(LOW).astype(F32)
    return high, mid, rest - mid


def key_extra(length, rows):
    key = lax.broadcasted_iota(jnp.int32, (rows, 128), 0)
    lane = lax.broadcasted_iota(jnp.int32, (rows, 128), 1)
    lost = jnp.where(key < length, 0.0, -1e30)
    return jnp.where(lane == 0, lost, jnp.where(lane < 4, 1.0, 0.0)).astype(LOW)


def fill_side(side, first, extra_rows):
    size = first[0].shape[0]
    blank = jnp.zeros((size, side.shape[2]), LOW)
    for half in range(2):
        side[half, half * size : (half + 1) * size] = first[half]
        side[half, (1 - half) * size : (2 - half) * size] = blank
        side[half, 2 * size :] = extra_rows[half]


def extra_of(lead, parts, wide):
    row = lax.broadcasted_iota(jnp.int32, (16, wide), 0)
    out = jnp.where(row == 0, lead, 0.0)
    if parts is not None:
        for n, part in enumerate(parts):
            out = jnp.where(row == n + 1, -part, out)
    return jnp.concatenate([out.astype(LOW), jnp.zeros((112, wide), LOW)], axis=0)


def attention_forward(qT, key, vT, extra, oT, top, side, scale, hook):
    heads, size, queries = qT.shape
    keys = key.shape[1]
    ones = jnp.ones((16, keys), LOW)

    @pl.loop(0, heads // 2)
    def _(pair):
        hook(pair)
        lead = extra_of(1.0, None, queries)
        fill_side(side, [qT[2 * pair], qT[2 * pair + 1]], [lead, lead])
        left = jnp.concatenate([key[pair], extra[...]], axis=1)
        for half in range(2):
            head = 2 * pair + half
            s = nn(left, side[half])
            m = jnp.max(s, 0, keepdims=True)
            p = jnp.exp2((s - m) * scale).astype(LOW)
            o = nn(jnp.concatenate([vT[head], ones], axis=0), p)
            total = o[size : size + 1]
            oT[rows_of(head, size)] = (o[:size] * (1.0 / total)).astype(LOW)
            top[pl.ds(head, 1)] = m + jnp.log2(total) * (1.0 / scale)


def attention_backward(
    qT, key, h_all, qkvT, extra, doT, delta, top, dqT, dk, dv, qside, oside, lows, grads, scale, shrink, hook, chunk=512
):
    heads, size, queries = qT.shape
    keys = key.shape[1]

    @pl.loop(0, heads // 2)
    def _(pair):
        hook(pair)
        tops = [split3(top[pl.ds(2 * pair + half, 1)]) for half in range(2)]
        deltas = [split3(delta[pl.ds(2 * pair + half, 1)]) for half in range(2)]
        fill_side(qside, [qT[2 * pair], qT[2 * pair + 1]], [extra_of(1.0, t, queries) for t in tops])
        fill_side(oside, [doT[2 * pair], doT[2 * pair + 1]], [extra_of(0.0, t, queries) for t in deltas])
        kT = nt(qkvT[1, rows_of(pair, 128)], h_all[...]).astype(LOW)
        wide_o = jnp.concatenate([oside[0, :128], oside[1, :128]], axis=1)
        wide_q = jnp.concatenate([qside[0, :128], qside[1, :128]], axis=1)
        totals = [None, None]
        for c in range(keys // chunk):
            at = slice(c * chunk, (c + 1) * chunk)
            value = nt(h_all[at], qkvT[2, rows_of(pair, 128)]).astype(LOW)
            left_k = jnp.concatenate([key[pair, at], extra[at]], axis=1)
            left_v = jnp.concatenate([value, extra[at]], axis=1)
            for half in range(2):
                lanes = slice(half * queries, (half + 1) * queries)
                p = jnp.exp2(nn(left_k, qside[half]) * scale)
                lows[:, lanes] = p.astype(LOW)
                grads[:, lanes] = (p * nn(left_v, oside[half])).astype(LOW)
            for half in range(2):
                lanes = slice(half * queries, (half + 1) * queries)
                got = nn(kT[half * size : (half + 1) * size, at], grads[:, lanes])
                totals[half] = got if c == 0 else totals[half] + got
            dv[pair, at] = nt(lows[...], wide_o).astype(LOW)
            dk[pair, at] = (nt(grads[...], wide_q) * shrink).astype(LOW)
        for half in range(2):
            dqT[rows_of(2 * pair + half, size)] = (totals[half] * shrink).astype(LOW)


def windows(pad_ref, at_row, block, lanes, shifts):
    for s in range(8):
        mine = [(tap, shift) for tap, shift in shifts if shift % 8 == s]
        low = min(shift for _, shift in mine)
        high = max(shift for _, shift in mine)
        window = pad_ref[at_row + low : at_row + high + block, lanes]
        for tap, shift in mine:
            yield tap, window[shift - low : shift - low + block]


def convolve(pad_ref, taps_wide, put, shift_of, rows, width, block=64):
    count = taps_wide.shape[0]
    shifts = [(tap, shift_of(tap)) for tap in range(count)]
    for lane in range(0, width, 128):
        lanes = slice(lane, lane + 128)
        for at_row in range(0, rows, block):
            total = jnp.zeros((block // 8, 8, 128), F32)
            for tap, values in windows(pad_ref, at_row, block, lanes, shifts):
                total = total + taps_wide[tap, :, lanes][None] * values.reshape(block // 8, 8, 128)
            put(at_row, block, lane, total.reshape(block, 128))


def convolve_weight(pad_ref, grad_ref, first, out_ref, shift_of, rows, width, block=64):
    taps = out_ref.shape[0]
    for lane in range(0, width, 128):
        lanes = slice(lane, lane + 128)
        for s in range(8):
            mine = [(tap, shift_of(tap)) for tap in range(taps) if shift_of(tap) % 8 == s]
            low = min(shift for _, shift in mine)
            high = max(shift for _, shift in mine)
            sums = {tap: jnp.zeros((8, 128), F32) for tap, _ in mine}
            for at_row in range(0, rows, block):
                grad = grad_ref[first + at_row : first + at_row + block, lanes]
                window = pad_ref[at_row + low : at_row + high + block, lanes]
                for tap, shift in mine:
                    sums[tap] = sums[tap] + fold(grad * window[shift - low : shift - low + block])
            for tap, _ in mine:
                out_ref[tap : tap + 1, lanes] = jnp.sum(sums[tap], 0, keepdims=True)


def place_halo(pad_ref, halo, core):
    rows = pad_ref.shape[0] - 2 * HALO
    got = halo[...]
    zero = jnp.zeros_like(got)
    pad_ref[0:HALO] = jnp.where(core == 1, got, zero)
    pad_ref[rows + HALO :] = jnp.where(core == 0, got, zero)


def layer_kernel(cfg, *refs):
    r = SimpleNamespace(**dict(zip(cfg.names, refs)))
    count, shard, hidden, inside = cfg.count, cfg.shard, cfg.hidden, cfg.inside
    rows, width = r.x_in.shape
    heads, size = cfg.heads, width // cfg.heads
    keys, pairs, taps = 2 * rows, heads // 2, r.kern.shape[0]
    scale, shrink = math.log2(math.e) / math.sqrt(size), 1.0 / math.sqrt(size)
    route = Routes(count).here()
    core, me = route.core, route.me
    scal, vec, g0, g1, sums = r.scal, r.vec, r.g0, r.g1, r.sums
    chunk, block = 256, 64
    own = pl.ds(pl.multiple_of(core * rows, rows), rows)
    theirs = pl.ds(pl.multiple_of((1 - core) * rows, rows), rows)
    zero8 = jnp.zeros((8, width), F32)

    def block_rows(at):
        return pl.ds(pl.multiple_of(at * shard, shard), shard)

    barrier = pltpu.get_barrier_semaphore()
    for k in range(1, count):
        pl.semaphore_signal(
            barrier, inc=1, device_id={"batch": lax.rem(me + k, count)}, device_id_type=MESH
        )
    pl.semaphore_signal(barrier, inc=1, device_id={"seq": 1 - core}, device_id_type=MESH)
    half = width // 2
    q_own = pl.ds(pl.multiple_of(core * half, half), half)
    loads = [pltpu.make_async_copy(r.qkv_mine, r.qkvT.at[:, q_own], r.local.at[0])]
    if inside:
        mine = block_rows(core * count + me)
        loads.append(pltpu.make_async_copy(r.shards.at[0], g0.at[:, mine], r.local.at[1]))
        loads.append(pltpu.make_async_copy(r.shards.at[1], g1.at[:, mine], r.local.at[2]))
    else:
        loads.append(pltpu.make_async_copy(r.shards.at[0], g0, r.local.at[1]))
        loads.append(pltpu.make_async_copy(r.shards.at[1], g1, r.local.at[2]))
    for load in loads:
        load.start()
    sums[...] = jnp.zeros_like(sums)
    masked_input(scal, r.x_in, r.x1)

    def put_h0(at, value):
        r.h0[at] = value

    norm_rows(r.x1, put_h0, vec, 0)
    for tap in range(taps):
        r.wide[tap] = jnp.broadcast_to(r.kern[tap : tap + 1], (8, width))
    for load in loads:
        load.wait()
    pl.semaphore_wait(barrier, count)

    def inner(at):
        u, slope = activate(nt(g0[0, at], r.h0[...]))
        r.act[at] = u.astype(LOW)
        r.slope[at] = slope.astype(LOW)

    def inner_group(which, places):
        ats = [block_rows(which * count + place) for place in places]
        weight = jnp.concatenate([g0[0, at] for at in ats], axis=0)
        u, slope = activate(nt(weight, r.h0[...]))
        u, slope = u.astype(LOW), slope.astype(LOW)
        for n, at in enumerate(ats):
            r.act[at] = u[n * shard : (n + 1) * shard]
            r.slope[at] = slope[n * shard : (n + 1) * shard]

    swap_q = to_core(r.qkvT.at[:, q_own], r.qkvT.at[:, q_own], r.swap.at[0], r.swap.at[1], 1 - core)
    if inside:
        first = Gather(route, lambda b: g0.at[:, block_rows(b)], r.g_send.at[0], r.g_recv.at[0])
        second = Gather(route, lambda b: g1.at[:, block_rows(b)], r.g_send.at[1], r.g_recv.at[1])
        deep, side = range(route.deep), range(route.side)
        first.step_mid()
        first.step_one()
        inner_group(core, [route.near(d, 0, 0) for d in deep])
        swap_q.start()
        for d in deep:
            first.arrive(route.near(d, 0, 0), 1 - core)
        inner_group(1 - core, [route.near(d, 0, 0) for d in deep])
        first.step_two()
        second.step_mid()
        for e in side[1:]:
            inner_group(core, [route.near(d, e, 0) for d in deep])
            for d in deep:
                first.arrive(route.near(d, 0, e), 1 - core)
            inner_group(1 - core, [route.near(d, 0, e) for d in deep])
        for f in side[1:]:
            for e in side:
                for d in deep:
                    first.arrive(route.near(d, e, f))
                    first.cross(route.near(d, e, f))
                inner_group(core, [route.near(d, e, f) for d in deep])
        for f in side[1:]:
            for e in side:
                for d in deep:
                    first.arrive(route.near(d, f, e), 1 - core)
                inner_group(1 - core, [route.near(d, f, e) for d in deep])
    else:
        swap_q.start()

        @pl.loop(0, hidden // chunk)
        def _(i):
            inner(rows_of(i, chunk))

    @pl.loop(0, rows // 256)
    def _(i):
        at = rows_of(i, 256)
        r.x1[at] = r.x1[at] + 0.5 * tn(r.act[:, at], g0[1])

    def put_h2(at, value):
        r.h_all[pl.ds(pl.multiple_of(core * rows + at.start, block), block)] = value

    norm_rows(r.x1, put_h2, vec, 2)
    swap = to_core(r.h_all.at[own], r.h_all.at[own], r.swap.at[2], r.swap.at[3], 1 - core)
    swap.start()
    away = [
        pltpu.make_async_copy(g0, r.far_g, r.local.at[0]),
        pltpu.make_async_copy(r.act, r.far_act, r.local.at[1]),
        pltpu.make_async_copy(r.slope, r.far_slope, r.local.at[2]),
    ]
    for copy in away:
        copy.start()
    swap_q.wait()

    def project(at, vT):
        here = r.h_all[at]
        for pair in range(pairs):
            r.key[pair, at] = nt(here, r.qkvT[1, pair * 128 : (pair + 1) * 128]).astype(LOW)
        vT[:, :, at] = nt(r.qkvT[2], here).astype(LOW).reshape(heads, size, rows)

    r.extra[...] = key_extra(scal[1], keys)

    def attend(vT, side_ref):
        r.qT[...] = nt(r.qkvT[0], r.h_all[own]).astype(LOW).reshape(heads, size, rows)
        project(own, vT)
        if inside:
            second.step_one()
        swap.wait()
        project(theirs, vT)

        def hook(pair):
            if inside:
                @pl.when(pair == 1)
                def _():
                    second.step_two()

        attention_forward(r.qT, r.key, vT, r.extra, r.oT, r.top, side_ref, scale, hook)

    pl.run_scoped(attend, pltpu.VMEM((heads, size, keys), LOW), pltpu.VMEM((2, 256, rows), LOW))

    @pl.loop(0, rows // 256)
    def _(i):
        at = rows_of(i, 256)
        r.x2[at] = r.x1[at] + tn(r.oT[:, at], r.w_att[...])

    def put_h3(at, value):
        r.h3[at] = value

    norm_rows(r.x2, put_h3, vec, 4)

    @pl.loop(0, rows // 256)
    def _(i):
        at = rows_of(i, 256)
        _, ok = valid_rows(scal, i * 256, 256)
        here = r.h3[at]
        gate = sigmoid(nn(here, r.conv_in[:, width:]))
        r.pad[pl.ds(pl.multiple_of(i * 256 + HALO, HALO), 256)] = nn(here, r.conv_in[:, :width]) * gate * ok

    edge = pl.ds(pl.multiple_of(HALO + (1 - core) * (rows - HALO), HALO), HALO)
    swap = to_core(r.pad.at[edge], r.halo.at[0], r.swap.at[4], r.swap.at[5], 1 - core)
    swap.start()
    if inside:
        second.step_last()
    swap.wait()
    place_halo(r.pad, r.halo.at[0], core)

    def put_depth(at_row, high, lane, total):
        r.depth[at_row : at_row + high, lane : lane + 128] = total

    convolve(r.pad, r.wide, put_depth, lambda tap: tap + 1, rows, width)

    def moments(i, carry):
        one, two = carry
        _, ok = valid_rows(scal, i * block, block)
        here = r.depth[rows_of(i, block)]
        held = here * ok
        return one + fold(held), two + fold(here * held)

    one, two = lax.fori_loop(0, rows // block, moments, (zero8, zero8))
    number = jnp.clip(scal[1] - scal[0], 0, rows).astype(F32)
    r.part_a[0:8] = to_tile(
        jnp.concatenate([jnp.sum(one, 0, keepdims=True), jnp.sum(two, 0, keepdims=True)], axis=0)
    )
    r.part_a[8:16] = jnp.full((8, 128), 1.0, F32) * number
    every = Everyone(count, r.pair_a, r.slots_a, r.pair_sems_a, r.sends_a, r.recvs_a)
    every.start(r.part_a)
    if inside:
        second.step_other()
        second.finish()
        first.finish()
    for copy in away:
        copy.wait()
    tile = every.total()
    number = tile[8:9, 0:1]
    mean = from_tile(tile, 0, width) / number
    var = from_tile(tile, 1, width) / number - mean * mean
    spread = lax.rsqrt(var + EPS)
    gain6 = vec[6:7]

    if inside:
        stages = [
            Reduce(route, source, [ref.at[k] for ref in (r.zero, r.one, r.two, r.three)],
                   [(getattr(r, f"r_send{n}").at[k], getattr(r, f"r_recv{n}").at[k]) for n in range(4)])
            for k, source in enumerate(
                [
                    lambda b: g0.at[0, block_rows(b)],
                    lambda b: g0.at[1, block_rows(b)],
                    lambda b: r.box.at[0, b],
                    lambda b: r.box.at[1, b],
                    lambda b: g0.at[0, block_rows(b)],
                    lambda b: g0.at[1, block_rows(b)],
                ]
            )
        ]
        in1, out1, rest, proj, in0, out0 = stages
    back_copies = [
        pltpu.make_async_copy(r.far_act, r.act, r.local.at[0]),
        pltpu.make_async_copy(r.far_slope, r.slope, r.local.at[1]),
        pltpu.make_async_copy(r.far_g, g1, r.local.at[2]),
    ]

    def ffn_grads(weight_out, h_ref, dy, da, pieces):
        chunks = hidden // chunk

        @pl.loop(0, chunks)
        def _(i):
            turned = lax.rem(i + (1 - core) * (chunks // 2), chunks)
            at = rows_of(turned, chunk)
            du = nt(weight_out[at], dy[...])
            low = (du * r.slope[at].astype(F32)).astype(LOW)
            da[at] = low
            g0[1, at] = nn(r.act[at], dy[...]).astype(LOW)
            g0[0, at] = nn(low, h_ref[...]).astype(LOW)
            if inside:
                @pl.when(i < chunks // 2)
                def _():
                    per = chunk // shard
                    for n in range(per):
                        place = i * per + n
                        for piece in pieces:
                            to_core(
                                piece.source((1 - core) * count + place),
                                piece.zero.at[place], piece.s0.at[place], piece.r0.at[place], 1 - core,
                            ).start()

    def middle(slope_z, da, dh):
        low, dy, h4 = r.d_conv_in.at[:, pl.ds(0, width)], r.d_conv_in.at[:, pl.ds(width, width)], r.d_att
        x3, x4 = r.input_grad, r.dz

        @pl.loop(0, rows // block)
        def _(i):
            at = rows_of(i, block)
            z = (r.depth[at] - mean) * spread * gain6 + vec[7:8]
            u, slope = activate(z)
            low[at] = u.astype(LOW)
            slope_z[at] = slope

        @pl.loop(0, rows // 256)
        def _(i):
            at = rows_of(i, 256)
            x3[at] = r.x2[at] + nn(low[at], r.conv_out[...])

        def put_h4(at, value):
            h4[at] = value

        norm_rows(x3, put_h4, vec, 8)

        @pl.loop(0, hidden // chunk)
        def _(i):
            at = rows_of(i, chunk)
            u, slope = activate(nt(g1[0, at], h4[...]))
            r.act[at] = u.astype(LOW)
            r.slope[at] = slope.astype(LOW)

        @pl.loop(0, rows // 256)
        def _(i):
            at = rows_of(i, 256)
            x4[at] = x3[at] + 0.5 * tn(r.act[:, at], g1[1])

        def last(i, carry):
            gain, bias = carry
            at = rows_of(i, block)
            hat, rate = normed(x4[at])
            r.out[at] = (hat * vec[10:11] + vec[11:12]).astype(LOW)
            g = r.cot[at].astype(F32)
            back = normed_back(g * vec[10:11], hat, rate)
            r.grad[at] = back
            dy[at] = (0.5 * back).astype(LOW)
            return gain + fold(g * hat), bias + fold(g)

        gain, bias = lax.fori_loop(0, rows // block, last, (zero8, zero8))
        sums[10:11] = jnp.sum(gain, 0, keepdims=True)
        sums[11:12] = jnp.sum(bias, 0, keepdims=True)
        ffn_grads(g1.at[1], h4, dy, da, [in1, out1] if inside else None)
        back_copies[0].start()
        back_copies[1].start()

        @pl.loop(0, rows // 256)
        def _(i):
            at = rows_of(i, 256)
            dh[at] = tn(da[:, at], g1[0])

        back_copies[2].start()

        def put(at, value):
            r.grad[at] = value
            dy[at] = value.astype(LOW)

        norm_rows_back(dh, x3, r.grad, put, vec, sums, 8)
        got = tn(low[...], dy[...]).astype(LOW)
        if inside:
            r.box[0, :, 0:16] = got.reshape(2 * count, 16, width)
        else:
            r.d_conv_out[...] = got

        @pl.loop(0, rows // 256)
        def _(i):
            at = rows_of(i, 256)
            r.dz[at] = nt(dy[at], r.conv_out[...])

        def close(i, carry):
            one, two = carry
            at = rows_of(i, block)
            here = r.dz[at] * slope_z[at]
            r.dz[at] = here
            return one + fold(here), two + fold(here * (r.depth[at] - mean))

        one, two = lax.fori_loop(0, rows // block, close, (zero8, zero8))
        r.part_b[...] = to_tile(
            jnp.concatenate([jnp.sum(one, 0, keepdims=True), jnp.sum(two, 0, keepdims=True)], axis=0)
        )

    square = (rows, width)
    vm = pltpu.VMEM
    pl.run_scoped(
        middle, vm(square, F32), vm((hidden, rows), LOW), vm(square, F32),
    )
    if not inside:
        copy = pltpu.make_async_copy(g0, r.d_ffn.at[1], r.local.at[3])
        copy.start()
        copy.wait()
    every = Everyone(count, r.pair_b, r.slots_b, r.pair_sems_b, r.sends_b, r.recvs_b)
    every.start(r.part_b)
    tile = every.total()
    grad_sum, grad_moment = from_tile(tile, 0, width), from_tile(tile, 1, width)
    if inside:
        out1.step_one()
        in1.step_one()
    var_grad = -0.5 * (gain6 * grad_moment) * spread * spread * spread
    flat = (-(gain6 * spread * grad_sum) - 2.0 * mean * var_grad) / number
    tilt = 2.0 * var_grad / number

    def convolution_back(back, p, datt):
        dp, dh = r.d_conv_in if inside else r.spare_wide, r.input_grad

        @pl.loop(0, rows // block)
        def _(i):
            at = rows_of(i, block)
            _, ok = valid_rows(scal, i * block, block)
            back[pl.ds(pl.multiple_of(i * block + HALO, HALO), block)] = gain6 * spread * r.dz[at] + ok * (
                flat + r.depth[at] * tilt
            )

        swap = to_core(back.at[edge], r.halo.at[1], r.swap.at[6], r.swap.at[7], 1 - core)
        swap.start()
        convolve_weight(r.pad, back, HALO, r.small.at[pl.ds(0, taps)], lambda tap: tap + 1, rows, width)
        if inside:
            out1.step_own()
            in1.step_own()

        @pl.loop(0, rows // 256)
        def _(i):
            at = rows_of(i, 256)
            p[at] = nn(r.h3[at], r.conv_in[...])

        swap.wait()
        place_halo(back, r.halo.at[1], core)

        def put(at_row, high, lane, total):
            at = slice(at_row, at_row + high)
            _, ok = valid_rows(scal, at_row, high)
            gate = sigmoid(p[at, width + lane : width + lane + 128])
            total = total * gate * ok
            dp[at, lane : lane + 128] = total.astype(LOW)
            dp[at, width + lane : width + lane + 128] = (
                total * p[at, lane : lane + 128] * (1.0 - gate)
            ).astype(LOW)

        convolve(back, r.wide, put, lambda tap: taps - 1 - tap, rows, width)
        if inside:
            out1.step_two()
            in1.step_two()
        got = tn(r.h3[...], dp[...]).astype(LOW)
        if inside:
            r.box[0, :, 16:32] = got[:, :width].reshape(2 * count, 16, width)
            r.box[0, :, 32:48] = got[:, width:].reshape(2 * count, 16, width)
        else:
            r.d_conv_in[...] = got

        @pl.loop(0, rows // 256)
        def _(i):
            at = rows_of(i, 256)
            dh[at] = nt(dp[at], r.conv_in[...])

        def put_first(at, got):
            r.grad[at] = got
            datt[at] = got.astype(LOW)

        norm_rows_back(dh, r.x2, r.grad, put_first, vec, sums, 4)
        got = nn(r.oT[...], datt[...]).astype(LOW)
        if inside:
            r.box[0, :, 48:64] = got.reshape(2 * count, 16, width)
            rest.start()
            out1.step_three()
            in1.step_three()
        else:
            r.d_att[...] = got
        r.doT[...] = nt(r.w_att[...], datt[...]).astype(LOW).reshape(heads, size, rows)

    pl.run_scoped(
        convolution_back, vm(r.pad.shape, F32), vm((rows, 2 * width), F32), vm(square, LOW),
    )

    def attend_back(delta, qside, oside, lows, grads, dk, dv):
        dqT = r.d_conv_out if inside else r.spare

        for head in range(heads):
            o = r.oT[head * size : (head + 1) * size].astype(F32)
            delta[head : head + 1] = jnp.sum(o * r.doT[head].astype(F32), 0, keepdims=True)

        def hook(pair):
            if inside:
                @pl.when(pair == 1)
                def _():
                    rest.step_one()
                    r.fin_out[1] = out1.total()
                    r.fin_in[1] = in1.total()

                @pl.when(pair == 3)
                def _():
                    rest.step_own()
                    rest.step_two()

        attention_backward(
            r.qT, r.key, r.h_all, r.qkvT, r.extra, r.doT, delta, r.top, dqT, dk, dv, qside, oside, lows, grads,
            scale, shrink, hook,
        )
        swaps = [
            to_core(dk.at[:, theirs], r.rk, r.swap.at[8], r.swap.at[9], 1 - core),
            to_core(dv.at[:, theirs], r.rv, r.swap.at[10], r.swap.at[11], 1 - core),
        ]
        for swap in swaps:
            swap.start()
        r.dq[...] = dqT[...].astype(F32).T.astype(LOW)
        for swap in swaps:
            swap.wait()
        for pair in range(pairs):
            lanes = slice(pair * 128, (pair + 1) * 128)
            r.h3[:, lanes] = (dk[pair, own].astype(F32) + r.rk[pair].astype(F32)).astype(LOW)
            r.own_v[:, lanes] = (dv[pair, own].astype(F32) + r.rv[pair].astype(F32)).astype(LOW)

    pl.run_scoped(
        attend_back, vm((heads, rows), F32), vm((2, 256, rows), LOW), vm((2, 256, rows), LOW),
        vm((keys // 2, 2 * rows), LOW), vm((keys // 2, 2 * rows), LOW),
        vm((pairs, keys, 128), LOW), vm((pairs, keys, 128), LOW),
    )
    if inside:
        rest.step_three()

    def put_qkv(s, got):
        if inside:
            for c in range(2):
                v = got[:, c * half : (c + 1) * half].reshape(count, 2, 16, half)
                r.box[1, c * count : (c + 1) * count, s * 16 : (s + 1) * 16] = jnp.concatenate(
                    [v[:, 0], v[:, 1]], axis=-1
                )
        else:
            r.d_qkv[s] = got

    def project_back(dh, dy, da, x0):
        own_k, own_v = r.h3, r.own_v
        h2 = r.h_all[own]
        put_qkv(0, tn(h2, r.dq[...]).astype(LOW))
        put_qkv(1, tn(h2, own_k[...]).astype(LOW))
        put_qkv(2, tn(h2, own_v[...]).astype(LOW))
        if inside:
            r.held[0, core * count + me] = rest.total().astype(LOW)
            third = Gather(route, lambda b: r.held.at[0, b], r.g_send.at[2], r.g_recv.at[2])
            third.step_mid()

        @pl.loop(0, rows // 256)
        def _(i):
            at = rows_of(i, 256)
            dh[at] = nn(r.dq[at], r.qkvT[0]) + nn(own_k[at], r.qkvT[1]) + nn(own_v[at], r.qkvT[2])

        def put_second(at, got):
            r.grad[at] = got
            dy[at] = (0.5 * got).astype(LOW)

        norm_rows_back(dh, r.x1, r.grad, put_second, vec, sums, 2)
        if inside:
            r.small[taps : taps + 16] = sums[...]
            r.box[1, :, 48:64] = jnp.zeros((2 * count, 16, width), LOW)
            for n in range((taps + 16) // 16):
                r.box[1, n, 48:64] = r.small[n * 16 : (n + 1) * 16].astype(LOW)
            proj.start()
            third.step_one()
            for piece in (in1, out1):
                piece.sent_core()
        for copy in back_copies:
            copy.wait()
        ffn_grads(g1.at[1], r.h0, dy, da, [in0, out0] if inside else None)
        if inside:
            proj.step_one()
            out0.step_one()
            in0.step_one()
            third.step_two()
            proj.step_own()
        masked_input(scal, r.x_in, x0)

        @pl.loop(0, rows // 256)
        def _(i):
            at = rows_of(i, 256)
            dh[at] = tn(da[:, at], g1[0])

        def put_input(at, got):
            r.input_grad[at] = got * keep_rows(scal, at.start, block, width)

        norm_rows_back(dh, x0, r.grad, put_input, vec, sums, 0)
        return third if inside else None

    def tail(dh, dy, da, x0):
        third = project_back(dh, dy, da, x0)
        if not inside:
            return
        proj.step_two()
        out0.step_own()
        in0.step_own()
        out0.step_two()
        in0.step_two()
        proj.step_three()
        third.step_last()
        out0.step_three()
        in0.step_three()
        r.held[1, core * count + me] = proj.total().astype(LOW)
        fourth = Gather(route, lambda b: r.held.at[1, b], r.g_send.at[3], r.g_recv.at[3])
        fourth.step_mid()
        r.part_c[...] = to_tile(sums[0:2])
        every = Everyone(count, r.pair_c, r.slots_c, r.pair_sems_c, r.sends_c, r.recvs_c)
        every.start(r.part_c)
        fourth.step_one()
        r.fin_out[0] = out0.total()
        fourth.step_two()
        r.fin_in[0] = in0.total()
        third.step_other()
        got = r.held[0]
        blocks = 2 * count
        r.d_conv_out[...] = got[:, 0:16].reshape(width, width)
        r.d_conv_in[:, :width] = got[:, 16:32].reshape(width, width)
        r.d_conv_in[:, width:] = got[:, 32:48].reshape(width, width)
        r.d_att[...] = got[:, 48:64].reshape(width, width)
        fourth.step_last()
        tile = every.total()
        fourth.step_other()
        got = r.held[1, pl.ds(core * count, count)]
        for s in range(3):
            v = got[:, s * 16 : (s + 1) * 16]
            v = jnp.concatenate([v[:, None, :, :half], v[:, None, :, half:]], axis=1)
            r.d_qkv[s] = v.reshape(width, half)
        got = r.held[1, 0 : (taps + 16) // 16, 48:64].reshape(taps + 16, width).astype(F32)
        r.d_kern[...] = got[:taps]
        r.d_vec[...] = jnp.concatenate(
            [
                from_tile(tile, 0, width), from_tile(tile, 1, width), got[taps + 2 : taps + 6],
                spread * grad_moment, grad_sum, got[taps + 8 : taps + 12],
            ],
            axis=0,
        )
        third.finish()
        fourth.finish()
        for piece in stages:
            piece.finish()
        for piece in (rest, proj, in0, out0):
            piece.sent_core()

    pl.run_scoped(
        tail, vm(square, F32), vm(square, LOW), vm((hidden, rows), LOW),
        vm(square, F32),
    )
    if not inside:
        r.small[taps : taps + 16] = sums[...]
        r.small[taps + 6 : taps + 7] = spread * grad_moment
        r.small[taps + 7 : taps + 8] = grad_sum
        copy = pltpu.make_async_copy(g0, r.d_ffn.at[0], r.local.at[3])
        copy.start()
        copy.wait()


def gather_steps(route, chunk, held, sends, recv, with_core=True):
    started = []
    core, count = route.core, route.count

    def block(place):
        return core * count + place

    def arrive(place):
        here = held.at[chunk, block(place)]
        to_batch(here, here, recv.at[chunk, block(place)], recv.at[chunk, block(place)], route.me).wait_recv()

    def send(place, target):
        slot = len(started)
        here = held.at[chunk, block(place)]
        copy = to_batch(here, here, sends.at[chunk, slot], recv.at[chunk, block(place)], target)
        copy.start()
        started.append(copy)

    def cross(place):
        if not with_core:
            return
        slot = len(started)
        here = held.at[chunk, block(place)]
        copy = to_core(here, here, sends.at[chunk, slot], recv.at[chunk, block(place)], 1 - core)
        copy.start()
        started.append(copy)

    def step_mid():
        for k in range(1, route.deep):
            send(route.me, route.index(lax.rem(route.z + k, route.deep), route.p, route.q))
        cross(route.me)

    def step_one():
        for d in range(route.deep):
            z = lax.rem(route.z + d, route.deep)
            place = route.index(z, route.p, route.q)
            if d:
                arrive(place)
            for k in range(1, route.side):
                send(place, route.index(route.z, lax.rem(route.p + k, route.side), route.q))
            if d:
                cross(place)

    def step_two():
        for d in range(route.deep):
            z = lax.rem(route.z + d, route.deep)
            for e in range(route.side):
                p = lax.rem(route.p + e, route.side)
                place = route.index(z, p, route.q)
                if e:
                    arrive(place)
                for k in range(1, route.side):
                    send(place, route.index(route.z, route.p, lax.rem(route.q + k, route.side)))
                if e:
                    cross(place)

    def step_last():
        for d in range(route.deep):
            z = lax.rem(route.z + d, route.deep)
            for e in range(route.side):
                p = lax.rem(route.p + e, route.side)
                for f in range(1, route.side):
                    place = route.index(z, p, lax.rem(route.q + f, route.side))
                    arrive(place)
                    cross(place)

    def step_end():
        if with_core:
            for place in range(count):
                other = held.at[chunk, (1 - core) * count + place]
                at = recv.at[chunk, (1 - core) * count + place]
                to_core(other, other, at, at, 1 - core).wait_recv()
        for copy in started:
            copy.wait_send()

    return [step_mid, step_one, step_two, step_last, step_end]


def sends_of(route):
    return (route.deep - 1) + route.deep * (route.side - 1) * (1 + route.side) + route.count


def run_steps(all_steps):
    depth = len(all_steps[0])
    for turn in range(depth + len(all_steps) - 1):
        for chunk, steps in enumerate(all_steps):
            if 0 <= turn - chunk < depth:
                steps[turn - chunk]()


def gather_kernel(count, mine, held, local, sends, recv):
    route = Routes(count).here()
    chunks = mine.shape[0]
    copies = []
    for chunk in range(chunks):
        own = held.at[chunk, route.core * count + route.me]
        copy = pltpu.make_async_copy(mine.at[chunk], own, local.at[chunk])
        copy.start()
        copies.append(copy)
    route.greet()
    for copy in copies:
        copy.wait()
    run_steps([gather_steps(route, chunk, held, sends, recv) for chunk in range(chunks)])


def gather_all(mine, count, collective_id):
    chunks, rows, width = mine.shape
    route = Routes(count)
    return pl.pallas_call(
        functools.partial(gather_kernel, count),
        out_shape=jax.ShapeDtypeStruct((chunks, 2 * count, rows, width), mine.dtype),
        in_specs=[pl.BlockSpec(memory_space=pltpu.VMEM)],
        out_specs=pl.BlockSpec(memory_space=pltpu.VMEM),
        scratch_shapes=[
            pltpu.SemaphoreType.DMA((chunks,)),
            pltpu.SemaphoreType.DMA((chunks, sends_of(route))),
            pltpu.SemaphoreType.DMA((chunks, 2 * count)),
        ],
        compiler_params=pltpu.CompilerParams(
            collective_id=collective_id, has_side_effects=True, vmem_limit_bytes=VMEM_BYTES
        ),
    )(mine)


def reduce_kernel(count, solo, n, *refs):
    pieces, (fin, held, grads, packing, *rest) = refs[:n], refs[n:]
    copies = []
    at = 0
    for i, piece in enumerate(pieces):
        lines = piece.shape[1]
        copy = pltpu.make_async_copy(piece, grads.at[:, pl.ds(at, lines)], packing.at[i])
        copy.start()
        copies.append(copy)
        at += lines
    for copy in copies:
        copy.wait()
    reduce_packed(count, solo, grads, fin, held, *rest)


def reduce_packed(count, solo, grads, fin, held, zero, one, two, three, s0, r0, s1, r1, s2, r2, s3, r3, sends, recv):
    route = Routes(count).here()
    core, me, side, deep = route.core, route.me, route.side, route.deep
    rows, width = grads.shape[1:]
    piece = 16

    def add(target, source):
        @pl.loop(0, rows // piece)
        def _(i):
            at = pl.ds(pl.multiple_of(i * piece, piece), piece)
            target[at] = (target[at].astype(jnp.float32) + source[at].astype(jnp.float32)).astype(target.dtype)

    route.greet()
    waits = []
    order = []
    for f in range(side - 1, -1, -1):
        for d in range(deep):
            for e in range(side - 1, -1, -1):
                order.append((d, e, f))
    for d, e, f in order:
        place = route.index(lax.rem(route.z + d, deep), lax.rem(route.p + e, side), lax.rem(route.q + f, side))
        copy = to_core(grads.at[(1 - core) * count + place], zero.at[place], s0.at[place], r0.at[place], 1 - core)
        copy.start()
        waits.append(copy)
    for e in range(side - 1, -1, -1):
        for d in range(deep):
            for f in range(side - 1, -1, -1):
                z, p, q = lax.rem(route.z + d, deep), lax.rem(route.p + e, side), lax.rem(route.q + f, side)
                place = route.index(z, p, q)
                to_core(zero.at[place], zero.at[place], s0.at[place], r0.at[place], 1 - core).wait_recv()
                add(zero.at[place], grads.at[core * count + place])
                if e:
                    slot = (e - 1) * deep * side + z * side + q
                    copy = to_batch(
                        zero.at[place], one.at[slot], s1.at[slot], r1.at[slot], route.index(route.z, p, route.q)
                    )
                    copy.start()
                    waits.append(copy)
    for f in range(side - 1, -1, -1):
        for d in range(deep):
            z, q = lax.rem(route.z + d, deep), lax.rem(route.q + f, side)
            place = route.index(z, route.p, q)
            for e in range(1, side):
                slot = (e - 1) * deep * side + z * side + q
                to_batch(one.at[slot], one.at[slot], s1.at[slot], r1.at[slot], me).wait_recv()
                add(zero.at[place], one.at[slot])
            if f:
                slot = (f - 1) * deep + z
                copy = to_batch(
                    zero.at[place], two.at[slot], s2.at[slot], r2.at[slot], route.index(route.z, route.p, q)
                )
                copy.start()
                waits.append(copy)
    for d in range(deep - 1, -1, -1):
        z = lax.rem(route.z + d, deep)
        place = route.index(z, route.p, route.q)
        for f in range(1, side):
            slot = (f - 1) * deep + z
            to_batch(two.at[slot], two.at[slot], s2.at[slot], r2.at[slot], me).wait_recv()
            add(zero.at[place], two.at[slot])
        if d:
            copy = to_batch(zero.at[place], three.at[d - 1], s3.at[d - 1], r3.at[d - 1], place)
            copy.start()
            waits.append(copy)
    for d in range(1, deep):
        to_batch(three.at[d - 1], three.at[d - 1], s3.at[d - 1], r3.at[d - 1], me).wait_recv()

    def final(at):
        total = zero[me, at].astype(jnp.float32)
        for d in range(1, deep):
            total = total + three[d - 1, at].astype(jnp.float32)
        return total

    mine = core * count + me

    @pl.loop(0, (rows - solo) // piece)
    def _(i):
        at = pl.ds(pl.multiple_of(i * piece, piece), piece)
        held[0, mine, at] = final(pl.ds(pl.multiple_of(solo + i * piece, piece), piece)).astype(held.dtype)

    steps = gather_steps(route, 0, held, sends, recv)
    steps[0]()

    @pl.loop(0, solo // piece)
    def _(i):
        at = pl.ds(pl.multiple_of(i * piece, piece), piece)
        fin[at] = final(at)

    for step in steps[1:]:
        step()
    for copy in waits:
        copy.wait_send()


def reduce_all(pieces, solo, count, collective_id):
    blocks, _, width = pieces[0].shape
    kind = pieces[0].dtype
    if any(piece.shape[1] % 16 for piece in pieces):
        used = sum(piece.shape[1] for piece in pieces)
        spare = jnp.zeros((blocks, -used % 16, width), kind)
        pieces = [jnp.concatenate([*pieces, spare], axis=1)]
    rows = sum(piece.shape[1] for piece in pieces)
    route = Routes(count)
    side, deep = route.side, route.deep
    n1 = max(1, (side - 1) * side * deep)
    n2 = max(1, (side - 1) * deep)
    n3 = max(1, deep - 1)
    dma = pltpu.SemaphoreType.DMA
    return pl.pallas_call(
        functools.partial(reduce_kernel, count, solo, len(pieces)),
        out_shape=(
            jax.ShapeDtypeStruct((solo, width), jnp.float32),
            jax.ShapeDtypeStruct((1, blocks, rows - solo, width), kind),
        ),
        in_specs=[pl.BlockSpec(memory_space=pl.ANY)] * len(pieces),
        out_specs=(pl.BlockSpec(memory_space=pltpu.VMEM), pl.BlockSpec(memory_space=pltpu.VMEM)),
        scratch_shapes=[
            pltpu.VMEM((blocks, rows, width), kind),
            dma((len(pieces),)),
            pltpu.VMEM((count, rows, width), kind),
            pltpu.VMEM((n1, rows, width), kind),
            pltpu.VMEM((n2, rows, width), kind),
            pltpu.VMEM((n3, rows, width), kind),
            dma((count,)), dma((count,)),
            dma((n1,)), dma((n1,)),
            dma((n2,)), dma((n2,)),
            dma((n3,)), dma((n3,)),
            dma((1, sends_of(route))), dma((1, blocks)),
        ],
        compiler_params=pltpu.CompilerParams(
            collective_id=collective_id, has_side_effects=True, vmem_limit_bytes=VMEM_BYTES
        ),
    )(*pieces)


def per_device(
    block_input, lengths, spans, cotangent, ffn_in, ffn_out, qkv_weight, out_weight, conv_in, kernel, conv_out, vectors,
):
    _, rows, width = block_input.shape
    count = lax.axis_size("batch")
    core = lax.axis_index("seq")
    shard = ffn_in.shape[1]
    blocks = 2 * count
    hidden = shard * blocks
    heads, size = HEADS, width // HEADS
    keys = 2 * rows
    taps = kernel.shape[0]
    inside = shard % 64 == 0 and width == 16 * blocks
    route = Routes(count)
    vm, dma = pltpu.VMEM, pltpu.SemaphoreType.DMA
    scal = jnp.concatenate(
        [jnp.reshape(core * rows, (1,)), lengths[:1], spans[0], jnp.zeros((2,), jnp.int32)]
    ).astype(jnp.int32)
    shards = jnp.stack([ffn_in, ffn_out], axis=1)
    if not inside:
        got = gather_all(shards.reshape(2, 2 * shard, width), count, 1).reshape(2, blocks, 2, shard, width)
        shards = got.transpose(0, 2, 1, 3, 4).reshape(2, 2, hidden, width)
    square, tall = (rows, width), (hidden, rows)
    weights = (2, hidden, width)
    here, hbm = pl.BlockSpec(memory_space=pltpu.VMEM), pl.BlockSpec(memory_space=pl.ANY)
    ins = dict(
        scal=scal, x_in=block_input[0], cot=cotangent[0], vec=vectors, w_att=out_weight, conv_in=conv_in,
        conv_out=conv_out, kern=kernel, qkv_mine=qkv_weight.transpose(0, 2, 1), shards=shards,
    )
    in_specs = [pl.BlockSpec(memory_space=pltpu.SMEM)] + [here] * (len(ins) - 1)
    if not inside:
        in_specs[-1] = hbm
    outs = dict(
        out=(square, LOW, here), input_grad=(square, F32, here), far_g=(weights, LOW, hbm), far_act=(tall, LOW, hbm),
        far_slope=(tall, LOW, hbm), d_att=((width, width), LOW, here), d_conv_in=((width, 2 * width), LOW, here),
        d_conv_out=((width, width), LOW, here),
    )
    if inside:
        outs |= dict(
            fin_in=((2, shard, width), F32, here), fin_out=((2, shard, width), F32, here),
            d_qkv=((3, width, width // 2), LOW, here), d_kern=((taps, width), F32, here), d_vec=((12, width), F32, here),
        )
    else:
        outs |= dict(
            d_qkv=((3, width, width), LOW, here), small=((taps + 16, width), F32, here),
            d_ffn=((2, 2, hidden, width), LOW, hbm),
        )
    scratch = dict(
        g0=vm(weights, LOW), g1=vm(weights, LOW), act=vm(tall, LOW), slope=vm(tall, LOW), qkvT=vm((3, width, width), LOW),
        x1=vm(square, F32), x2=vm(square, F32), grad=vm(square, F32), depth=vm(square, F32),
        dz=vm(square, F32), pad=vm((rows + 2 * HALO, width), F32), halo=vm((2, HALO, width), F32),
        h0=vm(square, LOW), h_all=vm((keys, width), LOW), h3=vm(square, LOW), key=vm((heads // 2, keys, 128), LOW),
        qT=vm((heads, size, rows), LOW), oT=vm((width, rows), LOW), doT=vm((heads, size, rows), LOW),
        top=vm((heads, rows), F32), extra=vm((keys, 128), LOW), wide=vm((taps, 8, width), F32), sums=vm((16, width), F32),
        own_v=vm(square, LOW),
        rk=vm((heads // 2, rows, 128), LOW), rv=vm((heads // 2, rows, 128), LOW), dq=vm(square, LOW),
        local=dma((4,)), swap=dma((12,)),
    )
    for name, lines in (("a", 16), ("b", 8), ("c", 8))[: 3 if inside else 2]:
        scratch[f"part_{name}"] = vm((lines, 128), F32)
        for key, kind in zip(("pair", "slots", "pair_sems", "sends", "recvs"), Everyone.scratch(count, lines)):
            scratch[f"{key}_{name}"] = kind
    if not inside:
        scratch |= dict(spare=vm((width, rows), LOW), spare_wide=vm((rows, 2 * width), LOW))
    if inside:
        numbers = stage_counts(route)
        for key, number in zip(("zero", "one", "two", "three"), numbers):
            scratch[key] = vm((6, number, shard, width), LOW)
        scratch |= dict(
            box=vm((2, blocks, 64, width), LOW), held=vm((2, blocks, 64, width), LOW),
            small=vm((taps + 16, width), F32),
            g_send=dma((4, sends_of(route))), g_recv=dma((4, blocks)),
        )
        for n, number in enumerate(numbers):
            scratch[f"r_send{n}"] = dma((6, number))
            scratch[f"r_recv{n}"] = dma((6, number))
    cfg = SimpleNamespace(
        names=[*ins, *outs, *scratch], count=count, shard=shard, hidden=hidden, heads=heads, inside=inside
    )
    results = pl.pallas_call(
        functools.partial(layer_kernel, cfg),
        out_shape=tuple(jax.ShapeDtypeStruct(shape, kind) for shape, kind, _ in outs.values()),
        in_specs=in_specs,
        out_specs=tuple(spec for _, _, spec in outs.values()),
        scratch_shapes=list(scratch.values()),
        compiler_params=pltpu.CompilerParams(collective_id=0, has_side_effects=True, vmem_limit_bytes=VMEM_BYTES),
    )(*ins.values())
    got = SimpleNamespace(**dict(zip(outs, results)))
    if inside:
        return (
            got.out[None], got.input_grad[None], got.fin_in, got.fin_out, got.d_qkv.astype(F32), got.d_att.astype(F32),
            got.d_conv_in.astype(F32), got.d_kern, got.d_conv_out.astype(F32), got.d_vec,
        )

    def spread(values):
        flat = values.astype(LOW).reshape(-1, width)
        lines = -(-flat.shape[0] // blocks)
        flat = jnp.pad(flat, ((0, lines * blocks - flat.shape[0]), (0, 0)))
        return flat.reshape(blocks, lines, width)

    lines = 3 * width // (2 * count)
    per_core = got.d_qkv.reshape(3 * width, 2, width // 2).transpose(1, 0, 2).reshape(blocks, -1, width)
    d_in0, d_out0, d_in1, d_out1 = (got.d_ffn[j, m] for j in range(2) for m in range(2))
    rest = (got.d_att, got.d_conv_in, got.d_conv_out, got.small)
    pieces = [spread(v) for v in (d_in0, d_out0, d_in1, d_out1, *rest)] + [per_core]
    fin, shared = reduce_all(pieces, 4 * shard, count, 2)
    at = 0
    whole = []
    for piece, like in zip(pieces[4:8], rest):
        part = shared[0, :, at : at + piece.shape[1]].reshape(-1, width)
        whole.append(part[: like.size // width].reshape(like.shape).astype(F32))
        at += piece.shape[1]
    mine = lax.dynamic_slice_in_dim(shared[0], core * count, count, axis=0)[:, at : at + per_core.shape[1]]
    row = lax.broadcasted_iota(jnp.int32, (12, 1), 0)
    d_vec = jnp.where((row == 6) | (row == 7), got.small[taps : taps + 12], whole[3][taps : taps + 12])
    return (
        got.out[None], got.input_grad[None], jnp.stack([fin[:shard], fin[2 * shard : 3 * shard]]),
        jnp.stack([fin[shard : 2 * shard], fin[3 * shard :]]),
        mine.reshape(3, width, width // 2).astype(F32), whole[0], whole[1], whole[3][:taps], whole[2], d_vec,
    )


def solution(mesh):
    placed = (
        P("batch", "seq", None),
        P("batch"),
        P("batch", None),
        P("batch", "seq", None),
        P(None, ("seq", "batch"), None),
        P(None, ("seq", "batch"), None),
        P(None, None, "seq"),
        P(),
        P(),
        P(),
        P(),
        P(),
    )
    return jax.shard_map(
        per_device,
        mesh=mesh,
        in_specs=placed,
        out_specs=(
            P("batch", "seq", None),
            P("batch", "seq", None),
            P(None, ("seq", "batch"), None),
            P(None, ("seq", "batch"), None),
            P(None, None, "seq"),
            P(),
            P(),
            P(),
            P(),
            P(),
        ),
        check_vma=False,
    )
```

```python
import functools
import math
from types import SimpleNamespace

import jax
import jax.numpy as jnp
from jax import lax
from jax.experimental import pallas as pl
from jax.experimental.pallas import tpu as pltpu
from jax.sharding import PartitionSpec as P

HEADS = 8
MESH = pl.DeviceIdType.MESH
VMEM_BYTES = 63 * 1024 * 1024
F32, LOW = jnp.float32, jnp.bfloat16
EPS = 1e-05
HALO = 16


class Routes:
    def __init__(self, count):
        if count == 16:
            first, last, middle = (1, 2), (2, 2), (4, 4)
        elif count == 128:
            first, last, middle = (1, 4), (32, 4), (4, 8)
        else:
            first, last, middle = (1, 1), (1, 1), (1, count)
        self.count = count
        self.side = first[1]
        self.deep = middle[1]
        self.first, self.last, self.middle = first, last, middle

    def here(self):
        self.core = lax.axis_index("seq")
        self.me = lax.axis_index("batch")
        turn = self.core * (self.last[0] - self.first[0])
        self.one = self.first[0] + turn
        self.two = self.last[0] - turn
        self.mid = self.middle[0]
        self.p = lax.rem(lax.div(self.me, self.one), self.side)
        self.q = lax.rem(lax.div(self.me, self.two), self.side)
        self.z = lax.rem(lax.div(self.me, self.mid), self.deep)
        return self

    def index(self, z, p, q):
        return z * self.mid + p * self.one + q * self.two

    def plane(self, d):
        if self.deep != 4 or d == 0:
            return lax.rem(self.z + d, self.deep) if d else self.z
        return (self.z + 1 - 2 * lax.rem(self.z, 2), lax.rem(self.z + 2, 4), 3 - self.z)[d - 1]

    def reach(self, i):
        far = lax.div(self.z, 2)
        first = self.z + far * (3 - 2 * self.z)
        turn = (first, 1 - first, 2, 3)[i]
        return turn + far * (3 - 2 * turn)

    def near(self, d, e, f):
        p = lax.rem(self.p + e, self.side) if e else self.p
        q = lax.rem(self.q + f, self.side) if f else self.q
        return self.index(self.plane(d), p, q)

    def peers(self):
        found = []
        for k in range(1, self.deep):
            found.append(self.index(lax.rem(self.z + k, self.deep), self.p, self.q))
        for k in range(1, self.side):
            found.append(self.index(self.z, lax.rem(self.p + k, self.side), self.q))
            found.append(self.index(self.z, self.p, lax.rem(self.q + k, self.side)))
        return found

    def greet(self):
        barrier = pltpu.get_barrier_semaphore()
        places = self.peers()
        for place in places:
            pl.semaphore_signal(
                barrier, inc=1, device_id={"batch": place}, device_id_type=MESH
            )
        pl.semaphore_signal(
            barrier, inc=1, device_id={"seq": 1 - self.core}, device_id_type=MESH
        )
        pl.semaphore_wait(barrier, len(places) + 1)


def to_batch(src, dst, send, recv, place):
    return pltpu.make_async_remote_copy(
        src_ref=src, dst_ref=dst, send_sem=send, recv_sem=recv,
        device_id={"batch": place}, device_id_type=MESH,
    )


def to_core(src, dst, send, recv, core):
    return pltpu.make_async_remote_copy(
        src_ref=src, dst_ref=dst, send_sem=send, recv_sem=recv,
        device_id={"seq": core}, device_id_type=MESH,
    )


class Gather:
    def __init__(self, route, at, sends, recv):
        self.route, self.at, self.sends, self.recv = route, at, sends, recv

    def block(self, place, core=None):
        return (self.route.core if core is None else core) * self.route.count + place

    def arrive(self, place, core=None):
        block = self.block(place, core)
        here = self.at(block)
        to_core(here, here, self.recv.at[block], self.recv.at[block], 1 - self.route.core).wait_recv()

    def put_on(self, place, slot, target, core=False):
        block = self.block(place)
        here = self.at(block)
        if core:
            to_core(here, here, self.sends.at[slot], self.recv.at[block], 1 - self.route.core).start()
        else:
            to_batch(here, here, self.sends.at[slot], self.recv.at[block], target).start()

    def along(self, z):
        route = self.route
        place = route.index(z, route.p, route.q)

        @pl.when((z <= route.z) & (route.z < route.deep - 1))
        def _():
            self.put_on(place, 28 + z, route.index(route.z + 1, route.p, route.q))

        @pl.when((z >= route.z) & (route.z > 0))
        def _():
            self.put_on(place, 32 + z, route.index(route.z - 1, route.p, route.q))

    def plane_one(self, i):
        route = self.route
        z = route.reach(i)
        place = route.index(z, route.p, route.q)
        if i:
            self.arrive(place)
        self.along(z)
        self.put_on(place, i, route.near(0, 1, 0))
        self.put_on(place, 4 + i, route.near(0, 0, 1))
        self.put_on(place, 8 + i, None, core=True)

    def plane_two(self, i):
        route = self.route
        place = route.index(route.reach(i), lax.rem(route.p + 1, 2), route.q)
        self.arrive(place)
        self.put_on(place, 12 + i, route.near(0, 0, 1))
        self.put_on(place, 16 + i, None, core=True)

    def plane_last(self, i):
        route = self.route
        for e in range(2):
            place = route.index(route.reach(i), lax.rem(route.p + e, 2), lax.rem(route.q + 1, 2))
            self.arrive(place)
            self.put_on(place, 20 + 4 * e + i, None, core=True)

    def plane_other(self, i):
        route = self.route
        for e in range(2):
            for f in range(2):
                place = route.index(route.reach(i), lax.rem(route.p + f, 2), lax.rem(route.q + e, 2))
                self.arrive(place, 1 - route.core)

    def finish(self):
        route = self.route
        here = self.at(0)

        def sent(slot):
            to_core(here, here, self.sends.at[slot], self.sends.at[slot], 1 - route.core).wait_send()

        for slot in range(28):
            sent(slot)
        for z in range(route.deep):
            pl.when((z <= route.z) & (route.z < route.deep - 1))(functools.partial(sent, 28 + z))
            pl.when((z >= route.z) & (route.z > 0))(functools.partial(sent, 32 + z))


class Reduce:
    def __init__(self, route, source, stage, sems):
        self.route, self.source = route, source
        self.zero, self.one, self.two, self.three = stage
        (self.s0, self.r0), (self.s1, self.r1), (self.s2, self.r2), (self.s3, self.r3) = sems

    def add(self, place, value):
        self.zero[place] = (self.zero[place].astype(F32) + value.astype(F32)).astype(LOW)

    def leave(self, d):
        route = self.route
        for f in (1, 0):
            for e in (1, 0):
                place = route.near(d, e, f)
                to_core(
                    self.source((1 - route.core) * route.count + place),
                    self.zero.at[place], self.s0.at[place], self.r0.at[place], 1 - route.core,
                ).start()

    def start(self):
        for d in range(self.route.deep - 1, -1, -1):
            self.leave(d)

    def merge(self, d, e, f):
        route = self.route
        place = route.near(d, e, f)
        here = self.zero.at[place]
        to_core(here, here, self.s0.at[place], self.r0.at[place], 1 - route.core).wait_recv()
        self.add(place, self.source(route.core * route.count + place)[...])
        return place

    def step_one(self, d):
        route = self.route
        for f in (1, 0):
            place = self.merge(d, 1, f)
            slot = d * 2 + f
            to_batch(
                self.zero.at[place], self.one.at[slot], self.s1.at[slot], self.r1.at[slot], route.near(0, 1, 0)
            ).start()

    def step_two(self, d):
        route = self.route
        for f in (1, 0):
            place = self.merge(d, 0, f)
            slot = d * 2 + f
            here = self.one.at[slot]
            to_core(here, here, self.s1.at[slot], self.r1.at[slot], 1 - route.core).wait_recv()
            self.add(place, self.one[slot])
            if f:
                to_batch(
                    self.zero.at[place], self.two.at[d], self.s2.at[d], self.r2.at[d], route.near(0, 0, 1)
                ).start()

    def step_three(self, d):
        route = self.route
        place = route.near(d, 0, 0)
        here = self.two.at[d]
        to_core(here, here, self.s2.at[d], self.r2.at[d], 1 - route.core).wait_recv()
        self.add(place, self.two[d])
        if d:
            to_batch(
                self.zero.at[place], self.three.at[d - 1], self.s3.at[d - 1], self.r3.at[d - 1], place
            ).start()

    def total(self):
        route = self.route
        out = self.zero[route.me].astype(F32)
        for d in range(1, route.deep):
            here = self.three.at[d - 1]
            to_core(here, here, self.s3.at[d - 1], self.r3.at[d - 1], 1 - route.core).wait_recv()
            out = out + self.three[d - 1].astype(F32)
        return out

    def sent_core(self):
        here = self.zero.at[0]
        for slot in range(self.s0.shape[0]):
            to_core(here, here, self.s0.at[slot], self.s0.at[slot], 1 - self.route.core).wait_send()

    def finish(self):
        here = self.zero.at[0]
        for sems in (self.s1, self.s2, self.s3):
            for slot in range(sems.shape[0]):
                to_core(here, here, sems.at[slot], sems.at[slot], 1 - self.route.core).wait_send()


def stage_counts(route):
    side, deep = route.side, route.deep
    return route.count, (side - 1) * side * deep, (side - 1) * deep, deep - 1


class Everyone:
    def __init__(self, count, pair, slots, pair_sems, sends, recvs):
        self.count, self.pair, self.slots = count, pair, slots
        self.pair_sems, self.sends, self.recvs = pair_sems, sends, recvs

    def start(self, x):
        core, me, count = lax.axis_index("seq"), lax.axis_index("batch"), self.count
        copy = to_core(x, self.pair, self.pair_sems.at[0], self.pair_sems.at[1], 1 - core)
        copy.start()
        copy.wait()
        self.slots[me] = x[...] + self.pair[...]
        for k in range(1, count):
            here = self.slots.at[me]
            to_batch(here, here, self.sends.at[k - 1], self.recvs.at[k - 1], lax.rem(me + k, count)).start()

    def total(self):
        me, count = lax.axis_index("batch"), self.count
        for k in range(1, count):
            here = self.slots.at[lax.rem(me + count - k, count)]
            to_batch(here, here, self.sends.at[k - 1], self.recvs.at[k - 1], me).wait_recv()
        out = self.slots[0]
        for place in range(1, count):
            out = out + self.slots[place]
        for k in range(1, count):
            here = self.slots.at[0]
            to_batch(here, here, self.sends.at[k - 1], self.recvs.at[k - 1], me).wait_send()
        return out

    @staticmethod
    def scratch(count, rows):
        return [
            pltpu.VMEM((rows, 128), F32),
            pltpu.VMEM((count, rows, 128), F32),
            pltpu.SemaphoreType.DMA((2,)),
            pltpu.SemaphoreType.DMA((count - 1,)),
            pltpu.SemaphoreType.DMA((count - 1,)),
        ]


def to_tile(rows):
    width = rows.shape[1]
    parts = [rows[i : i + 1, j : j + 128] for i in range(rows.shape[0]) for j in range(0, width, 128)]
    return jnp.concatenate(parts, axis=0)


def from_tile(tile, first, width):
    each = width // 128
    return jnp.concatenate([tile[first * each + j : first * each + j + 1] for j in range(each)], axis=1)


def nn(a, b):
    return lax.dot_general(a, b, (((1,), (0,)), ((), ())), preferred_element_type=F32)


def nt(a, b):
    return lax.dot_general(a, b, (((1,), (1,)), ((), ())), preferred_element_type=F32)


def tn(a, b):
    return lax.dot_general(a, b, (((0,), (0,)), ((), ())), preferred_element_type=F32)


def sigmoid(v):
    return 0.5 * jnp.tanh(0.5 * v) + 0.5


def rows_of(i, size):
    return pl.ds(pl.multiple_of(i * size, size), size)


def normed(v):
    centred = v - jnp.mean(v, -1, keepdims=True)
    scale = lax.rsqrt(jnp.mean(centred * centred, -1, keepdims=True) + EPS)
    return centred * scale, scale


def normed_back(grad, hat, scale):
    return scale * (
        grad - jnp.mean(grad, -1, keepdims=True) - hat * jnp.mean(grad * hat, -1, keepdims=True)
    )


def fold(values):
    return jnp.sum(values.reshape(values.shape[0] // 8, 8, values.shape[1]), 0)


def norm_rows(x_ref, put, vec, row, block=64):
    @pl.loop(0, x_ref.shape[0] // block)
    def _(i):
        at = rows_of(i, block)
        hat, _ = normed(x_ref[at])
        put(at, (hat * vec[row : row + 1] + vec[row + 1 : row + 2]).astype(LOW))


def norm_rows_back(grad_ref, x_ref, g_ref, put, vec, sums, row, block=64):
    width = x_ref.shape[1]

    def step(i, carry):
        gain, bias = carry
        at = rows_of(i, block)
        hat, scale = normed(x_ref[at])
        grad = grad_ref[at]
        put(at, g_ref[at] + normed_back(grad * vec[row : row + 1], hat, scale))
        return gain + fold(grad * hat), bias + fold(grad)

    zero = jnp.zeros((8, width), F32)
    gain, bias = lax.fori_loop(0, x_ref.shape[0] // block, step, (zero, zero))
    sums[row : row + 1] = jnp.sum(gain, 0, keepdims=True)
    sums[row + 1 : row + 2] = jnp.sum(bias, 0, keepdims=True)


def activate(a):
    s = sigmoid(a)
    u = a * s
    return u, s + u * (1.0 - s)


def valid_rows(scal, at_row, rows):
    frame = scal[0] + at_row + lax.broadcasted_iota(jnp.int32, (rows, 1), 0)
    return frame, jnp.where(frame < scal[1], 1.0, 0.0)


def keep_rows(scal, at_row, rows, width):
    frame, ok = valid_rows(scal, at_row, rows)
    cut = (frame >= scal[2]) & (frame < scal[2] + scal[3])
    channel = lax.broadcasted_iota(jnp.int32, (1, width), 1)
    lost = (channel >= scal[4]) & (channel < scal[4] + scal[5])
    return (ok * jnp.where(cut, 0.0, 1.0)) * jnp.where(lost, 0.0, 1.0)


def masked_input(scal, x_in, x_ref, block=64):
    @pl.loop(0, x_in.shape[0] // block)
    def _(i):
        at = rows_of(i, block)
        keep = keep_rows(scal, i * block, block, x_in.shape[1])
        x_ref[at] = x_in[at].astype(F32) * keep


def split3(v):
    high = v.astype(LOW).astype(F32)
    rest = v - high
    mid = rest.astype(LOW).astype(F32)
    return high, mid, rest - mid


def key_extra(length, rows):
    key = lax.broadcasted_iota(jnp.int32, (rows, 128), 0)
    lane = lax.broadcasted_iota(jnp.int32, (rows, 128), 1)
    lost = jnp.where(key < length, 0.0, -1e30)
    return jnp.where(lane == 0, lost, jnp.where(lane < 4, 1.0, 0.0)).astype(LOW)


def fill_side(side, first, extra_rows):
    size = first[0].shape[0]
    blank = jnp.zeros((size, side.shape[2]), LOW)
    for half in range(2):
        side[half, half * size : (half + 1) * size] = first[half]
        side[half, (1 - half) * size : (2 - half) * size] = blank
        side[half, 2 * size :] = extra_rows[half]


def extra_of(lead, parts, wide):
    row = lax.broadcasted_iota(jnp.int32, (16, wide), 0)
    out = jnp.where(row == 0, lead, 0.0)
    if parts is not None:
        for n, part in enumerate(parts):
            out = jnp.where(row == n + 1, -part, out)
    return jnp.concatenate([out.astype(LOW), jnp.zeros((112, wide), LOW)], axis=0)


def attention_forward(qT, key, vT, extra, oT, top, side, scale, hook):
    heads, size, queries = qT.shape
    keys = key.shape[1]
    ones = jnp.ones((16, keys), LOW)

    @pl.loop(0, heads // 2)
    def _(pair):
        hook(pair)
        lead = extra_of(1.0, None, queries)
        fill_side(side, [qT[2 * pair], qT[2 * pair + 1]], [lead, lead])
        left = jnp.concatenate([key[pair], extra[...]], axis=1)
        for half in range(2):
            head = 2 * pair + half
            s = nn(left, side[half])
            m = jnp.max(s, 0, keepdims=True)
            p = jnp.exp2((s - m) * scale).astype(LOW)
            o = nn(jnp.concatenate([vT[head], ones], axis=0), p)
            total = o[size : size + 1]
            oT[rows_of(head, size)] = (o[:size] * (1.0 / total)).astype(LOW)
            top[pl.ds(head, 1)] = m + jnp.log2(total) * (1.0 / scale)


def attention_backward(
    qT, key, h_all, qkvT, extra, doT, delta, top, dqT, dk, dv, qside, oside, lows, grads, scale, shrink, hook, chunk=512
):
    heads, size, queries = qT.shape
    keys = key.shape[1]

    @pl.loop(0, heads // 2)
    def _(pair):
        hook(pair)
        tops = [split3(top[pl.ds(2 * pair + half, 1)]) for half in range(2)]
        deltas = [split3(delta[pl.ds(2 * pair + half, 1)]) for half in range(2)]
        fill_side(qside, [qT[2 * pair], qT[2 * pair + 1]], [extra_of(1.0, t, queries) for t in tops])
        fill_side(oside, [doT[2 * pair], doT[2 * pair + 1]], [extra_of(0.0, t, queries) for t in deltas])
        kT = nt(qkvT[1, rows_of(pair, 128)], h_all[...]).astype(LOW)
        wide_o = jnp.concatenate([oside[0, :128], oside[1, :128]], axis=1)
        wide_q = jnp.concatenate([qside[0, :128], qside[1, :128]], axis=1)
        totals = [None, None]
        for c in range(keys // chunk):
            at = slice(c * chunk, (c + 1) * chunk)
            value = nt(h_all[at], qkvT[2, rows_of(pair, 128)]).astype(LOW)
            left_k = jnp.concatenate([key[pair, at], extra[at]], axis=1)
            left_v = jnp.concatenate([value, extra[at]], axis=1)
            for half in range(2):
                lanes = slice(half * queries, (half + 1) * queries)
                p = jnp.exp2(nn(left_k, qside[half]) * scale)
                lows[:, lanes] = p.astype(LOW)
                grads[:, lanes] = (p * nn(left_v, oside[half])).astype(LOW)
            for half in range(2):
                lanes = slice(half * queries, (half + 1) * queries)
                got = nn(kT[half * size : (half + 1) * size, at], grads[:, lanes])
                totals[half] = got if c == 0 else totals[half] + got
            dv[pair, at] = nt(lows[...], wide_o).astype(LOW)
            dk[pair, at] = (nt(grads[...], wide_q) * shrink).astype(LOW)
        for half in range(2):
            dqT[rows_of(2 * pair + half, size)] = (totals[half] * shrink).astype(LOW)


def windows(pad_ref, at_row, block, lanes, shifts):
    for s in range(8):
        mine = [(tap, shift) for tap, shift in shifts if shift % 8 == s]
        low = min(shift for _, shift in mine)
        high = max(shift for _, shift in mine)
        window = pad_ref[at_row + low : at_row + high + block, lanes]
        for tap, shift in mine:
            yield tap, window[shift - low : shift - low + block]


def convolve(pad_ref, taps_wide, put, shift_of, rows, width, hook=None, block=64):
    count = taps_wide.shape[0]
    shifts = [(tap, shift_of(tap)) for tap in range(count)]
    for lane in range(0, width, 128):
        lanes = slice(lane, lane + 128)
        for at_row in range(0, rows, block):
            total = jnp.zeros((block // 8, 8, 128), F32)
            for tap, values in windows(pad_ref, at_row, block, lanes, shifts):
                total = total + taps_wide[tap, :, lanes][None] * values.reshape(block // 8, 8, 128)
            put(at_row, block, lane, total.reshape(block, 128))
        if hook:
            hook(1)


def convolve_weight(pad_ref, grad_ref, first, out_ref, shift_of, rows, width, hook, block=64):
    taps = out_ref.shape[0]
    for lane in range(0, width, 128):
        lanes = slice(lane, lane + 128)
        for s in range(8):
            mine = [(tap, shift_of(tap)) for tap in range(taps) if shift_of(tap) % 8 == s]
            low = min(shift for _, shift in mine)
            high = max(shift for _, shift in mine)
            sums = {tap: jnp.zeros((8, 128), F32) for tap, _ in mine}
            for at_row in range(0, rows, block):
                grad = grad_ref[first + at_row : first + at_row + block, lanes]
                window = pad_ref[at_row + low : at_row + high + block, lanes]
                for tap, shift in mine:
                    sums[tap] = sums[tap] + fold(grad * window[shift - low : shift - low + block])
            for tap, _ in mine:
                out_ref[tap : tap + 1, lanes] = jnp.sum(sums[tap], 0, keepdims=True)
        hook(1)


def place_halo(pad_ref, halo, core):
    rows = pad_ref.shape[0] - 2 * HALO
    got = halo[...]
    zero = jnp.zeros_like(got)
    pad_ref[0:HALO] = jnp.where(core == 1, got, zero)
    pad_ref[rows + HALO :] = jnp.where(core == 0, got, zero)


def layer_kernel(cfg, *refs):
    r = SimpleNamespace(**dict(zip(cfg.names, refs)))
    count, shard, hidden, inside = cfg.count, cfg.shard, cfg.hidden, cfg.inside
    rows, width = r.x_in.shape
    heads, size = cfg.heads, width // cfg.heads
    keys, pairs, taps = 2 * rows, heads // 2, r.kern.shape[0]
    scale, shrink = math.log2(math.e) / math.sqrt(size), 1.0 / math.sqrt(size)
    route = Routes(count).here()
    core, me = route.core, route.me
    vec, g0, g1, sums = r.vec, r.g0, r.g1, r.sums
    chunk, block = 256, 64
    own = pl.ds(pl.multiple_of(core * rows, rows), rows)
    theirs = pl.ds(pl.multiple_of((1 - core) * rows, rows), rows)
    zero8 = jnp.zeros((8, width), F32)

    def block_rows(at):
        return pl.ds(pl.multiple_of(at * shard, shard), shard)

    barrier = pltpu.get_barrier_semaphore()
    for k in range(1, count):
        pl.semaphore_signal(
            barrier, inc=1, device_id={"batch": lax.rem(me + k, count)}, device_id_type=MESH
        )
    pl.semaphore_signal(barrier, inc=1, device_id={"seq": 1 - core}, device_id_type=MESH)
    half = width // 2
    q_own = pl.ds(pl.multiple_of(core * half, half), half)
    loads = []

    def load(source, target):
        copy = pltpu.make_async_copy(source, target, r.local.at[4 + len(loads)])
        copy.start()
        loads.append(copy)
        return copy

    if inside:
        mine = block_rows(core * count + me)
        near_loads = [
            load(part.at[j], g.at[m, mine]) for m, part in enumerate((r.ffn_in, r.ffn_out)) for j, g in enumerate((g0, g1))
        ]
    else:
        near_loads = [load(r.shards.at[0], g0), load(r.shards.at[1], g1)]
    load_qkv = load(r.qkv_far, r.qkv_mine)
    load_att = load(r.w_att_far, r.w_att)
    load_conv_in = load(r.conv_in_far, r.conv_in)
    load_conv_out = load(r.conv_out_far, r.conv_out)
    load_cot = load(r.cot_far, r.cot)
    frame0, length, span = core * rows, r.lengths[0], [r.spans[0, n] for n in range(4)]
    scal = [frame0, length, *span]
    sums[...] = jnp.zeros_like(sums)
    masked_input(scal, r.x_in, r.x1)

    def put_h0(at, value):
        r.h0[at] = value

    norm_rows(r.x1, put_h0, vec, 0)
    for tap in range(taps):
        r.wide[tap] = jnp.broadcast_to(r.kern[tap : tap + 1], (8, width))
    for copy in near_loads:
        copy.wait()
    pl.semaphore_wait(barrier, count)

    def inner(at):
        u, slope = activate(nt(g0[0, at], r.h0[...]))
        r.act[at] = u.astype(LOW)
        r.slope[at] = slope.astype(LOW)

    swap_q = to_core(r.qkvT.at[:, q_own], r.qkvT.at[:, q_own], r.swap.at[0], r.swap.at[1], 1 - core)

    def turn_qkv():
        load_qkv.wait()
        for s in range(3):
            r.qkvT[s, q_own] = r.qkv_mine[s].astype(F32).T.astype(LOW)
        swap_q.start()

    if inside:
        first = Gather(route, lambda b: g0.at[:, block_rows(b)], r.g_send.at[0], r.g_recv.at[0])
        second = Gather(route, lambda b: g1.at[:, block_rows(b)], r.g_send.at[1], r.g_recv.at[1])
        deep = route.deep

        def inner_plane(which, d):
            inner(rows_of(which * deep + route.reach(d), 4 * shard))

        first.plane_one(0)
        turn_qkv()
        first.plane_two(0)
        for d in range(deep):
            if d + 1 < deep:
                first.plane_one(d + 1)
            first.plane_last(d)
            if d + 1 < deep:
                first.plane_two(d + 1)
            else:
                second.plane_one(0)
            inner_plane(core, d)
            if d:
                first.plane_other(d - 1)
                inner_plane(1 - core, d - 1)
        first.plane_other(deep - 1)
        inner_plane(1 - core, deep - 1)
    else:
        turn_qkv()

        @pl.loop(0, hidden // chunk)
        def _(i):
            inner(rows_of(i, chunk))

    @pl.loop(0, rows // 256)
    def _(i):
        at = rows_of(i, 256)
        r.x1[at] = r.x1[at] + 0.5 * tn(r.act[:, at], g0[1])

    if inside:
        second.plane_one(1)
        second.plane_two(0)

    def put_h2(at, value):
        r.h_all[pl.ds(pl.multiple_of(core * rows + at.start, block), block)] = value

    norm_rows(r.x1, put_h2, vec, 2)
    swap = to_core(r.h_all.at[own], r.h_all.at[own], r.swap.at[2], r.swap.at[3], 1 - core)
    swap.start()
    away = [
        pltpu.make_async_copy(g0, r.far_g, r.local.at[0]),
        pltpu.make_async_copy(r.act, r.far_act, r.local.at[1]),
        pltpu.make_async_copy(r.slope, r.far_slope, r.local.at[2]),
    ]
    for copy in away:
        copy.start()
    swap_q.wait()

    def project(at, vT):
        here = r.h_all[at]
        for pair in range(pairs):
            r.key[pair, at] = nt(here, r.qkvT[1, pair * 128 : (pair + 1) * 128]).astype(LOW)
        vT[:, :, at] = nt(r.qkvT[2], here).astype(LOW).reshape(heads, size, rows)

    r.extra[...] = key_extra(scal[1], keys)

    def attend(vT, side_ref):
        r.qT[...] = nt(r.qkvT[0], r.h_all[own]).astype(LOW).reshape(heads, size, rows)
        project(own, vT)
        swap.wait()
        project(theirs, vT)
        if inside:
            second.plane_one(2)
            second.plane_two(1)
            second.plane_last(0)

        def hook(pair):
            if inside:
                @pl.when(pair == 1)
                def _():
                    second.plane_one(3)
                    second.plane_two(2)
                    second.plane_last(1)

                @pl.when(pair == 3)
                def _():
                    second.plane_two(3)
                    second.plane_last(2)

        attention_forward(r.qT, r.key, vT, r.extra, r.oT, r.top, side_ref, scale, hook)

    pl.run_scoped(attend, pltpu.VMEM((heads, size, keys), LOW), pltpu.VMEM((2, 256, rows), LOW))

    load_att.wait()

    @pl.loop(0, rows // 256)
    def _(i):
        at = rows_of(i, 256)
        r.x2[at] = r.x1[at] + tn(r.oT[:, at], r.w_att[...])

    def put_h3(at, value):
        r.h3[at] = value

    norm_rows(r.x2, put_h3, vec, 4)
    load_conv_in.wait()

    @pl.loop(0, rows // 256)
    def _(i):
        at = rows_of(i, 256)
        _, ok = valid_rows(scal, i * 256, 256)
        here = r.h3[at]
        gate = sigmoid(nn(here, r.conv_in[:, width:]))
        r.pad[pl.ds(pl.multiple_of(i * 256 + HALO, HALO), 256)] = nn(here, r.conv_in[:, :width]) * gate * ok

    edge = pl.ds(pl.multiple_of(HALO + (1 - core) * (rows - HALO), HALO), HALO)
    swap = to_core(r.pad.at[edge], r.halo.at[0], r.swap.at[4], r.swap.at[5], 1 - core)
    swap.start()
    if inside:
        second.plane_last(3)
    swap.wait()
    place_halo(r.pad, r.halo.at[0], core)

    def put_depth(at_row, high, lane, total):
        r.depth[at_row : at_row + high, lane : lane + 128] = total

    convolve(r.pad, r.wide, put_depth, lambda tap: tap + 1, rows, width)

    def moments(i, carry):
        one, two = carry
        _, ok = valid_rows(scal, i * block, block)
        here = r.depth[rows_of(i, block)]
        held = here * ok
        return one + fold(held), two + fold(here * held)

    one, two = lax.fori_loop(0, rows // block, moments, (zero8, zero8))
    number = jnp.clip(scal[1] - scal[0], 0, rows).astype(F32)
    r.part_a[0:8] = to_tile(
        jnp.concatenate([jnp.sum(one, 0, keepdims=True), jnp.sum(two, 0, keepdims=True)], axis=0)
    )
    r.part_a[8:16] = jnp.full((8, 128), 1.0, F32) * number
    every = Everyone(count, r.pair_a, r.slots_a, r.pair_sems_a, r.sends_a, r.recvs_a)
    every.start(r.part_a)
    if inside:
        for d in range(deep):
            second.plane_other(d)
        second.finish()
        first.finish()
    for copy in [*away, load_conv_out, load_cot]:
        copy.wait()
    tile = every.total()
    number = tile[8:9, 0:1]
    mean = from_tile(tile, 0, width) / number
    var = from_tile(tile, 1, width) / number - mean * mean
    spread = lax.rsqrt(var + EPS)
    gain6 = vec[6:7]

    if inside:
        stages = [
            Reduce(route, source, [ref.at[k] for ref in (r.zero, r.one, r.two, r.three)],
                   [(getattr(r, f"r_send{n}").at[k], getattr(r, f"r_recv{n}").at[k]) for n in range(4)])
            for k, source in enumerate(
                [
                    lambda b: g0.at[0, block_rows(b)],
                    lambda b: g0.at[1, block_rows(b)],
                    lambda b: r.box.at[0, b],
                    lambda b: r.box.at[1, b],
                    lambda b: g0.at[0, block_rows(b)],
                    lambda b: g0.at[1, block_rows(b)],
                ]
            )
        ]
        in1, out1, rest, proj, in0, out0 = stages
        queue = []

        def put_off(chunks, lag, ends):
            units = [(n, d) for n in range(len(chunks)) for d in range(deep - 1, -1, -1)]
            for t in range(len(units) + lag):
                if t < len(units):
                    n, d = units[t]
                    queue.append(functools.partial(chunks[n].step_two, d))
                if t >= lag:
                    n, d = units[t - lag]
                    queue.append(functools.partial(chunks[n].step_three, d))
                    if d == 0:
                        queue.append(ends[n])

        def tick(count):
            for _ in range(min(count, len(queue))):
                queue.pop(0)()

        def end_out1():
            r.fin_out[1] = out1.total()

        def end_in1():
            r.fin_in[1] = in1.total()

        def end_rest():
            r.held[0, core * count + me] = rest.total().astype(LOW)

        def end_proj():
            r.held[1, core * count + me] = proj.total().astype(LOW)

        def end_out0():
            r.fin_out[0] = out0.total()

        def end_in0():
            r.fin_in[0] = in0.total()

        third = Gather(route, lambda b: r.held.at[0, b], r.g_send.at[2], r.g_recv.at[2])
        fourth = Gather(route, lambda b: r.held.at[1, b], r.g_send.at[3], r.g_recv.at[3])
    else:
        def tick(count):
            pass
    back_copies = [
        pltpu.make_async_copy(r.far_act, r.act, r.local.at[0]),
        pltpu.make_async_copy(r.far_slope, r.slope, r.local.at[1]),
        pltpu.make_async_copy(r.far_g, g1, r.local.at[2]),
    ]

    def ffn_grads(weight_out, h_ref, dy, da, pieces, hooks=None):
        def grads_of(at):
            du = nt(weight_out[at], dy[...])
            low = (du * r.slope[at].astype(F32)).astype(LOW)
            da[at] = low
            g0[1, at] = nn(r.act[at], dy[...]).astype(LOW)
            g0[0, at] = nn(low, h_ref[...]).astype(LOW)

        if not inside:
            @pl.loop(0, hidden // chunk)
            def _(i):
                grads_of(rows_of(i, chunk))

            return
        for d in range(deep - 1, -1, -1):
            grads_of(rows_of((1 - core) * deep + route.plane(d), 4 * shard))
            for piece in pieces:
                piece.leave(d)
            hooks(deep - 1 - d)
        for d in range(deep - 1, -1, -1):
            grads_of(rows_of(core * deep + route.plane(d), 4 * shard))
            hooks(2 * deep - 1 - d)

    def middle(slope_z, da, dh):
        low, dy, h4 = r.d_conv_in.at[:, pl.ds(0, width)], r.d_conv_in.at[:, pl.ds(width, width)], r.d_att
        x3, x4 = r.input_grad, r.dz

        @pl.loop(0, rows // block)
        def _(i):
            at = rows_of(i, block)
            z = (r.depth[at] - mean) * spread * gain6 + vec[7:8]
            u, slope = activate(z)
            low[at] = u.astype(LOW)
            slope_z[at] = slope

        @pl.loop(0, rows // 256)
        def _(i):
            at = rows_of(i, 256)
            x3[at] = r.x2[at] + nn(low[at], r.conv_out[...])

        def put_h4(at, value):
            h4[at] = value

        norm_rows(x3, put_h4, vec, 8)

        @pl.loop(0, hidden // chunk)
        def _(i):
            at = rows_of(i, chunk)
            u, slope = activate(nt(g1[0, at], h4[...]))
            r.act[at] = u.astype(LOW)
            r.slope[at] = slope.astype(LOW)

        @pl.loop(0, rows // 256)
        def _(i):
            at = rows_of(i, 256)
            x4[at] = x3[at] + 0.5 * tn(r.act[:, at], g1[1])

        def last(i, carry):
            gain, bias = carry
            at = rows_of(i, block)
            hat, rate = normed(x4[at])
            r.out[at] = (hat * vec[10:11] + vec[11:12]).astype(LOW)
            g = r.cot[at].astype(F32)
            back = normed_back(g * vec[10:11], hat, rate)
            r.grad[at] = back
            dy[at] = (0.5 * back).astype(LOW)
            return gain + fold(g * hat), bias + fold(g)

        gain, bias = lax.fori_loop(0, rows // block, last, (zero8, zero8))
        sums[10:11] = jnp.sum(gain, 0, keepdims=True)
        sums[11:12] = jnp.sum(bias, 0, keepdims=True)
        def first_hooks(i):
            if i >= deep:
                out1.step_one(2 * deep - 1 - i)

        ffn_grads(g1.at[1], h4, dy, da, [out1, in1] if inside else None, first_hooks)
        back_copies[0].start()
        back_copies[1].start()

        @pl.loop(0, rows // 256)
        def _(i):
            at = rows_of(i, 256)
            dh[at] = tn(da[:, at], g1[0])

        back_copies[2].start()

        def put(at, value):
            r.grad[at] = value
            dy[at] = value.astype(LOW)

        norm_rows_back(dh, x3, r.grad, put, vec, sums, 8)
        got = tn(low[...], dy[...]).astype(LOW)
        if inside:
            r.box[0, :, 0:16] = got.reshape(2 * count, 16, width)
        else:
            r.d_conv_out[...] = got

        @pl.loop(0, rows // 256)
        def _(i):
            at = rows_of(i, 256)
            r.dz[at] = nt(dy[at], r.conv_out[...])

        def close(i, carry):
            one, two = carry
            at = rows_of(i, block)
            here = r.dz[at] * slope_z[at]
            r.dz[at] = here
            return one + fold(here), two + fold(here * (r.depth[at] - mean))

        one, two = lax.fori_loop(0, rows // block, close, (zero8, zero8))
        r.part_b[...] = to_tile(
            jnp.concatenate([jnp.sum(one, 0, keepdims=True), jnp.sum(two, 0, keepdims=True)], axis=0)
        )

    square = (rows, width)
    vm = pltpu.VMEM
    pl.run_scoped(
        middle, vm(square, F32), vm((hidden, rows), LOW), vm(square, F32),
    )
    if not inside:
        copy = pltpu.make_async_copy(g0, r.d_ffn.at[1], r.local.at[3])
        copy.start()
        copy.wait()
    every = Everyone(count, r.pair_b, r.slots_b, r.pair_sems_b, r.sends_b, r.recvs_b)
    every.start(r.part_b)
    tile = every.total()
    grad_sum, grad_moment = from_tile(tile, 0, width), from_tile(tile, 1, width)
    if inside:
        for d in range(deep - 1, -1, -1):
            in1.step_one(d)
        put_off([out1, in1], 2, [end_out1, end_in1])
    var_grad = -0.5 * (gain6 * grad_moment) * spread * spread * spread
    flat = (-(gain6 * spread * grad_sum) - 2.0 * mean * var_grad) / number
    tilt = 2.0 * var_grad / number

    def convolution_back(back, p, datt):
        dp, dh = r.d_conv_in if inside else r.spare_wide, r.input_grad

        @pl.loop(0, rows // block)
        def _(i):
            at = rows_of(i, block)
            _, ok = valid_rows(scal, i * block, block)
            back[pl.ds(pl.multiple_of(i * block + HALO, HALO), block)] = gain6 * spread * r.dz[at] + ok * (
                flat + r.depth[at] * tilt
            )

        swap = to_core(back.at[edge], r.halo.at[1], r.swap.at[6], r.swap.at[7], 1 - core)
        swap.start()
        convolve_weight(r.pad, back, HALO, r.small.at[pl.ds(0, taps)], lambda tap: tap + 1, rows, width, tick)

        @pl.loop(0, rows // 256)
        def _(i):
            at = rows_of(i, 256)
            p[at] = nn(r.h3[at], r.conv_in[...])

        tick(1)
        swap.wait()
        place_halo(back, r.halo.at[1], core)

        def put(at_row, high, lane, total):
            at = slice(at_row, at_row + high)
            _, ok = valid_rows(scal, at_row, high)
            gate = sigmoid(p[at, width + lane : width + lane + 128])
            total = total * gate * ok
            dp[at, lane : lane + 128] = total.astype(LOW)
            dp[at, width + lane : width + lane + 128] = (
                total * p[at, lane : lane + 128] * (1.0 - gate)
            ).astype(LOW)

        convolve(back, r.wide, put, lambda tap: taps - 1 - tap, rows, width, tick)
        got = tn(r.h3[...], dp[...]).astype(LOW)
        if inside:
            r.box[0, :, 16:32] = got[:, :width].reshape(2 * count, 16, width)
            r.box[0, :, 32:48] = got[:, width:].reshape(2 * count, 16, width)
            tick(1)
        else:
            r.d_conv_in[...] = got

        @pl.loop(0, rows // 256)
        def _(i):
            at = rows_of(i, 256)
            dh[at] = nt(dp[at], r.conv_in[...])

        def put_first(at, got):
            r.grad[at] = got
            datt[at] = got.astype(LOW)

        tick(1)
        norm_rows_back(dh, r.x2, r.grad, put_first, vec, sums, 4)
        tick(1)
        got = nn(r.oT[...], datt[...]).astype(LOW)
        if inside:
            r.box[0, :, 48:64] = got.reshape(2 * count, 16, width)
            rest.start()
        else:
            r.d_att[...] = got
        r.doT[...] = nt(r.w_att[...], datt[...]).astype(LOW).reshape(heads, size, rows)

    pl.run_scoped(
        convolution_back, vm(r.pad.shape, F32), vm((rows, 2 * width), F32), vm(square, LOW),
    )

    def attend_back(delta, qside, oside, lows, grads, dk, dv):
        dqT = r.d_conv_out if inside else r.spare

        for head in range(heads):
            o = r.oT[head * size : (head + 1) * size].astype(F32)
            delta[head : head + 1] = jnp.sum(o * r.doT[head].astype(F32), 0, keepdims=True)

        def hook(pair):
            if inside:
                @pl.when(pair == 0)
                def _():
                    tick(2)

                @pl.when(pair == 1)
                def _():
                    for d in range(deep - 1, -1, -1):
                        rest.step_one(d)
                    tick(len(queue))
                    put_off([rest], 2, [end_rest])

                @pl.when(pair == 2)
                def _():
                    tick(2)

                @pl.when(pair == 3)
                def _():
                    tick(4)

        attention_backward(
            r.qT, r.key, r.h_all, r.qkvT, r.extra, r.doT, delta, r.top, dqT, dk, dv, qside, oside, lows, grads,
            scale, shrink, hook,
        )
        swaps = [
            to_core(dk.at[:, theirs], r.rk, r.swap.at[8], r.swap.at[9], 1 - core),
            to_core(dv.at[:, theirs], r.rv, r.swap.at[10], r.swap.at[11], 1 - core),
        ]
        for swap in swaps:
            swap.start()
        r.dq[...] = dqT[...].astype(F32).T.astype(LOW)
        for swap in swaps:
            swap.wait()
        for pair in range(pairs):
            lanes = slice(pair * 128, (pair + 1) * 128)
            r.h3[:, lanes] = (dk[pair, own].astype(F32) + r.rk[pair].astype(F32)).astype(LOW)
            r.own_v[:, lanes] = (dv[pair, own].astype(F32) + r.rv[pair].astype(F32)).astype(LOW)

    pl.run_scoped(
        attend_back, vm((heads, rows), F32), vm((2, 256, rows), LOW), vm((2, 256, rows), LOW),
        vm((keys // 2, 2 * rows), LOW), vm((keys // 2, 2 * rows), LOW),
        vm((pairs, keys, 128), LOW), vm((pairs, keys, 128), LOW),
    )
    if inside:
        tick(len(queue))
        third.plane_one(0)

    def put_qkv(s, got):
        if inside:
            for c in range(2):
                v = got[:, c * half : (c + 1) * half].reshape(count, 2, 16, half)
                r.box[1, c * count : (c + 1) * count, s * 16 : (s + 1) * 16] = jnp.concatenate(
                    [v[:, 0], v[:, 1]], axis=-1
                )
        else:
            r.d_qkv[s] = got

    def project_back(dh, dy, da, x0):
        own_k, own_v = r.h3, r.own_v
        h2 = r.h_all[own]
        put_qkv(0, tn(h2, r.dq[...]).astype(LOW))
        put_qkv(1, tn(h2, own_k[...]).astype(LOW))
        put_qkv(2, tn(h2, own_v[...]).astype(LOW))
        @pl.loop(0, rows // 256)
        def _(i):
            at = rows_of(i, 256)
            dh[at] = nn(r.dq[at], r.qkvT[0]) + nn(own_k[at], r.qkvT[1]) + nn(own_v[at], r.qkvT[2])

        def put_second(at, got):
            r.grad[at] = got
            dy[at] = (0.5 * got).astype(LOW)

        norm_rows_back(dh, r.x1, r.grad, put_second, vec, sums, 2)
        if inside:
            r.small[taps : taps + 16] = sums[...]
            r.box[1, :, 48:64] = jnp.zeros((2 * count, 16, width), LOW)
            for n in range((taps + 16) // 16):
                r.box[1, n, 48:64] = r.small[n * 16 : (n + 1) * 16].astype(LOW)
            proj.start()
            third.plane_two(0)
            third.plane_one(1)
            for piece in (in1, out1):
                piece.sent_core()
        for copy in back_copies:
            copy.wait()

        def second_hooks(i):
            if i == 2:
                for d in range(deep - 1, -1, -1):
                    proj.step_one(d)
                put_off([proj, out0, in0], 2, [end_proj, end_out0, end_in0])
            if i >= deep:
                out0.step_one(2 * deep - 1 - i)
                in0.step_one(2 * deep - 1 - i)
            if i == deep:
                third.plane_two(1)
                third.plane_one(2)
            if i > deep:
                tick(1)

        ffn_grads(g1.at[1], r.h0, dy, da, [out0, in0] if inside else None, second_hooks)
        tick(2)
        masked_input(scal, r.x_in, x0)

        @pl.loop(0, rows // 256)
        def _(i):
            at = rows_of(i, 256)
            dh[at] = tn(da[:, at], g1[0])

        tick(2)

        def put_input(at, got):
            r.input_grad[at] = got * keep_rows(scal, at.start, block, width)

        norm_rows_back(dh, x0, r.grad, put_input, vec, sums, 0)

    def tail(dh, dy, da, x0):
        project_back(dh, dy, da, x0)
        if not inside:
            return
        third.plane_two(2)
        third.plane_one(3)
        while queue:
            thunk = queue.pop(0)
            thunk()
            if thunk is end_proj:
                break
        fourth.plane_one(0)
        r.part_c[...] = to_tile(sums[0:2])
        every = Everyone(count, r.pair_c, r.slots_c, r.pair_sems_c, r.sends_c, r.recvs_c)
        every.start(r.part_c)
        third.plane_two(3)
        tick(4)
        fourth.plane_one(1)
        fourth.plane_two(0)
        tick(4)
        fourth.plane_one(2)
        fourth.plane_two(1)
        tick(4)
        fourth.plane_one(3)
        fourth.plane_two(2)
        tick(len(queue))
        fourth.plane_two(3)
        for d in range(deep):
            third.plane_last(d)
        for d in range(deep):
            third.plane_other(d)
        got = r.held[0]
        blocks = 2 * count
        r.d_conv_out[...] = got[:, 0:16].reshape(width, width)
        r.d_conv_in[:, :width] = got[:, 16:32].reshape(width, width)
        r.d_conv_in[:, width:] = got[:, 32:48].reshape(width, width)
        r.d_att[...] = got[:, 48:64].reshape(width, width)
        for d in range(deep):
            fourth.plane_last(d)
        tile = every.total()
        for d in range(deep):
            fourth.plane_other(d)
        got = r.held[1, pl.ds(core * count, count)]
        for s in range(3):
            v = got[:, s * 16 : (s + 1) * 16]
            v = jnp.concatenate([v[:, None, :, :half], v[:, None, :, half:]], axis=1)
            r.d_qkv[s] = v.reshape(width, half)
        got = r.held[1, 0 : (taps + 16) // 16, 48:64].reshape(taps + 16, width).astype(F32)
        r.d_kern[...] = got[:taps]
        r.d_vec[...] = jnp.concatenate(
            [
                from_tile(tile, 0, width), from_tile(tile, 1, width), got[taps + 2 : taps + 6],
                spread * grad_moment, grad_sum, got[taps + 8 : taps + 12],
            ],
            axis=0,
        )
        third.finish()
        fourth.finish()
        for piece in stages:
            piece.finish()
        for piece in (rest, proj, in0, out0):
            piece.sent_core()

    pl.run_scoped(
        tail, vm(square, F32), vm(square, LOW), vm((hidden, rows), LOW),
        vm(square, F32),
    )
    if not inside:
        r.small[taps : taps + 16] = sums[...]
        r.small[taps + 6 : taps + 7] = spread * grad_moment
        r.small[taps + 7 : taps + 8] = grad_sum
        copy = pltpu.make_async_copy(g0, r.d_ffn.at[0], r.local.at[3])
        copy.start()
        copy.wait()


def gather_steps(route, chunk, held, sends, recv, with_core=True):
    started = []
    core, count = route.core, route.count

    def block(place):
        return core * count + place

    def arrive(place):
        here = held.at[chunk, block(place)]
        to_batch(here, here, recv.at[chunk, block(place)], recv.at[chunk, block(place)], route.me).wait_recv()

    def send(place, target):
        slot = len(started)
        here = held.at[chunk, block(place)]
        copy = to_batch(here, here, sends.at[chunk, slot], recv.at[chunk, block(place)], target)
        copy.start()
        started.append(copy)

    def cross(place):
        if not with_core:
            return
        slot = len(started)
        here = held.at[chunk, block(place)]
        copy = to_core(here, here, sends.at[chunk, slot], recv.at[chunk, block(place)], 1 - core)
        copy.start()
        started.append(copy)

    def step_mid():
        for k in range(1, route.deep):
            send(route.me, route.index(lax.rem(route.z + k, route.deep), route.p, route.q))
        cross(route.me)

    def step_one():
        for d in range(route.deep):
            z = lax.rem(route.z + d, route.deep)
            place = route.index(z, route.p, route.q)
            if d:
                arrive(place)
            for k in range(1, route.side):
                send(place, route.index(route.z, lax.rem(route.p + k, route.side), route.q))
            if d:
                cross(place)

    def step_two():
        for d in range(route.deep):
            z = lax.rem(route.z + d, route.deep)
            for e in range(route.side):
                p = lax.rem(route.p + e, route.side)
                place = route.index(z, p, route.q)
                if e:
                    arrive(place)
                for k in range(1, route.side):
                    send(place, route.index(route.z, route.p, lax.rem(route.q + k, route.side)))
                if e:
                    cross(place)

    def step_last():
        for d in range(route.deep):
            z = lax.rem(route.z + d, route.deep)
            for e in range(route.side):
                p = lax.rem(route.p + e, route.side)
                for f in range(1, route.side):
                    place = route.index(z, p, lax.rem(route.q + f, route.side))
                    arrive(place)
                    cross(place)

    def step_end():
        if with_core:
            for place in range(count):
                other = held.at[chunk, (1 - core) * count + place]
                at = recv.at[chunk, (1 - core) * count + place]
                to_core(other, other, at, at, 1 - core).wait_recv()
        for copy in started:
            copy.wait_send()

    return [step_mid, step_one, step_two, step_last, step_end]


def sends_of(route):
    return (route.deep - 1) + route.deep * (route.side - 1) * (1 + route.side) + route.count


def run_steps(all_steps):
    depth = len(all_steps[0])
    for turn in range(depth + len(all_steps) - 1):
        for chunk, steps in enumerate(all_steps):
            if 0 <= turn - chunk < depth:
                steps[turn - chunk]()


def gather_kernel(count, mine, held, local, sends, recv):
    route = Routes(count).here()
    chunks = mine.shape[0]
    copies = []
    for chunk in range(chunks):
        own = held.at[chunk, route.core * count + route.me]
        copy = pltpu.make_async_copy(mine.at[chunk], own, local.at[chunk])
        copy.start()
        copies.append(copy)
    route.greet()
    for copy in copies:
        copy.wait()
    run_steps([gather_steps(route, chunk, held, sends, recv) for chunk in range(chunks)])


def gather_all(mine, count, collective_id):
    chunks, rows, width = mine.shape
    route = Routes(count)
    return pl.pallas_call(
        functools.partial(gather_kernel, count),
        out_shape=jax.ShapeDtypeStruct((chunks, 2 * count, rows, width), mine.dtype),
        in_specs=[pl.BlockSpec(memory_space=pltpu.VMEM)],
        out_specs=pl.BlockSpec(memory_space=pltpu.VMEM),
        scratch_shapes=[
            pltpu.SemaphoreType.DMA((chunks,)),
            pltpu.SemaphoreType.DMA((chunks, sends_of(route))),
            pltpu.SemaphoreType.DMA((chunks, 2 * count)),
        ],
        compiler_params=pltpu.CompilerParams(
            collective_id=collective_id, has_side_effects=True, vmem_limit_bytes=VMEM_BYTES
        ),
    )(mine)


def reduce_kernel(count, solo, n, *refs):
    pieces, (fin, held, grads, packing, *rest) = refs[:n], refs[n:]
    copies = []
    at = 0
    for i, piece in enumerate(pieces):
        lines = piece.shape[1]
        copy = pltpu.make_async_copy(piece, grads.at[:, pl.ds(at, lines)], packing.at[i])
        copy.start()
        copies.append(copy)
        at += lines
    for copy in copies:
        copy.wait()
    reduce_packed(count, solo, grads, fin, held, *rest)


def reduce_packed(count, solo, grads, fin, held, zero, one, two, three, s0, r0, s1, r1, s2, r2, s3, r3, sends, recv):
    route = Routes(count).here()
    core, me, side, deep = route.core, route.me, route.side, route.deep
    rows, width = grads.shape[1:]
    piece = 16

    def add(target, source):
        @pl.loop(0, rows // piece)
        def _(i):
            at = pl.ds(pl.multiple_of(i * piece, piece), piece)
            target[at] = (target[at].astype(jnp.float32) + source[at].astype(jnp.float32)).astype(target.dtype)

    route.greet()
    waits = []
    order = []
    for f in range(side - 1, -1, -1):
        for d in range(deep):
            for e in range(side - 1, -1, -1):
                order.append((d, e, f))
    for d, e, f in order:
        place = route.index(lax.rem(route.z + d, deep), lax.rem(route.p + e, side), lax.rem(route.q + f, side))
        copy = to_core(grads.at[(1 - core) * count + place], zero.at[place], s0.at[place], r0.at[place], 1 - core)
        copy.start()
        waits.append(copy)
    for e in range(side - 1, -1, -1):
        for d in range(deep):
            for f in range(side - 1, -1, -1):
                z, p, q = lax.rem(route.z + d, deep), lax.rem(route.p + e, side), lax.rem(route.q + f, side)
                place = route.index(z, p, q)
                to_core(zero.at[place], zero.at[place], s0.at[place], r0.at[place], 1 - core).wait_recv()
                add(zero.at[place], grads.at[core * count + place])
                if e:
                    slot = (e - 1) * deep * side + z * side + q
                    copy = to_batch(
                        zero.at[place], one.at[slot], s1.at[slot], r1.at[slot], route.index(route.z, p, route.q)
                    )
                    copy.start()
                    waits.append(copy)
    for f in range(side - 1, -1, -1):
        for d in range(deep):
            z, q = lax.rem(route.z + d, deep), lax.rem(route.q + f, side)
            place = route.index(z, route.p, q)
            for e in range(1, side):
                slot = (e - 1) * deep * side + z * side + q
                to_batch(one.at[slot], one.at[slot], s1.at[slot], r1.at[slot], me).wait_recv()
                add(zero.at[place], one.at[slot])
            if f:
                slot = (f - 1) * deep + z
                copy = to_batch(
                    zero.at[place], two.at[slot], s2.at[slot], r2.at[slot], route.index(route.z, route.p, q)
                )
                copy.start()
                waits.append(copy)
    for d in range(deep - 1, -1, -1):
        z = lax.rem(route.z + d, deep)
        place = route.index(z, route.p, route.q)
        for f in range(1, side):
            slot = (f - 1) * deep + z
            to_batch(two.at[slot], two.at[slot], s2.at[slot], r2.at[slot], me).wait_recv()
            add(zero.at[place], two.at[slot])
        if d:
            copy = to_batch(zero.at[place], three.at[d - 1], s3.at[d - 1], r3.at[d - 1], place)
            copy.start()
            waits.append(copy)
    for d in range(1, deep):
        to_batch(three.at[d - 1], three.at[d - 1], s3.at[d - 1], r3.at[d - 1], me).wait_recv()

    def final(at):
        total = zero[me, at].astype(jnp.float32)
        for d in range(1, deep):
            total = total + three[d - 1, at].astype(jnp.float32)
        return total

    mine = core * count + me

    @pl.loop(0, (rows - solo) // piece)
    def _(i):
        at = pl.ds(pl.multiple_of(i * piece, piece), piece)
        held[0, mine, at] = final(pl.ds(pl.multiple_of(solo + i * piece, piece), piece)).astype(held.dtype)

    steps = gather_steps(route, 0, held, sends, recv)
    steps[0]()

    @pl.loop(0, solo // piece)
    def _(i):
        at = pl.ds(pl.multiple_of(i * piece, piece), piece)
        fin[at] = final(at)

    for step in steps[1:]:
        step()
    for copy in waits:
        copy.wait_send()


def reduce_all(pieces, solo, count, collective_id):
    blocks, _, width = pieces[0].shape
    kind = pieces[0].dtype
    if any(piece.shape[1] % 16 for piece in pieces):
        used = sum(piece.shape[1] for piece in pieces)
        spare = jnp.zeros((blocks, -used % 16, width), kind)
        pieces = [jnp.concatenate([*pieces, spare], axis=1)]
    rows = sum(piece.shape[1] for piece in pieces)
    route = Routes(count)
    side, deep = route.side, route.deep
    n1 = max(1, (side - 1) * side * deep)
    n2 = max(1, (side - 1) * deep)
    n3 = max(1, deep - 1)
    dma = pltpu.SemaphoreType.DMA
    return pl.pallas_call(
        functools.partial(reduce_kernel, count, solo, len(pieces)),
        out_shape=(
            jax.ShapeDtypeStruct((solo, width), jnp.float32),
            jax.ShapeDtypeStruct((1, blocks, rows - solo, width), kind),
        ),
        in_specs=[pl.BlockSpec(memory_space=pl.ANY)] * len(pieces),
        out_specs=(pl.BlockSpec(memory_space=pltpu.VMEM), pl.BlockSpec(memory_space=pltpu.VMEM)),
        scratch_shapes=[
            pltpu.VMEM((blocks, rows, width), kind),
            dma((len(pieces),)),
            pltpu.VMEM((count, rows, width), kind),
            pltpu.VMEM((n1, rows, width), kind),
            pltpu.VMEM((n2, rows, width), kind),
            pltpu.VMEM((n3, rows, width), kind),
            dma((count,)), dma((count,)),
            dma((n1,)), dma((n1,)),
            dma((n2,)), dma((n2,)),
            dma((n3,)), dma((n3,)),
            dma((1, sends_of(route))), dma((1, blocks)),
        ],
        compiler_params=pltpu.CompilerParams(
            collective_id=collective_id, has_side_effects=True, vmem_limit_bytes=VMEM_BYTES
        ),
    )(*pieces)


def last_kernel(count, *refs):
    for source, target in zip(refs[:count], refs[count:]):
        target[...] = source[...].astype(target.dtype)


def per_device(
    block_input, lengths, spans, cotangent, ffn_in, ffn_out, qkv_weight, out_weight, conv_in, kernel, conv_out, vectors,
):
    _, rows, width = block_input.shape
    count = lax.axis_size("batch")
    core = lax.axis_index("seq")
    shard = ffn_in.shape[1]
    blocks = 2 * count
    hidden = shard * blocks
    heads, size = HEADS, width // HEADS
    keys = 2 * rows
    taps = kernel.shape[0]
    inside = shard % 64 == 0 and width == 16 * blocks
    route = Routes(count)
    vm, dma = pltpu.VMEM, pltpu.SemaphoreType.DMA
    if inside:
        shards = dict(ffn_in=ffn_in, ffn_out=ffn_out)
    else:
        got = jnp.stack([ffn_in, ffn_out], axis=1).reshape(2, 2 * shard, width)
        got = gather_all(got, count, 1).reshape(2, blocks, 2, shard, width)
        shards = dict(shards=got.transpose(0, 2, 1, 3, 4).reshape(2, 2, hidden, width))
    square, tall = (rows, width), (hidden, rows)
    weights = (2, hidden, width)
    here, hbm = pl.BlockSpec(memory_space=pltpu.VMEM), pl.BlockSpec(memory_space=pl.ANY)
    scalars = dict(lengths=lengths, spans=spans)
    early = dict(x_in=block_input[0], vec=vectors, kern=kernel)
    late = dict(cot=cotangent[0], w_att=out_weight, conv_in=conv_in, conv_out=conv_out, qkv=qkv_weight)
    ins = scalars | early | {f"{key}_far": value for key, value in late.items()} | shards
    in_specs = [pl.BlockSpec(memory_space=pltpu.SMEM)] * len(scalars) + [here] * len(early)
    in_specs += [hbm] * (len(late) + len(shards))
    outs = dict(
        out=(square, LOW, here), input_grad=(square, F32, here), far_g=(weights, LOW, hbm), far_act=(tall, LOW, hbm),
        far_slope=(tall, LOW, hbm), d_att=((width, width), LOW, here), d_conv_in=((width, 2 * width), LOW, here),
        d_conv_out=((width, width), LOW, here),
    )
    if inside:
        outs |= dict(
            fin_in=((2, shard, width), F32, here), fin_out=((2, shard, width), F32, here),
            d_qkv=((3, width, width // 2), LOW, here), d_kern=((taps, width), F32, here), d_vec=((12, width), F32, here),
        )
    else:
        outs |= dict(
            d_qkv=((3, width, width), LOW, here), small=((taps + 16, width), F32, here),
            d_ffn=((2, 2, hidden, width), LOW, hbm),
        )
    scratch = dict(
        g0=vm(weights, LOW), g1=vm(weights, LOW), act=vm(tall, LOW), slope=vm(tall, LOW), qkvT=vm((3, width, width), LOW),
        x1=vm(square, F32), x2=vm(square, F32), grad=vm(square, F32), depth=vm(square, F32),
        dz=vm(square, F32), pad=vm((rows + 2 * HALO, width), F32), halo=vm((2, HALO, width), F32),
        h0=vm(square, LOW), h_all=vm((keys, width), LOW), h3=vm(square, LOW), key=vm((heads // 2, keys, 128), LOW),
        qT=vm((heads, size, rows), LOW), oT=vm((width, rows), LOW), doT=vm((heads, size, rows), LOW),
        top=vm((heads, rows), F32), extra=vm((keys, 128), LOW), wide=vm((taps, 8, width), F32), sums=vm((16, width), F32),
        own_v=vm(square, LOW),
        rk=vm((heads // 2, rows, 128), LOW), rv=vm((heads // 2, rows, 128), LOW), dq=vm(square, LOW),
        local=dma((14,)), swap=dma((12,)), qkv_mine=vm(qkv_weight.shape, LOW), cot=vm(square, LOW),
        w_att=vm((width, width), LOW), conv_in=vm((width, 2 * width), LOW), conv_out=vm((width, width), LOW),
    )
    for name, lines in (("a", 16), ("b", 8), ("c", 8))[: 3 if inside else 2]:
        scratch[f"part_{name}"] = vm((lines, 128), F32)
        for key, kind in zip(("pair", "slots", "pair_sems", "sends", "recvs"), Everyone.scratch(count, lines)):
            scratch[f"{key}_{name}"] = kind
    if not inside:
        scratch |= dict(spare=vm((width, rows), LOW), spare_wide=vm((rows, 2 * width), LOW))
    if inside:
        numbers = stage_counts(route)
        for key, number in zip(("zero", "one", "two", "three"), numbers):
            scratch[key] = vm((6, number, shard, width), LOW)
        scratch |= dict(
            box=vm((2, blocks, 64, width), LOW), held=vm((2, blocks, 64, width), LOW),
            small=vm((taps + 16, width), F32),
            g_send=dma((4, 36)), g_recv=dma((4, blocks)),
        )
        for n, number in enumerate(numbers):
            scratch[f"r_send{n}"] = dma((6, number))
            scratch[f"r_recv{n}"] = dma((6, number))
    cfg = SimpleNamespace(
        names=[*ins, *outs, *scratch], count=count, shard=shard, hidden=hidden, heads=heads, inside=inside
    )
    results = pl.pallas_call(
        functools.partial(layer_kernel, cfg),
        out_shape=tuple(jax.ShapeDtypeStruct(shape, kind) for shape, kind, _ in outs.values()),
        in_specs=in_specs,
        out_specs=tuple(spec for _, _, spec in outs.values()),
        scratch_shapes=list(scratch.values()),
        compiler_params=pltpu.CompilerParams(collective_id=0, has_side_effects=True, vmem_limit_bytes=VMEM_BYTES),
    )(*ins.values())
    got = SimpleNamespace(**dict(zip(outs, results)))
    if inside:
        plain = [got.out, got.input_grad, got.fin_in, got.fin_out, got.d_kern, got.d_vec]
        wide = [got.d_qkv, got.d_att, got.d_conv_in, got.d_conv_out]
        shapes = [(v.shape, v.dtype) for v in plain] + [(v.shape, F32) for v in wide]
        done = pl.pallas_call(
            functools.partial(last_kernel, len(shapes)),
            out_shape=tuple(jax.ShapeDtypeStruct(*shape) for shape in shapes),
            in_specs=[here] * len(shapes),
            out_specs=tuple([here] * len(shapes)),
            compiler_params=pltpu.CompilerParams(vmem_limit_bytes=VMEM_BYTES),
        )(*plain, *wide)
        out, input_grad, fin_in, fin_out, d_kern, d_vec, d_qkv, d_att, d_conv_in, d_conv_out = done
        return (
            out[None], input_grad[None], fin_in, fin_out, d_qkv, d_att, d_conv_in, d_kern, d_conv_out, d_vec,
        )

    def spread(values):
        flat = values.astype(LOW).reshape(-1, width)
        lines = -(-flat.shape[0] // blocks)
        flat = jnp.pad(flat, ((0, lines * blocks - flat.shape[0]), (0, 0)))
        return flat.reshape(blocks, lines, width)

    lines = 3 * width // (2 * count)
    per_core = got.d_qkv.reshape(3 * width, 2, width // 2).transpose(1, 0, 2).reshape(blocks, -1, width)
    d_in0, d_out0, d_in1, d_out1 = (got.d_ffn[j, m] for j in range(2) for m in range(2))
    rest = (got.d_att, got.d_conv_in, got.d_conv_out, got.small)
    pieces = [spread(v) for v in (d_in0, d_out0, d_in1, d_out1, *rest)] + [per_core]
    fin, shared = reduce_all(pieces, 4 * shard, count, 2)
    at = 0
    whole = []
    for piece, like in zip(pieces[4:8], rest):
        part = shared[0, :, at : at + piece.shape[1]].reshape(-1, width)
        whole.append(part[: like.size // width].reshape(like.shape).astype(F32))
        at += piece.shape[1]
    mine = lax.dynamic_slice_in_dim(shared[0], core * count, count, axis=0)[:, at : at + per_core.shape[1]]
    row = lax.broadcasted_iota(jnp.int32, (12, 1), 0)
    d_vec = jnp.where((row == 6) | (row == 7), got.small[taps : taps + 12], whole[3][taps : taps + 12])
    return (
        got.out[None], got.input_grad[None], jnp.stack([fin[:shard], fin[2 * shard : 3 * shard]]),
        jnp.stack([fin[shard : 2 * shard], fin[3 * shard :]]),
        mine.reshape(3, width, width // 2).astype(F32), whole[0], whole[1], whole[3][:taps], whole[2], d_vec,
    )


def solution(mesh):
    placed = (
        P("batch", "seq", None),
        P("batch"),
        P("batch", None),
        P("batch", "seq", None),
        P(None, ("seq", "batch"), None),
        P(None, ("seq", "batch"), None),
        P(None, None, "seq"),
        P(),
        P(),
        P(),
        P(),
        P(),
    )
    return jax.shard_map(
        per_device,
        mesh=mesh,
        in_specs=placed,
        out_specs=(
            P("batch", "seq", None),
            P("batch", "seq", None),
            P(None, ("seq", "batch"), None),
            P(None, ("seq", "batch"), None),
            P(None, None, "seq"),
            P(),
            P(),
            P(),
            P(),
            P(),
        ),
        check_vma=False,
    )
```

```python
import functools
import math
from types import SimpleNamespace

import jax
import jax.numpy as jnp
from jax import lax
from jax.experimental import pallas as pl
from jax.experimental.pallas import tpu as pltpu
from jax.sharding import PartitionSpec as P

HEADS = 8
MESH = pl.DeviceIdType.MESH
VMEM_BYTES = 63 * 1024 * 1024
F32, LOW = jnp.float32, jnp.bfloat16
EPS = 1e-05
HALO = 16


class Routes:
    def __init__(self, count):
        if count == 16:
            first, last, middle = (1, 2), (2, 2), (4, 4)
        elif count == 128:
            first, last, middle = (1, 4), (32, 4), (4, 8)
        else:
            first, last, middle = (1, 1), (1, 1), (1, count)
        self.count = count
        self.side = first[1]
        self.deep = middle[1]
        self.first, self.last, self.middle = first, last, middle

    def here(self):
        self.core = lax.axis_index("seq")
        self.me = lax.axis_index("batch")
        turn = self.core * (self.last[0] - self.first[0])
        self.one = self.first[0] + turn
        self.two = self.last[0] - turn
        self.mid = self.middle[0]
        self.p = lax.rem(lax.div(self.me, self.one), self.side)
        self.q = lax.rem(lax.div(self.me, self.two), self.side)
        self.z = lax.rem(lax.div(self.me, self.mid), self.deep)
        return self

    def index(self, z, p, q):
        return z * self.mid + p * self.one + q * self.two

    def plane(self, d):
        if self.deep != 4 or d == 0:
            return lax.rem(self.z + d, self.deep) if d else self.z
        return (self.z + 1 - 2 * lax.rem(self.z, 2), lax.rem(self.z + 2, 4), 3 - self.z)[d - 1]

    def reach(self, i):
        far = lax.div(self.z, 2)
        first = self.z + far * (3 - 2 * self.z)
        turn = (first, 1 - first, 2, 3)[i]
        return turn + far * (3 - 2 * turn)

    def near(self, d, e, f):
        p = lax.rem(self.p + e, self.side) if e else self.p
        q = lax.rem(self.q + f, self.side) if f else self.q
        return self.index(self.plane(d), p, q)

    def peers(self):
        found = []
        for k in range(1, self.deep):
            found.append(self.index(lax.rem(self.z + k, self.deep), self.p, self.q))
        for k in range(1, self.side):
            found.append(self.index(self.z, lax.rem(self.p + k, self.side), self.q))
            found.append(self.index(self.z, self.p, lax.rem(self.q + k, self.side)))
        return found

    def greet(self):
        barrier = pltpu.get_barrier_semaphore()
        places = self.peers()
        for place in places:
            pl.semaphore_signal(
                barrier, inc=1, device_id={"batch": place}, device_id_type=MESH
            )
        pl.semaphore_signal(
            barrier, inc=1, device_id={"seq": 1 - self.core}, device_id_type=MESH
        )
        pl.semaphore_wait(barrier, len(places) + 1)


def to_batch(src, dst, send, recv, place):
    return pltpu.make_async_remote_copy(
        src_ref=src, dst_ref=dst, send_sem=send, recv_sem=recv,
        device_id={"batch": place}, device_id_type=MESH,
    )


def to_core(src, dst, send, recv, core):
    return pltpu.make_async_remote_copy(
        src_ref=src, dst_ref=dst, send_sem=send, recv_sem=recv,
        device_id={"seq": core}, device_id_type=MESH,
    )


class Gather:
    def __init__(self, route, at, sends, recv, line):
        self.route, self.at, self.sends, self.recv, self.line = route, at, sends, recv, line

    def go(self, here, kind, z, send, place):
        if place is None:
            to_core(here, here, self.sends.at[send], self.recv.at[kind, z], 1 - self.route.core).start()
        else:
            to_batch(here, here, self.sends.at[send], self.recv.at[kind, z], place).start()

    def come(self, here, kind, z):
        to_core(here, here, self.recv.at[kind, z], self.recv.at[kind, z], 1 - self.route.core).wait_recv()

    def z_of(self, i):
        return self.route.reach(i) if self.line else self.route.plane(i)

    def plane_one(self, i):
        route = self.route
        z = self.z_of(i)
        here = self.at(route.core * route.deep + z, route.q, route.p)
        if i:
            self.come(here, 0, z)
        if self.line:
            @pl.when((z <= route.z) & (route.z < route.deep - 1))
            def _():
                self.go(here, 0, z, 3 + z, route.index(route.z + 1, route.p, route.q))

            @pl.when((z >= route.z) & (route.z > 0))
            def _():
                self.go(here, 0, z, 7 + z, route.index(route.z - 1, route.p, route.q))
        elif i == 0:
            for d in range(1, route.deep):
                self.go(here, 0, z, 2 + d, route.near(d, 0, 0))
        self.go(here, 1, z, 0, route.near(0, 1, 0))
        self.go(here, 2, z, 1, route.near(0, 0, 1))

    def plane_two(self, i):
        route = self.route
        z = self.z_of(i)
        cz = route.core * route.deep + z
        here = self.at(cz, route.q, 1 - route.p)
        self.come(here, 1, z)
        self.go(here, 2, z, 1, route.near(0, 0, 1))

    def plane_last(self, i):
        route = self.route
        z = self.z_of(i)
        cz = route.core * route.deep + z
        self.come(self.at(cz, route.q), 2, z)
        self.go(self.at(cz), 3, z, 2, None)

    def plane_other(self, i):
        route = self.route
        z = self.z_of(i)
        self.come(self.at((1 - route.core) * route.deep + z), 3, z)

    def finish(self):
        route = self.route

        def sent(here, send):
            to_core(here, here, self.sends.at[send], self.sends.at[send], 1 - route.core).wait_send()

        sent(self.at(0), 0)
        sent(self.at(pl.ds(0, 2)), 1)
        sent(self.at(pl.ds(0, 4)), 2)
        one = self.at(0, 0, 0)
        if not self.line:
            for d in range(1, route.deep):
                sent(one, 2 + d)
            return
        for z in range(route.deep):
            pl.when((z <= route.z) & (route.z < route.deep - 1))(functools.partial(sent, one, 3 + z))
            pl.when((z >= route.z) & (route.z > 0))(functools.partial(sent, one, 7 + z))


class Reduce:
    def __init__(self, route, source, stage, sends, recv):
        self.route, self.source, self.sends, self.recv = route, source, sends, recv
        self.zero, self.one, self.two, self.three = stage
        self.lead = self.zero.shape[0]

    def come(self, here, kind, n):
        to_core(here, here, self.recv.at[kind, n], self.recv.at[kind, n], 1 - self.route.core).wait_recv()

    def add(self, at, value):
        self.zero[at] = (self.zero[at].astype(F32) + value.astype(F32)).astype(LOW)

    def leave(self, d):
        route = self.route
        z = route.plane(d)
        to_core(
            self.source((1 - route.core) * route.deep + z), self.zero.at[:, z], self.sends.at[0],
            self.recv.at[0, z], 1 - route.core,
        ).start()

    def start(self):
        for d in range(self.route.deep - 1, -1, -1):
            self.leave(d)

    def step_one(self, d):
        route = self.route
        z = route.plane(d)
        self.come(self.zero.at[:, z], 0, z)
        mine = self.source(route.core * route.deep + z)
        for n in range(self.lead):
            for q in range(2):
                for p in range(2):
                    self.add((n, z, q, p), mine[n, q, p])
        to_batch(
            self.zero.at[:, z, :, 1 - route.p], self.one.at[:, d], self.sends.at[1], self.recv.at[1, d],
            route.near(0, 1, 0),
        ).start()

    def step_two(self, d):
        route = self.route
        z = route.plane(d)
        self.come(self.one.at[:, d], 1, d)
        for n in range(self.lead):
            for q in range(2):
                self.add((n, z, q, route.p), self.one[n, d, q])
        to_batch(
            self.zero.at[:, z, 1 - route.q, route.p], self.two.at[:, d], self.sends.at[2], self.recv.at[2, d],
            route.near(0, 0, 1),
        ).start()

    def step_three(self, d):
        route = self.route
        z = route.plane(d)
        self.come(self.two.at[:, d], 2, d)
        for n in range(self.lead):
            self.add((n, z, route.q, route.p), self.two[n, d])
        if d:
            to_batch(
                self.zero.at[:, z, route.q, route.p], self.three.at[:, d - 1], self.sends.at[3],
                self.recv.at[3, d - 1], route.near(d, 0, 0),
            ).start()

    def total(self):
        route = self.route
        for d in range(1, route.deep):
            self.come(self.three.at[:, d - 1], 3, d - 1)
        sums = []
        for n in range(self.lead):
            out = self.zero[n, route.z, route.q, route.p].astype(F32)
            for d in range(1, route.deep):
                out = out + self.three[n, d - 1].astype(F32)
            sums.append(out)
        return sums

    def sent(self, kind):
        here = (self.zero, self.one, self.two, self.three)[kind]
        to_core(here, here, self.sends.at[kind], self.sends.at[kind], 1 - self.route.core).wait_send()


class Everyone:
    def __init__(self, count, pair, slots, pair_sems, sends, recvs):
        self.count, self.pair, self.slots = count, pair, slots
        self.pair_sems, self.sends, self.recvs = pair_sems, sends, recvs

    def start(self, x):
        core, me, count = lax.axis_index("seq"), lax.axis_index("batch"), self.count
        copy = to_core(x, self.pair, self.pair_sems.at[0], self.pair_sems.at[1], 1 - core)
        copy.start()
        copy.wait()
        self.slots[me] = x[...] + self.pair[...]
        for k in range(1, count):
            here = self.slots.at[me]
            to_batch(here, here, self.sends, self.recvs, lax.rem(me + k, count)).start()

    def total(self):
        others = self.slots.at[pl.ds(0, self.count - 1)]
        copy = to_batch(others, others, self.sends, self.recvs, lax.axis_index("batch"))
        copy.wait_recv()
        out = self.slots[0]
        for place in range(1, self.count):
            out = out + self.slots[place]
        copy.wait_send()
        return out

    @staticmethod
    def scratch(count, rows):
        return [
            pltpu.VMEM((rows, 128), F32),
            pltpu.VMEM((count, rows, 128), F32),
            pltpu.SemaphoreType.DMA((2,)),
            pltpu.SemaphoreType.DMA,
            pltpu.SemaphoreType.DMA,
        ]


def to_tile(rows):
    width = rows.shape[1]
    parts = [rows[i : i + 1, j : j + 128] for i in range(rows.shape[0]) for j in range(0, width, 128)]
    return jnp.concatenate(parts, axis=0)


def from_tile(tile, first, width):
    each = width // 128
    return jnp.concatenate([tile[first * each + j : first * each + j + 1] for j in range(each)], axis=1)


def nn(a, b):
    return lax.dot_general(a, b, (((1,), (0,)), ((), ())), preferred_element_type=F32)


def nt(a, b):
    return lax.dot_general(a, b, (((1,), (1,)), ((), ())), preferred_element_type=F32)


def tn(a, b):
    return lax.dot_general(a, b, (((0,), (0,)), ((), ())), preferred_element_type=F32)


def sigmoid(v):
    return 0.5 * jnp.tanh(0.5 * v) + 0.5


def rows_of(i, size):
    return pl.ds(pl.multiple_of(i * size, size), size)


def normed(v):
    centred = v - jnp.mean(v, -1, keepdims=True)
    scale = lax.rsqrt(jnp.mean(centred * centred, -1, keepdims=True) + EPS)
    return centred * scale, scale


def normed_back(grad, hat, scale):
    return scale * (
        grad - jnp.mean(grad, -1, keepdims=True) - hat * jnp.mean(grad * hat, -1, keepdims=True)
    )


def fold(values):
    return jnp.sum(values.reshape(values.shape[0] // 8, 8, values.shape[1]), 0)


def norm_rows(x_ref, put, vec, row, block=64):
    @pl.loop(0, x_ref.shape[0] // block)
    def _(i):
        at = rows_of(i, block)
        hat, _ = normed(x_ref[at])
        put(at, (hat * vec[row : row + 1] + vec[row + 1 : row + 2]).astype(LOW))


def norm_rows_back(grad_ref, x_ref, g_ref, put, vec, sums, row, block=64):
    width = x_ref.shape[1]

    def step(i, carry):
        gain, bias = carry
        at = rows_of(i, block)
        hat, scale = normed(x_ref[at])
        grad = grad_ref[at]
        put(at, g_ref[at] + normed_back(grad * vec[row : row + 1], hat, scale))
        return gain + fold(grad * hat), bias + fold(grad)

    zero = jnp.zeros((8, width), F32)
    gain, bias = lax.fori_loop(0, x_ref.shape[0] // block, step, (zero, zero))
    sums[row : row + 1] = jnp.sum(gain, 0, keepdims=True)
    sums[row + 1 : row + 2] = jnp.sum(bias, 0, keepdims=True)


def activate(a):
    s = sigmoid(a)
    u = a * s
    return u, s + u * (1.0 - s)


def valid_rows(scal, at_row, rows):
    frame = scal[0] + at_row + lax.broadcasted_iota(jnp.int32, (rows, 1), 0)
    return frame, jnp.where(frame < scal[1], 1.0, 0.0)


def keep_rows(scal, at_row, rows, width):
    frame, ok = valid_rows(scal, at_row, rows)
    cut = (frame >= scal[2]) & (frame < scal[2] + scal[3])
    channel = lax.broadcasted_iota(jnp.int32, (1, width), 1)
    lost = (channel >= scal[4]) & (channel < scal[4] + scal[5])
    return (ok * jnp.where(cut, 0.0, 1.0)) * jnp.where(lost, 0.0, 1.0)


def masked_input(scal, x_in, x_ref, block=64):
    @pl.loop(0, x_in.shape[0] // block)
    def _(i):
        at = rows_of(i, block)
        keep = keep_rows(scal, i * block, block, x_in.shape[1])
        x_ref[at] = x_in[at].astype(F32) * keep


def split3(v):
    high = v.astype(LOW).astype(F32)
    rest = v - high
    mid = rest.astype(LOW).astype(F32)
    return high, mid, rest - mid


def key_extra(length, rows):
    key = lax.broadcasted_iota(jnp.int32, (rows, 128), 0)
    lane = lax.broadcasted_iota(jnp.int32, (rows, 128), 1)
    lost = jnp.where(key < length, 0.0, -1e30)
    return jnp.where(lane == 0, lost, jnp.where(lane < 4, 1.0, 0.0)).astype(LOW)


def fill_side(side, first, extra_rows):
    size = first[0].shape[0]
    blank = jnp.zeros((size, side.shape[2]), LOW)
    for half in range(2):
        side[half, half * size : (half + 1) * size] = first[half]
        side[half, (1 - half) * size : (2 - half) * size] = blank
        side[half, 2 * size :] = extra_rows[half]


def extra_of(lead, parts, wide):
    row = lax.broadcasted_iota(jnp.int32, (16, wide), 0)
    out = jnp.where(row == 0, lead, 0.0)
    if parts is not None:
        for n, part in enumerate(parts):
            out = jnp.where(row == n + 1, -part, out)
    return jnp.concatenate([out.astype(LOW), jnp.zeros((112, wide), LOW)], axis=0)


def attention_forward(qT, key, vT, extra, oT, top, side, scale, hook):
    heads, size, queries = qT.shape
    keys = key.shape[1]
    ones = jnp.ones((16, keys), LOW)

    @pl.loop(0, heads // 2)
    def _(pair):
        hook(pair)
        lead = extra_of(1.0, None, queries)
        fill_side(side, [qT[2 * pair], qT[2 * pair + 1]], [lead, lead])
        left = jnp.concatenate([key[pair], extra[...]], axis=1)
        for half in range(2):
            head = 2 * pair + half
            s = nn(left, side[half])
            m = jnp.max(s, 0, keepdims=True)
            p = jnp.exp2((s - m) * scale).astype(LOW)
            o = nn(jnp.concatenate([vT[head], ones], axis=0), p)
            total = o[size : size + 1]
            oT[rows_of(head, size)] = (o[:size] * (1.0 / total)).astype(LOW)
            top[pl.ds(head, 1)] = m + jnp.log2(total) * (1.0 / scale)


def attention_backward(
    qT, key, h_all, qkvT, extra, doT, delta, top, dqT, dk, dv, qside, oside, lows, grads, scale, shrink, hook, chunk=512
):
    heads, size, queries = qT.shape
    keys = key.shape[1]

    @pl.loop(0, heads // 2)
    def _(pair):
        hook(pair)
        tops = [split3(top[pl.ds(2 * pair + half, 1)]) for half in range(2)]
        deltas = [split3(delta[pl.ds(2 * pair + half, 1)]) for half in range(2)]
        fill_side(qside, [qT[2 * pair], qT[2 * pair + 1]], [extra_of(1.0, t, queries) for t in tops])
        fill_side(oside, [doT[2 * pair], doT[2 * pair + 1]], [extra_of(0.0, t, queries) for t in deltas])
        kT = nt(qkvT[1, rows_of(pair, 128)], h_all[...]).astype(LOW)
        wide_o = jnp.concatenate([oside[0, :128], oside[1, :128]], axis=1)
        wide_q = jnp.concatenate([qside[0, :128], qside[1, :128]], axis=1)
        totals = [None, None]
        for c in range(keys // chunk):
            at = slice(c * chunk, (c + 1) * chunk)
            value = nt(h_all[at], qkvT[2, rows_of(pair, 128)]).astype(LOW)
            left_k = jnp.concatenate([key[pair, at], extra[at]], axis=1)
            left_v = jnp.concatenate([value, extra[at]], axis=1)
            for half in range(2):
                lanes = slice(half * queries, (half + 1) * queries)
                p = jnp.exp2(nn(left_k, qside[half]) * scale)
                lows[:, lanes] = p.astype(LOW)
                grads[:, lanes] = (p * nn(left_v, oside[half])).astype(LOW)
            for half in range(2):
                lanes = slice(half * queries, (half + 1) * queries)
                got = nn(kT[half * size : (half + 1) * size, at], grads[:, lanes])
                totals[half] = got if c == 0 else totals[half] + got
            dv[pair, at] = nt(lows[...], wide_o).astype(LOW)
            dk[pair, at] = (nt(grads[...], wide_q) * shrink).astype(LOW)
        for half in range(2):
            dqT[rows_of(2 * pair + half, size)] = (totals[half] * shrink).astype(LOW)


def windows(pad_ref, at_row, block, lanes, shifts):
    for s in range(8):
        mine = [(tap, shift) for tap, shift in shifts if shift % 8 == s]
        low = min(shift for _, shift in mine)
        high = max(shift for _, shift in mine)
        window = pad_ref[at_row + low : at_row + high + block, lanes]
        for tap, shift in mine:
            yield tap, window[shift - low : shift - low + block]


def convolve(pad_ref, taps_wide, put, shift_of, rows, width, hook=None, block=64):
    count = taps_wide.shape[0]
    shifts = [(tap, shift_of(tap)) for tap in range(count)]
    for lane in range(0, width, 128):
        lanes = slice(lane, lane + 128)
        for at_row in range(0, rows, block):
            total = jnp.zeros((block // 8, 8, 128), F32)
            for tap, values in windows(pad_ref, at_row, block, lanes, shifts):
                total = total + taps_wide[tap, :, lanes][None] * values.reshape(block // 8, 8, 128)
            put(at_row, block, lane, total.reshape(block, 128))
        if hook:
            hook(1)


def convolve_weight(pad_ref, grad_ref, first, out_ref, shift_of, rows, width, hook, block=64):
    taps = out_ref.shape[0]
    for lane in range(0, width, 128):
        lanes = slice(lane, lane + 128)
        for s in range(8):
            mine = [(tap, shift_of(tap)) for tap in range(taps) if shift_of(tap) % 8 == s]
            low = min(shift for _, shift in mine)
            high = max(shift for _, shift in mine)
            sums = {tap: jnp.zeros((8, 128), F32) for tap, _ in mine}
            for at_row in range(0, rows, block):
                grad = grad_ref[first + at_row : first + at_row + block, lanes]
                window = pad_ref[at_row + low : at_row + high + block, lanes]
                for tap, shift in mine:
                    sums[tap] = sums[tap] + fold(grad * window[shift - low : shift - low + block])
            for tap, _ in mine:
                out_ref[tap : tap + 1, lanes] = jnp.sum(sums[tap], 0, keepdims=True)
        if hook:
            hook(1)


def place_halo(pad_ref, halo, core):
    rows = pad_ref.shape[0] - 2 * HALO
    got = halo[...]
    zero = jnp.zeros_like(got)
    pad_ref[0:HALO] = jnp.where(core == 1, got, zero)
    pad_ref[rows + HALO :] = jnp.where(core == 0, got, zero)


def layer_kernel(cfg, *refs):
    r = SimpleNamespace(**dict(zip(cfg.names, refs)))
    count, shard, hidden, inside = cfg.count, cfg.shard, cfg.hidden, cfg.inside
    rows, width = r.x_in.shape
    heads, size = cfg.heads, width // cfg.heads
    keys, pairs, taps = 2 * rows, heads // 2, r.kern.shape[0]
    scale, shrink = math.log2(math.e) / math.sqrt(size), 1.0 / math.sqrt(size)
    route = Routes(count).here()
    core, me = route.core, route.me
    vec, g0, g1, sums = r.vec, r.g0, r.g1, r.sums
    chunk, block = 256, 64
    own = pl.ds(pl.multiple_of(core * rows, rows), rows)
    theirs = pl.ds(pl.multiple_of((1 - core) * rows, rows), rows)
    zero8 = jnp.zeros((8, width), F32)

    def plane_of(g, m, i):
        return g[m, i].reshape(chunk, width)

    def whole_of(g, m):
        return g[m].reshape(hidden, width)

    barrier = pltpu.get_barrier_semaphore()
    for k in range(1, count):
        pl.semaphore_signal(
            barrier, inc=1, device_id={"batch": lax.rem(me + k, count)}, device_id_type=MESH
        )
    pl.semaphore_signal(barrier, inc=1, device_id={"seq": 1 - core}, device_id_type=MESH)
    half = width // 2
    q_own = pl.ds(pl.multiple_of(core * half, half), half)
    loads = []

    def load(source, target):
        copy = pltpu.make_async_copy(source, target, r.local.at[4 + len(loads)])
        copy.start()
        loads.append(copy)
        return copy

    if inside:
        cz = core * route.deep + route.z
        near_loads = [
            load(part.at[j], g.at[m, cz, route.q, route.p]) for m, part in enumerate((r.ffn_in, r.ffn_out)) for j, g in enumerate((g0, g1))
        ]
    else:
        near_loads = [load(r.shards.at[0], g0), load(r.shards.at[1], g1)]
    load_qkv = load(r.qkv_far, r.qkv_mine)
    load_att = load(r.w_att_far, r.w_att)
    load_conv_in = load(r.conv_in_far, r.conv_in)
    load_conv_out = load(r.conv_out_far, r.conv_out)
    load_cot = load(r.cot_far, r.cot)
    frame0, length, span = core * rows, r.lengths[0], [r.spans[0, n] for n in range(4)]
    scal = [frame0, length, *span]
    sums[...] = jnp.zeros_like(sums)
    masked_input(scal, r.x_in, r.x1)

    def put_h0(at, value):
        r.h0[at] = value

    norm_rows(r.x1, put_h0, vec, 0)
    for tap in range(taps):
        r.wide[tap] = jnp.broadcast_to(r.kern[tap : tap + 1], (8, width))
    for copy in near_loads:
        copy.wait()
    pl.semaphore_wait(barrier, count)

    def inner(i):
        at = rows_of(i, chunk)
        u, slope = activate(nt(plane_of(g0, 0, i), r.h0[...]))
        r.act[at] = u.astype(LOW)
        r.slope[at] = slope.astype(LOW)

    swap_q = to_core(r.qkvT.at[:, q_own], r.qkvT.at[:, q_own], r.swap.at[0], r.swap.at[1], 1 - core)

    def turn_qkv():
        load_qkv.wait()
        for s in range(3):
            r.qkvT[s, q_own] = r.qkv_mine[s].astype(F32).T.astype(LOW)
        swap_q.start()

    if inside:
        first = Gather(route, lambda *i: g0.at[(slice(None), *i)], r.g_send.at[0], r.g_recv.at[0], True)
        second = Gather(route, lambda *i: g1.at[(slice(None), *i)], r.g_send.at[1], r.g_recv.at[1], True)
        deep = route.deep

        def inner_plane(which, d):
            inner(which * deep + route.reach(d))

        first.plane_one(0)
        turn_qkv()
        first.plane_one(1)
        first.plane_one(2)
        first.plane_two(0)
        first.plane_one(3)
        for d in (1, 2, 3):
            first.plane_two(d)
        second.plane_one(0)
        for d in range(deep):
            first.plane_last(d)
            inner_plane(core, d)
            if d:
                first.plane_other(d - 1)
                inner_plane(1 - core, d - 1)
        first.plane_other(deep - 1)
        inner_plane(1 - core, deep - 1)
    else:
        turn_qkv()

        @pl.loop(0, hidden // chunk)
        def _(i):
            inner(i)

    @pl.loop(0, rows // 256)
    def _(i):
        at = rows_of(i, 256)
        r.x1[at] = r.x1[at] + 0.5 * tn(r.act[:, at], whole_of(g0, 1))

    def put_h2(at, value):
        r.h_all[pl.ds(pl.multiple_of(core * rows + at.start, block), block)] = value

    norm_rows(r.x1, put_h2, vec, 2)
    swap = to_core(r.h_all.at[own], r.h_all.at[own], r.swap.at[2], r.swap.at[3], 1 - core)
    swap.start()
    away = [
        pltpu.make_async_copy(g0, r.far_g, r.local.at[0]),
        pltpu.make_async_copy(r.act, r.far_act, r.local.at[1]),
        pltpu.make_async_copy(r.slope, r.far_slope, r.local.at[2]),
    ]
    for copy in away:
        copy.start()
    swap_q.wait()

    def project(at, vT):
        here = r.h_all[at]
        for pair in range(pairs):
            r.key[pair, at] = nt(here, r.qkvT[1, pair * 128 : (pair + 1) * 128]).astype(LOW)
        vT[:, :, at] = nt(r.qkvT[2], here).astype(LOW).reshape(heads, size, rows)

    r.extra[...] = key_extra(scal[1], keys)

    def attend(vT, side_ref):
        r.qT[...] = nt(r.qkvT[0], r.h_all[own]).astype(LOW).reshape(heads, size, rows)
        project(own, vT)
        if inside:
            second.plane_one(1)
            second.plane_two(0)
        swap.wait()
        project(theirs, vT)

        def hook(pair):
            if inside:
                @pl.when(pair == 2)
                def _():
                    second.plane_one(2)
                    second.plane_two(1)
                    second.plane_last(0)

        attention_forward(r.qT, r.key, vT, r.extra, r.oT, r.top, side_ref, scale, hook)

    pl.run_scoped(attend, pltpu.VMEM((heads, size, keys), LOW), pltpu.VMEM((2, 256, rows), LOW))

    load_att.wait()

    if inside:
        second.plane_one(3)
        second.plane_two(2)
        second.plane_last(1)

    @pl.loop(0, rows // 256)
    def _(i):
        at = rows_of(i, 256)
        r.x2[at] = r.x1[at] + tn(r.oT[:, at], r.w_att[...])

    def put_h3(at, value):
        r.h3[at] = value

    norm_rows(r.x2, put_h3, vec, 4)
    load_conv_in.wait()

    @pl.loop(0, rows // 256)
    def _(i):
        at = rows_of(i, 256)
        _, ok = valid_rows(scal, i * 256, 256)
        here = r.h3[at]
        gate = sigmoid(nn(here, r.conv_in[:, width:]))
        r.pad[pl.ds(pl.multiple_of(i * 256 + HALO, HALO), 256)] = nn(here, r.conv_in[:, :width]) * gate * ok

    edge = pl.ds(pl.multiple_of(HALO + (1 - core) * (rows - HALO), HALO), HALO)
    swap = to_core(r.pad.at[edge], r.halo.at[0], r.swap.at[4], r.swap.at[5], 1 - core)
    swap.start()
    if inside:
        second.plane_two(3)
        second.plane_last(2)
    swap.wait()
    place_halo(r.pad, r.halo.at[0], core)

    def put_depth(at_row, high, lane, total):
        r.depth[at_row : at_row + high, lane : lane + 128] = total

    convolve(r.pad, r.wide, put_depth, lambda tap: tap + 1, rows, width)

    if inside:
        second.plane_last(3)

    def moments(i, carry):
        one, two = carry
        _, ok = valid_rows(scal, i * block, block)
        here = r.depth[rows_of(i, block)]
        held = here * ok
        return one + fold(held), two + fold(here * held)

    one, two = lax.fori_loop(0, rows // block, moments, (zero8, zero8))
    number = jnp.clip(scal[1] - scal[0], 0, rows).astype(F32)
    r.part_a[0:8] = to_tile(
        jnp.concatenate([jnp.sum(one, 0, keepdims=True), jnp.sum(two, 0, keepdims=True)], axis=0)
    )
    r.part_a[8:16] = jnp.full((8, 128), 1.0, F32) * number
    every = Everyone(count, r.pair_a, r.slots_a, r.pair_sems_a, r.sends_a, r.recvs_a)
    every.start(r.part_a)
    if inside:
        for d in range(deep):
            second.plane_other(d)
        second.finish()
        first.finish()
    for copy in [*away, load_conv_out, load_cot]:
        copy.wait()
    tile = every.total()
    number = tile[8:9, 0:1]
    mean = from_tile(tile, 0, width) / number
    var = from_tile(tile, 1, width) / number - mean * mean
    spread = lax.rsqrt(var + EPS)
    gain6 = vec[6:7]

    if inside:
        stages = [
            Reduce(route, source, [ref.at[part] for ref in (r.zero, r.one, r.two, r.three)], r.r_send.at[k], r.r_recv.at[k])
            for k, (part, source) in enumerate(
                [
                    (pl.ds(0, 2), lambda cz: g0.at[:, cz]),
                    (pl.ds(2, 1), lambda cz: r.box.at[pl.ds(0, 1), cz]),
                    (pl.ds(3, 1), lambda cz: r.box.at[pl.ds(1, 1), cz]),
                    (pl.ds(4, 2), lambda cz: g0.at[:, cz]),
                ]
            )
        ]
        ffn1, rest, proj, ffn0 = stages
        queue = []

        def put_off(chunks, lag, ends):
            units = [(n, d) for n in range(len(chunks)) for d in range(deep - 1, -1, -1)]
            for t in range(len(units) + lag):
                if t < len(units):
                    n, d = units[t]
                    queue.append(functools.partial(chunks[n].step_two, d))
                if t >= lag:
                    n, d = units[t - lag]
                    queue.append(functools.partial(chunks[n].step_three, d))
                    if d == 0:
                        queue.append(ends[n])

        def tick(count):
            for _ in range(min(count, len(queue))):
                queue.pop(0)()

        own_at = (core * deep + route.z, route.q, route.p)

        def ticks(*counts):
            left = list(counts)
            return lambda _: tick(left.pop(0))

        def end_ffn(j, piece):
            r.fin_in[j], r.fin_out[j] = piece.total()

        def end_box(j, piece):
            r.held[(j, *own_at)] = piece.total()[0].astype(LOW)

        third = Gather(route, lambda *i: r.held.at[(0, *i)], r.g_send.at[2], r.g_recv.at[2], False)
        fourth = Gather(route, lambda *i: r.held.at[(1, *i)], r.g_send.at[3], r.g_recv.at[3], False)
    else:
        def tick(count):
            pass

        def ticks(*counts):
            return None
    back_copies = [
        pltpu.make_async_copy(r.far_act, r.act, r.local.at[0]),
        pltpu.make_async_copy(r.far_slope, r.slope, r.local.at[1]),
        pltpu.make_async_copy(r.far_g, g1, r.local.at[2]),
    ]

    def hidden_grad(weight, dy, da, i):
        at = rows_of(i, chunk)
        du = nt(plane_of(weight, 1, i), dy[...])
        low = (du * r.slope[at].astype(F32)).astype(LOW)
        da[at] = low
        return low

    def weight_grads(h_ref, dy, low, i):
        at = rows_of(i, chunk)
        g0[1, i] = nn(r.act[at], dy[...]).astype(LOW).reshape(g0.shape[2:])
        g0[0, i] = nn(low, h_ref[...]).astype(LOW).reshape(g0.shape[2:])

    def by_planes(grads, piece, hooks):
        if not inside:
            pl.loop(0, hidden // chunk)(grads)
            return
        for n, d in enumerate(range(deep - 1, -1, -1)):
            grads((1 - core) * deep + route.plane(d))
            piece.leave(d)
            hooks(n)
        for n, d in enumerate(range(deep - 1, -1, -1)):
            grads(core * deep + route.plane(d))
            piece.step_one(d)
            hooks(deep + n)

    def middle(slope_z, da, dh):
        low, dy, h4 = r.d_conv_in.at[:, pl.ds(0, width)], r.d_conv_in.at[:, pl.ds(width, width)], r.d_att
        dc = r.d_conv_out if inside else r.spare
        x3, x4 = r.input_grad, r.dz

        @pl.loop(0, rows // block)
        def _(i):
            at = rows_of(i, block)
            z = (r.depth[at] - mean) * spread * gain6 + vec[7:8]
            u, slope = activate(z)
            low[at] = u.astype(LOW)
            slope_z[at] = slope

        @pl.loop(0, rows // 256)
        def _(i):
            at = rows_of(i, 256)
            x3[at] = r.x2[at] + nn(low[at], r.conv_out[...])

        def put_h4(at, value):
            h4[at] = value

        norm_rows(x3, put_h4, vec, 8)

        @pl.loop(0, hidden // chunk)
        def _(i):
            at = rows_of(i, chunk)
            u, slope = activate(nt(plane_of(g1, 0, i), h4[...]))
            r.act[at] = u.astype(LOW)
            r.slope[at] = slope.astype(LOW)

        @pl.loop(0, rows // 256)
        def _(i):
            at = rows_of(i, 256)
            x4[at] = x3[at] + 0.5 * tn(r.act[:, at], whole_of(g1, 1))

        def last(i, carry):
            gain, bias = carry
            at = rows_of(i, block)
            hat, rate = normed(x4[at])
            r.out[at] = (hat * vec[10:11] + vec[11:12]).astype(LOW)
            g = r.cot[at].astype(F32)
            back = normed_back(g * vec[10:11], hat, rate)
            r.grad[at] = back
            dy[at] = (0.5 * back).astype(LOW)
            return gain + fold(g * hat), bias + fold(g)

        gain, bias = lax.fori_loop(0, rows // block, last, (zero8, zero8))
        sums[10:11] = jnp.sum(gain, 0, keepdims=True)
        sums[11:12] = jnp.sum(bias, 0, keepdims=True)
        @pl.loop(0, hidden // chunk)
        def _(i):
            hidden_grad(g1, dy, da, i)

        @pl.loop(0, rows // 256)
        def _(i):
            at = rows_of(i, 256)
            dh[at] = tn(da[:, at], whole_of(g1, 0))

        back_copies[2].start()

        def put(at, value):
            r.grad[at] = value
            dc[at] = value.astype(LOW)

        norm_rows_back(dh, x3, r.grad, put, vec, sums, 8)

        @pl.loop(0, rows // 256)
        def _(i):
            at = rows_of(i, 256)
            r.dz[at] = nt(dc[at], r.conv_out[...])

        def close(i, carry):
            one, two = carry
            at = rows_of(i, block)
            here = r.dz[at] * slope_z[at]
            r.dz[at] = here
            return one + fold(here), two + fold(here * (r.depth[at] - mean))

        one, two = lax.fori_loop(0, rows // block, close, (zero8, zero8))
        r.part_b[...] = to_tile(
            jnp.concatenate([jnp.sum(one, 0, keepdims=True), jnp.sum(two, 0, keepdims=True)], axis=0)
        )
        every = Everyone(count, r.pair_b, r.slots_b, r.pair_sems_b, r.sends_b, r.recvs_b)
        every.start(r.part_b)
        got = tn(low[...], dc[...]).astype(LOW)
        if inside:
            r.box[0, :, :, :, 0:16] = got.reshape(*r.box.shape[1:4], 16, width)
        else:
            r.d_conv_out[...] = got
        by_planes(
            lambda i: weight_grads(h4, dy, da[rows_of(i, chunk)], i), ffn1 if inside else None, lambda n: None
        )
        back_copies[0].start()
        back_copies[1].start()
        r.part_b[...] = every.total()

    square = (rows, width)
    vm = pltpu.VMEM
    pl.run_scoped(
        middle, vm(square, F32), vm((hidden, rows), LOW), vm(square, F32),
    )
    if not inside:
        copy = pltpu.make_async_copy(g0, r.d_ffn.at[1], r.local.at[3])
        copy.start()
        copy.wait()
    tile = r.part_b[...]
    grad_sum, grad_moment = from_tile(tile, 0, width), from_tile(tile, 1, width)
    if inside:
        put_off([ffn1], 1, [functools.partial(end_ffn, 1, ffn1)])
    var_grad = -0.5 * (gain6 * grad_moment) * spread * spread * spread
    flat = (-(gain6 * spread * grad_sum) - 2.0 * mean * var_grad) / number
    tilt = 2.0 * var_grad / number

    def convolution_back(back, p, datt):
        dp, dh = r.d_conv_in if inside else r.spare_wide, r.input_grad

        @pl.loop(0, rows // block)
        def _(i):
            at = rows_of(i, block)
            _, ok = valid_rows(scal, i * block, block)
            back[pl.ds(pl.multiple_of(i * block + HALO, HALO), block)] = gain6 * spread * r.dz[at] + ok * (
                flat + r.depth[at] * tilt
            )

        swap = to_core(back.at[edge], r.halo.at[1], r.swap.at[6], r.swap.at[7], 1 - core)
        swap.start()
        convolve_weight(r.pad, back, HALO, r.small.at[pl.ds(0, taps)], lambda tap: tap + 1, rows, width, ticks(0, 0, 1, 0))

        @pl.loop(0, rows // 256)
        def _(i):
            at = rows_of(i, 256)
            p[at] = nn(r.h3[at], r.conv_in[...])

        swap.wait()
        place_halo(back, r.halo.at[1], core)

        def put(at_row, high, lane, total):
            at = slice(at_row, at_row + high)
            _, ok = valid_rows(scal, at_row, high)
            gate = sigmoid(p[at, width + lane : width + lane + 128])
            total = total * gate * ok
            dp[at, lane : lane + 128] = total.astype(LOW)
            dp[at, width + lane : width + lane + 128] = (
                total * p[at, lane : lane + 128] * (1.0 - gate)
            ).astype(LOW)

        convolve(back, r.wide, put, lambda tap: taps - 1 - tap, rows, width, ticks(0, 1, 1, 0))
        got = tn(r.h3[...], dp[...]).astype(LOW)
        if inside:
            r.box[0, :, :, :, 16:32] = got[:, :width].reshape(*r.box.shape[1:4], 16, width)
            r.box[0, :, :, :, 32:48] = got[:, width:].reshape(*r.box.shape[1:4], 16, width)
        else:
            r.d_conv_in[...] = got

        @pl.loop(0, rows // 256)
        def _(i):
            at = rows_of(i, 256)
            dh[at] = nt(dp[at], r.conv_in[...])

        def put_first(at, got):
            r.grad[at] = got
            datt[at] = got.astype(LOW)

        norm_rows_back(dh, r.x2, r.grad, put_first, vec, sums, 4)
        tick(2)
        got = nn(r.oT[...], datt[...]).astype(LOW)
        if inside:
            r.box[0, :, :, :, 48:64] = got.reshape(*r.box.shape[1:4], 16, width)
            rest.start()
        else:
            r.d_att[...] = got
        r.doT[...] = nt(r.w_att[...], datt[...]).astype(LOW).reshape(heads, size, rows)

    pl.run_scoped(
        convolution_back, vm(r.pad.shape, F32), vm((rows, 2 * width), F32), vm(square, LOW),
    )

    def attend_back(delta, qside, oside, lows, grads, dk, dv):
        dqT = r.d_conv_out if inside else r.spare

        for head in range(heads):
            o = r.oT[head * size : (head + 1) * size].astype(F32)
            delta[head : head + 1] = jnp.sum(o * r.doT[head].astype(F32), 0, keepdims=True)

        def hook(pair):
            if inside:
                @pl.when(pair == 1)
                def _():
                    for d in range(deep - 1, -1, -1):
                        rest.step_one(d)
                    tick(2)

                @pl.when(pair == 2)
                def _():
                    put_off([rest], 2, [functools.partial(end_box, 0, rest)])
                    tick(1)
                    rests = queue[1:]
                    tick_rest = [rests.pop(0), rests.pop(0)]
                    queue[1:] = rests
                    for thunk in tick_rest:
                        thunk()

                @pl.when(pair == 3)
                def _():
                    tick(1)
                    tick(4)

        attention_backward(
            r.qT, r.key, r.h_all, r.qkvT, r.extra, r.doT, delta, r.top, dqT, dk, dv, qside, oside, lows, grads,
            scale, shrink, hook,
        )
        swaps = [
            to_core(dk.at[:, theirs], r.rk, r.swap.at[8], r.swap.at[9], 1 - core),
            to_core(dv.at[:, theirs], r.rv, r.swap.at[10], r.swap.at[11], 1 - core),
        ]
        for swap in swaps:
            swap.start()
        r.dq[...] = dqT[...].astype(F32).T.astype(LOW)
        for swap in swaps:
            swap.wait()
        for pair in range(pairs):
            lanes = slice(pair * 128, (pair + 1) * 128)
            r.h3[:, lanes] = (dk[pair, own].astype(F32) + r.rk[pair].astype(F32)).astype(LOW)
            r.own_v[:, lanes] = (dv[pair, own].astype(F32) + r.rv[pair].astype(F32)).astype(LOW)

    pl.run_scoped(
        attend_back, vm((heads, rows), F32), vm((2, 256, rows), LOW), vm((2, 256, rows), LOW),
        vm((keys // 2, 2 * rows), LOW), vm((keys // 2, 2 * rows), LOW),
        vm((pairs, keys, 128), LOW), vm((pairs, keys, 128), LOW),
    )
    if inside:
        tick(len(queue))
        third.plane_one(0)

    def put_qkv(s, got):
        if inside:
            for c in range(2):
                v = got[:, c * half : (c + 1) * half].reshape(count, 2, 16, half)
                r.box[1, c * deep : (c + 1) * deep, :, :, s * 16 : (s + 1) * 16] = jnp.concatenate(
                    [v[:, 0], v[:, 1]], axis=-1
                ).reshape(deep, 2, 2, 16, width)
        else:
            r.d_qkv[s] = got

    def project_back(dh, dy, da, x0):
        own_k, own_v = r.h3, r.own_v
        h2 = r.h_all[own]
        put_qkv(0, tn(h2, r.dq[...]).astype(LOW))
        put_qkv(1, tn(h2, own_k[...]).astype(LOW))
        put_qkv(2, tn(h2, own_v[...]).astype(LOW))
        if inside:
            r.small[taps : taps + 16] = sums[...]
            blank = jnp.zeros((16, width), LOW)
            for n in range(4):
                full = n < (taps + 16) // 16
                r.box[1, 0, n // 2, n % 2, 48:64] = r.small[n * 16 : (n + 1) * 16].astype(LOW) if full else blank
            r.box[1, 1:, :, :, 48:64] = jnp.zeros((2 * deep - 1, 2, 2, 16, width), LOW)
            proj.start()
        @pl.loop(0, rows // 256)
        def _(i):
            at = rows_of(i, 256)
            dh[at] = nn(r.dq[at], r.qkvT[0]) + nn(own_k[at], r.qkvT[1]) + nn(own_v[at], r.qkvT[2])

        def put_second(at, got):
            r.grad[at] = got
            dy[at] = (0.5 * got).astype(LOW)

        norm_rows_back(dh, r.x1, r.grad, put_second, vec, sums, 2)
        if inside:
            third.plane_two(0)
            ffn1.sent(0)
        for copy in back_copies:
            copy.wait()

        def hooks(n):
            if n == 3:
                put_off([proj, ffn0], 2, [functools.partial(end_box, 1, proj), functools.partial(end_ffn, 0, ffn0)])
                for d in (1, 2, 3):
                    third.plane_one(d)
                tick(1)
            if n == 5:
                tick(1)
            if n == 7:
                tick(2)
                third.plane_two(1)
                third.plane_two(2)

        if inside:
            for d in range(deep - 1, -1, -1):
                proj.step_one(d)
        by_planes(lambda i: weight_grads(r.h0, dy, hidden_grad(g1, dy, da, i), i), ffn0 if inside else None, hooks)
        tick(1)
        if inside:
            third.plane_two(3)
        masked_input(scal, r.x_in, x0)

        @pl.loop(0, rows // 256)
        def _(i):
            at = rows_of(i, 256)
            dh[at] = tn(da[:, at], whole_of(g1, 0))

        tick(2)
        if inside:
            for d in range(deep):
                third.plane_last(d)

        def put_input(at, got):
            r.input_grad[at] = got * keep_rows(scal, at.start, block, width)

        norm_rows_back(dh, x0, r.grad, put_input, vec, sums, 0)

    def tail(dh, dy, da, x0):
        project_back(dh, dy, da, x0)
        if not inside:
            return
        while len(queue) > 7:
            tick(1)
        fourth.plane_one(0)
        r.part_c[...] = to_tile(sums[0:4])
        every = Everyone(count, r.pair_c, r.slots_c, r.pair_sems_c, r.sends_c, r.recvs_c)
        every.start(r.part_c)
        tick(2)
        fourth.plane_two(0)
        tick(2)
        for d in (1, 2, 3):
            fourth.plane_one(d)
        for d in range(deep):
            third.plane_other(d)
        got = r.held[0]
        r.d_conv_out[...] = got[:, :, :, 0:16].reshape(width, width)
        r.d_conv_in[:, :width] = got[:, :, :, 16:32].reshape(width, width)
        r.d_conv_in[:, width:] = got[:, :, :, 32:48].reshape(width, width)
        r.d_att[...] = got[:, :, :, 48:64].reshape(width, width)
        tick(2)
        for d in (1, 2, 3):
            fourth.plane_two(d)
        tick(1)
        for d in range(deep):
            fourth.plane_last(d)
        tile = every.total()
        for d in range(deep):
            fourth.plane_other(d)
        got = r.held[1, pl.ds(core * deep, deep)].reshape(count, 64, width)
        for s in range(3):
            v = got[:, s * 16 : (s + 1) * 16]
            v = jnp.concatenate([v[:, None, :, :half], v[:, None, :, half:]], axis=1)
            r.d_qkv[s] = v.reshape(width, half)
        got = r.held[1, 0, :, :, 48:64].reshape(64, width).astype(F32)
        r.d_kern[...] = got[:taps]
        r.d_vec[...] = jnp.concatenate(
            [
                *[from_tile(tile, n, width) for n in range(4)], got[taps + 4 : taps + 6],
                spread * grad_moment, grad_sum, got[taps + 8 : taps + 12],
            ],
            axis=0,
        )
        third.finish()
        fourth.finish()
        for piece in stages:
            for kind in range(4):
                if kind or piece is not ffn1:
                    piece.sent(kind)

    pl.run_scoped(
        tail, vm(square, F32), vm(square, LOW), vm((hidden, rows), LOW),
        vm(square, F32),
    )
    if not inside:
        r.small[taps : taps + 16] = sums[...]
        r.small[taps + 6 : taps + 7] = spread * grad_moment
        r.small[taps + 7 : taps + 8] = grad_sum
        copy = pltpu.make_async_copy(g0, r.d_ffn.at[0], r.local.at[3])
        copy.start()
        copy.wait()


def gather_steps(route, chunk, held, sends, recv, with_core=True):
    started = []
    core, count = route.core, route.count

    def block(place):
        return core * count + place

    def arrive(place):
        here = held.at[chunk, block(place)]
        to_batch(here, here, recv.at[chunk, block(place)], recv.at[chunk, block(place)], route.me).wait_recv()

    def send(place, target):
        slot = len(started)
        here = held.at[chunk, block(place)]
        copy = to_batch(here, here, sends.at[chunk, slot], recv.at[chunk, block(place)], target)
        copy.start()
        started.append(copy)

    def cross(place):
        if not with_core:
            return
        slot = len(started)
        here = held.at[chunk, block(place)]
        copy = to_core(here, here, sends.at[chunk, slot], recv.at[chunk, block(place)], 1 - core)
        copy.start()
        started.append(copy)

    def step_mid():
        for k in range(1, route.deep):
            send(route.me, route.index(lax.rem(route.z + k, route.deep), route.p, route.q))
        cross(route.me)

    def step_one():
        for d in range(route.deep):
            z = lax.rem(route.z + d, route.deep)
            place = route.index(z, route.p, route.q)
            if d:
                arrive(place)
            for k in range(1, route.side):
                send(place, route.index(route.z, lax.rem(route.p + k, route.side), route.q))
            if d:
                cross(place)

    def step_two():
        for d in range(route.deep):
            z = lax.rem(route.z + d, route.deep)
            for e in range(route.side):
                p = lax.rem(route.p + e, route.side)
                place = route.index(z, p, route.q)
                if e:
                    arrive(place)
                for k in range(1, route.side):
                    send(place, route.index(route.z, route.p, lax.rem(route.q + k, route.side)))
                if e:
                    cross(place)

    def step_last():
        for d in range(route.deep):
            z = lax.rem(route.z + d, route.deep)
            for e in range(route.side):
                p = lax.rem(route.p + e, route.side)
                for f in range(1, route.side):
                    place = route.index(z, p, lax.rem(route.q + f, route.side))
                    arrive(place)
                    cross(place)

    def step_end():
        if with_core:
            for place in range(count):
                other = held.at[chunk, (1 - core) * count + place]
                at = recv.at[chunk, (1 - core) * count + place]
                to_core(other, other, at, at, 1 - core).wait_recv()
        for copy in started:
            copy.wait_send()

    return [step_mid, step_one, step_two, step_last, step_end]


def sends_of(route):
    return (route.deep - 1) + route.deep * (route.side - 1) * (1 + route.side) + route.count


def run_steps(all_steps):
    depth = len(all_steps[0])
    for turn in range(depth + len(all_steps) - 1):
        for chunk, steps in enumerate(all_steps):
            if 0 <= turn - chunk < depth:
                steps[turn - chunk]()


def gather_kernel(count, mine, held, local, sends, recv):
    route = Routes(count).here()
    chunks = mine.shape[0]
    copies = []
    for chunk in range(chunks):
        own = held.at[chunk, route.core * count + route.me]
        copy = pltpu.make_async_copy(mine.at[chunk], own, local.at[chunk])
        copy.start()
        copies.append(copy)
    route.greet()
    for copy in copies:
        copy.wait()
    run_steps([gather_steps(route, chunk, held, sends, recv) for chunk in range(chunks)])


def gather_all(mine, count, collective_id):
    chunks, rows, width = mine.shape
    route = Routes(count)
    return pl.pallas_call(
        functools.partial(gather_kernel, count),
        out_shape=jax.ShapeDtypeStruct((chunks, 2 * count, rows, width), mine.dtype),
        in_specs=[pl.BlockSpec(memory_space=pltpu.VMEM)],
        out_specs=pl.BlockSpec(memory_space=pltpu.VMEM),
        scratch_shapes=[
            pltpu.SemaphoreType.DMA((chunks,)),
            pltpu.SemaphoreType.DMA((chunks, sends_of(route))),
            pltpu.SemaphoreType.DMA((chunks, 2 * count)),
        ],
        compiler_params=pltpu.CompilerParams(
            collective_id=collective_id, has_side_effects=True, vmem_limit_bytes=VMEM_BYTES
        ),
    )(mine)


def reduce_kernel(count, solo, n, *refs):
    pieces, (fin, held, grads, packing, *rest) = refs[:n], refs[n:]
    copies = []
    at = 0
    for i, piece in enumerate(pieces):
        lines = piece.shape[1]
        copy = pltpu.make_async_copy(piece, grads.at[:, pl.ds(at, lines)], packing.at[i])
        copy.start()
        copies.append(copy)
        at += lines
    for copy in copies:
        copy.wait()
    reduce_packed(count, solo, grads, fin, held, *rest)


def reduce_packed(count, solo, grads, fin, held, zero, one, two, three, s0, r0, s1, r1, s2, r2, s3, r3, sends, recv):
    route = Routes(count).here()
    core, me, side, deep = route.core, route.me, route.side, route.deep
    rows, width = grads.shape[1:]
    piece = 16

    def add(target, source):
        @pl.loop(0, rows // piece)
        def _(i):
            at = pl.ds(pl.multiple_of(i * piece, piece), piece)
            target[at] = (target[at].astype(jnp.float32) + source[at].astype(jnp.float32)).astype(target.dtype)

    route.greet()
    waits = []
    order = []
    for f in range(side - 1, -1, -1):
        for d in range(deep):
            for e in range(side - 1, -1, -1):
                order.append((d, e, f))
    for d, e, f in order:
        place = route.index(lax.rem(route.z + d, deep), lax.rem(route.p + e, side), lax.rem(route.q + f, side))
        copy = to_core(grads.at[(1 - core) * count + place], zero.at[place], s0.at[place], r0.at[place], 1 - core)
        copy.start()
        waits.append(copy)
    for e in range(side - 1, -1, -1):
        for d in range(deep):
            for f in range(side - 1, -1, -1):
                z, p, q = lax.rem(route.z + d, deep), lax.rem(route.p + e, side), lax.rem(route.q + f, side)
                place = route.index(z, p, q)
                to_core(zero.at[place], zero.at[place], s0.at[place], r0.at[place], 1 - core).wait_recv()
                add(zero.at[place], grads.at[core * count + place])
                if e:
                    slot = (e - 1) * deep * side + z * side + q
                    copy = to_batch(
                        zero.at[place], one.at[slot], s1.at[slot], r1.at[slot], route.index(route.z, p, route.q)
                    )
                    copy.start()
                    waits.append(copy)
    for f in range(side - 1, -1, -1):
        for d in range(deep):
            z, q = lax.rem(route.z + d, deep), lax.rem(route.q + f, side)
            place = route.index(z, route.p, q)
            for e in range(1, side):
                slot = (e - 1) * deep * side + z * side + q
                to_batch(one.at[slot], one.at[slot], s1.at[slot], r1.at[slot], me).wait_recv()
                add(zero.at[place], one.at[slot])
            if f:
                slot = (f - 1) * deep + z
                copy = to_batch(
                    zero.at[place], two.at[slot], s2.at[slot], r2.at[slot], route.index(route.z, route.p, q)
                )
                copy.start()
                waits.append(copy)
    for d in range(deep - 1, -1, -1):
        z = lax.rem(route.z + d, deep)
        place = route.index(z, route.p, route.q)
        for f in range(1, side):
            slot = (f - 1) * deep + z
            to_batch(two.at[slot], two.at[slot], s2.at[slot], r2.at[slot], me).wait_recv()
            add(zero.at[place], two.at[slot])
        if d:
            copy = to_batch(zero.at[place], three.at[d - 1], s3.at[d - 1], r3.at[d - 1], place)
            copy.start()
            waits.append(copy)
    for d in range(1, deep):
        to_batch(three.at[d - 1], three.at[d - 1], s3.at[d - 1], r3.at[d - 1], me).wait_recv()

    def final(at):
        total = zero[me, at].astype(jnp.float32)
        for d in range(1, deep):
            total = total + three[d - 1, at].astype(jnp.float32)
        return total

    mine = core * count + me

    @pl.loop(0, (rows - solo) // piece)
    def _(i):
        at = pl.ds(pl.multiple_of(i * piece, piece), piece)
        held[0, mine, at] = final(pl.ds(pl.multiple_of(solo + i * piece, piece), piece)).astype(held.dtype)

    steps = gather_steps(route, 0, held, sends, recv)
    steps[0]()

    @pl.loop(0, solo // piece)
    def _(i):
        at = pl.ds(pl.multiple_of(i * piece, piece), piece)
        fin[at] = final(at)

    for step in steps[1:]:
        step()
    for copy in waits:
        copy.wait_send()


def reduce_all(pieces, solo, count, collective_id):
    blocks, _, width = pieces[0].shape
    kind = pieces[0].dtype
    if any(piece.shape[1] % 16 for piece in pieces):
        used = sum(piece.shape[1] for piece in pieces)
        spare = jnp.zeros((blocks, -used % 16, width), kind)
        pieces = [jnp.concatenate([*pieces, spare], axis=1)]
    rows = sum(piece.shape[1] for piece in pieces)
    route = Routes(count)
    side, deep = route.side, route.deep
    n1 = max(1, (side - 1) * side * deep)
    n2 = max(1, (side - 1) * deep)
    n3 = max(1, deep - 1)
    dma = pltpu.SemaphoreType.DMA
    return pl.pallas_call(
        functools.partial(reduce_kernel, count, solo, len(pieces)),
        out_shape=(
            jax.ShapeDtypeStruct((solo, width), jnp.float32),
            jax.ShapeDtypeStruct((1, blocks, rows - solo, width), kind),
        ),
        in_specs=[pl.BlockSpec(memory_space=pl.ANY)] * len(pieces),
        out_specs=(pl.BlockSpec(memory_space=pltpu.VMEM), pl.BlockSpec(memory_space=pltpu.VMEM)),
        scratch_shapes=[
            pltpu.VMEM((blocks, rows, width), kind),
            dma((len(pieces),)),
            pltpu.VMEM((count, rows, width), kind),
            pltpu.VMEM((n1, rows, width), kind),
            pltpu.VMEM((n2, rows, width), kind),
            pltpu.VMEM((n3, rows, width), kind),
            dma((count,)), dma((count,)),
            dma((n1,)), dma((n1,)),
            dma((n2,)), dma((n2,)),
            dma((n3,)), dma((n3,)),
            dma((1, sends_of(route))), dma((1, blocks)),
        ],
        compiler_params=pltpu.CompilerParams(
            collective_id=collective_id, has_side_effects=True, vmem_limit_bytes=VMEM_BYTES
        ),
    )(*pieces)


def last_kernel(count, *refs):
    for source, target in zip(refs[:count], refs[count:]):
        target[...] = source[...].astype(target.dtype)


def per_device(
    block_input, lengths, spans, cotangent, ffn_in, ffn_out, qkv_weight, out_weight, conv_in, kernel, conv_out, vectors,
):
    _, rows, width = block_input.shape
    count = lax.axis_size("batch")
    core = lax.axis_index("seq")
    shard = ffn_in.shape[1]
    blocks = 2 * count
    hidden = shard * blocks
    heads, size = HEADS, width // HEADS
    keys = 2 * rows
    taps = kernel.shape[0]
    inside = shard % 64 == 0 and width == 16 * blocks
    route = Routes(count)
    vm, dma = pltpu.VMEM, pltpu.SemaphoreType.DMA
    weights = (2, 8, 2, 2, hidden // 32, width)
    if inside:
        shards = dict(ffn_in=ffn_in, ffn_out=ffn_out)
    else:
        got = jnp.stack([ffn_in, ffn_out], axis=1).reshape(2, 2 * shard, width)
        got = gather_all(got, count, 1).reshape(2, blocks, 2, shard, width)
        shards = dict(shards=got.transpose(0, 2, 1, 3, 4).reshape(2, *weights))
    square, tall = (rows, width), (hidden, rows)
    here, hbm = pl.BlockSpec(memory_space=pltpu.VMEM), pl.BlockSpec(memory_space=pl.ANY)
    scalars = dict(lengths=lengths, spans=spans)
    early = dict(x_in=block_input[0], vec=vectors, kern=kernel)
    late = dict(cot=cotangent[0], w_att=out_weight, conv_in=conv_in, conv_out=conv_out, qkv=qkv_weight)
    ins = scalars | early | {f"{key}_far": value for key, value in late.items()} | shards
    in_specs = [pl.BlockSpec(memory_space=pltpu.SMEM)] * len(scalars) + [here] * len(early)
    in_specs += [hbm] * (len(late) + len(shards))
    outs = dict(
        out=(square, LOW, here), input_grad=(square, F32, here), far_g=(weights, LOW, hbm), far_act=(tall, LOW, hbm),
        far_slope=(tall, LOW, hbm), d_att=((width, width), LOW, here), d_conv_in=((width, 2 * width), LOW, here),
        d_conv_out=((width, width), LOW, here),
    )
    if inside:
        outs |= dict(
            fin_in=((2, shard, width), F32, here), fin_out=((2, shard, width), F32, here),
            d_qkv=((3, width, width // 2), LOW, here), d_kern=((taps, width), F32, here), d_vec=((12, width), F32, here),
        )
    else:
        outs |= dict(
            d_qkv=((3, width, width), LOW, here), small=((taps + 16, width), F32, here),
            d_ffn=((2, *weights), LOW, hbm),
        )
    scratch = dict(
        g0=vm(weights, LOW), g1=vm(weights, LOW), act=vm(tall, LOW), slope=vm(tall, LOW), qkvT=vm((3, width, width), LOW),
        x1=vm(square, F32), x2=vm(square, F32), grad=vm(square, F32), depth=vm(square, F32),
        dz=vm(square, F32), pad=vm((rows + 2 * HALO, width), F32), halo=vm((2, HALO, width), F32),
        h0=vm(square, LOW), h_all=vm((keys, width), LOW), h3=vm(square, LOW), key=vm((heads // 2, keys, 128), LOW),
        qT=vm((heads, size, rows), LOW), oT=vm((width, rows), LOW), doT=vm((heads, size, rows), LOW),
        top=vm((heads, rows), F32), extra=vm((keys, 128), LOW), wide=vm((taps, 8, width), F32), sums=vm((16, width), F32),
        own_v=vm(square, LOW),
        rk=vm((heads // 2, rows, 128), LOW), rv=vm((heads // 2, rows, 128), LOW), dq=vm(square, LOW),
        local=dma((14,)), swap=dma((12,)), qkv_mine=vm(qkv_weight.shape, LOW), cot=vm(square, LOW),
        w_att=vm((width, width), LOW), conv_in=vm((width, 2 * width), LOW), conv_out=vm((width, width), LOW),
    )
    for name, lines in (("a", 16), ("b", 8), ("c", 16))[: 3 if inside else 2]:
        scratch[f"part_{name}"] = vm((lines, 128), F32)
        for key, kind in zip(("pair", "slots", "pair_sems", "sends", "recvs"), Everyone.scratch(count, lines)):
            scratch[f"{key}_{name}"] = kind
    if not inside:
        scratch |= dict(spare=vm((width, rows), LOW), spare_wide=vm((rows, 2 * width), LOW))
    if inside:
        for key, shape in zip(("zero", "one", "two", "three"), ((4, 2, 2), (4, 2), (4,), (3,))):
            scratch[key] = vm((6, *shape, shard, width), LOW)
        scratch |= dict(
            box=vm((2, 8, 2, 2, 64, width), LOW), held=vm((2, 8, 2, 2, 64, width), LOW), small=vm((taps + 16, width), F32),
            g_send=dma((4, 11)), g_recv=dma((4, 4, 4)), r_send=dma((4, 4)), r_recv=dma((4, 4, 4)),
        )
    cfg = SimpleNamespace(
        names=[*ins, *outs, *scratch], count=count, shard=shard, hidden=hidden, heads=heads, inside=inside
    )
    results = pl.pallas_call(
        functools.partial(layer_kernel, cfg),
        out_shape=tuple(jax.ShapeDtypeStruct(shape, kind) for shape, kind, _ in outs.values()),
        in_specs=in_specs,
        out_specs=tuple(spec for _, _, spec in outs.values()),
        scratch_shapes=list(scratch.values()),
        compiler_params=pltpu.CompilerParams(collective_id=0, has_side_effects=True, vmem_limit_bytes=VMEM_BYTES),
    )(*ins.values())
    got = SimpleNamespace(**dict(zip(outs, results)))
    if inside:
        plain = [got.out, got.input_grad, got.fin_in, got.fin_out, got.d_kern, got.d_vec]
        wide = [got.d_qkv, got.d_att, got.d_conv_in, got.d_conv_out]
        shapes = [(v.shape, v.dtype) for v in plain] + [(v.shape, F32) for v in wide]
        steps = 4

        def part(shape):
            if shape[-2] % (8 * steps):
                return pl.BlockSpec(shape, lambda i: (0,) * len(shape))
            lines = shape[-2] // steps
            return pl.BlockSpec((*shape[:-2], lines, shape[-1]), lambda i: (0,) * (len(shape) - 2) + (i, 0))

        parts = [part(shape) for shape, _ in shapes]
        done = pl.pallas_call(
            functools.partial(last_kernel, len(shapes)),
            grid=(steps,),
            out_shape=tuple(jax.ShapeDtypeStruct(*shape) for shape in shapes),
            in_specs=parts,
            out_specs=tuple(parts),
            compiler_params=pltpu.CompilerParams(vmem_limit_bytes=VMEM_BYTES),
        )(*plain, *wide)
        out, input_grad, fin_in, fin_out, d_kern, d_vec, d_qkv, d_att, d_conv_in, d_conv_out = done
        return (
            out[None], input_grad[None], fin_in, fin_out, d_qkv, d_att, d_conv_in, d_kern, d_conv_out, d_vec,
        )

    def spread(values):
        flat = values.astype(LOW).reshape(-1, width)
        lines = -(-flat.shape[0] // blocks)
        flat = jnp.pad(flat, ((0, lines * blocks - flat.shape[0]), (0, 0)))
        return flat.reshape(blocks, lines, width)

    lines = 3 * width // (2 * count)
    per_core = got.d_qkv.reshape(3 * width, 2, width // 2).transpose(1, 0, 2).reshape(blocks, -1, width)
    d_in0, d_out0, d_in1, d_out1 = (got.d_ffn[j, m].reshape(hidden, width) for j in range(2) for m in range(2))
    rest = (got.d_att, got.d_conv_in, got.d_conv_out, got.small)
    pieces = [spread(v) for v in (d_in0, d_out0, d_in1, d_out1, *rest)] + [per_core]
    fin, shared = reduce_all(pieces, 4 * shard, count, 2)
    at = 0
    whole = []
    for piece, like in zip(pieces[4:8], rest):
        part = shared[0, :, at : at + piece.shape[1]].reshape(-1, width)
        whole.append(part[: like.size // width].reshape(like.shape).astype(F32))
        at += piece.shape[1]
    mine = lax.dynamic_slice_in_dim(shared[0], core * count, count, axis=0)[:, at : at + per_core.shape[1]]
    row = lax.broadcasted_iota(jnp.int32, (12, 1), 0)
    d_vec = jnp.where((row == 6) | (row == 7), got.small[taps : taps + 12], whole[3][taps : taps + 12])
    return (
        got.out[None], got.input_grad[None], jnp.stack([fin[:shard], fin[2 * shard : 3 * shard]]),
        jnp.stack([fin[shard : 2 * shard], fin[3 * shard :]]),
        mine.reshape(3, width, width // 2).astype(F32), whole[0], whole[1], whole[3][:taps], whole[2], d_vec,
    )


def solution(mesh):
    placed = (
        P("batch", "seq", None),
        P("batch"),
        P("batch", None),
        P("batch", "seq", None),
        P(None, ("seq", "batch"), None),
        P(None, ("seq", "batch"), None),
        P(None, None, "seq"),
        P(),
        P(),
        P(),
        P(),
        P(),
    )
    return jax.shard_map(
        per_device,
        mesh=mesh,
        in_specs=placed,
        out_specs=(
            P("batch", "seq", None),
            P("batch", "seq", None),
            P(None, ("seq", "batch"), None),
            P(None, ("seq", "batch"), None),
            P(None, None, "seq"),
            P(),
            P(),
            P(),
            P(),
            P(),
        ),
        check_vma=False,
    )
```

```python
import functools
import math
from types import SimpleNamespace

import jax
import jax.numpy as jnp
from jax import lax
from jax.experimental import pallas as pl
from jax.experimental.pallas import tpu as pltpu
from jax.sharding import PartitionSpec as P

HEADS = 8
MESH = pl.DeviceIdType.MESH
VMEM_BYTES = 63 * 1024 * 1024
F32, LOW = jnp.float32, jnp.bfloat16
EPS = 1e-05
HALO = 16


class Routes:
    def __init__(self, count):
        if count == 16:
            first, last, middle = (1, 2), (2, 2), (4, 4)
        elif count == 128:
            first, last, middle = (1, 4), (32, 4), (4, 8)
        else:
            first, last, middle = (1, 1), (1, 1), (1, count)
        self.count = count
        self.side = first[1]
        self.deep = middle[1]
        self.first, self.last, self.middle = first, last, middle

    def here(self):
        self.core = lax.axis_index("seq")
        self.me = lax.axis_index("batch")
        turn = self.core * (self.last[0] - self.first[0])
        self.one = self.first[0] + turn
        self.two = self.last[0] - turn
        self.mid = self.middle[0]
        self.p = lax.rem(lax.div(self.me, self.one), self.side)
        self.q = lax.rem(lax.div(self.me, self.two), self.side)
        self.z = lax.rem(lax.div(self.me, self.mid), self.deep)
        return self

    def index(self, z, p, q):
        return z * self.mid + p * self.one + q * self.two

    def plane(self, d):
        if self.deep != 4 or d == 0:
            return lax.rem(self.z + d, self.deep) if d else self.z
        return (self.z + 1 - 2 * lax.rem(self.z, 2), lax.rem(self.z + 2, 4), 3 - self.z)[d - 1]

    def reach(self, i):
        far = lax.div(self.z, 2)
        first = self.z + far * (3 - 2 * self.z)
        turn = (first, 1 - first, 2, 3)[i]
        return turn + far * (3 - 2 * turn)

    def near(self, d, e, f):
        p = lax.rem(self.p + e, self.side) if e else self.p
        q = lax.rem(self.q + f, self.side) if f else self.q
        return self.index(self.plane(d), p, q)

    def peers(self):
        found = []
        for k in range(1, self.deep):
            found.append(self.index(lax.rem(self.z + k, self.deep), self.p, self.q))
        for k in range(1, self.side):
            found.append(self.index(self.z, lax.rem(self.p + k, self.side), self.q))
            found.append(self.index(self.z, self.p, lax.rem(self.q + k, self.side)))
        return found

    def greet(self):
        barrier = pltpu.get_barrier_semaphore()
        places = self.peers()
        for place in places:
            pl.semaphore_signal(
                barrier, inc=1, device_id={"batch": place}, device_id_type=MESH
            )
        pl.semaphore_signal(
            barrier, inc=1, device_id={"seq": 1 - self.core}, device_id_type=MESH
        )
        pl.semaphore_wait(barrier, len(places) + 1)


def to_batch(src, dst, send, recv, place):
    return pltpu.make_async_remote_copy(
        src_ref=src, dst_ref=dst, send_sem=send, recv_sem=recv,
        device_id={"batch": place}, device_id_type=MESH,
    )


def to_core(src, dst, send, recv, core):
    return pltpu.make_async_remote_copy(
        src_ref=src, dst_ref=dst, send_sem=send, recv_sem=recv,
        device_id={"seq": core}, device_id_type=MESH,
    )


class Gather:
    def __init__(self, route, at, sends, recv, line):
        self.route, self.at, self.sends, self.recv, self.line = route, at, sends, recv, line

    def go(self, here, kind, z, send, place):
        if place is None:
            to_core(here, here, self.sends.at[send], self.recv.at[kind, z], 1 - self.route.core).start()
        else:
            to_batch(here, here, self.sends.at[send], self.recv.at[kind, z], place).start()

    def come(self, here, kind, z):
        to_core(here, here, self.recv.at[kind, z], self.recv.at[kind, z], 1 - self.route.core).wait_recv()

    def z_of(self, i):
        return self.route.reach(i) if self.line else self.route.plane(i)

    def plane_one(self, i):
        route = self.route
        z = self.z_of(i)
        here = self.at(route.core * route.deep + z, route.q, route.p)
        if i:
            self.come(here, 0, z)
        if self.line:
            @pl.when((z <= route.z) & (route.z < route.deep - 1))
            def _():
                self.go(here, 0, z, 3 + z, route.index(route.z + 1, route.p, route.q))

            @pl.when((z >= route.z) & (route.z > 0))
            def _():
                self.go(here, 0, z, 7 + z, route.index(route.z - 1, route.p, route.q))
        elif i == 0:
            for d in range(1, route.deep):
                self.go(here, 0, z, 2 + d, route.near(d, 0, 0))
        self.go(here, 1, z, 0, route.near(0, 1, 0))
        self.go(here, 2, z, 1, route.near(0, 0, 1))

    def plane_two(self, i):
        route = self.route
        z = self.z_of(i)
        cz = route.core * route.deep + z
        here = self.at(cz, route.q, 1 - route.p)
        self.come(here, 1, z)
        self.go(here, 2, z, 1, route.near(0, 0, 1))

    def plane_last(self, i):
        route = self.route
        z = self.z_of(i)
        cz = route.core * route.deep + z
        self.come(self.at(cz, route.q), 2, z)
        self.go(self.at(cz), 3, z, 2, None)

    def plane_other(self, i):
        route = self.route
        z = self.z_of(i)
        self.come(self.at((1 - route.core) * route.deep + z), 3, z)

    def finish(self):
        route = self.route

        def sent(here, send):
            to_core(here, here, self.sends.at[send], self.sends.at[send], 1 - route.core).wait_send()

        sent(self.at(0), 0)
        sent(self.at(pl.ds(0, 2)), 1)
        sent(self.at(pl.ds(0, 4)), 2)
        one = self.at(0, 0, 0)
        if not self.line:
            for d in range(1, route.deep):
                sent(one, 2 + d)
            return
        for z in range(route.deep):
            pl.when((z <= route.z) & (route.z < route.deep - 1))(functools.partial(sent, one, 3 + z))
            pl.when((z >= route.z) & (route.z > 0))(functools.partial(sent, one, 7 + z))


class Reduce:
    def __init__(self, route, source, stage, sends, recv):
        self.route, self.source, self.sends, self.recv = route, source, sends, recv
        self.zero, self.one, self.two, self.three = stage
        self.lead = self.zero.shape[0]

    def come(self, here, kind, n):
        to_core(here, here, self.recv.at[kind, n], self.recv.at[kind, n], 1 - self.route.core).wait_recv()

    def add(self, at, value):
        self.zero[at] = (self.zero[at].astype(F32) + value.astype(F32)).astype(LOW)

    def leave(self, d):
        route = self.route
        z = route.plane(d)
        to_core(
            self.source((1 - route.core) * route.deep + z), self.zero.at[:, z], self.sends.at[0],
            self.recv.at[0, z], 1 - route.core,
        ).start()

    def start(self):
        for d in range(self.route.deep - 1, -1, -1):
            self.leave(d)

    def step_one(self, d):
        route = self.route
        z = route.plane(d)
        self.come(self.zero.at[:, z], 0, z)
        mine = self.source(route.core * route.deep + z)
        for n in range(self.lead):
            for q in range(2):
                for p in range(2):
                    self.add((n, z, q, p), mine[n, q, p])
        to_batch(
            self.zero.at[:, z, :, 1 - route.p], self.one.at[:, d], self.sends.at[1], self.recv.at[1, d],
            route.near(0, 1, 0),
        ).start()

    def step_two(self, d):
        route = self.route
        z = route.plane(d)
        self.come(self.one.at[:, d], 1, d)
        for n in range(self.lead):
            for q in range(2):
                self.add((n, z, q, route.p), self.one[n, d, q])
        to_batch(
            self.zero.at[:, z, 1 - route.q, route.p], self.two.at[:, d], self.sends.at[2], self.recv.at[2, d],
            route.near(0, 0, 1),
        ).start()

    def step_three(self, d):
        route = self.route
        z = route.plane(d)
        self.come(self.two.at[:, d], 2, d)
        for n in range(self.lead):
            self.add((n, z, route.q, route.p), self.two[n, d])
        if d:
            to_batch(
                self.zero.at[:, z, route.q, route.p], self.three.at[:, d - 1], self.sends.at[3],
                self.recv.at[3, d - 1], route.near(d, 0, 0),
            ).start()

    def total(self):
        route = self.route
        for d in range(1, route.deep):
            self.come(self.three.at[:, d - 1], 3, d - 1)
        sums = []
        for n in range(self.lead):
            out = self.zero[n, route.z, route.q, route.p].astype(F32)
            for d in range(1, route.deep):
                out = out + self.three[n, d - 1].astype(F32)
            sums.append(out)
        return sums

    def sent(self, kind):
        here = (self.zero, self.one, self.two, self.three)[kind]
        to_core(here, here, self.sends.at[kind], self.sends.at[kind], 1 - self.route.core).wait_send()


class Everyone:
    def __init__(self, count, pair, slots, pair_sems, sends, recvs):
        self.count, self.pair, self.slots = count, pair, slots
        self.pair_sems, self.sends, self.recvs = pair_sems, sends, recvs

    def start(self, x):
        core, me, count = lax.axis_index("seq"), lax.axis_index("batch"), self.count
        copy = to_core(x, self.pair, self.pair_sems.at[0], self.pair_sems.at[1], 1 - core)
        copy.start()
        copy.wait()
        self.slots[me] = x[...] + self.pair[...]
        for k in range(1, count):
            here = self.slots.at[me]
            to_batch(here, here, self.sends, self.recvs, lax.rem(me + k, count)).start()

    def total(self):
        others = self.slots.at[pl.ds(0, self.count - 1)]
        copy = to_batch(others, others, self.sends, self.recvs, lax.axis_index("batch"))
        copy.wait_recv()
        out = self.slots[0]
        for place in range(1, self.count):
            out = out + self.slots[place]
        copy.wait_send()
        return out

    @staticmethod
    def scratch(count, rows):
        return [
            pltpu.VMEM((rows, 128), F32),
            pltpu.VMEM((count, rows, 128), F32),
            pltpu.SemaphoreType.DMA((2,)),
            pltpu.SemaphoreType.DMA,
            pltpu.SemaphoreType.DMA,
        ]


def to_tile(rows):
    width = rows.shape[1]
    parts = [rows[i : i + 1, j : j + 128] for i in range(rows.shape[0]) for j in range(0, width, 128)]
    return jnp.concatenate(parts, axis=0)


def from_tile(tile, first, width):
    each = width // 128
    return jnp.concatenate([tile[first * each + j : first * each + j + 1] for j in range(each)], axis=1)


def nn(a, b):
    return lax.dot_general(a, b, (((1,), (0,)), ((), ())), preferred_element_type=F32)


def nt(a, b):
    return lax.dot_general(a, b, (((1,), (1,)), ((), ())), preferred_element_type=F32)


def tn(a, b):
    return lax.dot_general(a, b, (((0,), (0,)), ((), ())), preferred_element_type=F32)


def sigmoid(v):
    return 0.5 * jnp.tanh(0.5 * v) + 0.5


def rows_of(i, size):
    return pl.ds(pl.multiple_of(i * size, size), size)


def normed(v):
    centred = v - jnp.mean(v, -1, keepdims=True)
    scale = lax.rsqrt(jnp.mean(centred * centred, -1, keepdims=True) + EPS)
    return centred * scale, scale


def normed_back(grad, hat, scale):
    return scale * (
        grad - jnp.mean(grad, -1, keepdims=True) - hat * jnp.mean(grad * hat, -1, keepdims=True)
    )


def fold(values):
    return jnp.sum(values.reshape(values.shape[0] // 8, 8, values.shape[1]), 0)


def norm_rows(x_ref, put, vec, row, block=256):
    @pl.loop(0, x_ref.shape[0] // block)
    def _(i):
        at = rows_of(i, block)
        hat, _ = normed(x_ref[at])
        put(at, (hat * vec[row : row + 1] + vec[row + 1 : row + 2]).astype(LOW))


def norm_rows_back(grad_ref, x_ref, g_ref, put, vec, sums, row, block=256):
    width = x_ref.shape[1]

    def step(i, carry):
        gain, bias = carry
        at = rows_of(i, block)
        hat, scale = normed(x_ref[at])
        grad = grad_ref[at]
        put(at, g_ref[at] + normed_back(grad * vec[row : row + 1], hat, scale))
        return gain + fold(grad * hat), bias + fold(grad)

    zero = jnp.zeros((8, width), F32)
    gain, bias = lax.fori_loop(0, x_ref.shape[0] // block, step, (zero, zero))
    sums[row : row + 1] = jnp.sum(gain, 0, keepdims=True)
    sums[row + 1 : row + 2] = jnp.sum(bias, 0, keepdims=True)


def activate(a):
    s = sigmoid(a)
    u = a * s
    return u, s + u * (1.0 - s)


def valid_rows(scal, at_row, rows):
    frame = scal[0] + at_row + lax.broadcasted_iota(jnp.int32, (rows, 1), 0)
    return frame, jnp.where(frame < scal[1], 1.0, 0.0)


def keep_rows(scal, at_row, rows, width):
    frame, ok = valid_rows(scal, at_row, rows)
    cut = (frame >= scal[2]) & (frame < scal[2] + scal[3])
    channel = lax.broadcasted_iota(jnp.int32, (1, width), 1)
    lost = (channel >= scal[4]) & (channel < scal[4] + scal[5])
    return (ok * jnp.where(cut, 0.0, 1.0)) * jnp.where(lost, 0.0, 1.0)


def masked_input(scal, x_in, x_ref, block=256):
    @pl.loop(0, x_in.shape[0] // block)
    def _(i):
        at = rows_of(i, block)
        keep = keep_rows(scal, i * block, block, x_in.shape[1])
        x_ref[at] = x_in[at].astype(F32) * keep


def split3(v):
    high = v.astype(LOW).astype(F32)
    rest = v - high
    mid = rest.astype(LOW).astype(F32)
    return high, mid, rest - mid


def key_extra(length, rows):
    key = lax.broadcasted_iota(jnp.int32, (rows, 128), 0)
    lane = lax.broadcasted_iota(jnp.int32, (rows, 128), 1)
    lost = jnp.where(key < length, 0.0, -1e30)
    return jnp.where(lane == 0, lost, jnp.where(lane < 4, 1.0, 0.0)).astype(LOW)


def fill_side(side, first, extra_rows):
    size = first[0].shape[0]
    blank = jnp.zeros((size, side.shape[2]), LOW)
    for half in range(2):
        side[half, half * size : (half + 1) * size] = first[half]
        side[half, (1 - half) * size : (2 - half) * size] = blank
        side[half, 2 * size :] = extra_rows[half]


def extra_of(lead, parts, wide):
    row = lax.broadcasted_iota(jnp.int32, (16, wide), 0)
    out = jnp.where(row == 0, lead, 0.0)
    if parts is not None:
        for n, part in enumerate(parts):
            out = jnp.where(row == n + 1, -part, out)
    return jnp.concatenate([out.astype(LOW), jnp.zeros((112, wide), LOW)], axis=0)


def attention_forward(qT, key, vT, extra, oT, top, side, scale, hook):
    heads, size, queries = qT.shape
    keys = key.shape[1]
    ones = jnp.ones((16, keys), LOW)

    @pl.loop(0, heads // 2)
    def _(pair):
        hook(pair)
        lead = extra_of(1.0, None, queries)
        fill_side(side, [qT[2 * pair], qT[2 * pair + 1]], [lead, lead])
        left = jnp.concatenate([key[pair], extra[...]], axis=1)
        for half in range(2):
            head = 2 * pair + half
            s = nn(left, side[half])
            m = jnp.max(s, 0, keepdims=True)
            p = jnp.exp2((s - m) * scale).astype(LOW)
            o = nn(jnp.concatenate([vT[head], ones], axis=0), p)
            total = o[size : size + 1]
            oT[rows_of(head, size)] = (o[:size] * (1.0 / total)).astype(LOW)
            top[pl.ds(head, 1)] = m + jnp.log2(total) * (1.0 / scale)


def attention_backward(
    qT, key, h_all, qkvT, extra, doT, delta, top, dqT, dk, dv, qside, oside, lows, grads, scale, shrink, hook, done, chunk=512
):
    heads, size, queries = qT.shape
    keys = key.shape[1]

    @pl.loop(0, heads // 2)
    def _(pair):
        hook(pair)
        tops = [split3(top[pl.ds(2 * pair + half, 1)]) for half in range(2)]
        deltas = [split3(delta[pl.ds(2 * pair + half, 1)]) for half in range(2)]
        fill_side(qside, [qT[2 * pair], qT[2 * pair + 1]], [extra_of(1.0, t, queries) for t in tops])
        fill_side(oside, [doT[2 * pair], doT[2 * pair + 1]], [extra_of(0.0, t, queries) for t in deltas])
        kT = nt(qkvT[1, rows_of(pair, 128)], h_all[...]).astype(LOW)
        wide_o = jnp.concatenate([oside[0, :128], oside[1, :128]], axis=1)
        wide_q = jnp.concatenate([qside[0, :128], qside[1, :128]], axis=1)
        totals = [None, None]
        for c in range(keys // chunk):
            at = slice(c * chunk, (c + 1) * chunk)
            value = nt(h_all[at], qkvT[2, rows_of(pair, 128)]).astype(LOW)
            left_k = jnp.concatenate([key[pair, at], extra[at]], axis=1)
            left_v = jnp.concatenate([value, extra[at]], axis=1)
            for half in range(2):
                lanes = slice(half * queries, (half + 1) * queries)
                p = jnp.exp2(nn(left_k, qside[half]) * scale)
                lows[:, lanes] = p.astype(LOW)
                grads[:, lanes] = (p * nn(left_v, oside[half])).astype(LOW)
            for half in range(2):
                lanes = slice(half * queries, (half + 1) * queries)
                got = nn(kT[half * size : (half + 1) * size, at], grads[:, lanes])
                totals[half] = got if c == 0 else totals[half] + got
            dv[pair, at] = nt(lows[...], wide_o).astype(LOW)
            dk[pair, at] = (nt(grads[...], wide_q) * shrink).astype(LOW)
        for half in range(2):
            dqT[rows_of(2 * pair + half, size)] = (totals[half] * shrink).astype(LOW)
        done(pair)


def windows(pad_ref, at_row, block, lanes, shifts):
    for s in range(8):
        mine = [(tap, shift) for tap, shift in shifts if shift % 8 == s]
        low = min(shift for _, shift in mine)
        high = max(shift for _, shift in mine)
        window = pad_ref[at_row + low : at_row + high + block, lanes]
        for tap, shift in mine:
            yield tap, window[shift - low : shift - low + block]


def convolve(pad_ref, taps_wide, put, shift_of, rows, width, hook=None, block=64):
    count = taps_wide.shape[0]
    shifts = [(tap, shift_of(tap)) for tap in range(count)]
    for lane in range(0, width, 128):
        lanes = slice(lane, lane + 128)
        for at_row in range(0, rows, block):
            total = jnp.zeros((block // 8, 8, 128), F32)
            for tap, values in windows(pad_ref, at_row, block, lanes, shifts):
                total = total + taps_wide[tap, :, lanes][None] * values.reshape(block // 8, 8, 128)
            put(at_row, block, lane, total.reshape(block, 128))
        if hook:
            hook(1)


def convolve_weight(pad_ref, grad_ref, first, out_ref, shift_of, rows, width, hook, block=64):
    taps = out_ref.shape[0]
    for lane in range(0, width, 128):
        lanes = slice(lane, lane + 128)
        for s in range(8):
            mine = [(tap, shift_of(tap)) for tap in range(taps) if shift_of(tap) % 8 == s]
            low = min(shift for _, shift in mine)
            high = max(shift for _, shift in mine)
            sums = {tap: jnp.zeros((8, 128), F32) for tap, _ in mine}
            for at_row in range(0, rows, block):
                grad = grad_ref[first + at_row : first + at_row + block, lanes]
                window = pad_ref[at_row + low : at_row + high + block, lanes]
                for tap, shift in mine:
                    sums[tap] = sums[tap] + fold(grad * window[shift - low : shift - low + block])
            for tap, _ in mine:
                out_ref[tap : tap + 1, lanes] = jnp.sum(sums[tap], 0, keepdims=True)
        if hook:
            hook(1)


def place_halo(pad_ref, halo, core):
    rows = pad_ref.shape[0] - 2 * HALO
    got = halo[...]
    zero = jnp.zeros_like(got)
    pad_ref[0:HALO] = jnp.where(core == 1, got, zero)
    pad_ref[rows + HALO :] = jnp.where(core == 0, got, zero)


def layer_kernel(cfg, *refs):
    r = SimpleNamespace(**dict(zip(cfg.names, refs)))
    count, shard, hidden, inside = cfg.count, cfg.shard, cfg.hidden, cfg.inside
    rows, width = r.x_in.shape
    heads, size = cfg.heads, width // cfg.heads
    keys, pairs, taps = 2 * rows, heads // 2, r.kern.shape[0]
    scale, shrink = math.log2(math.e) / math.sqrt(size), 1.0 / math.sqrt(size)
    route = Routes(count).here()
    core, me = route.core, route.me
    vec, g0, g1, sums = r.vec, r.g0, r.g1, r.sums
    chunk, block = 256, 256
    own = pl.ds(pl.multiple_of(core * rows, rows), rows)
    theirs = pl.ds(pl.multiple_of((1 - core) * rows, rows), rows)
    zero8 = jnp.zeros((8, width), F32)

    def plane_of(g, m, i):
        return g[m, i].reshape(chunk, width)

    def whole_of(g, m):
        return g[m].reshape(hidden, width)

    barrier = pltpu.get_barrier_semaphore()
    for k in range(1, count):
        pl.semaphore_signal(
            barrier, inc=1, device_id={"batch": lax.rem(me + k, count)}, device_id_type=MESH
        )
    pl.semaphore_signal(barrier, inc=1, device_id={"seq": 1 - core}, device_id_type=MESH)
    half = width // 2
    q_own = pl.ds(pl.multiple_of(core * half, half), half)
    loads = []

    def load(source, target):
        copy = pltpu.make_async_copy(source, target, r.local.at[4 + len(loads)])
        copy.start()
        loads.append(copy)
        return copy

    if inside:
        cz = core * route.deep + route.z
        near_loads = [
            load(part.at[j], g.at[m, cz, route.q, route.p]) for m, part in enumerate((r.ffn_in, r.ffn_out)) for j, g in enumerate((g0, g1))
        ]
    else:
        near_loads = [load(r.shards.at[0], g0), load(r.shards.at[1], g1)]
    load_x, load_vec, load_kern = load(r.x_in_far, r.x_in), load(r.vec_far, r.vec), load(r.kern_far, r.kern)
    load_qkv = load(r.qkv_far, r.qkv_mine)
    load_att = load(r.w_att_far, r.w_att)
    load_conv_in = load(r.conv_in_far, r.conv_in)
    load_conv_out = load(r.conv_out_far, r.conv_out)
    load_cot = load(r.cot_far, r.cot)
    frame0, length, span = core * rows, r.lengths[0], [r.spans[0, n] for n in range(4)]
    scal = [frame0, length, *span]
    sums[...] = jnp.zeros_like(sums)
    for copy in near_loads:
        copy.wait()
    pl.semaphore_wait(barrier, count)

    def put_h0(at, value):
        r.h0[at] = value

    def begin():
        load_x.wait()
        load_vec.wait()
        masked_input(scal, r.x_in, r.x1)
        norm_rows(r.x1, put_h0, vec, 0)
        load_kern.wait()
        for tap in range(taps):
            r.wide[tap] = jnp.broadcast_to(r.kern[tap : tap + 1], (8, width))

    def inner(i):
        at = rows_of(i, chunk)
        u, slope = activate(nt(plane_of(g0, 0, i), r.h0[...]))
        r.act[at] = u.astype(LOW)
        r.slope[at] = slope.astype(LOW)

    swap_q = to_core(r.qkvT.at[:, q_own], r.qkvT.at[:, q_own], r.swap.at[0], r.swap.at[1], 1 - core)

    def turn_qkv():
        load_qkv.wait()
        for s in range(3):
            r.qkvT[s, q_own] = r.qkv_mine[s].astype(F32).T.astype(LOW)
        swap_q.start()

    if inside:
        first = Gather(route, lambda *i: g0.at[(slice(None), *i)], r.g_send.at[0], r.g_recv.at[0], True)
        second = Gather(route, lambda *i: g1.at[(slice(None), *i)], r.g_send.at[1], r.g_recv.at[1], True)
        deep = route.deep

        def inner_plane(which, d):
            inner(which * deep + route.reach(d))

        first.plane_one(0)
        begin()
        first.plane_one(1)
        turn_qkv()
        first.plane_one(2)
        first.plane_two(0)
        first.plane_one(3)
        for d in (1, 2, 3):
            first.plane_two(d)
        second.plane_one(0)
        for d in range(deep):
            first.plane_last(d)
            inner_plane(core, d)
            if d:
                first.plane_other(d - 1)
                inner_plane(1 - core, d - 1)
        first.plane_other(deep - 1)
        inner_plane(1 - core, deep - 1)
    else:
        begin()
        turn_qkv()

        @pl.loop(0, hidden // chunk)
        def _(i):
            inner(i)

    @pl.loop(0, rows // 256)
    def _(i):
        at = rows_of(i, 256)
        r.x1[at] = r.x1[at] + 0.5 * tn(r.act[:, at], whole_of(g0, 1))

    def put_h2(at, value):
        r.h_all[pl.ds(pl.multiple_of(core * rows + at.start, block), block)] = value

    norm_rows(r.x1, put_h2, vec, 2)
    swap = to_core(r.h_all.at[own], r.h_all.at[own], r.swap.at[2], r.swap.at[3], 1 - core)
    swap.start()
    away = [
        pltpu.make_async_copy(g0, r.far_g, r.local.at[0]),
        pltpu.make_async_copy(r.act, r.far_act, r.local.at[1]),
        pltpu.make_async_copy(r.slope, r.far_slope, r.local.at[2]),
    ]
    for copy in away:
        copy.start()
    swap_q.wait()

    def project(at, vT):
        here = r.h_all[at]
        for pair in range(pairs):
            r.key[pair, at] = nt(here, r.qkvT[1, pair * 128 : (pair + 1) * 128]).astype(LOW)
        vT[:, :, at] = nt(r.qkvT[2], here).astype(LOW).reshape(heads, size, rows)

    r.extra[...] = key_extra(scal[1], keys)

    def attend(vT, side_ref):
        r.qT[...] = nt(r.qkvT[0], r.h_all[own]).astype(LOW).reshape(heads, size, rows)
        project(own, vT)
        if inside:
            second.plane_one(1)
        swap.wait()
        project(theirs, vT)
        if inside:
            second.plane_one(2)
            second.plane_two(0)

        def hook(pair):
            if inside:
                @pl.when(pair == 1)
                def _():
                    second.plane_one(3)
                    second.plane_two(1)

                @pl.when(pair == 2)
                def _():
                    second.plane_two(2)
                    second.plane_last(0)

                @pl.when(pair == 3)
                def _():
                    second.plane_two(3)
                    second.plane_last(1)

        attention_forward(r.qT, r.key, vT, r.extra, r.oT, r.top, side_ref, scale, hook)

    pl.run_scoped(attend, pltpu.VMEM((heads, size, keys), LOW), pltpu.VMEM((2, 256, rows), LOW))

    load_att.wait()

    @pl.loop(0, rows // 256)
    def _(i):
        at = rows_of(i, 256)
        r.x2[at] = r.x1[at] + tn(r.oT[:, at], r.w_att[...])

    def put_h3(at, value):
        r.h3[at] = value

    norm_rows(r.x2, put_h3, vec, 4)
    load_conv_in.wait()

    @pl.loop(0, rows // 256)
    def _(i):
        at = rows_of(i, 256)
        _, ok = valid_rows(scal, i * 256, 256)
        here = r.h3[at]
        gate = sigmoid(nn(here, r.conv_in[:, width:]))
        r.pad[pl.ds(pl.multiple_of(i * 256 + HALO, HALO), 256)] = nn(here, r.conv_in[:, :width]) * gate * ok

    edge = pl.ds(pl.multiple_of(HALO + (1 - core) * (rows - HALO), HALO), HALO)
    swap = to_core(r.pad.at[edge], r.halo.at[0], r.swap.at[4], r.swap.at[5], 1 - core)
    swap.start()
    if inside:
        second.plane_last(2)
    swap.wait()
    place_halo(r.pad, r.halo.at[0], core)

    def put_depth(at_row, high, lane, total):
        r.depth[at_row : at_row + high, lane : lane + 128] = total

    spots = [lambda: None] * 4
    if inside:
        pass
    convolve(r.pad, r.wide, put_depth, lambda tap: tap + 1, rows, width, lambda _: spots.pop(0)())

    if inside:
        second.plane_last(3)

    def moments(i, carry):
        one, two = carry
        _, ok = valid_rows(scal, i * block, block)
        here = r.depth[rows_of(i, block)]
        held = here * ok
        return one + fold(held), two + fold(here * held)

    one, two = lax.fori_loop(0, rows // block, moments, (zero8, zero8))
    number = jnp.clip(scal[1] - scal[0], 0, rows).astype(F32)
    r.part_a[0:8] = to_tile(
        jnp.concatenate([jnp.sum(one, 0, keepdims=True), jnp.sum(two, 0, keepdims=True)], axis=0)
    )
    r.part_a[8:16] = jnp.full((8, 128), 1.0, F32) * number
    every = Everyone(count, r.pair_a, r.slots_a, r.pair_sems_a, r.sends_a, r.recvs_a)
    every.start(r.part_a)
    if inside:
        for d in range(deep):
            second.plane_other(d)
        second.finish()
        first.finish()
    for copy in [*away, load_conv_out, load_cot]:
        copy.wait()
    tile = every.total()
    number = tile[8:9, 0:1]
    mean = from_tile(tile, 0, width) / number
    var = from_tile(tile, 1, width) / number - mean * mean
    spread = lax.rsqrt(var + EPS)
    gain6 = vec[6:7]

    if inside:
        stages = [
            Reduce(route, source, [ref.at[part] for ref in (r.zero, r.one, r.two, r.three)], r.r_send.at[k], r.r_recv.at[k])
            for k, (part, source) in enumerate(
                [
                    (pl.ds(0, 2), lambda cz: g0.at[:, cz]),
                    (pl.ds(2, 1), lambda cz: r.box.at[pl.ds(0, 1), cz]),
                    (pl.ds(3, 1), lambda cz: r.box.at[pl.ds(1, 1), cz]),
                    (pl.ds(4, 1), lambda cz: g0.at[pl.ds(1, 1), cz]),
                    (pl.ds(5, 1), lambda cz: g0.at[pl.ds(0, 1), cz]),
                ]
            )
        ]
        ffn1, rest, proj, out0, in0 = stages
        queue = []

        def put_off(units, lag, ends):
            for t in range(len(units) + lag):
                if t < len(units):
                    piece, d = units[t]
                    queue.append(functools.partial(piece.step_two, d))
                if t >= lag:
                    piece, d = units[t - lag]
                    queue.append(functools.partial(piece.step_three, d))
                    if d == 0 and piece in ends:
                        queue.append(ends[piece])

        def planes_of(*pieces):
            return [(piece, d) for d in range(deep - 1, -1, -1) for piece in pieces]

        def tick(count):
            for _ in range(min(count, len(queue))):
                queue.pop(0)()

        own_at = (core * deep + route.z, route.q, route.p)

        def ticks(*counts):
            left = list(counts)
            return lambda _: tick(left.pop(0))

        def end_ffn1():
            r.fin_in[1], r.fin_out[1] = ffn1.total()

        def end_ffn0():
            (r.fin_out[0],) = out0.total()
            (r.fin_in[0],) = in0.total()

        def end_box(j, piece):
            r.held[(j, *own_at)] = piece.total()[0].astype(LOW)

        third = Gather(route, lambda *i: r.held.at[(0, *i)], r.g_send.at[2], r.g_recv.at[2], False)
        fourth = Gather(route, lambda *i: r.held.at[(1, *i)], r.g_send.at[3], r.g_recv.at[3], False)
    else:
        def tick(count):
            pass

        def ticks(*counts):
            return None
    back_copies = [
        pltpu.make_async_copy(r.far_act, r.act, r.local.at[0]),
        pltpu.make_async_copy(r.far_slope, r.slope, r.local.at[1]),
        pltpu.make_async_copy(r.far_g, g1, r.local.at[2]),
    ]

    def hidden_grad(weight, dy, da, i):
        at = rows_of(i, chunk)
        du = nt(plane_of(weight, 1, i), dy[...])
        low = (du * r.slope[at].astype(F32)).astype(LOW)
        da[at] = low
        return low

    def weight_grads(h_ref, dy, low, i):
        at = rows_of(i, chunk)
        g0[1, i] = nn(r.act[at], dy[...]).astype(LOW).reshape(g0.shape[2:])
        g0[0, i] = nn(low, h_ref[...]).astype(LOW).reshape(g0.shape[2:])

    def by_planes(grads, pieces, hooks):
        if not inside:
            pl.loop(0, hidden // chunk)(grads)
            return
        for n, d in enumerate(range(deep - 1, -1, -1)):
            grads((1 - core) * deep + route.plane(d))
            for piece in pieces:
                piece.leave(d)
            hooks(n)
        for n, d in enumerate(range(deep - 1, -1, -1)):
            grads(core * deep + route.plane(d))
            for piece in pieces:
                piece.step_one(d)
            hooks(deep + n)

    def middle(slope_z, da, dh):
        low, dy, h4 = r.d_conv_in.at[:, pl.ds(0, width)], r.d_conv_in.at[:, pl.ds(width, width)], r.d_att
        dc = r.d_conv_out if inside else r.spare
        x3, x4 = r.input_grad, r.dz

        @pl.loop(0, rows // block)
        def _(i):
            at = rows_of(i, block)
            z = (r.depth[at] - mean) * spread * gain6 + vec[7:8]
            u, slope = activate(z)
            low[at] = u.astype(LOW)
            slope_z[at] = slope

        @pl.loop(0, rows // 256)
        def _(i):
            at = rows_of(i, 256)
            x3[at] = r.x2[at] + nn(low[at], r.conv_out[...])

        def put_h4(at, value):
            h4[at] = value

        norm_rows(x3, put_h4, vec, 8)

        @pl.loop(0, hidden // chunk)
        def _(i):
            at = rows_of(i, chunk)
            u, slope = activate(nt(plane_of(g1, 0, i), h4[...]))
            r.act[at] = u.astype(LOW)
            r.slope[at] = slope.astype(LOW)

        @pl.loop(0, rows // 256)
        def _(i):
            at = rows_of(i, 256)
            x4[at] = x3[at] + 0.5 * tn(r.act[:, at], whole_of(g1, 1))

        def last(i, carry):
            gain, bias = carry
            at = rows_of(i, block)
            hat, rate = normed(x4[at])
            r.out[at] = (hat * vec[10:11] + vec[11:12]).astype(LOW)
            g = r.cot[at].astype(F32)
            back = normed_back(g * vec[10:11], hat, rate)
            r.grad[at] = back
            dy[at] = (0.5 * back).astype(LOW)
            return gain + fold(g * hat), bias + fold(g)

        gain, bias = lax.fori_loop(0, rows // block, last, (zero8, zero8))
        sums[10:11] = jnp.sum(gain, 0, keepdims=True)
        sums[11:12] = jnp.sum(bias, 0, keepdims=True)
        @pl.loop(0, hidden // chunk)
        def _(i):
            hidden_grad(g1, dy, da, i)

        @pl.loop(0, rows // 256)
        def _(i):
            at = rows_of(i, 256)
            dh[at] = tn(da[:, at], whole_of(g1, 0))

        back_copies[2].start()

        def put(at, value):
            r.grad[at] = value
            dc[at] = value.astype(LOW)

        norm_rows_back(dh, x3, r.grad, put, vec, sums, 8)

        @pl.loop(0, rows // 256)
        def _(i):
            at = rows_of(i, 256)
            r.dz[at] = nt(dc[at], r.conv_out[...])

        def close(i, carry):
            one, two = carry
            at = rows_of(i, block)
            here = r.dz[at] * slope_z[at]
            r.dz[at] = here
            return one + fold(here), two + fold(here * (r.depth[at] - mean))

        one, two = lax.fori_loop(0, rows // block, close, (zero8, zero8))
        r.part_b[...] = to_tile(
            jnp.concatenate([jnp.sum(one, 0, keepdims=True), jnp.sum(two, 0, keepdims=True)], axis=0)
        )
        every = Everyone(count, r.pair_b, r.slots_b, r.pair_sems_b, r.sends_b, r.recvs_b)
        every.start(r.part_b)
        got = tn(low[...], dc[...]).astype(LOW)
        if inside:
            r.box[0, :, :, :, 0:16] = got.reshape(*r.box.shape[1:4], 16, width)
        else:
            r.d_conv_out[...] = got
        by_planes(
            lambda i: weight_grads(h4, dy, da[rows_of(i, chunk)], i), [ffn1] if inside else None, lambda n: None
        )
        back_copies[0].start()
        back_copies[1].start()
        r.part_b[...] = every.total()

    square = (rows, width)
    vm = pltpu.VMEM
    pl.run_scoped(
        middle, vm(square, F32), vm((hidden, rows), LOW), vm(square, F32),
    )
    leaving = {
        name: pltpu.make_async_copy(getattr(r, name), getattr(r, "far_" + name), r.local.at[20 + n])
        for n, name in enumerate(("out", "input_grad", "d_conv_out", "d_conv_in", "d_att"))
    }
    leaving["out"].start()
    if not inside:
        copy = pltpu.make_async_copy(g0, r.d_ffn.at[1], r.local.at[3])
        copy.start()
        copy.wait()
    tile = r.part_b[...]
    grad_sum, grad_moment = from_tile(tile, 0, width), from_tile(tile, 1, width)
    if inside:
        put_off(planes_of(ffn1), 1, {ffn1: end_ffn1})
    var_grad = -0.5 * (gain6 * grad_moment) * spread * spread * spread
    flat = (-(gain6 * spread * grad_sum) - 2.0 * mean * var_grad) / number
    tilt = 2.0 * var_grad / number

    def convolution_back(back, datt):
        dp, dh = r.d_conv_in if inside else r.spare_wide, r.input_grad
        left, right = r.dz, r.depth

        @pl.loop(0, rows // block)
        def _(i):
            at = rows_of(i, block)
            _, ok = valid_rows(scal, i * block, block)
            back[pl.ds(pl.multiple_of(i * block + HALO, HALO), block)] = gain6 * spread * r.dz[at] + ok * (
                flat + r.depth[at] * tilt
            )

        swap = to_core(back.at[edge], r.halo.at[1], r.swap.at[6], r.swap.at[7], 1 - core)
        swap.start()
        convolve_weight(r.pad, back, HALO, r.small.at[pl.ds(0, taps)], lambda tap: tap + 1, rows, width, ticks(0, 0, 1, 0))

        @pl.loop(0, rows // 256)
        def _(i):
            at = rows_of(i, 256)
            left[at] = nn(r.h3[at], r.conv_in[:, :width])
            right[at] = nn(r.h3[at], r.conv_in[:, width:])

        swap.wait()
        place_halo(back, r.halo.at[1], core)

        def put(at_row, high, lane, total):
            at = slice(at_row, at_row + high)
            _, ok = valid_rows(scal, at_row, high)
            gate = sigmoid(right[at, lane : lane + 128])
            total = total * gate * ok
            dp[at, lane : lane + 128] = total.astype(LOW)
            dp[at, width + lane : width + lane + 128] = (
                total * left[at, lane : lane + 128] * (1.0 - gate)
            ).astype(LOW)

        convolve(back, r.wide, put, lambda tap: taps - 1 - tap, rows, width, ticks(0, 1, 1, 0))
        got = tn(r.h3[...], dp[...]).astype(LOW)
        if inside:
            r.box[0, :, :, :, 16:32] = got[:, :width].reshape(*r.box.shape[1:4], 16, width)
            r.box[0, :, :, :, 32:48] = got[:, width:].reshape(*r.box.shape[1:4], 16, width)
        else:
            r.d_conv_in[...] = got

        @pl.loop(0, rows // 256)
        def _(i):
            at = rows_of(i, 256)
            dh[at] = nt(dp[at], r.conv_in[...])

        def put_first(at, got):
            r.grad[at] = got
            datt[at] = got.astype(LOW)

        norm_rows_back(dh, r.x2, r.grad, put_first, vec, sums, 4)
        tick(2)
        got = nn(r.oT[...], datt[...]).astype(LOW)
        if inside:
            r.box[0, :, :, :, 48:64] = got.reshape(*r.box.shape[1:4], 16, width)
            rest.start()
        else:
            r.d_att[...] = got
        r.doT[...] = nt(r.w_att[...], datt[...]).astype(LOW).reshape(heads, size, rows)

    pl.run_scoped(
        convolution_back, vm(r.pad.shape, F32), vm(square, LOW),
    )

    def attend_back(delta, qside, oside, grads, dk, dv):
        lows = r.conv_in
        dqT = r.d_conv_out if inside else r.spare

        for head in range(heads):
            o = r.oT[head * size : (head + 1) * size].astype(F32)
            delta[head : head + 1] = jnp.sum(o * r.doT[head].astype(F32), 0, keepdims=True)

        def hook(pair):
            if inside:
                @pl.when(pair == 1)
                def _():
                    for d in range(deep - 1, -1, -1):
                        rest.step_one(d)
                    tick(2)

                @pl.when(pair == 2)
                def _():
                    put_off(planes_of(rest), 2, {rest: functools.partial(end_box, 0, rest)})
                    tick(1)
                    rests = queue[1:]
                    tick_rest = [rests.pop(0), rests.pop(0)]
                    queue[1:] = rests
                    for thunk in tick_rest:
                        thunk()

                @pl.when(pair == 3)
                def _():
                    tick(1)
                    tick(4)

        def done(pair):
            to_core(dk.at[pair, theirs], r.rk.at[pair], r.swap.at[8], r.swap.at[9], 1 - core).start()
            to_core(dv.at[pair, theirs], r.rv.at[pair], r.swap.at[10], r.swap.at[11], 1 - core).start()

        attention_backward(
            r.qT, r.key, r.h_all, r.qkvT, r.extra, r.doT, delta, r.top, dqT, dk, dv, qside, oside, lows, grads,
            scale, shrink, hook, done,
        )
        r.dq[...] = dqT[...].astype(F32).T.astype(LOW)
        to_core(dk.at[:, theirs], r.rk, r.swap.at[8], r.swap.at[9], 1 - core).wait()
        to_core(dv.at[:, theirs], r.rv, r.swap.at[10], r.swap.at[11], 1 - core).wait()
        for pair in range(pairs):
            lanes = slice(pair * 128, (pair + 1) * 128)
            r.h3[:, lanes] = (dk[pair, own].astype(F32) + r.rk[pair].astype(F32)).astype(LOW)
            r.own_v[:, lanes] = (dv[pair, own].astype(F32) + r.rv[pair].astype(F32)).astype(LOW)

    pl.run_scoped(
        attend_back, vm((heads, rows), F32), vm((2, 256, rows), LOW), vm((2, 256, rows), LOW),
        vm((keys // 2, 2 * rows), LOW),
        vm((pairs, keys, 128), LOW), vm((pairs, keys, 128), LOW),
    )
    if inside:
        tick(len(queue))
        third.plane_one(0)

    def put_qkv(s, got):
        if inside:
            for c in range(2):
                v = got[:, c * half : (c + 1) * half].reshape(count, 2, 16, half)
                r.box[1, c * deep : (c + 1) * deep, :, :, s * 16 : (s + 1) * 16] = jnp.concatenate(
                    [v[:, 0], v[:, 1]], axis=-1
                ).reshape(deep, 2, 2, 16, width)
        else:
            r.d_qkv[s] = got

    def project_back(dh, dy, da, x0):
        own_k, own_v = r.h3, r.own_v
        h2 = r.h_all[own]
        put_qkv(0, tn(h2, r.dq[...]).astype(LOW))
        put_qkv(1, tn(h2, own_k[...]).astype(LOW))
        put_qkv(2, tn(h2, own_v[...]).astype(LOW))
        if inside:
            r.small[taps : taps + 16] = sums[...]
            blank = jnp.zeros((16, width), LOW)
            for n in range(4):
                full = n < (taps + 16) // 16
                r.box[1, 0, n // 2, n % 2, 48:64] = r.small[n * 16 : (n + 1) * 16].astype(LOW) if full else blank
            r.box[1, 1:, :, :, 48:64] = jnp.zeros((2 * deep - 1, 2, 2, 16, width), LOW)
            proj.start()
        @pl.loop(0, rows // 256)
        def _(i):
            at = rows_of(i, 256)
            dh[at] = nn(r.dq[at], r.qkvT[0]) + nn(own_k[at], r.qkvT[1]) + nn(own_v[at], r.qkvT[2])

        def put_second(at, got):
            r.grad[at] = got
            dy[at] = (0.5 * got).astype(LOW)

        norm_rows_back(dh, r.x1, r.grad, put_second, vec, sums, 2)
        if inside:
            third.plane_two(0)
            ffn1.sent(0)
        for copy in back_copies:
            copy.wait()

        def hooks(n):
            if n == 3:
                put_off(planes_of(proj) + planes_of(out0, in0), 2, {proj: functools.partial(end_box, 1, proj), in0: end_ffn0})
                for d in (1, 2, 3):
                    third.plane_one(d)
                tick(1)
            if n == 5:
                tick(1)
            if n == 7:
                tick(2)
                third.plane_two(1)
                third.plane_two(2)

        if inside:
            for d in range(deep - 1, -1, -1):
                proj.step_one(d)
        by_planes(lambda i: weight_grads(r.h0, dy, hidden_grad(g1, dy, da, i), i), [out0, in0] if inside else None, hooks)
        tick(1)
        if inside:
            third.plane_two(3)
        masked_input(scal, r.x_in, x0)

        @pl.loop(0, rows // 256)
        def _(i):
            at = rows_of(i, 256)
            dh[at] = tn(da[:, at], whole_of(g1, 0))

        tick(2)
        if inside:
            for d in range(deep):
                third.plane_last(d)

        def put_input(at, got):
            r.input_grad[at] = got * keep_rows(scal, at.start, block, width)

        norm_rows_back(dh, x0, r.grad, put_input, vec, sums, 0)

    def tail(dy, da):
        dh, x0 = r.dz, r.x2
        project_back(dh, dy, da, x0)
        leaving["input_grad"].start()
        if not inside:
            return
        while len(queue) > 15:
            tick(1)
        fourth.plane_one(0)
        r.part_c[...] = to_tile(sums[0:4])
        every = Everyone(count, r.pair_c, r.slots_c, r.pair_sems_c, r.sends_c, r.recvs_c)
        every.start(r.part_c)
        tick(4)
        fourth.plane_two(0)
        tick(3)
        for d in (1, 2, 3):
            fourth.plane_one(d)
        for d in range(deep):
            third.plane_other(d)
        tick(2)
        got = r.held[0]
        r.d_conv_out[...] = got[:, :, :, 0:16].reshape(width, width)
        r.d_conv_in[:, :width] = got[:, :, :, 16:32].reshape(width, width)
        r.d_conv_in[:, width:] = got[:, :, :, 32:48].reshape(width, width)
        r.d_att[...] = got[:, :, :, 48:64].reshape(width, width)
        for name in ("d_conv_out", "d_conv_in", "d_att"):
            leaving[name].start()
        tick(2)
        for d in (1, 2, 3):
            fourth.plane_two(d)
        tick(len(queue))
        for d in range(deep):
            fourth.plane_last(d)
        tile = every.total()
        for d in range(deep):
            fourth.plane_other(d)
        got = r.held[1, pl.ds(core * deep, deep)].reshape(count, 64, width)
        for s in range(3):
            v = got[:, s * 16 : (s + 1) * 16]
            v = jnp.concatenate([v[:, None, :, :half], v[:, None, :, half:]], axis=1)
            r.d_qkv[s] = v.reshape(width, half)
        got = r.held[1, 0, :, :, 48:64].reshape(64, width).astype(F32)
        r.d_kern[...] = got[:taps]
        r.d_vec[...] = jnp.concatenate(
            [
                *[from_tile(tile, n, width) for n in range(4)], got[taps + 4 : taps + 6],
                spread * grad_moment, grad_sum, got[taps + 8 : taps + 12],
            ],
            axis=0,
        )
        third.finish()
        fourth.finish()
        for piece in stages:
            for kind in range(4):
                if kind or piece is not ffn1:
                    piece.sent(kind)

    pl.run_scoped(
        tail, vm(square, LOW), vm((hidden, rows), LOW),
    )
    if not inside:
        for name in ("d_conv_out", "d_conv_in", "d_att"):
            leaving[name].start()
        r.small[taps : taps + 16] = sums[...]
        r.small[taps + 6 : taps + 7] = spread * grad_moment
        r.small[taps + 7 : taps + 8] = grad_sum
        copy = pltpu.make_async_copy(g0, r.d_ffn.at[0], r.local.at[3])
        copy.start()
        copy.wait()
    for copy in leaving.values():
        copy.wait()


def gather_steps(route, chunk, held, sends, recv, with_core=True):
    started = []
    core, count = route.core, route.count

    def block(place):
        return core * count + place

    def arrive(place):
        here = held.at[chunk, block(place)]
        to_batch(here, here, recv.at[chunk, block(place)], recv.at[chunk, block(place)], route.me).wait_recv()

    def send(place, target):
        slot = len(started)
        here = held.at[chunk, block(place)]
        copy = to_batch(here, here, sends.at[chunk, slot], recv.at[chunk, block(place)], target)
        copy.start()
        started.append(copy)

    def cross(place):
        if not with_core:
            return
        slot = len(started)
        here = held.at[chunk, block(place)]
        copy = to_core(here, here, sends.at[chunk, slot], recv.at[chunk, block(place)], 1 - core)
        copy.start()
        started.append(copy)

    def step_mid():
        for k in range(1, route.deep):
            send(route.me, route.index(lax.rem(route.z + k, route.deep), route.p, route.q))
        cross(route.me)

    def step_one():
        for d in range(route.deep):
            z = lax.rem(route.z + d, route.deep)
            place = route.index(z, route.p, route.q)
            if d:
                arrive(place)
            for k in range(1, route.side):
                send(place, route.index(route.z, lax.rem(route.p + k, route.side), route.q))
            if d:
                cross(place)

    def step_two():
        for d in range(route.deep):
            z = lax.rem(route.z + d, route.deep)
            for e in range(route.side):
                p = lax.rem(route.p + e, route.side)
                place = route.index(z, p, route.q)
                if e:
                    arrive(place)
                for k in range(1, route.side):
                    send(place, route.index(route.z, route.p, lax.rem(route.q + k, route.side)))
                if e:
                    cross(place)

    def step_last():
        for d in range(route.deep):
            z = lax.rem(route.z + d, route.deep)
            for e in range(route.side):
                p = lax.rem(route.p + e, route.side)
                for f in range(1, route.side):
                    place = route.index(z, p, lax.rem(route.q + f, route.side))
                    arrive(place)
                    cross(place)

    def step_end():
        if with_core:
            for place in range(count):
                other = held.at[chunk, (1 - core) * count + place]
                at = recv.at[chunk, (1 - core) * count + place]
                to_core(other, other, at, at, 1 - core).wait_recv()
        for copy in started:
            copy.wait_send()

    return [step_mid, step_one, step_two, step_last, step_end]


def sends_of(route):
    return (route.deep - 1) + route.deep * (route.side - 1) * (1 + route.side) + route.count


def run_steps(all_steps):
    depth = len(all_steps[0])
    for turn in range(depth + len(all_steps) - 1):
        for chunk, steps in enumerate(all_steps):
            if 0 <= turn - chunk < depth:
                steps[turn - chunk]()


def gather_kernel(count, mine, held, local, sends, recv):
    route = Routes(count).here()
    chunks = mine.shape[0]
    copies = []
    for chunk in range(chunks):
        own = held.at[chunk, route.core * count + route.me]
        copy = pltpu.make_async_copy(mine.at[chunk], own, local.at[chunk])
        copy.start()
        copies.append(copy)
    route.greet()
    for copy in copies:
        copy.wait()
    run_steps([gather_steps(route, chunk, held, sends, recv) for chunk in range(chunks)])


def gather_all(mine, count, collective_id):
    chunks, rows, width = mine.shape
    route = Routes(count)
    return pl.pallas_call(
        functools.partial(gather_kernel, count),
        out_shape=jax.ShapeDtypeStruct((chunks, 2 * count, rows, width), mine.dtype),
        in_specs=[pl.BlockSpec(memory_space=pltpu.VMEM)],
        out_specs=pl.BlockSpec(memory_space=pltpu.VMEM),
        scratch_shapes=[
            pltpu.SemaphoreType.DMA((chunks,)),
            pltpu.SemaphoreType.DMA((chunks, sends_of(route))),
            pltpu.SemaphoreType.DMA((chunks, 2 * count)),
        ],
        compiler_params=pltpu.CompilerParams(
            collective_id=collective_id, has_side_effects=True, vmem_limit_bytes=VMEM_BYTES
        ),
    )(mine)


def reduce_kernel(count, solo, n, *refs):
    pieces, (fin, held, grads, packing, *rest) = refs[:n], refs[n:]
    copies = []
    at = 0
    for i, piece in enumerate(pieces):
        lines = piece.shape[1]
        copy = pltpu.make_async_copy(piece, grads.at[:, pl.ds(at, lines)], packing.at[i])
        copy.start()
        copies.append(copy)
        at += lines
    for copy in copies:
        copy.wait()
    reduce_packed(count, solo, grads, fin, held, *rest)


def reduce_packed(count, solo, grads, fin, held, zero, one, two, three, s0, r0, s1, r1, s2, r2, s3, r3, sends, recv):
    route = Routes(count).here()
    core, me, side, deep = route.core, route.me, route.side, route.deep
    rows, width = grads.shape[1:]
    piece = 16

    def add(target, source):
        @pl.loop(0, rows // piece)
        def _(i):
            at = pl.ds(pl.multiple_of(i * piece, piece), piece)
            target[at] = (target[at].astype(jnp.float32) + source[at].astype(jnp.float32)).astype(target.dtype)

    route.greet()
    waits = []
    order = []
    for f in range(side - 1, -1, -1):
        for d in range(deep):
            for e in range(side - 1, -1, -1):
                order.append((d, e, f))
    for d, e, f in order:
        place = route.index(lax.rem(route.z + d, deep), lax.rem(route.p + e, side), lax.rem(route.q + f, side))
        copy = to_core(grads.at[(1 - core) * count + place], zero.at[place], s0.at[place], r0.at[place], 1 - core)
        copy.start()
        waits.append(copy)
    for e in range(side - 1, -1, -1):
        for d in range(deep):
            for f in range(side - 1, -1, -1):
                z, p, q = lax.rem(route.z + d, deep), lax.rem(route.p + e, side), lax.rem(route.q + f, side)
                place = route.index(z, p, q)
                to_core(zero.at[place], zero.at[place], s0.at[place], r0.at[place], 1 - core).wait_recv()
                add(zero.at[place], grads.at[core * count + place])
                if e:
                    slot = (e - 1) * deep * side + z * side + q
                    copy = to_batch(
                        zero.at[place], one.at[slot], s1.at[slot], r1.at[slot], route.index(route.z, p, route.q)
                    )
                    copy.start()
                    waits.append(copy)
    for f in range(side - 1, -1, -1):
        for d in range(deep):
            z, q = lax.rem(route.z + d, deep), lax.rem(route.q + f, side)
            place = route.index(z, route.p, q)
            for e in range(1, side):
                slot = (e - 1) * deep * side + z * side + q
                to_batch(one.at[slot], one.at[slot], s1.at[slot], r1.at[slot], me).wait_recv()
                add(zero.at[place], one.at[slot])
            if f:
                slot = (f - 1) * deep + z
                copy = to_batch(
                    zero.at[place], two.at[slot], s2.at[slot], r2.at[slot], route.index(route.z, route.p, q)
                )
                copy.start()
                waits.append(copy)
    for d in range(deep - 1, -1, -1):
        z = lax.rem(route.z + d, deep)
        place = route.index(z, route.p, route.q)
        for f in range(1, side):
            slot = (f - 1) * deep + z
            to_batch(two.at[slot], two.at[slot], s2.at[slot], r2.at[slot], me).wait_recv()
            add(zero.at[place], two.at[slot])
        if d:
            copy = to_batch(zero.at[place], three.at[d - 1], s3.at[d - 1], r3.at[d - 1], place)
            copy.start()
            waits.append(copy)
    for d in range(1, deep):
        to_batch(three.at[d - 1], three.at[d - 1], s3.at[d - 1], r3.at[d - 1], me).wait_recv()

    def final(at):
        total = zero[me, at].astype(jnp.float32)
        for d in range(1, deep):
            total = total + three[d - 1, at].astype(jnp.float32)
        return total

    mine = core * count + me

    @pl.loop(0, (rows - solo) // piece)
    def _(i):
        at = pl.ds(pl.multiple_of(i * piece, piece), piece)
        held[0, mine, at] = final(pl.ds(pl.multiple_of(solo + i * piece, piece), piece)).astype(held.dtype)

    steps = gather_steps(route, 0, held, sends, recv)
    steps[0]()

    @pl.loop(0, solo // piece)
    def _(i):
        at = pl.ds(pl.multiple_of(i * piece, piece), piece)
        fin[at] = final(at)

    for step in steps[1:]:
        step()
    for copy in waits:
        copy.wait_send()


def reduce_all(pieces, solo, count, collective_id):
    blocks, _, width = pieces[0].shape
    kind = pieces[0].dtype
    if any(piece.shape[1] % 16 for piece in pieces):
        used = sum(piece.shape[1] for piece in pieces)
        spare = jnp.zeros((blocks, -used % 16, width), kind)
        pieces = [jnp.concatenate([*pieces, spare], axis=1)]
    rows = sum(piece.shape[1] for piece in pieces)
    route = Routes(count)
    side, deep = route.side, route.deep
    n1 = max(1, (side - 1) * side * deep)
    n2 = max(1, (side - 1) * deep)
    n3 = max(1, deep - 1)
    dma = pltpu.SemaphoreType.DMA
    return pl.pallas_call(
        functools.partial(reduce_kernel, count, solo, len(pieces)),
        out_shape=(
            jax.ShapeDtypeStruct((solo, width), jnp.float32),
            jax.ShapeDtypeStruct((1, blocks, rows - solo, width), kind),
        ),
        in_specs=[pl.BlockSpec(memory_space=pl.ANY)] * len(pieces),
        out_specs=(pl.BlockSpec(memory_space=pltpu.VMEM), pl.BlockSpec(memory_space=pltpu.VMEM)),
        scratch_shapes=[
            pltpu.VMEM((blocks, rows, width), kind),
            dma((len(pieces),)),
            pltpu.VMEM((count, rows, width), kind),
            pltpu.VMEM((n1, rows, width), kind),
            pltpu.VMEM((n2, rows, width), kind),
            pltpu.VMEM((n3, rows, width), kind),
            dma((count,)), dma((count,)),
            dma((n1,)), dma((n1,)),
            dma((n2,)), dma((n2,)),
            dma((n3,)), dma((n3,)),
            dma((1, sends_of(route))), dma((1, blocks)),
        ],
        compiler_params=pltpu.CompilerParams(
            collective_id=collective_id, has_side_effects=True, vmem_limit_bytes=VMEM_BYTES
        ),
    )(*pieces)


def last_kernel(count, *refs):
    for source, target in zip(refs[:count], refs[count:]):
        target[...] = source[...].astype(target.dtype)


def per_device(
    block_input, lengths, spans, cotangent, ffn_in, ffn_out, qkv_weight, out_weight, conv_in, kernel, conv_out, vectors,
):
    _, rows, width = block_input.shape
    count = lax.axis_size("batch")
    core = lax.axis_index("seq")
    shard = ffn_in.shape[1]
    blocks = 2 * count
    hidden = shard * blocks
    heads, size = HEADS, width // HEADS
    keys = 2 * rows
    taps = kernel.shape[0]
    inside = shard % 64 == 0 and width == 16 * blocks
    route = Routes(count)
    vm, dma = pltpu.VMEM, pltpu.SemaphoreType.DMA
    weights = (2, 8, 2, 2, hidden // 32, width)
    if inside:
        shards = dict(ffn_in=ffn_in, ffn_out=ffn_out)
    else:
        got = jnp.stack([ffn_in, ffn_out], axis=1).reshape(2, 2 * shard, width)
        got = gather_all(got, count, 1).reshape(2, blocks, 2, shard, width)
        shards = dict(shards=got.transpose(0, 2, 1, 3, 4).reshape(2, *weights))
    square, tall = (rows, width), (hidden, rows)
    here, hbm = pl.BlockSpec(memory_space=pltpu.VMEM), pl.BlockSpec(memory_space=pl.ANY)
    scalars = dict(lengths=lengths, spans=spans)
    late = dict(x_in=block_input[0], vec=vectors, kern=kernel, cot=cotangent[0], w_att=out_weight, conv_in=conv_in, conv_out=conv_out, qkv=qkv_weight)
    ins = scalars | {f"{key}_far": value for key, value in late.items()} | shards
    in_specs = [pl.BlockSpec(memory_space=pltpu.SMEM)] * len(scalars)
    in_specs += [hbm] * (len(late) + len(shards))
    lent = dict(
        out=(square, LOW), input_grad=(square, F32), d_att=((width, width), LOW), d_conv_in=((width, 2 * width), LOW),
        d_conv_out=((width, width), LOW),
    )
    outs = {f"far_{key}": (*value, hbm) for key, value in lent.items()} | dict(
        far_g=(weights, LOW, hbm), far_act=(tall, LOW, hbm), far_slope=(tall, LOW, hbm),
    )
    if inside:
        outs |= dict(
            fin_in=((2, shard, width), F32, here), fin_out=((2, shard, width), F32, here),
            d_qkv=((3, width, width // 2), LOW, here), d_kern=((taps, width), F32, here), d_vec=((12, width), F32, here),
        )
    else:
        outs |= dict(
            d_qkv=((3, width, width), LOW, here), small=((taps + 16, width), F32, here),
            d_ffn=((2, *weights), LOW, hbm),
        )
    scratch = dict(
        g0=vm(weights, LOW), g1=vm(weights, LOW), act=vm(tall, LOW), slope=vm(tall, LOW), qkvT=vm((3, width, width), LOW),
        x1=vm(square, F32), x2=vm(square, F32), grad=vm(square, F32), depth=vm(square, F32),
        dz=vm(square, F32), pad=vm((rows + 2 * HALO, width), F32), halo=vm((2, HALO, width), F32),
        h0=vm(square, LOW), h_all=vm((keys, width), LOW), h3=vm(square, LOW), key=vm((heads // 2, keys, 128), LOW),
        qT=vm((heads, size, rows), LOW), oT=vm((width, rows), LOW), doT=vm((heads, size, rows), LOW),
        top=vm((heads, rows), F32), extra=vm((keys, 128), LOW), wide=vm((taps, 8, width), F32), sums=vm((16, width), F32),
        own_v=vm(square, LOW),
        rk=vm((heads // 2, rows, 128), LOW), rv=vm((heads // 2, rows, 128), LOW), dq=vm(square, LOW),
        x_in=vm(square, LOW), vec=vm((12, width), F32), kern=vm((taps, width), F32), **{k: vm(*v) for k, v in lent.items()},
        local=dma((26,)), swap=dma((12,)), qkv_mine=vm(qkv_weight.shape, LOW), cot=vm(square, LOW),
        w_att=vm((width, width), LOW), conv_in=vm((width, 2 * width), LOW), conv_out=vm((width, width), LOW),
    )
    for name, lines in (("a", 16), ("b", 8), ("c", 16))[: 3 if inside else 2]:
        scratch[f"part_{name}"] = vm((lines, 128), F32)
        for key, kind in zip(("pair", "slots", "pair_sems", "sends", "recvs"), Everyone.scratch(count, lines)):
            scratch[f"{key}_{name}"] = kind
    if not inside:
        scratch |= dict(spare=vm((width, rows), LOW), spare_wide=vm((rows, 2 * width), LOW))
    if inside:
        for key, shape in zip(("zero", "one", "two", "three"), ((4, 2, 2), (4, 2), (4,), (3,))):
            scratch[key] = vm((6, *shape, shard, width), LOW)
        scratch |= dict(
            box=vm((2, 8, 2, 2, 64, width), LOW), held=vm((2, 8, 2, 2, 64, width), LOW), small=vm((taps + 16, width), F32),
            g_send=dma((4, 11)), g_recv=dma((4, 4, 4)), r_send=dma((5, 4)), r_recv=dma((5, 4, 4)),
        )
    cfg = SimpleNamespace(
        names=[*ins, *outs, *scratch], count=count, shard=shard, hidden=hidden, heads=heads, inside=inside
    )
    results = pl.pallas_call(
        functools.partial(layer_kernel, cfg),
        out_shape=tuple(jax.ShapeDtypeStruct(shape, kind) for shape, kind, _ in outs.values()),
        in_specs=in_specs,
        out_specs=tuple(spec for _, _, spec in outs.values()),
        scratch_shapes=list(scratch.values()),
        compiler_params=pltpu.CompilerParams(collective_id=0, has_side_effects=True, vmem_limit_bytes=VMEM_BYTES),
    )(*ins.values())
    got = SimpleNamespace(**dict(zip(outs, results)))
    if inside:
        plain = [got.far_out, got.far_input_grad, got.fin_in, got.fin_out, got.d_kern, got.d_vec]
        wide = [got.d_qkv, got.far_d_att, got.far_d_conv_in, got.far_d_conv_out]
        shapes = [(v.shape, v.dtype) for v in plain] + [(v.shape, F32) for v in wide]
        steps = 4

        def part(shape):
            if shape[-2] % (8 * steps):
                return pl.BlockSpec(shape, lambda i: (0,) * len(shape))
            lines = shape[-2] // steps
            return pl.BlockSpec((*shape[:-2], lines, shape[-1]), lambda i: (0,) * (len(shape) - 2) + (i, 0))

        parts = [part(shape) for shape, _ in shapes]
        done = pl.pallas_call(
            functools.partial(last_kernel, len(shapes)),
            grid=(steps,),
            out_shape=tuple(jax.ShapeDtypeStruct(*shape) for shape in shapes),
            in_specs=parts,
            out_specs=tuple(parts),
            compiler_params=pltpu.CompilerParams(vmem_limit_bytes=VMEM_BYTES),
        )(*plain, *wide)
        out, input_grad, fin_in, fin_out, d_kern, d_vec, d_qkv, d_att, d_conv_in, d_conv_out = done
        return (
            out[None], input_grad[None], fin_in, fin_out, d_qkv, d_att, d_conv_in, d_kern, d_conv_out, d_vec,
        )

    def spread(values):
        flat = values.astype(LOW).reshape(-1, width)
        lines = -(-flat.shape[0] // blocks)
        flat = jnp.pad(flat, ((0, lines * blocks - flat.shape[0]), (0, 0)))
        return flat.reshape(blocks, lines, width)

    lines = 3 * width // (2 * count)
    per_core = got.d_qkv.reshape(3 * width, 2, width // 2).transpose(1, 0, 2).reshape(blocks, -1, width)
    d_in0, d_out0, d_in1, d_out1 = (got.d_ffn[j, m].reshape(hidden, width) for j in range(2) for m in range(2))
    rest = (got.far_d_att, got.far_d_conv_in, got.far_d_conv_out, got.small)
    pieces = [spread(v) for v in (d_in0, d_out0, d_in1, d_out1, *rest)] + [per_core]
    fin, shared = reduce_all(pieces, 4 * shard, count, 2)
    at = 0
    whole = []
    for piece, like in zip(pieces[4:8], rest):
        part = shared[0, :, at : at + piece.shape[1]].reshape(-1, width)
        whole.append(part[: like.size // width].reshape(like.shape).astype(F32))
        at += piece.shape[1]
    mine = lax.dynamic_slice_in_dim(shared[0], core * count, count, axis=0)[:, at : at + per_core.shape[1]]
    row = lax.broadcasted_iota(jnp.int32, (12, 1), 0)
    d_vec = jnp.where((row == 6) | (row == 7), got.small[taps : taps + 12], whole[3][taps : taps + 12])
    return (
        got.far_out[None], got.far_input_grad[None], jnp.stack([fin[:shard], fin[2 * shard : 3 * shard]]),
        jnp.stack([fin[shard : 2 * shard], fin[3 * shard :]]),
        mine.reshape(3, width, width // 2).astype(F32), whole[0], whole[1], whole[3][:taps], whole[2], d_vec,
    )


def solution(mesh):
    placed = (
        P("batch", "seq", None),
        P("batch"),
        P("batch", None),
        P("batch", "seq", None),
        P(None, ("seq", "batch"), None),
        P(None, ("seq", "batch"), None),
        P(None, None, "seq"),
        P(),
        P(),
        P(),
        P(),
        P(),
    )
    return jax.shard_map(
        per_device,
        mesh=mesh,
        in_specs=placed,
        out_specs=(
            P("batch", "seq", None),
            P("batch", "seq", None),
            P(None, ("seq", "batch"), None),
            P(None, ("seq", "batch"), None),
            P(None, None, "seq"),
            P(),
            P(),
            P(),
            P(),
            P(),
        ),
        check_vma=False,
    )
```

```python
import functools
import math
from types import SimpleNamespace

import jax
import jax.numpy as jnp
from jax import lax
from jax.experimental import pallas as pl
from jax.experimental.pallas import tpu as pltpu
from jax.sharding import PartitionSpec as P

HEADS = 8
MESH = pl.DeviceIdType.MESH
VMEM_BYTES = 63 * 1024 * 1024
F32, LOW = jnp.float32, jnp.bfloat16
EPS = 1e-05
HALO = 16


class Routes:
    def __init__(self, count):
        if count == 16:
            first, last, middle = (1, 2), (2, 2), (4, 4)
        elif count == 128:
            first, last, middle = (1, 4), (32, 4), (4, 8)
        else:
            first, last, middle = (1, 1), (1, 1), (1, count)
        self.count = count
        self.side = first[1]
        self.deep = middle[1]
        self.first, self.last, self.middle = first, last, middle

    def here(self):
        self.core = lax.axis_index("seq")
        self.me = lax.axis_index("batch")
        turn = self.core * (self.last[0] - self.first[0])
        self.one = self.first[0] + turn
        self.two = self.last[0] - turn
        self.mid = self.middle[0]
        self.p = lax.rem(lax.div(self.me, self.one), self.side)
        self.q = lax.rem(lax.div(self.me, self.two), self.side)
        self.z = lax.rem(lax.div(self.me, self.mid), self.deep)
        return self

    def index(self, z, p, q):
        return z * self.mid + p * self.one + q * self.two

    def plane(self, d):
        if self.deep != 4 or d == 0:
            return lax.rem(self.z + d, self.deep) if d else self.z
        return (self.z + 1 - 2 * lax.rem(self.z, 2), lax.rem(self.z + 2, 4), 3 - self.z)[d - 1]

    def reach(self, i):
        far = lax.div(self.z, 2)
        first = self.z + far * (3 - 2 * self.z)
        turn = (first, 1 - first, 2, 3)[i]
        return turn + far * (3 - 2 * turn)

    def near(self, d, e, f):
        p = lax.rem(self.p + e, self.side) if e else self.p
        q = lax.rem(self.q + f, self.side) if f else self.q
        return self.index(self.plane(d), p, q)

    def peers(self):
        found = []
        for k in range(1, self.deep):
            found.append(self.index(lax.rem(self.z + k, self.deep), self.p, self.q))
        for k in range(1, self.side):
            found.append(self.index(self.z, lax.rem(self.p + k, self.side), self.q))
            found.append(self.index(self.z, self.p, lax.rem(self.q + k, self.side)))
        return found

    def greet(self):
        barrier = pltpu.get_barrier_semaphore()
        places = self.peers()
        for place in places:
            pl.semaphore_signal(
                barrier, inc=1, device_id={"batch": place}, device_id_type=MESH
            )
        pl.semaphore_signal(
            barrier, inc=1, device_id={"seq": 1 - self.core}, device_id_type=MESH
        )
        pl.semaphore_wait(barrier, len(places) + 1)


def to_batch(src, dst, send, recv, place):
    return pltpu.make_async_remote_copy(
        src_ref=src, dst_ref=dst, send_sem=send, recv_sem=recv,
        device_id={"batch": place}, device_id_type=MESH,
    )


def to_core(src, dst, send, recv, core):
    return pltpu.make_async_remote_copy(
        src_ref=src, dst_ref=dst, send_sem=send, recv_sem=recv,
        device_id={"seq": core}, device_id_type=MESH,
    )


class Gather:
    def __init__(self, route, at, sends, recv, line):
        self.route, self.at, self.sends, self.recv, self.line = route, at, sends, recv, line

    def go(self, here, kind, z, send, place):
        if place is None:
            to_core(here, here, self.sends.at[send], self.recv.at[kind, z], 1 - self.route.core).start()
        else:
            to_batch(here, here, self.sends.at[send], self.recv.at[kind, z], place).start()

    def come(self, here, kind, z):
        to_core(here, here, self.recv.at[kind, z], self.recv.at[kind, z], 1 - self.route.core).wait_recv()

    def z_of(self, i):
        return self.route.reach(i) if self.line else self.route.plane(i)

    def plane_one(self, i):
        route = self.route
        z = self.z_of(i)
        here = self.at(route.core * route.deep + z, route.q, route.p)
        if i:
            self.come(here, 0, z)
        if self.line:
            @pl.when((z <= route.z) & (route.z < route.deep - 1))
            def _():
                self.go(here, 0, z, 3 + z, route.index(route.z + 1, route.p, route.q))

            @pl.when((z >= route.z) & (route.z > 0))
            def _():
                self.go(here, 0, z, 7 + z, route.index(route.z - 1, route.p, route.q))
        elif i == 0:
            for d in range(1, route.deep):
                self.go(here, 0, z, 2 + d, route.near(d, 0, 0))
        self.go(here, 1, z, 0, route.near(0, 1, 0))
        self.go(here, 2, z, 1, route.near(0, 0, 1))

    def plane_two(self, i):
        route = self.route
        z = self.z_of(i)
        cz = route.core * route.deep + z
        here = self.at(cz, route.q, 1 - route.p)
        self.come(here, 1, z)
        self.go(here, 2, z, 1, route.near(0, 0, 1))

    def plane_last(self, i, cross=True):
        route = self.route
        z = self.z_of(i)
        cz = route.core * route.deep + z
        self.come(self.at(cz, route.q), 2, z)
        if cross:
            self.go(self.at(cz), 3, z, 2, None)

    def plane_other(self, i):
        route = self.route
        z = self.z_of(i)
        self.come(self.at((1 - route.core) * route.deep + z), 3, z)

    def finish(self, cross=True):
        route = self.route

        def sent(here, send):
            to_core(here, here, self.sends.at[send], self.sends.at[send], 1 - route.core).wait_send()

        sent(self.at(0), 0)
        sent(self.at(pl.ds(0, 2)), 1)
        if cross:
            sent(self.at(pl.ds(0, 4)), 2)
        one = self.at(0, 0, 0)
        if not self.line:
            for d in range(1, route.deep):
                sent(one, 2 + d)
            return
        for z in range(route.deep):
            pl.when((z <= route.z) & (route.z < route.deep - 1))(functools.partial(sent, one, 3 + z))
            pl.when((z >= route.z) & (route.z > 0))(functools.partial(sent, one, 7 + z))


class Reduce:
    def __init__(self, route, source, stage, sends, recv):
        self.route, self.source, self.sends, self.recv = route, source, sends, recv
        self.zero, self.one, self.two, self.three = stage
        self.lead = self.zero.shape[0]

    def come(self, here, kind, n):
        to_core(here, here, self.recv.at[kind, n], self.recv.at[kind, n], 1 - self.route.core).wait_recv()

    def add(self, at, value):
        self.zero[at] = self.zero[at] + value

    def leave(self, d):
        route = self.route
        z = route.plane(d)
        to_core(
            self.source((1 - route.core) * route.deep + z), self.zero.at[:, z], self.sends.at[0],
            self.recv.at[0, z], 1 - route.core,
        ).start()

    def start(self):
        for d in range(self.route.deep - 1, -1, -1):
            self.leave(d)

    def step_one(self, d):
        route = self.route
        z = route.plane(d)
        self.come(self.zero.at[:, z], 0, z)
        mine = self.source(route.core * route.deep + z)
        for n in range(self.lead):
            for q in range(2):
                for p in range(2):
                    self.add((n, z, q, p), mine[n, q, p])
        to_batch(
            self.zero.at[:, z, :, 1 - route.p], self.one.at[:, d], self.sends.at[1], self.recv.at[1, d],
            route.near(0, 1, 0),
        ).start()

    def step_two(self, d):
        route = self.route
        z = route.plane(d)
        self.come(self.one.at[:, d], 1, d)
        for n in range(self.lead):
            for q in range(2):
                self.add((n, z, q, route.p), self.one[n, d, q])
        to_batch(
            self.zero.at[:, z, 1 - route.q, route.p], self.two.at[:, d], self.sends.at[2], self.recv.at[2, d],
            route.near(0, 0, 1),
        ).start()

    def step_three(self, d):
        route = self.route
        z = route.plane(d)
        self.come(self.two.at[:, d], 2, d)
        for n in range(self.lead):
            self.add((n, z, route.q, route.p), self.two[n, d])
        if d:
            to_batch(
                self.zero.at[:, z, route.q, route.p], self.three.at[:, d - 1], self.sends.at[3],
                self.recv.at[3, d - 1], route.near(d, 0, 0),
            ).start()

    def total(self):
        route = self.route
        for d in range(1, route.deep):
            self.come(self.three.at[:, d - 1], 3, d - 1)
        sums = []
        for n in range(self.lead):
            out = self.zero[n, route.z, route.q, route.p].astype(F32)
            for d in range(1, route.deep):
                out = out + self.three[n, d - 1].astype(F32)
            sums.append(out)
        return sums

    def sent(self, kind):
        here = (self.zero, self.one, self.two, self.three)[kind]
        to_core(here, here, self.sends.at[kind], self.sends.at[kind], 1 - self.route.core).wait_send()


class Everyone:
    def __init__(self, count, pair, slots, pair_sems, sends, recvs):
        self.count, self.pair, self.slots = count, pair, slots
        self.pair_sems, self.sends, self.recvs = pair_sems, sends, recvs

    def start(self, x):
        core, me, count = lax.axis_index("seq"), lax.axis_index("batch"), self.count
        copy = to_core(x, self.pair, self.pair_sems.at[0], self.pair_sems.at[1], 1 - core)
        copy.start()
        copy.wait()
        self.slots[me] = x[...] + self.pair[...]
        for k in range(1, count):
            here = self.slots.at[me]
            to_batch(here, here, self.sends, self.recvs, lax.rem(me + k, count)).start()

    def total(self):
        others = self.slots.at[pl.ds(0, self.count - 1)]
        copy = to_batch(others, others, self.sends, self.recvs, lax.axis_index("batch"))
        copy.wait_recv()
        out = self.slots[0]
        for place in range(1, self.count):
            out = out + self.slots[place]
        copy.wait_send()
        return out

    @staticmethod
    def scratch(count, rows):
        return [
            pltpu.VMEM((rows, 128), F32),
            pltpu.VMEM((count, rows, 128), F32),
            pltpu.SemaphoreType.DMA((2,)),
            pltpu.SemaphoreType.DMA,
            pltpu.SemaphoreType.DMA,
        ]


def to_tile(rows):
    width = rows.shape[1]
    parts = [rows[i : i + 1, j : j + 128] for i in range(rows.shape[0]) for j in range(0, width, 128)]
    return jnp.concatenate(parts, axis=0)


def from_tile(tile, first, width):
    each = width // 128
    return jnp.concatenate([tile[first * each + j : first * each + j + 1] for j in range(each)], axis=1)


def nn(a, b):
    return lax.dot_general(a, b, (((1,), (0,)), ((), ())), preferred_element_type=F32)


def nt(a, b):
    return lax.dot_general(a, b, (((1,), (1,)), ((), ())), preferred_element_type=F32)


def tn(a, b):
    return lax.dot_general(a, b, (((0,), (0,)), ((), ())), preferred_element_type=F32)


def sigmoid(v):
    return 0.5 * jnp.tanh(0.5 * v) + 0.5


def rows_of(i, size):
    return pl.ds(pl.multiple_of(i * size, size), size)


def normed(v):
    centred = v - jnp.mean(v, -1, keepdims=True)
    scale = lax.rsqrt(jnp.mean(centred * centred, -1, keepdims=True) + EPS)
    return centred * scale, scale


def normed_back(grad, hat, scale):
    return scale * (
        grad - jnp.mean(grad, -1, keepdims=True) - hat * jnp.mean(grad * hat, -1, keepdims=True)
    )


def fold(values):
    return jnp.sum(values.reshape(values.shape[0] // 8, 8, values.shape[1]), 0)


def norm_rows(x_ref, put, vec, row, block=256):
    @pl.loop(0, x_ref.shape[0] // block)
    def _(i):
        at = rows_of(i, block)
        hat, _ = normed(x_ref[at])
        put(at, (hat * vec[row : row + 1] + vec[row + 1 : row + 2]).astype(LOW))


def norm_rows_back(grad_ref, x_ref, g_ref, put, vec, sums, row, block=256):
    width = x_ref.shape[1]

    def step(i, carry):
        gain, bias = carry
        at = rows_of(i, block)
        hat, scale = normed(x_ref[at])
        grad = grad_ref[at]
        put(at, g_ref[at] + normed_back(grad * vec[row : row + 1], hat, scale))
        return gain + fold(grad * hat), bias + fold(grad)

    zero = jnp.zeros((8, width), F32)
    gain, bias = lax.fori_loop(0, x_ref.shape[0] // block, step, (zero, zero))
    sums[row : row + 1] = jnp.sum(gain, 0, keepdims=True)
    sums[row + 1 : row + 2] = jnp.sum(bias, 0, keepdims=True)


def activate(a):
    s = sigmoid(a)
    u = a * s
    return u, s + u * (1.0 - s)


def valid_rows(scal, at_row, rows):
    frame = scal[0] + at_row + lax.broadcasted_iota(jnp.int32, (rows, 1), 0)
    return frame, jnp.where(frame < scal[1], 1.0, 0.0)


def keep_rows(scal, at_row, rows, width):
    frame, ok = valid_rows(scal, at_row, rows)
    cut = (frame >= scal[2]) & (frame < scal[2] + scal[3])
    channel = lax.broadcasted_iota(jnp.int32, (1, width), 1)
    lost = (channel >= scal[4]) & (channel < scal[4] + scal[5])
    return (ok * jnp.where(cut, 0.0, 1.0)) * jnp.where(lost, 0.0, 1.0)


def masked_input(scal, x_in, x_ref, block=256):
    @pl.loop(0, x_in.shape[0] // block)
    def _(i):
        at = rows_of(i, block)
        keep = keep_rows(scal, i * block, block, x_in.shape[1])
        x_ref[at] = x_in[at].astype(F32) * keep


def split3(v):
    high = v.astype(LOW).astype(F32)
    rest = v - high
    mid = rest.astype(LOW).astype(F32)
    return high, mid, rest - mid


def key_extra(length, rows):
    key = lax.broadcasted_iota(jnp.int32, (rows, 128), 0)
    lane = lax.broadcasted_iota(jnp.int32, (rows, 128), 1)
    lost = jnp.where(key < length, 0.0, -1e30)
    return jnp.where(lane == 0, lost, jnp.where(lane < 4, 1.0, 0.0)).astype(LOW)


def fill_side(side, first, extra_rows):
    size = first[0].shape[0]
    blank = jnp.zeros((size, side.shape[2]), LOW)
    for half in range(2):
        side[half, half * size : (half + 1) * size] = first[half]
        side[half, (1 - half) * size : (2 - half) * size] = blank
        side[half, 2 * size :] = extra_rows[half]


def extra_of(lead, parts, wide):
    row = lax.broadcasted_iota(jnp.int32, (16, wide), 0)
    out = jnp.where(row == 0, lead, 0.0)
    if parts is not None:
        for n, part in enumerate(parts):
            out = jnp.where(row == n + 1, -part, out)
    return jnp.concatenate([out.astype(LOW), jnp.zeros((112, wide), LOW)], axis=0)


def attention_forward(qT, key, vT, extra, oT, top, side, scale, hook):
    heads, size, queries = qT.shape
    keys = key.shape[1]
    ones = jnp.ones((16, keys), LOW)

    @pl.loop(0, heads // 2)
    def _(pair):
        hook(pair)
        lead = extra_of(1.0, None, queries)
        fill_side(side, [qT[2 * pair], qT[2 * pair + 1]], [lead, lead])
        left = jnp.concatenate([key[pair], extra[...]], axis=1)
        for half in range(2):
            head = 2 * pair + half
            s = nn(left, side[half])
            m = jnp.max(s, 0, keepdims=True)
            p = jnp.exp2((s - m) * scale).astype(LOW)
            o = nn(jnp.concatenate([vT[head], ones], axis=0), p)
            total = o[size : size + 1]
            oT[rows_of(head, size)] = (o[:size] * (1.0 / total)).astype(LOW)
            top[pl.ds(head, 1)] = m + jnp.log2(total) * (1.0 / scale)


def attention_backward(
    qT, key, h_all, qkvT, extra, doT, delta, top, dqT, dk, dv, qside, oside, lows, grads, scale, shrink, hook, done, chunk=512
):
    heads, size, queries = qT.shape
    keys = key.shape[1]

    @pl.loop(0, heads // 2)
    def _(pair):
        hook(pair)
        tops = [split3(top[pl.ds(2 * pair + half, 1)]) for half in range(2)]
        deltas = [split3(delta[pl.ds(2 * pair + half, 1)]) for half in range(2)]
        fill_side(qside, [qT[2 * pair], qT[2 * pair + 1]], [extra_of(1.0, t, queries) for t in tops])
        fill_side(oside, [doT[2 * pair], doT[2 * pair + 1]], [extra_of(0.0, t, queries) for t in deltas])
        kT = nt(qkvT[1, rows_of(pair, 128)], h_all[...]).astype(LOW)
        wide_o = jnp.concatenate([oside[0, :128], oside[1, :128]], axis=1)
        wide_q = jnp.concatenate([qside[0, :128], qside[1, :128]], axis=1)
        totals = [None, None]
        for c in range(keys // chunk):
            at = slice(c * chunk, (c + 1) * chunk)
            value = nt(h_all[at], qkvT[2, rows_of(pair, 128)]).astype(LOW)
            left_k = jnp.concatenate([key[pair, at], extra[at]], axis=1)
            left_v = jnp.concatenate([value, extra[at]], axis=1)
            for half in range(2):
                lanes = slice(half * queries, (half + 1) * queries)
                p = jnp.exp2(nn(left_k, qside[half]) * scale)
                lows[:, lanes] = p.astype(LOW)
                grads[:, lanes] = (p * nn(left_v, oside[half])).astype(LOW)
            for half in range(2):
                lanes = slice(half * queries, (half + 1) * queries)
                got = nn(kT[half * size : (half + 1) * size, at], grads[:, lanes])
                totals[half] = got if c == 0 else totals[half] + got
            dv[pair, at] = nt(lows[...], wide_o).astype(LOW)
            dk[pair, at] = (nt(grads[...], wide_q) * shrink).astype(LOW)
        for half in range(2):
            dqT[rows_of(2 * pair + half, size)] = (totals[half] * shrink).astype(LOW)
        done(pair)


def windows(pad_ref, at_row, block, lanes, shifts):
    for s in range(8):
        mine = [(tap, shift) for tap, shift in shifts if shift % 8 == s]
        low = min(shift for _, shift in mine)
        high = max(shift for _, shift in mine)
        window = pad_ref[at_row + low : at_row + high + block, lanes]
        for tap, shift in mine:
            yield tap, window[shift - low : shift - low + block]


def convolve(pad_ref, taps_wide, put, shift_of, rows, width, hook=None, block=64):
    count = taps_wide.shape[0]
    shifts = [(tap, shift_of(tap)) for tap in range(count)]
    for lane in range(0, width, 128):
        lanes = slice(lane, lane + 128)
        for at_row in range(0, rows, block):
            total = jnp.zeros((block // 8, 8, 128), F32)
            for tap, values in windows(pad_ref, at_row, block, lanes, shifts):
                total = total + taps_wide[tap, :, lanes][None] * values.reshape(block // 8, 8, 128)
            put(at_row, block, lane, total.reshape(block, 128))
        if hook:
            hook(1)


def convolve_weight(pad_ref, grad_ref, first, out_ref, shift_of, rows, width, hook, block=64):
    taps = out_ref.shape[0]
    for lane in range(0, width, 128):
        lanes = slice(lane, lane + 128)
        for s in range(8):
            mine = [(tap, shift_of(tap)) for tap in range(taps) if shift_of(tap) % 8 == s]
            low = min(shift for _, shift in mine)
            high = max(shift for _, shift in mine)
            sums = {tap: jnp.zeros((8, 128), F32) for tap, _ in mine}
            for at_row in range(0, rows, block):
                grad = grad_ref[first + at_row : first + at_row + block, lanes]
                window = pad_ref[at_row + low : at_row + high + block, lanes]
                for tap, shift in mine:
                    sums[tap] = sums[tap] + fold(grad * window[shift - low : shift - low + block])
            for tap, _ in mine:
                out_ref[tap : tap + 1, lanes] = jnp.sum(sums[tap], 0, keepdims=True)
        if hook:
            hook(1)


def place_halo(pad_ref, halo, core):
    rows = pad_ref.shape[0] - 2 * HALO
    got = halo[...]
    zero = jnp.zeros_like(got)
    pad_ref[0:HALO] = jnp.where(core == 1, got, zero)
    pad_ref[rows + HALO :] = jnp.where(core == 0, got, zero)


def layer_kernel(cfg, *refs):
    r = SimpleNamespace(**dict(zip(cfg.names, refs)))
    count, shard, hidden, inside = cfg.count, cfg.shard, cfg.hidden, cfg.inside
    rows, width = r.x_in.shape
    heads, size = cfg.heads, width // cfg.heads
    keys, pairs, taps = 2 * rows, heads // 2, r.kern.shape[0]
    scale, shrink = math.log2(math.e) / math.sqrt(size), 1.0 / math.sqrt(size)
    route = Routes(count).here()
    core, me = route.core, route.me
    vec, g0, g1, sums = r.vec, r.g0, r.g1, r.sums
    chunk, block = 256, 256
    own = pl.ds(pl.multiple_of(core * rows, rows), rows)
    theirs = pl.ds(pl.multiple_of((1 - core) * rows, rows), rows)
    zero8 = jnp.zeros((8, width), F32)

    def plane_of(g, m, i):
        return g[m, i].reshape(chunk, width)

    def whole_of(g, m):
        return g[m].reshape(hidden, width)

    barrier = pltpu.get_barrier_semaphore()
    for k in range(1, count):
        pl.semaphore_signal(
            barrier, inc=1, device_id={"batch": lax.rem(me + k, count)}, device_id_type=MESH
        )
    pl.semaphore_signal(barrier, inc=1, device_id={"seq": 1 - core}, device_id_type=MESH)
    half = width // 2
    q_own = pl.ds(pl.multiple_of(core * half, half), half)
    loads = []

    def load(source, target):
        copy = pltpu.make_async_copy(source, target, r.local.at[4 + len(loads)])
        copy.start()
        loads.append(copy)
        return copy

    if inside:
        cz = core * route.deep + route.z
        near_loads = [
            load(part.at[j], g.at[m, cz, route.q, route.p]) for m, part in enumerate((r.ffn_in, r.ffn_out)) for j, g in enumerate((g0, g1))
        ]
    else:
        near_loads = [load(r.shards.at[0], g0), load(r.shards.at[1], g1)]
    load_x, load_vec, load_kern = load(r.x_in_far, r.x_in), load(r.vec_far, r.vec), load(r.kern_far, r.kern)
    load_qkv = load(r.qkv_far, r.qkv_mine)
    load_att = load(r.w_att_far, r.w_att)
    load_conv_in = load(r.conv_in_far, r.conv_in)
    load_conv_out = load(r.conv_out_far, r.conv_out)
    load_cot = load(r.cot_far, r.cot)
    frame0, length, span = core * rows, r.lengths[0], [r.spans[0, n] for n in range(4)]
    scal = [frame0, length, *span]
    sums[...] = jnp.zeros_like(sums)
    for copy in near_loads:
        copy.wait()
    pl.semaphore_wait(barrier, count)

    def put_h0(at, value):
        r.h0[at] = value

    def begin():
        load_x.wait()
        load_vec.wait()
        masked_input(scal, r.x_in, r.x1)
        norm_rows(r.x1, put_h0, vec, 0)
        load_kern.wait()
        for tap in range(taps):
            r.wide[tap] = jnp.broadcast_to(r.kern[tap : tap + 1], (8, width))

    def inner(i):
        at = rows_of(i, chunk)
        u, slope = activate(nt(plane_of(g0, 0, i), r.h0[...]))
        r.act[at] = u.astype(LOW)
        r.slope[at] = slope.astype(LOW)

    swap_q = to_core(r.qkvT.at[:, q_own], r.qkvT.at[:, q_own], r.swap.at[0], r.swap.at[1], 1 - core)

    def turn_qkv():
        load_qkv.wait()
        for s in range(3):
            r.qkvT[s, q_own] = r.qkv_mine[s].astype(F32).T.astype(LOW)
        swap_q.start()

    if inside:
        first = Gather(route, lambda *i: g0.at[(slice(None), *i)], r.g_send.at[0], r.g_recv.at[0], True)
        second = Gather(route, lambda *i: g1.at[(slice(None), *i)], r.g_send.at[1], r.g_recv.at[1], True)
        deep = route.deep

        def inner_plane(which, d):
            inner(which * deep + route.reach(d))

        first.plane_one(0)
        begin()
        first.plane_one(1)
        turn_qkv()
        first.plane_one(2)
        first.plane_two(0)
        first.plane_one(3)
        for d in (1, 2, 3):
            first.plane_two(d)
        second.plane_one(0)
        for d in range(deep):
            first.plane_last(d)
            inner_plane(core, d)
            if d:
                first.plane_other(d - 1)
                inner_plane(1 - core, d - 1)
        first.plane_other(deep - 1)
        inner_plane(1 - core, deep - 1)
    else:
        begin()
        turn_qkv()

        @pl.loop(0, hidden // chunk)
        def _(i):
            inner(i)

    @pl.loop(0, rows // 256)
    def _(i):
        at = rows_of(i, 256)
        r.x1[at] = r.x1[at] + 0.5 * tn(r.act[:, at], whole_of(g0, 1))

    def put_h2(at, value):
        r.h_all[pl.ds(pl.multiple_of(core * rows + at.start, block), block)] = value

    norm_rows(r.x1, put_h2, vec, 2)
    swap = to_core(r.h_all.at[own], r.h_all.at[own], r.swap.at[2], r.swap.at[3], 1 - core)
    swap.start()
    away = [
        pltpu.make_async_copy(g0, r.far_g, r.local.at[0]),
        pltpu.make_async_copy(r.act, r.far_act, r.local.at[1]),
        pltpu.make_async_copy(r.slope, r.far_slope, r.local.at[2]),
    ]
    for copy in away:
        copy.start()
    swap_q.wait()

    def project(at, vT):
        here = r.h_all[at]
        for pair in range(pairs):
            r.key[pair, at] = nt(here, r.qkvT[1, pair * 128 : (pair + 1) * 128]).astype(LOW)
        vT[:, :, at] = nt(r.qkvT[2], here).astype(LOW).reshape(heads, size, rows)

    r.extra[...] = key_extra(scal[1], keys)

    def attend(vT, side_ref):
        r.qT[...] = nt(r.qkvT[0], r.h_all[own]).astype(LOW).reshape(heads, size, rows)
        project(own, vT)
        if inside:
            second.plane_one(1)
        swap.wait()
        project(theirs, vT)
        if inside:
            second.plane_one(2)
            second.plane_two(0)

        def hook(pair):
            if inside:
                @pl.when(pair == 1)
                def _():
                    second.plane_one(3)
                    second.plane_two(1)

                @pl.when(pair == 2)
                def _():
                    second.plane_two(2)
                    second.plane_last(0)

                @pl.when(pair == 3)
                def _():
                    second.plane_two(3)
                    second.plane_last(1)

        attention_forward(r.qT, r.key, vT, r.extra, r.oT, r.top, side_ref, scale, hook)

    pl.run_scoped(attend, pltpu.VMEM((heads, size, keys), LOW), pltpu.VMEM((2, 256, rows), LOW))

    load_att.wait()

    @pl.loop(0, rows // 256)
    def _(i):
        at = rows_of(i, 256)
        r.x2[at] = r.x1[at] + tn(r.oT[:, at], r.w_att[...])

    def put_h3(at, value):
        r.h3[at] = value

    norm_rows(r.x2, put_h3, vec, 4)
    load_conv_in.wait()

    @pl.loop(0, rows // 256)
    def _(i):
        at = rows_of(i, 256)
        _, ok = valid_rows(scal, i * 256, 256)
        here = r.h3[at]
        gate = sigmoid(nn(here, r.conv_in[:, width:]))
        r.pad[pl.ds(pl.multiple_of(i * 256 + HALO, HALO), 256)] = nn(here, r.conv_in[:, :width]) * gate * ok

    edge = pl.ds(pl.multiple_of(HALO + (1 - core) * (rows - HALO), HALO), HALO)
    swap = to_core(r.pad.at[edge], r.halo.at[0], r.swap.at[4], r.swap.at[5], 1 - core)
    swap.start()
    if inside:
        second.plane_last(2)
    swap.wait()
    place_halo(r.pad, r.halo.at[0], core)

    def put_depth(at_row, high, lane, total):
        r.depth[at_row : at_row + high, lane : lane + 128] = total

    spots = [lambda: None] * 4
    if inside:
        pass
    convolve(r.pad, r.wide, put_depth, lambda tap: tap + 1, rows, width, lambda _: spots.pop(0)())

    if inside:
        second.plane_last(3)

    def moments(i, carry):
        one, two = carry
        _, ok = valid_rows(scal, i * block, block)
        here = r.depth[rows_of(i, block)]
        held = here * ok
        return one + fold(held), two + fold(here * held)

    one, two = lax.fori_loop(0, rows // block, moments, (zero8, zero8))
    number = jnp.clip(scal[1] - scal[0], 0, rows).astype(F32)
    r.part_a[0:8] = to_tile(
        jnp.concatenate([jnp.sum(one, 0, keepdims=True), jnp.sum(two, 0, keepdims=True)], axis=0)
    )
    r.part_a[8:16] = jnp.full((8, 128), 1.0, F32) * number
    every = Everyone(count, r.pair_a, r.slots_a, r.pair_sems_a, r.sends_a, r.recvs_a)
    every.start(r.part_a)
    if inside:
        for d in range(deep):
            second.plane_other(d)
        second.finish()
        first.finish()
    for copy in [*away, load_conv_out, load_cot]:
        copy.wait()
    tile = every.total()
    number = tile[8:9, 0:1]
    mean = from_tile(tile, 0, width) / number
    var = from_tile(tile, 1, width) / number - mean * mean
    spread = lax.rsqrt(var + EPS)
    gain6 = vec[6:7]

    if inside:
        stages = [
            Reduce(route, source, [ref.at[part] for ref in (r.zero, r.one, r.two, r.three)], r.r_send.at[k], r.r_recv.at[k])
            for k, (part, source) in enumerate(
                [
                    (pl.ds(0, 2), lambda cz: g0.at[:, cz]),
                    (pl.ds(2, 1), lambda cz: r.box.at[pl.ds(0, 1), cz]),
                    (pl.ds(3, 1), lambda cz: r.box.at[pl.ds(1, 1), cz]),
                    (pl.ds(4, 1), lambda cz: g0.at[pl.ds(1, 1), cz]),
                    (pl.ds(5, 1), lambda cz: g0.at[pl.ds(0, 1), cz]),
                ]
            )
        ]
        ffn1, rest, proj, out0, in0 = stages
        queue = []

        def put_off(units, lag, ends):
            for t in range(len(units) + lag):
                if t < len(units):
                    piece, d = units[t]
                    queue.append(functools.partial(piece.step_two, d))
                if t >= lag:
                    piece, d = units[t - lag]
                    queue.append(functools.partial(piece.step_three, d))
                    if d == 0 and piece in ends:
                        queue.append(ends[piece])

        def planes_of(*pieces):
            return [(piece, d) for d in range(deep - 1, -1, -1) for piece in pieces]

        def tick(count):
            for _ in range(min(count, len(queue))):
                queue.pop(0)()

        own_at = (core * deep + route.z, route.q, route.p)

        def ticks(*counts):
            left = list(counts)
            return lambda _: tick(left.pop(0))

        def end_ffn1():
            r.fin_in[1], r.fin_out[1] = ffn1.total()

        def end_ffn0():
            (r.fin_out[0],) = out0.total()
            (r.fin_in[0],) = in0.total()

        def end_box(j, piece):
            r.held[(j, *own_at)] = piece.total()[0].astype(LOW)

        third = Gather(route, lambda *i: r.held.at[(0, *i)], r.g_send.at[2], r.g_recv.at[2], False)
        fourth = Gather(route, lambda *i: r.held.at[(1, *i)], r.g_send.at[3], r.g_recv.at[3], False)
    else:
        def tick(count):
            pass

        def ticks(*counts):
            return None
    back_copies = [
        pltpu.make_async_copy(r.far_act, r.act, r.local.at[0]),
        pltpu.make_async_copy(r.far_slope, r.slope, r.local.at[1]),
        pltpu.make_async_copy(r.far_g, g1, r.local.at[2]),
    ]

    def hidden_grad(weight, dy, da, i):
        at = rows_of(i, chunk)
        du = nt(plane_of(weight, 1, i), dy[...])
        low = (du * r.slope[at].astype(F32)).astype(LOW)
        da[at] = low
        return low

    def weight_grads(h_ref, dy, low, i):
        at = rows_of(i, chunk)
        g0[1, i] = nn(r.act[at], dy[...]).astype(LOW).reshape(g0.shape[2:])
        g0[0, i] = nn(low, h_ref[...]).astype(LOW).reshape(g0.shape[2:])

    def by_planes(grads, pieces, hooks):
        if not inside:
            pl.loop(0, hidden // chunk)(grads)
            return
        for n, d in enumerate(range(deep - 1, -1, -1)):
            grads((1 - core) * deep + route.plane(d))
            for piece in pieces:
                piece.leave(d)
            hooks(n)
        for n, d in enumerate(range(deep - 1, -1, -1)):
            grads(core * deep + route.plane(d))
            for piece in pieces:
                piece.step_one(d)
            hooks(deep + n)

    def middle(slope_z, da, dh):
        low, dy, h4 = r.d_conv_in.at[:, pl.ds(0, width)], r.d_conv_in.at[:, pl.ds(width, width)], r.d_att
        dc = r.d_conv_out if inside else r.spare
        x3, x4 = r.input_grad, r.dz

        @pl.loop(0, rows // block)
        def _(i):
            at = rows_of(i, block)
            z = (r.depth[at] - mean) * spread * gain6 + vec[7:8]
            u, slope = activate(z)
            low[at] = u.astype(LOW)
            slope_z[at] = slope

        @pl.loop(0, rows // 256)
        def _(i):
            at = rows_of(i, 256)
            x3[at] = r.x2[at] + nn(low[at], r.conv_out[...])

        def put_h4(at, value):
            h4[at] = value

        norm_rows(x3, put_h4, vec, 8)

        @pl.loop(0, hidden // chunk)
        def _(i):
            at = rows_of(i, chunk)
            u, slope = activate(nt(plane_of(g1, 0, i), h4[...]))
            r.act[at] = u.astype(LOW)
            r.slope[at] = slope.astype(LOW)

        @pl.loop(0, rows // 256)
        def _(i):
            at = rows_of(i, 256)
            x4[at] = x3[at] + 0.5 * tn(r.act[:, at], whole_of(g1, 1))

        def last(i, carry):
            gain, bias = carry
            at = rows_of(i, block)
            hat, rate = normed(x4[at])
            r.out[at] = (hat * vec[10:11] + vec[11:12]).astype(LOW)
            g = r.cot[at].astype(F32)
            back = normed_back(g * vec[10:11], hat, rate)
            r.grad[at] = back
            dy[at] = (0.5 * back).astype(LOW)
            return gain + fold(g * hat), bias + fold(g)

        gain, bias = lax.fori_loop(0, rows // block, last, (zero8, zero8))
        sums[10:11] = jnp.sum(gain, 0, keepdims=True)
        sums[11:12] = jnp.sum(bias, 0, keepdims=True)
        @pl.loop(0, hidden // chunk)
        def _(i):
            hidden_grad(g1, dy, da, i)

        @pl.loop(0, rows // 256)
        def _(i):
            at = rows_of(i, 256)
            dh[at] = tn(da[:, at], whole_of(g1, 0))

        back_copies[2].start()

        def put(at, value):
            r.grad[at] = value
            dc[at] = value.astype(LOW)

        norm_rows_back(dh, x3, r.grad, put, vec, sums, 8)

        @pl.loop(0, rows // 256)
        def _(i):
            at = rows_of(i, 256)
            r.dz[at] = nt(dc[at], r.conv_out[...])

        def close(i, carry):
            one, two = carry
            at = rows_of(i, block)
            here = r.dz[at] * slope_z[at]
            r.dz[at] = here
            return one + fold(here), two + fold(here * (r.depth[at] - mean))

        one, two = lax.fori_loop(0, rows // block, close, (zero8, zero8))
        r.part_b[...] = to_tile(
            jnp.concatenate([jnp.sum(one, 0, keepdims=True), jnp.sum(two, 0, keepdims=True)], axis=0)
        )
        every = Everyone(count, r.pair_b, r.slots_b, r.pair_sems_b, r.sends_b, r.recvs_b)
        every.start(r.part_b)
        got = tn(low[...], dc[...]).astype(LOW)
        if inside:
            r.box[0, :, :, :, 0:16] = got.reshape(*r.box.shape[1:4], 16, width)
        else:
            r.d_conv_out[...] = got
        by_planes(
            lambda i: weight_grads(h4, dy, da[rows_of(i, chunk)], i), [ffn1] if inside else None, lambda n: None
        )
        back_copies[0].start()
        back_copies[1].start()
        r.part_b[...] = every.total()

    square = (rows, width)
    vm = pltpu.VMEM
    pl.run_scoped(
        middle, vm(square, F32), vm((hidden, rows), LOW), vm(square, F32),
    )
    leaving = {
        name: pltpu.make_async_copy(getattr(r, name), getattr(r, "far_" + name), r.local.at[20 + n])
        for n, name in enumerate(("out", "input_grad", "d_conv_out", "d_conv_in", "d_att"))
    }
    leaving["out"].start()
    if not inside:
        copy = pltpu.make_async_copy(g0, r.d_ffn.at[1], r.local.at[3])
        copy.start()
        copy.wait()
    tile = r.part_b[...]
    grad_sum, grad_moment = from_tile(tile, 0, width), from_tile(tile, 1, width)
    if inside:
        put_off(planes_of(ffn1), 1, {ffn1: end_ffn1})
    var_grad = -0.5 * (gain6 * grad_moment) * spread * spread * spread
    flat = (-(gain6 * spread * grad_sum) - 2.0 * mean * var_grad) / number
    tilt = 2.0 * var_grad / number

    def convolution_back(back, datt):
        dp, dh = r.d_conv_in if inside else r.spare_wide, r.input_grad
        left, right = r.dz, r.depth

        @pl.loop(0, rows // block)
        def _(i):
            at = rows_of(i, block)
            _, ok = valid_rows(scal, i * block, block)
            back[pl.ds(pl.multiple_of(i * block + HALO, HALO), block)] = gain6 * spread * r.dz[at] + ok * (
                flat + r.depth[at] * tilt
            )

        swap = to_core(back.at[edge], r.halo.at[1], r.swap.at[6], r.swap.at[7], 1 - core)
        swap.start()
        convolve_weight(r.pad, back, HALO, r.small.at[pl.ds(0, taps)], lambda tap: tap + 1, rows, width, ticks(0, 0, 1, 0))

        @pl.loop(0, rows // 256)
        def _(i):
            at = rows_of(i, 256)
            left[at] = nn(r.h3[at], r.conv_in[:, :width])
            right[at] = nn(r.h3[at], r.conv_in[:, width:])

        swap.wait()
        place_halo(back, r.halo.at[1], core)

        def put(at_row, high, lane, total):
            at = slice(at_row, at_row + high)
            _, ok = valid_rows(scal, at_row, high)
            gate = sigmoid(right[at, lane : lane + 128])
            total = total * gate * ok
            dp[at, lane : lane + 128] = total.astype(LOW)
            dp[at, width + lane : width + lane + 128] = (
                total * left[at, lane : lane + 128] * (1.0 - gate)
            ).astype(LOW)

        convolve(back, r.wide, put, lambda tap: taps - 1 - tap, rows, width, ticks(0, 1, 1, 0))
        got = tn(r.h3[...], dp[...]).astype(LOW)
        if inside:
            r.box[0, :, :, :, 16:32] = got[:, :width].reshape(*r.box.shape[1:4], 16, width)
            r.box[0, :, :, :, 32:48] = got[:, width:].reshape(*r.box.shape[1:4], 16, width)
        else:
            r.d_conv_in[...] = got

        @pl.loop(0, rows // 256)
        def _(i):
            at = rows_of(i, 256)
            dh[at] = nt(dp[at], r.conv_in[...])

        def put_first(at, got):
            r.grad[at] = got
            datt[at] = got.astype(LOW)

        norm_rows_back(dh, r.x2, r.grad, put_first, vec, sums, 4)
        tick(2)
        got = nn(r.oT[...], datt[...]).astype(LOW)
        if inside:
            r.box[0, :, :, :, 48:64] = got.reshape(*r.box.shape[1:4], 16, width)
            rest.start()
        else:
            r.d_att[...] = got
        r.doT[...] = nt(r.w_att[...], datt[...]).astype(LOW).reshape(heads, size, rows)

    pl.run_scoped(
        convolution_back, vm(r.pad.shape, F32), vm(square, LOW),
    )

    def attend_back(delta, qside, oside, grads, dk, dv):
        lows = r.conv_in
        dqT = r.d_conv_out if inside else r.spare

        for head in range(heads):
            o = r.oT[head * size : (head + 1) * size].astype(F32)
            delta[head : head + 1] = jnp.sum(o * r.doT[head].astype(F32), 0, keepdims=True)

        def hook(pair):
            if inside:
                @pl.when(pair == 1)
                def _():
                    for d in range(deep - 1, -1, -1):
                        rest.step_one(d)
                    tick(2)

                @pl.when(pair == 2)
                def _():
                    put_off(planes_of(rest), 2, {rest: functools.partial(end_box, 0, rest)})
                    tick(1)
                    rests = queue[1:]
                    tick_rest = [rests.pop(0), rests.pop(0)]
                    queue[1:] = rests
                    for thunk in tick_rest:
                        thunk()

                @pl.when(pair == 3)
                def _():
                    tick(1)
                    tick(4)

        def done(pair):
            to_core(dk.at[pair, theirs], r.rk.at[pair], r.swap.at[8], r.swap.at[9], 1 - core).start()
            to_core(dv.at[pair, theirs], r.rv.at[pair], r.swap.at[10], r.swap.at[11], 1 - core).start()

        attention_backward(
            r.qT, r.key, r.h_all, r.qkvT, r.extra, r.doT, delta, r.top, dqT, dk, dv, qside, oside, lows, grads,
            scale, shrink, hook, done,
        )
        r.dq[...] = dqT[...].astype(F32).T.astype(LOW)
        to_core(dk.at[:, theirs], r.rk, r.swap.at[8], r.swap.at[9], 1 - core).wait()
        to_core(dv.at[:, theirs], r.rv, r.swap.at[10], r.swap.at[11], 1 - core).wait()
        for pair in range(pairs):
            lanes = slice(pair * 128, (pair + 1) * 128)
            r.h3[:, lanes] = (dk[pair, own].astype(F32) + r.rk[pair].astype(F32)).astype(LOW)
            r.own_v[:, lanes] = (dv[pair, own].astype(F32) + r.rv[pair].astype(F32)).astype(LOW)

    pl.run_scoped(
        attend_back, vm((heads, rows), F32), vm((2, 256, rows), LOW), vm((2, 256, rows), LOW),
        vm((keys // 2, 2 * rows), LOW),
        vm((pairs, keys, 128), LOW), vm((pairs, keys, 128), LOW),
    )
    if inside:
        tick(len(queue))
        third.plane_one(0)

    def put_qkv(s, got):
        if inside:
            for c in range(2):
                v = got[:, c * half : (c + 1) * half].reshape(count, 2, 16, half)
                r.box[1, c * deep : (c + 1) * deep, :, :, s * 16 : (s + 1) * 16] = jnp.concatenate(
                    [v[:, 0], v[:, 1]], axis=-1
                ).reshape(deep, 2, 2, 16, width)
        else:
            r.d_qkv[s] = got

    def project_back(dh, dy, da, x0):
        own_k, own_v = r.h3, r.own_v
        h2 = r.h_all[own]
        put_qkv(0, tn(h2, r.dq[...]).astype(LOW))
        put_qkv(1, tn(h2, own_k[...]).astype(LOW))
        put_qkv(2, tn(h2, own_v[...]).astype(LOW))
        if inside:
            r.small[taps : taps + 16] = sums[...]
            blank = jnp.zeros((16, width), LOW)
            for n in range(4):
                full = n < (taps + 16) // 16
                r.box[1, 0, n // 2, n % 2, 48:64] = r.small[n * 16 : (n + 1) * 16].astype(LOW) if full else blank
            r.box[1, 1:, :, :, 48:64] = jnp.zeros((2 * deep - 1, 2, 2, 16, width), LOW)
            proj.start()
        @pl.loop(0, rows // 256)
        def _(i):
            at = rows_of(i, 256)
            dh[at] = nn(r.dq[at], r.qkvT[0]) + nn(own_k[at], r.qkvT[1]) + nn(own_v[at], r.qkvT[2])

        def put_second(at, got):
            r.grad[at] = got
            dy[at] = (0.5 * got).astype(LOW)

        norm_rows_back(dh, r.x1, r.grad, put_second, vec, sums, 2)
        if inside:
            third.plane_two(0)
            ffn1.sent(0)
        for copy in back_copies:
            copy.wait()

        def hooks(n):
            if n == 3:
                put_off(planes_of(proj) + planes_of(out0, in0), 2, {proj: functools.partial(end_box, 1, proj), in0: end_ffn0})
                for d in (1, 2, 3):
                    third.plane_one(d)
                tick(1)
            if n == 5:
                tick(1)
            if n == 7:
                tick(2)
                third.plane_two(1)
                third.plane_two(2)

        if inside:
            for d in range(deep - 1, -1, -1):
                proj.step_one(d)
        by_planes(lambda i: weight_grads(r.h0, dy, hidden_grad(g1, dy, da, i), i), [out0, in0] if inside else None, hooks)
        tick(1)
        if inside:
            third.plane_two(3)
        masked_input(scal, r.x_in, x0)

        @pl.loop(0, rows // 256)
        def _(i):
            at = rows_of(i, 256)
            dh[at] = tn(da[:, at], whole_of(g1, 0))

        tick(2)
        if inside:
            for d in range(deep):
                third.plane_last(d)

        def put_input(at, got):
            r.input_grad[at] = got * keep_rows(scal, at.start, block, width)

        norm_rows_back(dh, x0, r.grad, put_input, vec, sums, 0)

    def tail(dy, da):
        dh, x0 = r.dz, r.x2
        project_back(dh, dy, da, x0)
        leaving["input_grad"].start()
        if not inside:
            return
        while len(queue) > 15:
            tick(1)
        fourth.plane_one(0)
        r.part_c[...] = to_tile(sums[0:4])
        every = Everyone(count, r.pair_c, r.slots_c, r.pair_sems_c, r.sends_c, r.recvs_c)
        every.start(r.part_c)
        tick(4)
        fourth.plane_two(0)
        tick(3)
        for d in (1, 2, 3):
            fourth.plane_one(d)
        for d in range(deep):
            third.plane_other(d)
        tick(2)
        got = r.held[0]
        r.d_conv_out[...] = got[:, :, :, 0:16].reshape(width, width)
        r.d_conv_in[:, :width] = got[:, :, :, 16:32].reshape(width, width)
        r.d_conv_in[:, width:] = got[:, :, :, 32:48].reshape(width, width)
        r.d_att[...] = got[:, :, :, 48:64].reshape(width, width)
        for name in ("d_conv_out", "d_conv_in", "d_att"):
            leaving[name].start()
        tick(2)
        for d in (1, 2, 3):
            fourth.plane_two(d)
        tick(len(queue))
        for d in range(deep):
            fourth.plane_last(d, False)
        few = r.held.at[1, 0, :, :, pl.ds(48, 16)]
        cross = to_core(few, few, fourth.sends.at[2], fourth.recv.at[3, 0], 1 - core)
        pl.when(core == 0)(cross.start)
        tile = every.total()
        got = r.held[1, pl.ds(core * deep, deep)].reshape(count, 64, width)
        for s in range(3):
            v = got[:, s * 16 : (s + 1) * 16]
            v = jnp.concatenate([v[:, None, :, :half], v[:, None, :, half:]], axis=1)
            r.d_qkv[s] = v.reshape(width, half)
        pl.when(core == 1)(cross.wait_recv)
        got = r.held[1, 0, :, :, 48:64].reshape(64, width).astype(F32)
        r.d_kern[...] = got[:taps]
        r.d_vec[...] = jnp.concatenate(
            [
                *[from_tile(tile, n, width) for n in range(4)], got[taps + 4 : taps + 6],
                spread * grad_moment, grad_sum, got[taps + 8 : taps + 12],
            ],
            axis=0,
        )
        third.finish()
        fourth.finish(False)
        pl.when(core == 0)(cross.wait_send)
        for piece in stages:
            for kind in range(4):
                if kind or piece is not ffn1:
                    piece.sent(kind)

    pl.run_scoped(
        tail, vm(square, LOW), vm((hidden, rows), LOW),
    )
    if not inside:
        for name in ("d_conv_out", "d_conv_in", "d_att"):
            leaving[name].start()
        r.small[taps : taps + 16] = sums[...]
        r.small[taps + 6 : taps + 7] = spread * grad_moment
        r.small[taps + 7 : taps + 8] = grad_sum
        copy = pltpu.make_async_copy(g0, r.d_ffn.at[0], r.local.at[3])
        copy.start()
        copy.wait()
    for copy in leaving.values():
        copy.wait()


def gather_steps(route, chunk, held, sends, recv, with_core=True):
    started = []
    core, count = route.core, route.count

    def block(place):
        return core * count + place

    def arrive(place):
        here = held.at[chunk, block(place)]
        to_batch(here, here, recv.at[chunk, block(place)], recv.at[chunk, block(place)], route.me).wait_recv()

    def send(place, target):
        slot = len(started)
        here = held.at[chunk, block(place)]
        copy = to_batch(here, here, sends.at[chunk, slot], recv.at[chunk, block(place)], target)
        copy.start()
        started.append(copy)

    def cross(place):
        if not with_core:
            return
        slot = len(started)
        here = held.at[chunk, block(place)]
        copy = to_core(here, here, sends.at[chunk, slot], recv.at[chunk, block(place)], 1 - core)
        copy.start()
        started.append(copy)

    def step_mid():
        for k in range(1, route.deep):
            send(route.me, route.index(lax.rem(route.z + k, route.deep), route.p, route.q))
        cross(route.me)

    def step_one():
        for d in range(route.deep):
            z = lax.rem(route.z + d, route.deep)
            place = route.index(z, route.p, route.q)
            if d:
                arrive(place)
            for k in range(1, route.side):
                send(place, route.index(route.z, lax.rem(route.p + k, route.side), route.q))
            if d:
                cross(place)

    def step_two():
        for d in range(route.deep):
            z = lax.rem(route.z + d, route.deep)
            for e in range(route.side):
                p = lax.rem(route.p + e, route.side)
                place = route.index(z, p, route.q)
                if e:
                    arrive(place)
                for k in range(1, route.side):
                    send(place, route.index(route.z, route.p, lax.rem(route.q + k, route.side)))
                if e:
                    cross(place)

    def step_last():
        for d in range(route.deep):
            z = lax.rem(route.z + d, route.deep)
            for e in range(route.side):
                p = lax.rem(route.p + e, route.side)
                for f in range(1, route.side):
                    place = route.index(z, p, lax.rem(route.q + f, route.side))
                    arrive(place)
                    cross(place)

    def step_end():
        if with_core:
            for place in range(count):
                other = held.at[chunk, (1 - core) * count + place]
                at = recv.at[chunk, (1 - core) * count + place]
                to_core(other, other, at, at, 1 - core).wait_recv()
        for copy in started:
            copy.wait_send()

    return [step_mid, step_one, step_two, step_last, step_end]


def sends_of(route):
    return (route.deep - 1) + route.deep * (route.side - 1) * (1 + route.side) + route.count


def run_steps(all_steps):
    depth = len(all_steps[0])
    for turn in range(depth + len(all_steps) - 1):
        for chunk, steps in enumerate(all_steps):
            if 0 <= turn - chunk < depth:
                steps[turn - chunk]()


def gather_kernel(count, mine, held, local, sends, recv):
    route = Routes(count).here()
    chunks = mine.shape[0]
    copies = []
    for chunk in range(chunks):
        own = held.at[chunk, route.core * count + route.me]
        copy = pltpu.make_async_copy(mine.at[chunk], own, local.at[chunk])
        copy.start()
        copies.append(copy)
    route.greet()
    for copy in copies:
        copy.wait()
    run_steps([gather_steps(route, chunk, held, sends, recv) for chunk in range(chunks)])


def gather_all(mine, count, collective_id):
    chunks, rows, width = mine.shape
    route = Routes(count)
    return pl.pallas_call(
        functools.partial(gather_kernel, count),
        out_shape=jax.ShapeDtypeStruct((chunks, 2 * count, rows, width), mine.dtype),
        in_specs=[pl.BlockSpec(memory_space=pltpu.VMEM)],
        out_specs=pl.BlockSpec(memory_space=pltpu.VMEM),
        scratch_shapes=[
            pltpu.SemaphoreType.DMA((chunks,)),
            pltpu.SemaphoreType.DMA((chunks, sends_of(route))),
            pltpu.SemaphoreType.DMA((chunks, 2 * count)),
        ],
        compiler_params=pltpu.CompilerParams(
            collective_id=collective_id, has_side_effects=True, vmem_limit_bytes=VMEM_BYTES
        ),
    )(mine)


def reduce_kernel(count, solo, n, *refs):
    pieces, (fin, held, grads, packing, *rest) = refs[:n], refs[n:]
    copies = []
    at = 0
    for i, piece in enumerate(pieces):
        lines = piece.shape[1]
        copy = pltpu.make_async_copy(piece, grads.at[:, pl.ds(at, lines)], packing.at[i])
        copy.start()
        copies.append(copy)
        at += lines
    for copy in copies:
        copy.wait()
    reduce_packed(count, solo, grads, fin, held, *rest)


def reduce_packed(count, solo, grads, fin, held, zero, one, two, three, s0, r0, s1, r1, s2, r2, s3, r3, sends, recv):
    route = Routes(count).here()
    core, me, side, deep = route.core, route.me, route.side, route.deep
    rows, width = grads.shape[1:]
    piece = 16

    def add(target, source):
        @pl.loop(0, rows // piece)
        def _(i):
            at = pl.ds(pl.multiple_of(i * piece, piece), piece)
            target[at] = (target[at].astype(jnp.float32) + source[at].astype(jnp.float32)).astype(target.dtype)

    route.greet()
    waits = []
    order = []
    for f in range(side - 1, -1, -1):
        for d in range(deep):
            for e in range(side - 1, -1, -1):
                order.append((d, e, f))
    for d, e, f in order:
        place = route.index(lax.rem(route.z + d, deep), lax.rem(route.p + e, side), lax.rem(route.q + f, side))
        copy = to_core(grads.at[(1 - core) * count + place], zero.at[place], s0.at[place], r0.at[place], 1 - core)
        copy.start()
        waits.append(copy)
    for e in range(side - 1, -1, -1):
        for d in range(deep):
            for f in range(side - 1, -1, -1):
                z, p, q = lax.rem(route.z + d, deep), lax.rem(route.p + e, side), lax.rem(route.q + f, side)
                place = route.index(z, p, q)
                to_core(zero.at[place], zero.at[place], s0.at[place], r0.at[place], 1 - core).wait_recv()
                add(zero.at[place], grads.at[core * count + place])
                if e:
                    slot = (e - 1) * deep * side + z * side + q
                    copy = to_batch(
                        zero.at[place], one.at[slot], s1.at[slot], r1.at[slot], route.index(route.z, p, route.q)
                    )
                    copy.start()
                    waits.append(copy)
    for f in range(side - 1, -1, -1):
        for d in range(deep):
            z, q = lax.rem(route.z + d, deep), lax.rem(route.q + f, side)
            place = route.index(z, route.p, q)
            for e in range(1, side):
                slot = (e - 1) * deep * side + z * side + q
                to_batch(one.at[slot], one.at[slot], s1.at[slot], r1.at[slot], me).wait_recv()
                add(zero.at[place], one.at[slot])
            if f:
                slot = (f - 1) * deep + z
                copy = to_batch(
                    zero.at[place], two.at[slot], s2.at[slot], r2.at[slot], route.index(route.z, route.p, q)
                )
                copy.start()
                waits.append(copy)
    for d in range(deep - 1, -1, -1):
        z = lax.rem(route.z + d, deep)
        place = route.index(z, route.p, route.q)
        for f in range(1, side):
            slot = (f - 1) * deep + z
            to_batch(two.at[slot], two.at[slot], s2.at[slot], r2.at[slot], me).wait_recv()
            add(zero.at[place], two.at[slot])
        if d:
            copy = to_batch(zero.at[place], three.at[d - 1], s3.at[d - 1], r3.at[d - 1], place)
            copy.start()
            waits.append(copy)
    for d in range(1, deep):
        to_batch(three.at[d - 1], three.at[d - 1], s3.at[d - 1], r3.at[d - 1], me).wait_recv()

    def final(at):
        total = zero[me, at].astype(jnp.float32)
        for d in range(1, deep):
            total = total + three[d - 1, at].astype(jnp.float32)
        return total

    mine = core * count + me

    @pl.loop(0, (rows - solo) // piece)
    def _(i):
        at = pl.ds(pl.multiple_of(i * piece, piece), piece)
        held[0, mine, at] = final(pl.ds(pl.multiple_of(solo + i * piece, piece), piece)).astype(held.dtype)

    steps = gather_steps(route, 0, held, sends, recv)
    steps[0]()

    @pl.loop(0, solo // piece)
    def _(i):
        at = pl.ds(pl.multiple_of(i * piece, piece), piece)
        fin[at] = final(at)

    for step in steps[1:]:
        step()
    for copy in waits:
        copy.wait_send()


def reduce_all(pieces, solo, count, collective_id):
    blocks, _, width = pieces[0].shape
    kind = pieces[0].dtype
    if any(piece.shape[1] % 16 for piece in pieces):
        used = sum(piece.shape[1] for piece in pieces)
        spare = jnp.zeros((blocks, -used % 16, width), kind)
        pieces = [jnp.concatenate([*pieces, spare], axis=1)]
    rows = sum(piece.shape[1] for piece in pieces)
    route = Routes(count)
    side, deep = route.side, route.deep
    n1 = max(1, (side - 1) * side * deep)
    n2 = max(1, (side - 1) * deep)
    n3 = max(1, deep - 1)
    dma = pltpu.SemaphoreType.DMA
    return pl.pallas_call(
        functools.partial(reduce_kernel, count, solo, len(pieces)),
        out_shape=(
            jax.ShapeDtypeStruct((solo, width), jnp.float32),
            jax.ShapeDtypeStruct((1, blocks, rows - solo, width), kind),
        ),
        in_specs=[pl.BlockSpec(memory_space=pl.ANY)] * len(pieces),
        out_specs=(pl.BlockSpec(memory_space=pltpu.VMEM), pl.BlockSpec(memory_space=pltpu.VMEM)),
        scratch_shapes=[
            pltpu.VMEM((blocks, rows, width), kind),
            dma((len(pieces),)),
            pltpu.VMEM((count, rows, width), kind),
            pltpu.VMEM((n1, rows, width), kind),
            pltpu.VMEM((n2, rows, width), kind),
            pltpu.VMEM((n3, rows, width), kind),
            dma((count,)), dma((count,)),
            dma((n1,)), dma((n1,)),
            dma((n2,)), dma((n2,)),
            dma((n3,)), dma((n3,)),
            dma((1, sends_of(route))), dma((1, blocks)),
        ],
        compiler_params=pltpu.CompilerParams(
            collective_id=collective_id, has_side_effects=True, vmem_limit_bytes=VMEM_BYTES
        ),
    )(*pieces)


def last_kernel(count, *refs):
    for source, target in zip(refs[:count], refs[count:]):
        target[...] = source[...].astype(target.dtype)


def per_device(
    block_input, lengths, spans, cotangent, ffn_in, ffn_out, qkv_weight, out_weight, conv_in, kernel, conv_out, vectors,
):
    _, rows, width = block_input.shape
    count = lax.axis_size("batch")
    core = lax.axis_index("seq")
    shard = ffn_in.shape[1]
    blocks = 2 * count
    hidden = shard * blocks
    heads, size = HEADS, width // HEADS
    keys = 2 * rows
    taps = kernel.shape[0]
    inside = shard % 64 == 0 and width == 16 * blocks
    route = Routes(count)
    vm, dma = pltpu.VMEM, pltpu.SemaphoreType.DMA
    weights = (2, 8, 2, 2, hidden // 32, width)
    if inside:
        shards = dict(ffn_in=ffn_in, ffn_out=ffn_out)
    else:
        got = jnp.stack([ffn_in, ffn_out], axis=1).reshape(2, 2 * shard, width)
        got = gather_all(got, count, 1).reshape(2, blocks, 2, shard, width)
        shards = dict(shards=got.transpose(0, 2, 1, 3, 4).reshape(2, *weights))
    square, tall = (rows, width), (hidden, rows)
    here, hbm = pl.BlockSpec(memory_space=pltpu.VMEM), pl.BlockSpec(memory_space=pl.ANY)
    scalars = dict(lengths=lengths, spans=spans)
    late = dict(x_in=block_input[0], vec=vectors, kern=kernel, cot=cotangent[0], w_att=out_weight, conv_in=conv_in, conv_out=conv_out, qkv=qkv_weight)
    ins = scalars | {f"{key}_far": value for key, value in late.items()} | shards
    in_specs = [pl.BlockSpec(memory_space=pltpu.SMEM)] * len(scalars)
    in_specs += [hbm] * (len(late) + len(shards))
    lent = dict(
        out=(square, LOW), input_grad=(square, F32), d_att=((width, width), LOW), d_conv_in=((width, 2 * width), LOW),
        d_conv_out=((width, width), LOW),
    )
    outs = {f"far_{key}": (*value, hbm) for key, value in lent.items()} | dict(
        far_g=(weights, LOW, hbm), far_act=(tall, LOW, hbm), far_slope=(tall, LOW, hbm),
    )
    if inside:
        outs |= dict(
            fin_in=((2, shard, width), F32, here), fin_out=((2, shard, width), F32, here),
            d_qkv=((3, width, width // 2), LOW, here), d_kern=((taps, width), F32, here), d_vec=((12, width), F32, here),
        )
    else:
        outs |= dict(
            d_qkv=((3, width, width), LOW, here), small=((taps + 16, width), F32, here),
            d_ffn=((2, *weights), LOW, hbm),
        )
    scratch = dict(
        g0=vm(weights, LOW), g1=vm(weights, LOW), act=vm(tall, LOW), slope=vm(tall, LOW), qkvT=vm((3, width, width), LOW),
        x1=vm(square, F32), x2=vm(square, F32), grad=vm(square, F32), depth=vm(square, F32),
        dz=vm(square, F32), pad=vm((rows + 2 * HALO, width), F32), halo=vm((2, HALO, width), F32),
        h0=vm(square, LOW), h_all=vm((keys, width), LOW), h3=vm(square, LOW), key=vm((heads // 2, keys, 128), LOW),
        qT=vm((heads, size, rows), LOW), oT=vm((width, rows), LOW), doT=vm((heads, size, rows), LOW),
        top=vm((heads, rows), F32), extra=vm((keys, 128), LOW), wide=vm((taps, 8, width), F32), sums=vm((16, width), F32),
        own_v=vm(square, LOW),
        rk=vm((heads // 2, rows, 128), LOW), rv=vm((heads // 2, rows, 128), LOW), dq=vm(square, LOW),
        x_in=vm(square, LOW), vec=vm((12, width), F32), kern=vm((taps, width), F32), **{k: vm(*v) for k, v in lent.items()},
        local=dma((26,)), swap=dma((12,)), qkv_mine=vm(qkv_weight.shape, LOW), cot=vm(square, LOW),
        w_att=vm((width, width), LOW), conv_in=vm((width, 2 * width), LOW), conv_out=vm((width, width), LOW),
    )
    for name, lines in (("a", 16), ("b", 8), ("c", 16))[: 3 if inside else 2]:
        scratch[f"part_{name}"] = vm((lines, 128), F32)
        for key, kind in zip(("pair", "slots", "pair_sems", "sends", "recvs"), Everyone.scratch(count, lines)):
            scratch[f"{key}_{name}"] = kind
    if not inside:
        scratch |= dict(spare=vm((width, rows), LOW), spare_wide=vm((rows, 2 * width), LOW))
    if inside:
        for key, shape in zip(("zero", "one", "two", "three"), ((4, 2, 2), (4, 2), (4,), (3,))):
            scratch[key] = vm((6, *shape, shard, width), LOW)
        scratch |= dict(
            box=vm((2, 8, 2, 2, 64, width), LOW), held=vm((2, 8, 2, 2, 64, width), LOW), small=vm((taps + 16, width), F32),
            g_send=dma((4, 11)), g_recv=dma((4, 4, 4)), r_send=dma((5, 4)), r_recv=dma((5, 4, 4)),
        )
    cfg = SimpleNamespace(
        names=[*ins, *outs, *scratch], count=count, shard=shard, hidden=hidden, heads=heads, inside=inside
    )
    results = pl.pallas_call(
        functools.partial(layer_kernel, cfg),
        out_shape=tuple(jax.ShapeDtypeStruct(shape, kind) for shape, kind, _ in outs.values()),
        in_specs=in_specs,
        out_specs=tuple(spec for _, _, spec in outs.values()),
        scratch_shapes=list(scratch.values()),
        compiler_params=pltpu.CompilerParams(collective_id=0, has_side_effects=True, vmem_limit_bytes=VMEM_BYTES),
    )(*ins.values())
    got = SimpleNamespace(**dict(zip(outs, results)))
    if inside:
        plain = [got.far_out, got.far_input_grad, got.fin_in, got.fin_out, got.d_kern, got.d_vec]
        wide = [got.d_qkv, got.far_d_att, got.far_d_conv_in, got.far_d_conv_out]
        shapes = [(v.shape, v.dtype) for v in plain] + [(v.shape, F32) for v in wide]
        steps = 4

        def part(shape):
            if shape[-2] % (8 * steps):
                return pl.BlockSpec(shape, lambda i: (0,) * len(shape))
            lines = shape[-2] // steps
            return pl.BlockSpec((*shape[:-2], lines, shape[-1]), lambda i: (0,) * (len(shape) - 2) + (i, 0))

        parts = [part(shape) for shape, _ in shapes]
        done = pl.pallas_call(
            functools.partial(last_kernel, len(shapes)),
            grid=(steps,),
            out_shape=tuple(jax.ShapeDtypeStruct(*shape) for shape in shapes),
            in_specs=parts,
            out_specs=tuple(parts),
            compiler_params=pltpu.CompilerParams(vmem_limit_bytes=VMEM_BYTES),
        )(*plain, *wide)
        out, input_grad, fin_in, fin_out, d_kern, d_vec, d_qkv, d_att, d_conv_in, d_conv_out = done
        return (
            out[None], input_grad[None], fin_in, fin_out, d_qkv, d_att, d_conv_in, d_kern, d_conv_out, d_vec,
        )

    def spread(values):
        flat = values.astype(LOW).reshape(-1, width)
        lines = -(-flat.shape[0] // blocks)
        flat = jnp.pad(flat, ((0, lines * blocks - flat.shape[0]), (0, 0)))
        return flat.reshape(blocks, lines, width)

    lines = 3 * width // (2 * count)
    per_core = got.d_qkv.reshape(3 * width, 2, width // 2).transpose(1, 0, 2).reshape(blocks, -1, width)
    d_in0, d_out0, d_in1, d_out1 = (got.d_ffn[j, m].reshape(hidden, width) for j in range(2) for m in range(2))
    rest = (got.far_d_att, got.far_d_conv_in, got.far_d_conv_out, got.small)
    pieces = [spread(v) for v in (d_in0, d_out0, d_in1, d_out1, *rest)] + [per_core]
    fin, shared = reduce_all(pieces, 4 * shard, count, 2)
    at = 0
    whole = []
    for piece, like in zip(pieces[4:8], rest):
        part = shared[0, :, at : at + piece.shape[1]].reshape(-1, width)
        whole.append(part[: like.size // width].reshape(like.shape).astype(F32))
        at += piece.shape[1]
    mine = lax.dynamic_slice_in_dim(shared[0], core * count, count, axis=0)[:, at : at + per_core.shape[1]]
    row = lax.broadcasted_iota(jnp.int32, (12, 1), 0)
    d_vec = jnp.where((row == 6) | (row == 7), got.small[taps : taps + 12], whole[3][taps : taps + 12])
    return (
        got.far_out[None], got.far_input_grad[None], jnp.stack([fin[:shard], fin[2 * shard : 3 * shard]]),
        jnp.stack([fin[shard : 2 * shard], fin[3 * shard :]]),
        mine.reshape(3, width, width // 2).astype(F32), whole[0], whole[1], whole[3][:taps], whole[2], d_vec,
    )


def solution(mesh):
    placed = (
        P("batch", "seq", None),
        P("batch"),
        P("batch", None),
        P("batch", "seq", None),
        P(None, ("seq", "batch"), None),
        P(None, ("seq", "batch"), None),
        P(None, None, "seq"),
        P(),
        P(),
        P(),
        P(),
        P(),
    )
    return jax.shard_map(
        per_device,
        mesh=mesh,
        in_specs=placed,
        out_specs=(
            P("batch", "seq", None),
            P("batch", "seq", None),
            P(None, ("seq", "batch"), None),
            P(None, ("seq", "batch"), None),
            P(None, None, "seq"),
            P(),
            P(),
            P(),
            P(),
            P(),
        ),
        check_vma=False,
    )
```

```python
import functools
import math
from types import SimpleNamespace

import jax
import jax.numpy as jnp
from jax import lax
from jax.experimental import pallas as pl
from jax.experimental.pallas import tpu as pltpu
from jax.sharding import PartitionSpec as P

HEADS = 8
MESH = pl.DeviceIdType.MESH
VMEM_BYTES = 63 * 1024 * 1024
F32, LOW = jnp.float32, jnp.bfloat16
EPS = 1e-05
HALO = 16


class Routes:
    def __init__(self, count):
        if count == 16:
            first, last, middle = (1, 2), (2, 2), (4, 4)
        elif count == 128:
            first, last, middle = (1, 4), (32, 4), (4, 8)
        else:
            first, last, middle = (1, 1), (1, 1), (1, count)
        self.count = count
        self.side = first[1]
        self.deep = middle[1]
        self.first, self.last, self.middle = first, last, middle

    def here(self):
        self.core = lax.axis_index("seq")
        self.me = lax.axis_index("batch")
        turn = self.core * (self.last[0] - self.first[0])
        self.one = self.first[0] + turn
        self.two = self.last[0] - turn
        self.mid = self.middle[0]
        self.p = lax.rem(lax.div(self.me, self.one), self.side)
        self.q = lax.rem(lax.div(self.me, self.two), self.side)
        self.z = lax.rem(lax.div(self.me, self.mid), self.deep)
        return self

    def index(self, z, p, q):
        return z * self.mid + p * self.one + q * self.two

    def plane(self, d):
        if self.deep != 4 or d == 0:
            return lax.rem(self.z + d, self.deep) if d else self.z
        return (self.z + 1 - 2 * lax.rem(self.z, 2), lax.rem(self.z + 2, 4), 3 - self.z)[d - 1]

    def reach(self, i):
        far = lax.div(self.z, 2)
        first = self.z + far * (3 - 2 * self.z)
        turn = (first, 1 - first, 2, 3)[i]
        return turn + far * (3 - 2 * turn)

    def near(self, d, e, f):
        p = lax.rem(self.p + e, self.side) if e else self.p
        q = lax.rem(self.q + f, self.side) if f else self.q
        return self.index(self.plane(d), p, q)

    def peers(self):
        found = []
        for k in range(1, self.deep):
            found.append(self.index(lax.rem(self.z + k, self.deep), self.p, self.q))
        for k in range(1, self.side):
            found.append(self.index(self.z, lax.rem(self.p + k, self.side), self.q))
            found.append(self.index(self.z, self.p, lax.rem(self.q + k, self.side)))
        return found

    def greet(self):
        barrier = pltpu.get_barrier_semaphore()
        places = self.peers()
        for place in places:
            pl.semaphore_signal(
                barrier, inc=1, device_id={"batch": place}, device_id_type=MESH
            )
        pl.semaphore_signal(
            barrier, inc=1, device_id={"seq": 1 - self.core}, device_id_type=MESH
        )
        pl.semaphore_wait(barrier, len(places) + 1)


def to_batch(src, dst, send, recv, place):
    return pltpu.make_async_remote_copy(
        src_ref=src, dst_ref=dst, send_sem=send, recv_sem=recv,
        device_id={"batch": place}, device_id_type=MESH,
    )


def to_core(src, dst, send, recv, core):
    return pltpu.make_async_remote_copy(
        src_ref=src, dst_ref=dst, send_sem=send, recv_sem=recv,
        device_id={"seq": core}, device_id_type=MESH,
    )


class Gather:
    def __init__(self, route, at, sends, recv, line):
        self.route, self.at, self.sends, self.recv, self.line = route, at, sends, recv, line

    def go(self, here, kind, z, send, place):
        if place is None:
            to_core(here, here, self.sends.at[send], self.recv.at[kind, z], 1 - self.route.core).start()
        else:
            to_batch(here, here, self.sends.at[send], self.recv.at[kind, z], place).start()

    def come(self, here, kind, z):
        to_core(here, here, self.recv.at[kind, z], self.recv.at[kind, z], 1 - self.route.core).wait_recv()

    def z_of(self, i):
        return self.route.reach(i) if self.line else self.route.plane(i)

    def plane_one(self, i):
        route = self.route
        z = self.z_of(i)
        here = self.at(route.core * route.deep + z, route.q, route.p)
        if i:
            self.come(here, 0, z)
        if self.line:
            @pl.when((z <= route.z) & (route.z < route.deep - 1))
            def _():
                self.go(here, 0, z, 3 + z, route.index(route.z + 1, route.p, route.q))

            @pl.when((z >= route.z) & (route.z > 0))
            def _():
                self.go(here, 0, z, 7 + z, route.index(route.z - 1, route.p, route.q))
        elif i == 0:
            for d in range(1, route.deep):
                self.go(here, 0, z, 2 + d, route.near(d, 0, 0))
        self.go(here, 1, z, 0, route.near(0, 1, 0))
        self.go(here, 2, z, 1, route.near(0, 0, 1))

    def plane_two(self, i):
        route = self.route
        z = self.z_of(i)
        cz = route.core * route.deep + z
        here = self.at(cz, route.q, 1 - route.p)
        self.come(here, 1, z)
        self.go(here, 2, z, 1, route.near(0, 0, 1))

    def plane_last(self, i, cross=True):
        route = self.route
        z = self.z_of(i)
        cz = route.core * route.deep + z
        self.come(self.at(cz, route.q), 2, z)
        if cross:
            self.go(self.at(cz), 3, z, 2, None)

    def plane_other(self, i):
        route = self.route
        z = self.z_of(i)
        self.come(self.at((1 - route.core) * route.deep + z), 3, z)

    def finish(self, cross=True):
        route = self.route

        def sent(here, send):
            to_core(here, here, self.sends.at[send], self.sends.at[send], 1 - route.core).wait_send()

        sent(self.at(0), 0)
        sent(self.at(pl.ds(0, 2)), 1)
        if cross:
            sent(self.at(pl.ds(0, 4)), 2)
        one = self.at(0, 0, 0)
        if not self.line:
            for d in range(1, route.deep):
                sent(one, 2 + d)
            return
        for z in range(route.deep):
            pl.when((z <= route.z) & (route.z < route.deep - 1))(functools.partial(sent, one, 3 + z))
            pl.when((z >= route.z) & (route.z > 0))(functools.partial(sent, one, 7 + z))


class Reduce:
    def __init__(self, route, source, stage, sends, recv):
        self.route, self.source, self.sends, self.recv = route, source, sends, recv
        self.zero, self.one, self.two, self.three = stage
        self.lead = self.zero.shape[0]

    def come(self, here, kind, n):
        to_core(here, here, self.recv.at[kind, n], self.recv.at[kind, n], 1 - self.route.core).wait_recv()

    def add(self, at, value):
        self.zero[at] = self.zero[at] + value

    def leave(self, d):
        route = self.route
        z = route.plane(d)
        to_core(
            self.source((1 - route.core) * route.deep + z), self.zero.at[:, z], self.sends.at[0],
            self.recv.at[0, z], 1 - route.core,
        ).start()

    def start(self):
        for d in range(self.route.deep - 1, -1, -1):
            self.leave(d)

    def step_one(self, d):
        route = self.route
        z = route.plane(d)
        self.come(self.zero.at[:, z], 0, z)
        mine = self.source(route.core * route.deep + z)
        for n in range(self.lead):
            for q in range(2):
                for p in range(2):
                    self.add((n, z, q, p), mine[n, q, p])
        to_batch(
            self.zero.at[:, z, :, 1 - route.p], self.one.at[:, d], self.sends.at[1], self.recv.at[1, d],
            route.near(0, 1, 0),
        ).start()

    def step_two(self, d):
        route = self.route
        z = route.plane(d)
        self.come(self.one.at[:, d], 1, d)
        for n in range(self.lead):
            for q in range(2):
                self.add((n, z, q, route.p), self.one[n, d, q])
        to_batch(
            self.zero.at[:, z, 1 - route.q, route.p], self.two.at[:, d], self.sends.at[2], self.recv.at[2, d],
            route.near(0, 0, 1),
        ).start()

    def step_three(self, d):
        route = self.route
        z = route.plane(d)
        self.come(self.two.at[:, d], 2, d)
        for n in range(self.lead):
            self.add((n, z, route.q, route.p), self.two[n, d])
        if d:
            to_batch(
                self.zero.at[:, z, route.q, route.p], self.three.at[:, d - 1], self.sends.at[3],
                self.recv.at[3, d - 1], route.near(d, 0, 0),
            ).start()

    def total(self):
        route = self.route
        for d in range(1, route.deep):
            self.come(self.three.at[:, d - 1], 3, d - 1)
        sums = []
        for n in range(self.lead):
            out = self.zero[n, route.z, route.q, route.p].astype(F32)
            for d in range(1, route.deep):
                out = out + self.three[n, d - 1].astype(F32)
            sums.append(out)
        return sums

    def sent(self, kind):
        here = (self.zero, self.one, self.two, self.three)[kind]
        to_core(here, here, self.sends.at[kind], self.sends.at[kind], 1 - self.route.core).wait_send()


class Everyone:
    def __init__(self, count, pair, slots, pair_sems, sends, recvs):
        self.count, self.pair, self.slots = count, pair, slots
        self.pair_sems, self.sends, self.recvs = pair_sems, sends, recvs

    def start(self, x):
        core, me, count = lax.axis_index("seq"), lax.axis_index("batch"), self.count
        copy = to_core(x, self.pair, self.pair_sems.at[0], self.pair_sems.at[1], 1 - core)
        copy.start()
        copy.wait()
        self.slots[me] = x[...] + self.pair[...]
        for k in range(1, count):
            here = self.slots.at[me]
            to_batch(here, here, self.sends, self.recvs, lax.rem(me + k, count)).start()

    def total(self):
        others = self.slots.at[pl.ds(0, self.count - 1)]
        copy = to_batch(others, others, self.sends, self.recvs, lax.axis_index("batch"))
        copy.wait_recv()
        out = self.slots[0]
        for place in range(1, self.count):
            out = out + self.slots[place]
        copy.wait_send()
        return out

    @staticmethod
    def scratch(count, rows):
        return [
            pltpu.VMEM((rows, 128), F32),
            pltpu.VMEM((count, rows, 128), F32),
            pltpu.SemaphoreType.DMA((2,)),
            pltpu.SemaphoreType.DMA,
            pltpu.SemaphoreType.DMA,
        ]


def to_tile(rows):
    width = rows.shape[1]
    parts = [rows[i : i + 1, j : j + 128] for i in range(rows.shape[0]) for j in range(0, width, 128)]
    return jnp.concatenate(parts, axis=0)


def from_tile(tile, first, width):
    each = width // 128
    return jnp.concatenate([tile[first * each + j : first * each + j + 1] for j in range(each)], axis=1)


def nn(a, b):
    return lax.dot_general(a, b, (((1,), (0,)), ((), ())), preferred_element_type=F32)


def nt(a, b):
    return lax.dot_general(a, b, (((1,), (1,)), ((), ())), preferred_element_type=F32)


def tn(a, b):
    return lax.dot_general(a, b, (((0,), (0,)), ((), ())), preferred_element_type=F32)


def sigmoid(v):
    return 0.5 * jnp.tanh(0.5 * v) + 0.5


def rows_of(i, size):
    return pl.ds(pl.multiple_of(i * size, size), size)


def normed(v):
    centred = v - jnp.mean(v, -1, keepdims=True)
    scale = lax.rsqrt(jnp.mean(centred * centred, -1, keepdims=True) + EPS)
    return centred * scale, scale


def normed_back(grad, hat, scale):
    return scale * (
        grad - jnp.mean(grad, -1, keepdims=True) - hat * jnp.mean(grad * hat, -1, keepdims=True)
    )


def fold(values):
    return jnp.sum(values.reshape(values.shape[0] // 8, 8, values.shape[1]), 0)


def norm_rows(x_ref, put, vec, row, block=256):
    @pl.loop(0, x_ref.shape[0] // block)
    def _(i):
        at = rows_of(i, block)
        hat, _ = normed(x_ref[at])
        put(at, (hat * vec[row : row + 1] + vec[row + 1 : row + 2]).astype(LOW))


def norm_rows_back(grad_ref, x_ref, g_ref, put, vec, sums, row, block=256):
    width = x_ref.shape[1]

    def step(i, carry):
        gain, bias = carry
        at = rows_of(i, block)
        hat, scale = normed(x_ref[at])
        grad = grad_ref[at]
        put(at, g_ref[at] + normed_back(grad * vec[row : row + 1], hat, scale))
        return gain + fold(grad * hat), bias + fold(grad)

    zero = jnp.zeros((8, width), F32)
    gain, bias = lax.fori_loop(0, x_ref.shape[0] // block, step, (zero, zero))
    sums[row : row + 1] = jnp.sum(gain, 0, keepdims=True)
    sums[row + 1 : row + 2] = jnp.sum(bias, 0, keepdims=True)


def activate(a):
    s = sigmoid(a)
    u = a * s
    return u, s + u * (1.0 - s)


def valid_rows(scal, at_row, rows):
    frame = scal[0] + at_row + lax.broadcasted_iota(jnp.int32, (rows, 1), 0)
    return frame, jnp.where(frame < scal[1], 1.0, 0.0)


def keep_rows(scal, at_row, rows, width):
    frame, ok = valid_rows(scal, at_row, rows)
    cut = (frame >= scal[2]) & (frame < scal[2] + scal[3])
    channel = lax.broadcasted_iota(jnp.int32, (1, width), 1)
    lost = (channel >= scal[4]) & (channel < scal[4] + scal[5])
    return (ok * jnp.where(cut, 0.0, 1.0)) * jnp.where(lost, 0.0, 1.0)


def masked_input(scal, x_in, x_ref, block=256):
    @pl.loop(0, x_in.shape[0] // block)
    def _(i):
        at = rows_of(i, block)
        keep = keep_rows(scal, i * block, block, x_in.shape[1])
        x_ref[at] = x_in[at].astype(F32) * keep


def split3(v):
    high = v.astype(LOW).astype(F32)
    rest = v - high
    mid = rest.astype(LOW).astype(F32)
    return high, mid, rest - mid


def key_extra(length, rows):
    key = lax.broadcasted_iota(jnp.int32, (rows, 128), 0)
    lane = lax.broadcasted_iota(jnp.int32, (rows, 128), 1)
    lost = jnp.where(key < length, 0.0, -1e30)
    return jnp.where(lane == 0, lost, jnp.where(lane < 4, 1.0, 0.0)).astype(LOW)


def fill_side(side, first, extra_rows):
    size = first[0].shape[0]
    blank = jnp.zeros((size, side.shape[2]), LOW)
    for half in range(2):
        side[half, half * size : (half + 1) * size] = first[half]
        side[half, (1 - half) * size : (2 - half) * size] = blank
        side[half, 2 * size :] = extra_rows[half]


def extra_of(lead, parts, wide):
    row = lax.broadcasted_iota(jnp.int32, (16, wide), 0)
    out = jnp.where(row == 0, lead, 0.0)
    if parts is not None:
        for n, part in enumerate(parts):
            out = jnp.where(row == n + 1, -part, out)
    return jnp.concatenate([out.astype(LOW), jnp.zeros((112, wide), LOW)], axis=0)


def attention_forward(qT, key, vT, extra, oT, top, side, scale, hook):
    heads, size, queries = qT.shape
    keys = key.shape[1]
    ones = jnp.ones((16, keys), LOW)

    @pl.loop(0, heads // 2)
    def _(pair):
        hook(pair)
        lead = extra_of(1.0, None, queries)
        fill_side(side, [qT[2 * pair], qT[2 * pair + 1]], [lead, lead])
        left = jnp.concatenate([key[pair], extra[...]], axis=1)
        for half in range(2):
            head = 2 * pair + half
            s = nn(left, side[half])
            m = jnp.max(s, 0, keepdims=True)
            p = jnp.exp2((s - m) * scale).astype(LOW)
            o = nn(jnp.concatenate([vT[head], ones], axis=0), p)
            total = o[size : size + 1]
            oT[rows_of(head, size)] = (o[:size] * (1.0 / total)).astype(LOW)
            top[pl.ds(head, 1)] = m + jnp.log2(total) * (1.0 / scale)


def attention_backward(
    qT, key, h_all, qkvT, extra, doT, delta, top, dqT, dk, dv, qside, oside, lows, grads, scale, shrink, hook, done, chunk=512
):
    heads, size, queries = qT.shape
    keys = key.shape[1]

    @pl.loop(0, heads // 2)
    def _(pair):
        hook(pair)
        tops = [split3(top[pl.ds(2 * pair + half, 1)]) for half in range(2)]
        deltas = [split3(delta[pl.ds(2 * pair + half, 1)]) for half in range(2)]
        fill_side(qside, [qT[2 * pair], qT[2 * pair + 1]], [extra_of(1.0, t, queries) for t in tops])
        fill_side(oside, [doT[2 * pair], doT[2 * pair + 1]], [extra_of(0.0, t, queries) for t in deltas])
        kT = nt(qkvT[1, rows_of(pair, 128)], h_all[...]).astype(LOW)
        wide_o = jnp.concatenate([oside[0, :128], oside[1, :128]], axis=1)
        wide_q = jnp.concatenate([qside[0, :128], qside[1, :128]], axis=1)
        totals = [None, None]
        for c in range(keys // chunk):
            at = slice(c * chunk, (c + 1) * chunk)
            value = nt(h_all[at], qkvT[2, rows_of(pair, 128)]).astype(LOW)
            left_k = jnp.concatenate([key[pair, at], extra[at]], axis=1)
            left_v = jnp.concatenate([value, extra[at]], axis=1)
            for half in range(2):
                lanes = slice(half * queries, (half + 1) * queries)
                p = jnp.exp2(nn(left_k, qside[half]) * scale)
                lows[:, lanes] = p.astype(LOW)
                grads[:, lanes] = (p * nn(left_v, oside[half])).astype(LOW)
            for half in range(2):
                lanes = slice(half * queries, (half + 1) * queries)
                got = nn(kT[half * size : (half + 1) * size, at], grads[:, lanes])
                totals[half] = got if c == 0 else totals[half] + got
            dv[pair, at] = nt(lows[...], wide_o).astype(LOW)
            dk[pair, at] = (nt(grads[...], wide_q) * shrink).astype(LOW)
        for half in range(2):
            dqT[rows_of(2 * pair + half, size)] = (totals[half] * shrink).astype(LOW)
        done(pair)


def windows(pad_ref, at_row, block, lanes, shifts):
    for s in range(8):
        mine = [(tap, shift) for tap, shift in shifts if shift % 8 == s]
        low = min(shift for _, shift in mine)
        high = max(shift for _, shift in mine)
        window = pad_ref[at_row + low : at_row + high + block, lanes]
        for tap, shift in mine:
            yield tap, window[shift - low : shift - low + block]


def convolve(pad_ref, taps_wide, put, shift_of, rows, width, hook=None, block=64):
    count = taps_wide.shape[0]
    shifts = [(tap, shift_of(tap)) for tap in range(count)]
    for lane in range(0, width, 128):
        lanes = slice(lane, lane + 128)
        for at_row in range(0, rows, block):
            total = jnp.zeros((block // 8, 8, 128), F32)
            for tap, values in windows(pad_ref, at_row, block, lanes, shifts):
                total = total + taps_wide[tap, :, lanes][None] * values.reshape(block // 8, 8, 128)
            put(at_row, block, lane, total.reshape(block, 128))
        if hook:
            hook(1)


def convolve_weight(pad_ref, grad_ref, first, out_ref, shift_of, rows, width, hook, block=64):
    taps = out_ref.shape[0]
    for lane in range(0, width, 128):
        lanes = slice(lane, lane + 128)
        for s in range(8):
            mine = [(tap, shift_of(tap)) for tap in range(taps) if shift_of(tap) % 8 == s]
            low = min(shift for _, shift in mine)
            high = max(shift for _, shift in mine)
            sums = {tap: jnp.zeros((8, 128), F32) for tap, _ in mine}
            for at_row in range(0, rows, block):
                grad = grad_ref[first + at_row : first + at_row + block, lanes]
                window = pad_ref[at_row + low : at_row + high + block, lanes]
                for tap, shift in mine:
                    sums[tap] = sums[tap] + fold(grad * window[shift - low : shift - low + block])
            for tap, _ in mine:
                out_ref[tap : tap + 1, lanes] = jnp.sum(sums[tap], 0, keepdims=True)
        if hook:
            hook(1)


def place_halo(pad_ref, halo, core):
    rows = pad_ref.shape[0] - 2 * HALO
    got = halo[...]
    zero = jnp.zeros_like(got)
    pad_ref[0:HALO] = jnp.where(core == 1, got, zero)
    pad_ref[rows + HALO :] = jnp.where(core == 0, got, zero)


def layer_kernel(cfg, *refs):
    r = SimpleNamespace(**dict(zip(cfg.names, refs)))
    count, shard, hidden, inside = cfg.count, cfg.shard, cfg.hidden, cfg.inside
    rows, width = r.x_in.shape
    heads, size = cfg.heads, width // cfg.heads
    keys, pairs, taps = 2 * rows, heads // 2, r.kern.shape[0]
    scale, shrink = math.log2(math.e) / math.sqrt(size), 1.0 / math.sqrt(size)
    route = Routes(count).here()
    core, me = route.core, route.me
    vec, g0, g1, sums = r.vec, r.g0, r.g1, r.sums
    chunk, block = 256, 256
    own = pl.ds(pl.multiple_of(core * rows, rows), rows)
    theirs = pl.ds(pl.multiple_of((1 - core) * rows, rows), rows)
    zero8 = jnp.zeros((8, width), F32)

    def plane_of(g, m, i):
        return g[m, i].reshape(chunk, width)

    def whole_of(g, m):
        return g[m].reshape(hidden, width)

    barrier = pltpu.get_barrier_semaphore()
    for k in range(1, count):
        pl.semaphore_signal(
            barrier, inc=1, device_id={"batch": lax.rem(me + k, count)}, device_id_type=MESH
        )
    pl.semaphore_signal(barrier, inc=1, device_id={"seq": 1 - core}, device_id_type=MESH)
    half = width // 2
    q_own = pl.ds(pl.multiple_of(core * half, half), half)
    loads = []

    def load(source, target):
        copy = pltpu.make_async_copy(source, target, r.local.at[4 + len(loads)])
        copy.start()
        loads.append(copy)
        return copy

    if inside:
        cz = core * route.deep + route.z
        near_loads = [
            load(part.at[j], g.at[m, cz, route.q, route.p]) for m, part in enumerate((r.ffn_in, r.ffn_out)) for j, g in enumerate((g0, g1))
        ]
    else:
        near_loads = [load(r.shards.at[0], g0), load(r.shards.at[1], g1)]
    load_x, load_vec, load_kern = load(r.x_in_far, r.x_in), load(r.vec_far, r.vec), load(r.kern_far, r.kern)
    load_qkv = load(r.qkv_far, r.qkv_mine)
    load_att = load(r.w_att_far, r.w_att)
    load_conv_in = load(r.conv_in_far, r.conv_in)
    load_conv_out = load(r.conv_out_far, r.conv_out)
    load_cot = load(r.cot_far, r.cot)
    frame0, length, span = core * rows, r.lengths[0], [r.spans[0, n] for n in range(4)]
    scal = [frame0, length, *span]
    sums[...] = jnp.zeros_like(sums)
    for copy in near_loads:
        copy.wait()
    pl.semaphore_wait(barrier, count)

    def put_h0(at, value):
        r.h0[at] = value

    def begin():
        load_x.wait()
        load_vec.wait()
        masked_input(scal, r.x_in, r.x1)
        norm_rows(r.x1, put_h0, vec, 0)
        load_kern.wait()
        for tap in range(taps):
            r.wide[tap] = jnp.broadcast_to(r.kern[tap : tap + 1], (8, width))

    def inner(i):
        at = rows_of(i, chunk)
        u, slope = activate(nt(plane_of(g0, 0, i), r.h0[...]))
        r.act[at] = u.astype(LOW)
        r.slope[at] = slope.astype(LOW)

    swap_q = to_core(r.qkvT.at[:, q_own], r.qkvT.at[:, q_own], r.swap.at[0], r.swap.at[1], 1 - core)

    def turn_qkv():
        load_qkv.wait()
        for s in range(3):
            r.qkvT[s, q_own] = r.qkv_mine[s].astype(F32).T.astype(LOW)
        swap_q.start()

    if inside:
        first = Gather(route, lambda *i: g0.at[(slice(None), *i)], r.g_send.at[0], r.g_recv.at[0], True)
        second = Gather(route, lambda *i: g1.at[(slice(None), *i)], r.g_send.at[1], r.g_recv.at[1], True)
        deep = route.deep

        def inner_plane(which, d):
            inner(which * deep + route.reach(d))

        first.plane_one(0)
        begin()
        first.plane_one(1)
        turn_qkv()
        first.plane_one(2)
        first.plane_two(0)
        first.plane_one(3)
        for d in (1, 2, 3):
            first.plane_two(d)
        second.plane_one(0)
        for d in range(deep):
            first.plane_last(d)
            inner_plane(core, d)
            if d:
                first.plane_other(d - 1)
                inner_plane(1 - core, d - 1)
        first.plane_other(deep - 1)
        inner_plane(1 - core, deep - 1)
    else:
        begin()
        turn_qkv()

        @pl.loop(0, hidden // chunk)
        def _(i):
            inner(i)

    @pl.loop(0, rows // 256)
    def _(i):
        at = rows_of(i, 256)
        r.x1[at] = r.x1[at] + 0.5 * tn(r.act[:, at], whole_of(g0, 1))

    def put_h2(at, value):
        r.h_all[pl.ds(pl.multiple_of(core * rows + at.start, block), block)] = value

    norm_rows(r.x1, put_h2, vec, 2)
    swap = to_core(r.h_all.at[own], r.h_all.at[own], r.swap.at[2], r.swap.at[3], 1 - core)
    swap.start()
    away = [
        pltpu.make_async_copy(g0, r.far_g, r.local.at[0]),
        pltpu.make_async_copy(r.act, r.far_act, r.local.at[1]),
        pltpu.make_async_copy(r.slope, r.far_slope, r.local.at[2]),
    ]
    for copy in away:
        copy.start()
    swap_q.wait()

    def project(at, vT):
        here = r.h_all[at]
        for pair in range(pairs):
            r.key[pair, at] = nt(here, r.qkvT[1, pair * 128 : (pair + 1) * 128]).astype(LOW)
        vT[:, :, at] = nt(r.qkvT[2], here).astype(LOW).reshape(heads, size, rows)

    r.extra[...] = key_extra(scal[1], keys)

    def attend(vT, side_ref):
        r.qT[...] = nt(r.qkvT[0], r.h_all[own]).astype(LOW).reshape(heads, size, rows)
        project(own, vT)
        if inside:
            second.plane_one(1)
        swap.wait()
        project(theirs, vT)
        if inside:
            second.plane_one(2)
            second.plane_two(0)

        def hook(pair):
            if inside:
                @pl.when(pair == 1)
                def _():
                    second.plane_one(3)
                    second.plane_two(1)

                @pl.when(pair == 2)
                def _():
                    second.plane_two(2)
                    second.plane_last(0)

                @pl.when(pair == 3)
                def _():
                    second.plane_two(3)
                    second.plane_last(1)

        attention_forward(r.qT, r.key, vT, r.extra, r.oT, r.top, side_ref, scale, hook)

    pl.run_scoped(attend, pltpu.VMEM((heads, size, keys), LOW), pltpu.VMEM((2, 256, rows), LOW))

    load_att.wait()

    @pl.loop(0, rows // 256)
    def _(i):
        at = rows_of(i, 256)
        r.x2[at] = r.x1[at] + tn(r.oT[:, at], r.w_att[...])

    def put_h3(at, value):
        r.h3[at] = value

    norm_rows(r.x2, put_h3, vec, 4)
    load_conv_in.wait()

    @pl.loop(0, rows // 256)
    def _(i):
        at = rows_of(i, 256)
        _, ok = valid_rows(scal, i * 256, 256)
        here = r.h3[at]
        gate = sigmoid(nn(here, r.conv_in[:, width:]))
        r.pad[pl.ds(pl.multiple_of(i * 256 + HALO, HALO), 256)] = nn(here, r.conv_in[:, :width]) * gate * ok

    edge = pl.ds(pl.multiple_of(HALO + (1 - core) * (rows - HALO), HALO), HALO)
    swap = to_core(r.pad.at[edge], r.halo.at[0], r.swap.at[4], r.swap.at[5], 1 - core)
    swap.start()
    if inside:
        second.plane_last(2)
    swap.wait()
    place_halo(r.pad, r.halo.at[0], core)

    def put_depth(at_row, high, lane, total):
        r.depth[at_row : at_row + high, lane : lane + 128] = total

    spots = [lambda: None] * 4
    if inside:
        pass
    convolve(r.pad, r.wide, put_depth, lambda tap: tap + 1, rows, width, lambda _: spots.pop(0)())

    if inside:
        second.plane_last(3)

    def moments(i, carry):
        one, two = carry
        _, ok = valid_rows(scal, i * block, block)
        here = r.depth[rows_of(i, block)]
        held = here * ok
        return one + fold(held), two + fold(here * held)

    one, two = lax.fori_loop(0, rows // block, moments, (zero8, zero8))
    number = jnp.clip(scal[1] - scal[0], 0, rows).astype(F32)
    r.part_a[0:8] = to_tile(
        jnp.concatenate([jnp.sum(one, 0, keepdims=True), jnp.sum(two, 0, keepdims=True)], axis=0)
    )
    r.part_a[8:16] = jnp.full((8, 128), 1.0, F32) * number
    every = Everyone(count, r.pair_a, r.slots_a, r.pair_sems_a, r.sends_a, r.recvs_a)
    every.start(r.part_a)
    if inside:
        for d in range(deep):
            second.plane_other(d)
        second.finish()
        first.finish()
    for copy in [*away, load_conv_out, load_cot]:
        copy.wait()
    tile = every.total()
    number = tile[8:9, 0:1]
    mean = from_tile(tile, 0, width) / number
    var = from_tile(tile, 1, width) / number - mean * mean
    spread = lax.rsqrt(var + EPS)
    gain6 = vec[6:7]

    if inside:
        stages = [
            Reduce(route, source, [ref.at[part] for ref in (r.zero, r.one, r.two, r.three)], r.r_send.at[k], r.r_recv.at[k])
            for k, (part, source) in enumerate(
                [
                    (pl.ds(0, 2), lambda cz: g0.at[:, cz]),
                    (pl.ds(2, 1), lambda cz: r.box.at[pl.ds(0, 1), cz]),
                    (pl.ds(3, 1), lambda cz: r.box.at[pl.ds(1, 1), cz]),
                    (pl.ds(4, 1), lambda cz: g0.at[pl.ds(1, 1), cz]),
                    (pl.ds(5, 1), lambda cz: g0.at[pl.ds(0, 1), cz]),
                ]
            )
        ]
        ffn1, rest, proj, out0, in0 = stages
        queue = []

        def put_off(units, lag, ends):
            for t in range(len(units) + lag):
                if t < len(units):
                    piece, d = units[t]
                    queue.append(functools.partial(piece.step_two, d))
                if t >= lag:
                    piece, d = units[t - lag]
                    queue.append(functools.partial(piece.step_three, d))
                    if d == 0 and piece in ends:
                        queue.append(ends[piece])

        def planes_of(*pieces):
            return [(piece, d) for d in range(deep - 1, -1, -1) for piece in pieces]

        def tick(count):
            for _ in range(min(count, len(queue))):
                queue.pop(0)()

        own_at = (core * deep + route.z, route.q, route.p)

        def ticks(*counts):
            left = list(counts)
            return lambda _: tick(left.pop(0))

        def end_ffn1():
            r.fin_in[1], r.fin_out[1] = ffn1.total()

        def end_ffn0():
            (r.fin_out[0],) = out0.total()
            (r.fin_in[0],) = in0.total()

        def end_box(j, piece):
            r.held[(j, *own_at)] = piece.total()[0].astype(LOW)

        third = Gather(route, lambda *i: r.held.at[(0, *i)], r.g_send.at[2], r.g_recv.at[2], False)
        fourth = Gather(route, lambda *i: r.held.at[(1, *i)], r.g_send.at[3], r.g_recv.at[3], False)
    else:
        def tick(count):
            pass

        def ticks(*counts):
            return None
    back_copies = [
        pltpu.make_async_copy(r.far_act, r.act, r.local.at[0]),
        pltpu.make_async_copy(r.far_slope, r.slope, r.local.at[1]),
        pltpu.make_async_copy(r.far_g, g1, r.local.at[2]),
    ]

    def hidden_grad(weight, dy, da, i):
        at = rows_of(i, chunk)
        du = nt(plane_of(weight, 1, i), dy[...])
        low = (du * r.slope[at].astype(F32)).astype(LOW)
        da[at] = low
        return low

    def weight_grads(h_ref, dy, low, i):
        at = rows_of(i, chunk)
        g0[1, i] = nn(r.act[at], dy[...]).astype(LOW).reshape(g0.shape[2:])
        g0[0, i] = nn(low, h_ref[...]).astype(LOW).reshape(g0.shape[2:])

    def by_planes(grads, pieces, hooks):
        if not inside:
            pl.loop(0, hidden // chunk)(grads)
            return
        for n, d in enumerate(range(deep - 1, -1, -1)):
            grads((1 - core) * deep + route.plane(d))
            for piece in pieces:
                piece.leave(d)
            hooks(n)
        for n, d in enumerate(range(deep - 1, -1, -1)):
            grads(core * deep + route.plane(d))
            for piece in pieces:
                piece.step_one(d)
            hooks(deep + n)

    def middle(slope_z, da, dh):
        low, dy, h4 = r.d_conv_in.at[:, pl.ds(0, width)], r.d_conv_in.at[:, pl.ds(width, width)], r.d_att
        dc = r.d_conv_out if inside else r.spare
        x3, x4 = r.input_grad, r.dz

        @pl.loop(0, rows // block)
        def _(i):
            at = rows_of(i, block)
            z = (r.depth[at] - mean) * spread * gain6 + vec[7:8]
            u, slope = activate(z)
            low[at] = u.astype(LOW)
            slope_z[at] = slope

        @pl.loop(0, rows // 256)
        def _(i):
            at = rows_of(i, 256)
            x3[at] = r.x2[at] + nn(low[at], r.conv_out[...])

        def put_h4(at, value):
            h4[at] = value

        norm_rows(x3, put_h4, vec, 8)

        @pl.loop(0, hidden // chunk)
        def _(i):
            at = rows_of(i, chunk)
            u, slope = activate(nt(plane_of(g1, 0, i), h4[...]))
            r.act[at] = u.astype(LOW)
            r.slope[at] = slope.astype(LOW)

        @pl.loop(0, rows // 256)
        def _(i):
            at = rows_of(i, 256)
            x4[at] = x3[at] + 0.5 * tn(r.act[:, at], whole_of(g1, 1))

        def last(i, carry):
            gain, bias = carry
            at = rows_of(i, block)
            hat, rate = normed(x4[at])
            r.out[at] = (hat * vec[10:11] + vec[11:12]).astype(LOW)
            g = r.cot[at].astype(F32)
            back = normed_back(g * vec[10:11], hat, rate)
            r.grad[at] = back
            dy[at] = (0.5 * back).astype(LOW)
            return gain + fold(g * hat), bias + fold(g)

        gain, bias = lax.fori_loop(0, rows // block, last, (zero8, zero8))
        sums[10:11] = jnp.sum(gain, 0, keepdims=True)
        sums[11:12] = jnp.sum(bias, 0, keepdims=True)
        @pl.loop(0, hidden // chunk)
        def _(i):
            hidden_grad(g1, dy, da, i)

        @pl.loop(0, rows // 256)
        def _(i):
            at = rows_of(i, 256)
            dh[at] = tn(da[:, at], whole_of(g1, 0))

        back_copies[2].start()

        def put(at, value):
            r.grad[at] = value
            dc[at] = value.astype(LOW)

        norm_rows_back(dh, x3, r.grad, put, vec, sums, 8)

        @pl.loop(0, rows // 256)
        def _(i):
            at = rows_of(i, 256)
            r.dz[at] = nt(dc[at], r.conv_out[...])

        def close(i, carry):
            one, two = carry
            at = rows_of(i, block)
            here = r.dz[at] * slope_z[at]
            r.dz[at] = here
            return one + fold(here), two + fold(here * (r.depth[at] - mean))

        one, two = lax.fori_loop(0, rows // block, close, (zero8, zero8))
        r.part_b[...] = to_tile(
            jnp.concatenate([jnp.sum(one, 0, keepdims=True), jnp.sum(two, 0, keepdims=True)], axis=0)
        )
        every = Everyone(count, r.pair_b, r.slots_b, r.pair_sems_b, r.sends_b, r.recvs_b)
        every.start(r.part_b)
        got = tn(low[...], dc[...]).astype(LOW)
        if inside:
            r.box[0, :, :, :, 0:16] = got.reshape(*r.box.shape[1:4], 16, width)
        else:
            r.d_conv_out[...] = got
        by_planes(
            lambda i: weight_grads(h4, dy, da[rows_of(i, chunk)], i), [ffn1] if inside else None, lambda n: None
        )
        back_copies[0].start()
        back_copies[1].start()
        r.part_b[...] = every.total()

    square = (rows, width)
    vm = pltpu.VMEM
    pl.run_scoped(
        middle, vm(square, F32), vm((hidden, rows), LOW), vm(square, F32),
    )
    leaving = {
        name: pltpu.make_async_copy(getattr(r, name), getattr(r, "far_" + name), r.local.at[20 + n])
        for n, name in enumerate(("out", "input_grad", "d_conv_out", "d_conv_in", "d_att"))
    }
    leaving["out"].start()
    if not inside:
        copy = pltpu.make_async_copy(g0, r.d_ffn.at[1], r.local.at[3])
        copy.start()
        copy.wait()
    tile = r.part_b[...]
    grad_sum, grad_moment = from_tile(tile, 0, width), from_tile(tile, 1, width)
    if inside:
        put_off(planes_of(ffn1), 1, {ffn1: end_ffn1})
    var_grad = -0.5 * (gain6 * grad_moment) * spread * spread * spread
    flat = (-(gain6 * spread * grad_sum) - 2.0 * mean * var_grad) / number
    tilt = 2.0 * var_grad / number

    def convolution_back(back, datt):
        dp, dh = r.d_conv_in if inside else r.spare_wide, r.input_grad
        left, right = r.dz, r.depth

        @pl.loop(0, rows // block)
        def _(i):
            at = rows_of(i, block)
            _, ok = valid_rows(scal, i * block, block)
            back[pl.ds(pl.multiple_of(i * block + HALO, HALO), block)] = gain6 * spread * r.dz[at] + ok * (
                flat + r.depth[at] * tilt
            )

        swap = to_core(back.at[edge], r.halo.at[1], r.swap.at[6], r.swap.at[7], 1 - core)
        swap.start()
        convolve_weight(r.pad, back, HALO, r.small.at[pl.ds(0, taps)], lambda tap: tap + 1, rows, width, ticks(0, 0, 1, 0))

        @pl.loop(0, rows // 256)
        def _(i):
            at = rows_of(i, 256)
            left[at] = nn(r.h3[at], r.conv_in[:, :width])
            right[at] = nn(r.h3[at], r.conv_in[:, width:])

        swap.wait()
        place_halo(back, r.halo.at[1], core)

        def put(at_row, high, lane, total):
            at = slice(at_row, at_row + high)
            _, ok = valid_rows(scal, at_row, high)
            gate = sigmoid(right[at, lane : lane + 128])
            total = total * gate * ok
            dp[at, lane : lane + 128] = total.astype(LOW)
            dp[at, width + lane : width + lane + 128] = (
                total * left[at, lane : lane + 128] * (1.0 - gate)
            ).astype(LOW)

        convolve(back, r.wide, put, lambda tap: taps - 1 - tap, rows, width, ticks(0, 1, 1, 0))
        got = tn(r.h3[...], dp[...]).astype(LOW)
        if inside:
            r.box[0, :, :, :, 16:32] = got[:, :width].reshape(*r.box.shape[1:4], 16, width)
            r.box[0, :, :, :, 32:48] = got[:, width:].reshape(*r.box.shape[1:4], 16, width)
        else:
            r.d_conv_in[...] = got

        @pl.loop(0, rows // 256)
        def _(i):
            at = rows_of(i, 256)
            dh[at] = nt(dp[at], r.conv_in[...])

        def put_first(at, got):
            r.grad[at] = got
            datt[at] = got.astype(LOW)

        norm_rows_back(dh, r.x2, r.grad, put_first, vec, sums, 4)
        tick(2)
        got = nn(r.oT[...], datt[...]).astype(LOW)
        if inside:
            r.box[0, :, :, :, 48:64] = got.reshape(*r.box.shape[1:4], 16, width)
            rest.start()
        else:
            r.d_att[...] = got
        r.doT[...] = nt(r.w_att[...], datt[...]).astype(LOW).reshape(heads, size, rows)

    pl.run_scoped(
        convolution_back, vm(r.pad.shape, F32), vm(square, LOW),
    )

    def attend_back(delta, qside, oside, grads, dk, dv):
        lows = r.conv_in
        dqT = r.d_conv_out if inside else r.spare

        for head in range(heads):
            o = r.oT[head * size : (head + 1) * size].astype(F32)
            delta[head : head + 1] = jnp.sum(o * r.doT[head].astype(F32), 0, keepdims=True)

        def hook(pair):
            if inside:
                @pl.when(pair == 1)
                def _():
                    for d in range(deep - 1, -1, -1):
                        rest.step_one(d)
                    tick(2)

                @pl.when(pair == 2)
                def _():
                    put_off(planes_of(rest), 2, {rest: functools.partial(end_box, 0, rest)})
                    tick(1)
                    rests = queue[1:]
                    tick_rest = [rests.pop(0), rests.pop(0)]
                    queue[1:] = rests
                    for thunk in tick_rest:
                        thunk()

                @pl.when(pair == 3)
                def _():
                    tick(1)
                    tick(4)

        def done(pair):
            to_core(dk.at[pair, theirs], r.rk.at[pair], r.swap.at[8], r.swap.at[9], 1 - core).start()
            to_core(dv.at[pair, theirs], r.rv.at[pair], r.swap.at[10], r.swap.at[11], 1 - core).start()

        attention_backward(
            r.qT, r.key, r.h_all, r.qkvT, r.extra, r.doT, delta, r.top, dqT, dk, dv, qside, oside, lows, grads,
            scale, shrink, hook, done,
        )
        r.dq[...] = dqT[...].astype(F32).T.astype(LOW)
        to_core(dk.at[:, theirs], r.rk, r.swap.at[8], r.swap.at[9], 1 - core).wait()
        to_core(dv.at[:, theirs], r.rv, r.swap.at[10], r.swap.at[11], 1 - core).wait()
        for pair in range(pairs):
            lanes = slice(pair * 128, (pair + 1) * 128)
            r.h3[:, lanes] = (dk[pair, own].astype(F32) + r.rk[pair].astype(F32)).astype(LOW)
            r.own_v[:, lanes] = (dv[pair, own].astype(F32) + r.rv[pair].astype(F32)).astype(LOW)

    pl.run_scoped(
        attend_back, vm((heads, rows), F32), vm((2, 256, rows), LOW), vm((2, 256, rows), LOW),
        vm((keys // 2, 2 * rows), LOW),
        vm((pairs, keys, 128), LOW), vm((pairs, keys, 128), LOW),
    )
    if inside:
        tick(len(queue))
        third.plane_one(0)

    def put_qkv(s, got):
        if inside:
            for c in range(2):
                v = got[:, c * half : (c + 1) * half].reshape(count, 2, 16, half)
                r.box[1, c * deep : (c + 1) * deep, :, :, s * 16 : (s + 1) * 16] = jnp.concatenate(
                    [v[:, 0], v[:, 1]], axis=-1
                ).reshape(deep, 2, 2, 16, width)
        else:
            r.d_qkv[s] = got

    def project_back(dh, dy, da, x0):
        own_k, own_v = r.h3, r.own_v
        h2 = r.h_all[own]
        put_qkv(0, tn(h2, r.dq[...]).astype(LOW))
        put_qkv(1, tn(h2, own_k[...]).astype(LOW))
        put_qkv(2, tn(h2, own_v[...]).astype(LOW))
        if inside:
            r.small[taps : taps + 16] = sums[...]
            blank = jnp.zeros((16, width), LOW)
            for n in range(4):
                full = n < (taps + 16) // 16
                r.box[1, 0, n // 2, n % 2, 48:64] = r.small[n * 16 : (n + 1) * 16].astype(LOW) if full else blank
            r.box[1, 1:, :, :, 48:64] = jnp.zeros((2 * deep - 1, 2, 2, 16, width), LOW)
            proj.start()
        @pl.loop(0, rows // 256)
        def _(i):
            at = rows_of(i, 256)
            dh[at] = nn(r.dq[at], r.qkvT[0]) + nn(own_k[at], r.qkvT[1]) + nn(own_v[at], r.qkvT[2])

        def put_second(at, got):
            r.grad[at] = got
            dy[at] = (0.5 * got).astype(LOW)

        norm_rows_back(dh, r.x1, r.grad, put_second, vec, sums, 2)
        if inside:
            third.plane_two(0)
            ffn1.sent(0)
        for copy in back_copies:
            copy.wait()

        def hooks(n):
            if n == 3:
                put_off(planes_of(proj) + planes_of(out0, in0), 2, {proj: functools.partial(end_box, 1, proj), in0: end_ffn0})
                for d in (1, 2, 3):
                    third.plane_one(d)
                tick(1)
            if n == 5:
                tick(1)
            if n == 7:
                tick(2)
                third.plane_two(1)
                third.plane_two(2)

        if inside:
            for d in range(deep - 1, -1, -1):
                proj.step_one(d)
        by_planes(lambda i: weight_grads(r.h0, dy, hidden_grad(g1, dy, da, i), i), [out0, in0] if inside else None, hooks)
        tick(1)
        if inside:
            third.plane_two(3)
        masked_input(scal, r.x_in, x0)

        @pl.loop(0, rows // 256)
        def _(i):
            at = rows_of(i, 256)
            dh[at] = tn(da[:, at], whole_of(g1, 0))

        tick(2)
        if inside:
            for d in range(deep):
                third.plane_last(d)

        def put_input(at, got):
            r.input_grad[at] = got * keep_rows(scal, at.start, block, width)

        norm_rows_back(dh, x0, r.grad, put_input, vec, sums, 0)

    def tail(dy, da):
        dh, x0 = r.dz, r.x2
        project_back(dh, dy, da, x0)
        leaving["input_grad"].start()
        if not inside:
            return
        while len(queue) > 15:
            tick(1)
        fourth.plane_one(0)
        tick(4)
        fourth.plane_two(0)
        tick(3)
        r.part_c[...] = to_tile(sums[0:4])
        every = Everyone(count, r.pair_c, r.slots_c, r.pair_sems_c, r.sends_c, r.recvs_c)
        every.start(r.part_c)
        for d in (1, 2, 3):
            fourth.plane_one(d)
        for d in range(deep):
            third.plane_other(d)
        tick(2)
        got = r.held[0]
        r.d_conv_out[...] = got[:, :, :, 0:16].reshape(width, width)
        r.d_conv_in[:, :width] = got[:, :, :, 16:32].reshape(width, width)
        r.d_conv_in[:, width:] = got[:, :, :, 32:48].reshape(width, width)
        r.d_att[...] = got[:, :, :, 48:64].reshape(width, width)
        for name in ("d_conv_out", "d_conv_in", "d_att"):
            leaving[name].start()
        tick(2)
        for d in (1, 2, 3):
            fourth.plane_two(d)
        tick(len(queue))
        for d in range(deep):
            fourth.plane_last(d, False)
        few = r.held.at[1, 0, :, :, pl.ds(48, 16)]
        cross = to_core(few, few, fourth.sends.at[2], fourth.recv.at[3, 0], 1 - core)
        pl.when(core == 0)(cross.start)
        tile = every.total()
        got = r.held[1, pl.ds(core * deep, deep)].reshape(count, 64, width)
        for s in range(3):
            v = got[:, s * 16 : (s + 1) * 16]
            v = jnp.concatenate([v[:, None, :, :half], v[:, None, :, half:]], axis=1)
            r.d_qkv[s] = v.reshape(width, half)
        pl.when(core == 1)(cross.wait_recv)
        got = r.held[1, 0, :, :, 48:64].reshape(64, width).astype(F32)
        r.d_kern[...] = got[:taps]
        r.d_vec[...] = jnp.concatenate(
            [
                *[from_tile(tile, n, width) for n in range(4)], got[taps + 4 : taps + 6],
                spread * grad_moment, grad_sum, got[taps + 8 : taps + 12],
            ],
            axis=0,
        )
        third.finish()
        fourth.finish(False)
        pl.when(core == 0)(cross.wait_send)
        for piece in stages:
            for kind in range(4):
                if kind or piece is not ffn1:
                    piece.sent(kind)

    pl.run_scoped(
        tail, vm(square, LOW), vm((hidden, rows), LOW),
    )
    if not inside:
        for name in ("d_conv_out", "d_conv_in", "d_att"):
            leaving[name].start()
        r.small[taps : taps + 16] = sums[...]
        r.small[taps + 6 : taps + 7] = spread * grad_moment
        r.small[taps + 7 : taps + 8] = grad_sum
        copy = pltpu.make_async_copy(g0, r.d_ffn.at[0], r.local.at[3])
        copy.start()
        copy.wait()
    for copy in leaving.values():
        copy.wait()


def gather_steps(route, chunk, held, sends, recv, with_core=True):
    started = []
    core, count = route.core, route.count

    def block(place):
        return core * count + place

    def arrive(place):
        here = held.at[chunk, block(place)]
        to_batch(here, here, recv.at[chunk, block(place)], recv.at[chunk, block(place)], route.me).wait_recv()

    def send(place, target):
        slot = len(started)
        here = held.at[chunk, block(place)]
        copy = to_batch(here, here, sends.at[chunk, slot], recv.at[chunk, block(place)], target)
        copy.start()
        started.append(copy)

    def cross(place):
        if not with_core:
            return
        slot = len(started)
        here = held.at[chunk, block(place)]
        copy = to_core(here, here, sends.at[chunk, slot], recv.at[chunk, block(place)], 1 - core)
        copy.start()
        started.append(copy)

    def step_mid():
        for k in range(1, route.deep):
            send(route.me, route.index(lax.rem(route.z + k, route.deep), route.p, route.q))
        cross(route.me)

    def step_one():
        for d in range(route.deep):
            z = lax.rem(route.z + d, route.deep)
            place = route.index(z, route.p, route.q)
            if d:
                arrive(place)
            for k in range(1, route.side):
                send(place, route.index(route.z, lax.rem(route.p + k, route.side), route.q))
            if d:
                cross(place)

    def step_two():
        for d in range(route.deep):
            z = lax.rem(route.z + d, route.deep)
            for e in range(route.side):
                p = lax.rem(route.p + e, route.side)
                place = route.index(z, p, route.q)
                if e:
                    arrive(place)
                for k in range(1, route.side):
                    send(place, route.index(route.z, route.p, lax.rem(route.q + k, route.side)))
                if e:
                    cross(place)

    def step_last():
        for d in range(route.deep):
            z = lax.rem(route.z + d, route.deep)
            for e in range(route.side):
                p = lax.rem(route.p + e, route.side)
                for f in range(1, route.side):
                    place = route.index(z, p, lax.rem(route.q + f, route.side))
                    arrive(place)
                    cross(place)

    def step_end():
        if with_core:
            for place in range(count):
                other = held.at[chunk, (1 - core) * count + place]
                at = recv.at[chunk, (1 - core) * count + place]
                to_core(other, other, at, at, 1 - core).wait_recv()
        for copy in started:
            copy.wait_send()

    return [step_mid, step_one, step_two, step_last, step_end]


def sends_of(route):
    return (route.deep - 1) + route.deep * (route.side - 1) * (1 + route.side) + route.count


def run_steps(all_steps):
    depth = len(all_steps[0])
    for turn in range(depth + len(all_steps) - 1):
        for chunk, steps in enumerate(all_steps):
            if 0 <= turn - chunk < depth:
                steps[turn - chunk]()


def gather_kernel(count, mine, held, local, sends, recv):
    route = Routes(count).here()
    chunks = mine.shape[0]
    copies = []
    for chunk in range(chunks):
        own = held.at[chunk, route.core * count + route.me]
        copy = pltpu.make_async_copy(mine.at[chunk], own, local.at[chunk])
        copy.start()
        copies.append(copy)
    route.greet()
    for copy in copies:
        copy.wait()
    run_steps([gather_steps(route, chunk, held, sends, recv) for chunk in range(chunks)])


def gather_all(mine, count, collective_id):
    chunks, rows, width = mine.shape
    route = Routes(count)
    return pl.pallas_call(
        functools.partial(gather_kernel, count),
        out_shape=jax.ShapeDtypeStruct((chunks, 2 * count, rows, width), mine.dtype),
        in_specs=[pl.BlockSpec(memory_space=pltpu.VMEM)],
        out_specs=pl.BlockSpec(memory_space=pltpu.VMEM),
        scratch_shapes=[
            pltpu.SemaphoreType.DMA((chunks,)),
            pltpu.SemaphoreType.DMA((chunks, sends_of(route))),
            pltpu.SemaphoreType.DMA((chunks, 2 * count)),
        ],
        compiler_params=pltpu.CompilerParams(
            collective_id=collective_id, has_side_effects=True, vmem_limit_bytes=VMEM_BYTES
        ),
    )(mine)


def reduce_kernel(count, solo, n, *refs):
    pieces, (fin, held, grads, packing, *rest) = refs[:n], refs[n:]
    copies = []
    at = 0
    for i, piece in enumerate(pieces):
        lines = piece.shape[1]
        copy = pltpu.make_async_copy(piece, grads.at[:, pl.ds(at, lines)], packing.at[i])
        copy.start()
        copies.append(copy)
        at += lines
    for copy in copies:
        copy.wait()
    reduce_packed(count, solo, grads, fin, held, *rest)


def reduce_packed(count, solo, grads, fin, held, zero, one, two, three, s0, r0, s1, r1, s2, r2, s3, r3, sends, recv):
    route = Routes(count).here()
    core, me, side, deep = route.core, route.me, route.side, route.deep
    rows, width = grads.shape[1:]
    piece = 16

    def add(target, source):
        @pl.loop(0, rows // piece)
        def _(i):
            at = pl.ds(pl.multiple_of(i * piece, piece), piece)
            target[at] = (target[at].astype(jnp.float32) + source[at].astype(jnp.float32)).astype(target.dtype)

    route.greet()
    waits = []
    order = []
    for f in range(side - 1, -1, -1):
        for d in range(deep):
            for e in range(side - 1, -1, -1):
                order.append((d, e, f))
    for d, e, f in order:
        place = route.index(lax.rem(route.z + d, deep), lax.rem(route.p + e, side), lax.rem(route.q + f, side))
        copy = to_core(grads.at[(1 - core) * count + place], zero.at[place], s0.at[place], r0.at[place], 1 - core)
        copy.start()
        waits.append(copy)
    for e in range(side - 1, -1, -1):
        for d in range(deep):
            for f in range(side - 1, -1, -1):
                z, p, q = lax.rem(route.z + d, deep), lax.rem(route.p + e, side), lax.rem(route.q + f, side)
                place = route.index(z, p, q)
                to_core(zero.at[place], zero.at[place], s0.at[place], r0.at[place], 1 - core).wait_recv()
                add(zero.at[place], grads.at[core * count + place])
                if e:
                    slot = (e - 1) * deep * side + z * side + q
                    copy = to_batch(
                        zero.at[place], one.at[slot], s1.at[slot], r1.at[slot], route.index(route.z, p, route.q)
                    )
                    copy.start()
                    waits.append(copy)
    for f in range(side - 1, -1, -1):
        for d in range(deep):
            z, q = lax.rem(route.z + d, deep), lax.rem(route.q + f, side)
            place = route.index(z, route.p, q)
            for e in range(1, side):
                slot = (e - 1) * deep * side + z * side + q
                to_batch(one.at[slot], one.at[slot], s1.at[slot], r1.at[slot], me).wait_recv()
                add(zero.at[place], one.at[slot])
            if f:
                slot = (f - 1) * deep + z
                copy = to_batch(
                    zero.at[place], two.at[slot], s2.at[slot], r2.at[slot], route.index(route.z, route.p, q)
                )
                copy.start()
                waits.append(copy)
    for d in range(deep - 1, -1, -1):
        z = lax.rem(route.z + d, deep)
        place = route.index(z, route.p, route.q)
        for f in range(1, side):
            slot = (f - 1) * deep + z
            to_batch(two.at[slot], two.at[slot], s2.at[slot], r2.at[slot], me).wait_recv()
            add(zero.at[place], two.at[slot])
        if d:
            copy = to_batch(zero.at[place], three.at[d - 1], s3.at[d - 1], r3.at[d - 1], place)
            copy.start()
            waits.append(copy)
    for d in range(1, deep):
        to_batch(three.at[d - 1], three.at[d - 1], s3.at[d - 1], r3.at[d - 1], me).wait_recv()

    def final(at):
        total = zero[me, at].astype(jnp.float32)
        for d in range(1, deep):
            total = total + three[d - 1, at].astype(jnp.float32)
        return total

    mine = core * count + me

    @pl.loop(0, (rows - solo) // piece)
    def _(i):
        at = pl.ds(pl.multiple_of(i * piece, piece), piece)
        held[0, mine, at] = final(pl.ds(pl.multiple_of(solo + i * piece, piece), piece)).astype(held.dtype)

    steps = gather_steps(route, 0, held, sends, recv)
    steps[0]()

    @pl.loop(0, solo // piece)
    def _(i):
        at = pl.ds(pl.multiple_of(i * piece, piece), piece)
        fin[at] = final(at)

    for step in steps[1:]:
        step()
    for copy in waits:
        copy.wait_send()


def reduce_all(pieces, solo, count, collective_id):
    blocks, _, width = pieces[0].shape
    kind = pieces[0].dtype
    if any(piece.shape[1] % 16 for piece in pieces):
        used = sum(piece.shape[1] for piece in pieces)
        spare = jnp.zeros((blocks, -used % 16, width), kind)
        pieces = [jnp.concatenate([*pieces, spare], axis=1)]
    rows = sum(piece.shape[1] for piece in pieces)
    route = Routes(count)
    side, deep = route.side, route.deep
    n1 = max(1, (side - 1) * side * deep)
    n2 = max(1, (side - 1) * deep)
    n3 = max(1, deep - 1)
    dma = pltpu.SemaphoreType.DMA
    return pl.pallas_call(
        functools.partial(reduce_kernel, count, solo, len(pieces)),
        out_shape=(
            jax.ShapeDtypeStruct((solo, width), jnp.float32),
            jax.ShapeDtypeStruct((1, blocks, rows - solo, width), kind),
        ),
        in_specs=[pl.BlockSpec(memory_space=pl.ANY)] * len(pieces),
        out_specs=(pl.BlockSpec(memory_space=pltpu.VMEM), pl.BlockSpec(memory_space=pltpu.VMEM)),
        scratch_shapes=[
            pltpu.VMEM((blocks, rows, width), kind),
            dma((len(pieces),)),
            pltpu.VMEM((count, rows, width), kind),
            pltpu.VMEM((n1, rows, width), kind),
            pltpu.VMEM((n2, rows, width), kind),
            pltpu.VMEM((n3, rows, width), kind),
            dma((count,)), dma((count,)),
            dma((n1,)), dma((n1,)),
            dma((n2,)), dma((n2,)),
            dma((n3,)), dma((n3,)),
            dma((1, sends_of(route))), dma((1, blocks)),
        ],
        compiler_params=pltpu.CompilerParams(
            collective_id=collective_id, has_side_effects=True, vmem_limit_bytes=VMEM_BYTES
        ),
    )(*pieces)


def last_kernel(count, *refs):
    for source, target in zip(refs[:count], refs[count:]):
        target[...] = source[...].astype(target.dtype)


def per_device(
    block_input, lengths, spans, cotangent, ffn_in, ffn_out, qkv_weight, out_weight, conv_in, kernel, conv_out, vectors,
):
    _, rows, width = block_input.shape
    count = lax.axis_size("batch")
    core = lax.axis_index("seq")
    shard = ffn_in.shape[1]
    blocks = 2 * count
    hidden = shard * blocks
    heads, size = HEADS, width // HEADS
    keys = 2 * rows
    taps = kernel.shape[0]
    inside = shard % 64 == 0 and width == 16 * blocks
    route = Routes(count)
    vm, dma = pltpu.VMEM, pltpu.SemaphoreType.DMA
    weights = (2, 8, 2, 2, hidden // 32, width)
    if inside:
        shards = dict(ffn_in=ffn_in, ffn_out=ffn_out)
    else:
        got = jnp.stack([ffn_in, ffn_out], axis=1).reshape(2, 2 * shard, width)
        got = gather_all(got, count, 1).reshape(2, blocks, 2, shard, width)
        shards = dict(shards=got.transpose(0, 2, 1, 3, 4).reshape(2, *weights))
    square, tall = (rows, width), (hidden, rows)
    here, hbm = pl.BlockSpec(memory_space=pltpu.VMEM), pl.BlockSpec(memory_space=pl.ANY)
    scalars = dict(lengths=lengths, spans=spans)
    late = dict(x_in=block_input[0], vec=vectors, kern=kernel, cot=cotangent[0], w_att=out_weight, conv_in=conv_in, conv_out=conv_out, qkv=qkv_weight)
    ins = scalars | {f"{key}_far": value for key, value in late.items()} | shards
    in_specs = [pl.BlockSpec(memory_space=pltpu.SMEM)] * len(scalars)
    in_specs += [hbm] * (len(late) + len(shards))
    lent = dict(
        out=(square, LOW), input_grad=(square, F32), d_att=((width, width), LOW), d_conv_in=((width, 2 * width), LOW),
        d_conv_out=((width, width), LOW),
    )
    outs = {f"far_{key}": (*value, hbm) for key, value in lent.items()} | dict(
        far_g=(weights, LOW, hbm), far_act=(tall, LOW, hbm), far_slope=(tall, LOW, hbm),
    )
    if inside:
        outs |= dict(
            fin_in=((2, shard, width), F32, here), fin_out=((2, shard, width), F32, here),
            d_qkv=((3, width, width // 2), LOW, here), d_kern=((taps, width), F32, here), d_vec=((12, width), F32, here),
        )
    else:
        outs |= dict(
            d_qkv=((3, width, width), LOW, here), small=((taps + 16, width), F32, here),
            d_ffn=((2, *weights), LOW, hbm),
        )
    scratch = dict(
        g0=vm(weights, LOW), g1=vm(weights, LOW), act=vm(tall, LOW), slope=vm(tall, LOW), qkvT=vm((3, width, width), LOW),
        x1=vm(square, F32), x2=vm(square, F32), grad=vm(square, F32), depth=vm(square, F32),
        dz=vm(square, F32), pad=vm((rows + 2 * HALO, width), F32), halo=vm((2, HALO, width), F32),
        h0=vm(square, LOW), h_all=vm((keys, width), LOW), h3=vm(square, LOW), key=vm((heads // 2, keys, 128), LOW),
        qT=vm((heads, size, rows), LOW), oT=vm((width, rows), LOW), doT=vm((heads, size, rows), LOW),
        top=vm((heads, rows), F32), extra=vm((keys, 128), LOW), wide=vm((taps, 8, width), F32), sums=vm((16, width), F32),
        own_v=vm(square, LOW),
        rk=vm((heads // 2, rows, 128), LOW), rv=vm((heads // 2, rows, 128), LOW), dq=vm(square, LOW),
        x_in=vm(square, LOW), vec=vm((12, width), F32), kern=vm((taps, width), F32), **{k: vm(*v) for k, v in lent.items()},
        local=dma((26,)), swap=dma((12,)), qkv_mine=vm(qkv_weight.shape, LOW), cot=vm(square, LOW),
        w_att=vm((width, width), LOW), conv_in=vm((width, 2 * width), LOW), conv_out=vm((width, width), LOW),
    )
    for name, lines in (("a", 16), ("b", 8), ("c", 16))[: 3 if inside else 2]:
        scratch[f"part_{name}"] = vm((lines, 128), F32)
        for key, kind in zip(("pair", "slots", "pair_sems", "sends", "recvs"), Everyone.scratch(count, lines)):
            scratch[f"{key}_{name}"] = kind
    if not inside:
        scratch |= dict(spare=vm((width, rows), LOW), spare_wide=vm((rows, 2 * width), LOW))
    if inside:
        for key, shape in zip(("zero", "one", "two", "three"), ((4, 2, 2), (4, 2), (4,), (3,))):
            scratch[key] = vm((6, *shape, shard, width), LOW)
        scratch |= dict(
            box=vm((2, 8, 2, 2, 64, width), LOW), held=vm((2, 8, 2, 2, 64, width), LOW), small=vm((taps + 16, width), F32),
            g_send=dma((4, 11)), g_recv=dma((4, 4, 4)), r_send=dma((5, 4)), r_recv=dma((5, 4, 4)),
        )
    cfg = SimpleNamespace(
        names=[*ins, *outs, *scratch], count=count, shard=shard, hidden=hidden, heads=heads, inside=inside
    )
    results = pl.pallas_call(
        functools.partial(layer_kernel, cfg),
        out_shape=tuple(jax.ShapeDtypeStruct(shape, kind) for shape, kind, _ in outs.values()),
        in_specs=in_specs,
        out_specs=tuple(spec for _, _, spec in outs.values()),
        scratch_shapes=list(scratch.values()),
        compiler_params=pltpu.CompilerParams(collective_id=0, has_side_effects=True, vmem_limit_bytes=VMEM_BYTES),
    )(*ins.values())
    got = SimpleNamespace(**dict(zip(outs, results)))
    if inside:
        plain = [got.far_out, got.far_input_grad, got.fin_in, got.fin_out, got.d_kern, got.d_vec]
        wide = [got.d_qkv, got.far_d_att, got.far_d_conv_in, got.far_d_conv_out]
        shapes = [(v.shape, v.dtype) for v in plain] + [(v.shape, F32) for v in wide]
        steps = 4

        def part(shape):
            if shape[-2] % (8 * steps):
                return pl.BlockSpec(shape, lambda i: (0,) * len(shape))
            lines = shape[-2] // steps
            return pl.BlockSpec((*shape[:-2], lines, shape[-1]), lambda i: (0,) * (len(shape) - 2) + (i, 0))

        parts = [part(shape) for shape, _ in shapes]
        done = pl.pallas_call(
            functools.partial(last_kernel, len(shapes)),
            grid=(steps,),
            out_shape=tuple(jax.ShapeDtypeStruct(*shape) for shape in shapes),
            in_specs=parts,
            out_specs=tuple(parts),
            compiler_params=pltpu.CompilerParams(vmem_limit_bytes=VMEM_BYTES),
        )(*plain, *wide)
        out, input_grad, fin_in, fin_out, d_kern, d_vec, d_qkv, d_att, d_conv_in, d_conv_out = done
        return (
            out[None], input_grad[None], fin_in, fin_out, d_qkv, d_att, d_conv_in, d_kern, d_conv_out, d_vec,
        )

    def spread(values):
        flat = values.astype(LOW).reshape(-1, width)
        lines = -(-flat.shape[0] // blocks)
        flat = jnp.pad(flat, ((0, lines * blocks - flat.shape[0]), (0, 0)))
        return flat.reshape(blocks, lines, width)

    lines = 3 * width // (2 * count)
    per_core = got.d_qkv.reshape(3 * width, 2, width // 2).transpose(1, 0, 2).reshape(blocks, -1, width)
    d_in0, d_out0, d_in1, d_out1 = (got.d_ffn[j, m].reshape(hidden, width) for j in range(2) for m in range(2))
    rest = (got.far_d_att, got.far_d_conv_in, got.far_d_conv_out, got.small)
    pieces = [spread(v) for v in (d_in0, d_out0, d_in1, d_out1, *rest)] + [per_core]
    fin, shared = reduce_all(pieces, 4 * shard, count, 2)
    at = 0
    whole = []
    for piece, like in zip(pieces[4:8], rest):
        part = shared[0, :, at : at + piece.shape[1]].reshape(-1, width)
        whole.append(part[: like.size // width].reshape(like.shape).astype(F32))
        at += piece.shape[1]
    mine = lax.dynamic_slice_in_dim(shared[0], core * count, count, axis=0)[:, at : at + per_core.shape[1]]
    row = lax.broadcasted_iota(jnp.int32, (12, 1), 0)
    d_vec = jnp.where((row == 6) | (row == 7), got.small[taps : taps + 12], whole[3][taps : taps + 12])
    return (
        got.far_out[None], got.far_input_grad[None], jnp.stack([fin[:shard], fin[2 * shard : 3 * shard]]),
        jnp.stack([fin[shard : 2 * shard], fin[3 * shard :]]),
        mine.reshape(3, width, width // 2).astype(F32), whole[0], whole[1], whole[3][:taps], whole[2], d_vec,
    )


def solution(mesh):
    placed = (
        P("batch", "seq", None),
        P("batch"),
        P("batch", None),
        P("batch", "seq", None),
        P(None, ("seq", "batch"), None),
        P(None, ("seq", "batch"), None),
        P(None, None, "seq"),
        P(),
        P(),
        P(),
        P(),
        P(),
    )
    return jax.shard_map(
        per_device,
        mesh=mesh,
        in_specs=placed,
        out_specs=(
            P("batch", "seq", None),
            P("batch", "seq", None),
            P(None, ("seq", "batch"), None),
            P(None, ("seq", "batch"), None),
            P(None, None, "seq"),
            P(),
            P(),
            P(),
            P(),
            P(),
        ),
        check_vma=False,
    )
```
